32 devices in a mesh: grp: 2 (over x), pipe: 2 (over core), patch: 8 (over z, y).
Axes of the slice: x: 2, y: 2, z: 4, core: 2. Of those that a mesh axis runs over, the one named last changes fastest.
Arguments:
- tokens: bfloat16 [2, 512, 1152], P(None, ('grp', 'patch')), parts along dimension 1, may hold values from -6 to 6
- stale_kv: bfloat16 [2, 2, 512, 1152], P('pipe', None, ('grp', 'patch')), parts along dimension 2, may hold values from -40 to 40
- w_qkv: bfloat16 [2, 1152, 1728], P('pipe'), may hold values from -0.1875 to 0.1875
- w_out: bfloat16 [2, 576, 1152], P('pipe'), may hold values from -0.25 to 0.25
- block_table: float32 [2, 3, 1152], P('pipe'), may hold values from -3 to 3
- time_table: float32 [100, 5, 1152], replicated, may hold values from -3 to 3
- t_index: int32 [2], P('grp'), parts along dimension 0, may hold values from 0 to 99
- w_final: bfloat16 [1152, 16], replicated, may hold values from -0.1875 to 0.1875
- w_in: bfloat16 [36, 512], replicated, may hold values from -1 to 1
- b_in: float32 [512], replicated, may hold values from -3 to 3
- w_up: bfloat16 [9, 512, 512], replicated, may hold values from -0.09375 to 0.09375
- b_up: float32 [512], replicated, may hold values from -3 to 3
Outputs:
- decoded: bfloat16 [16, 1024, 512], P(('grp', 'pipe'), 'patch'), parts along dimension 0
The draws below stay inside these ranges and needn't reach their ends.
There are 2 independent parts, one for each index of `grp`. The reference program is written for one: setup_inputs(seed, part) draws one part's arguments, and reference() takes and returns one part's arrays. A program takes and returns all parts, laid end to end along the dimension named above; an argument that names none is the same for every part. Nothing has to cross between parts.
All inputs are finite; a program needn't handle non-finite values.
Results may differ from the reference program's by a relative error of at most 0.03.
Values may be sent and summed in bfloat16 or wider, within the bound.
No kernel may reach another device: no remote copies, remote signals or barrier semaphores. Data moves between devices by JAX's collectives and lax.ppermute only.
A program may use at most 128 MiB of HBM per device.

```python
import math
import jax
import jax.numpy as jnp
from jax import lax

D = 1152
DH = 72
HEADS = 8
CH = 512
LATC = 4
TC = 256
TSTEPS = 100
MICRO = 2
BLK = 2
DA = 576
TOK_MB = 256
RPM = 1
LH = 4
LW = 512


def draw_stale_kv(key, part):
    half_shape = (BLK, MICRO, TOK_MB, DA)
    key_keys, key_noise = jax.random.split(key, 2)
    keys = jnp.clip(1.6 * jax.random.normal(key_keys, half_shape, jnp.float32), -9.6, 9.6)
    noise = jnp.clip(jax.random.normal(key_noise, half_shape, jnp.float32), -6.0, 6.0)
    values = 0.8 * keys + 0.6 * noise
    return jnp.concatenate([keys, values], axis=-1).astype(jnp.bfloat16)


def level_of(own_key, dims, cuts, smallest, largest):
    level, own = 1.0, jax.random.fold_in(own_key, 6)
    for position, blocks in cuts:
        heights = jnp.exp(jax.random.uniform(jax.random.fold_in(own, position), (blocks,), jnp.float32, smallest / len(cuts), largest / len(cuts)))
        level = level * jnp.repeat(heights, dims[position] // blocks).reshape([-1 if axis == position else 1 for axis in range(len(dims))])
    return level


def scatter_about(rng, extent, width, bound, shards=(), dtype=jnp.bfloat16):
    entries = jax.random.normal(rng, extent, jnp.float32) * width
    if len(shards) > 0:
        entries = level_of(rng, extent, shards, -0.22, 0.18) * entries
    return jnp.clip(entries, min=-bound, max=bound).astype(dtype)


def setup_inputs(seed: int = 0, part: int = 0) -> dict:
    key_list = jax.random.split(jax.random.key(seed), 13)
    part_splits = jax.random.split(jax.random.fold_in(key_list[12], part), 13)
    return {
        "tokens": scatter_about(part_splits[0], (MICRO, TOK_MB, D), 1.0, 6.0, ((1, 8),)),
        "stale_kv": draw_stale_kv(jax.random.fold_in(jax.random.fold_in(key_list[12], part), 71), part),
        "w_qkv": scatter_about(key_list[2], (BLK, D, 3 * DA), D ** -0.5, 0.1875, ((0, 2),)),
        "w_out": scatter_about(key_list[3], (BLK, DA, D), DA ** -0.5, 0.25, ((0, 2),)),
        "block_table": scatter_about(key_list[4], (BLK, 3, D), 0.5, 3.0, ((0, 2),), jnp.float32),
        "time_table": scatter_about(key_list[5], (TSTEPS, 5, D), 0.5, 3.0, (), jnp.float32),
        "t_index": jax.random.randint(part_splits[6], (1,), 0, TSTEPS).astype(jnp.int32),
        "w_final": scatter_about(key_list[7], (D, 4 * LATC), D ** -0.5, 0.1875),
        "w_in": scatter_about(key_list[8], (9 * LATC, CH), (9 * LATC) ** -0.5, 1.0),
        "b_in": scatter_about(key_list[9], (CH,), 0.5, 3.0, (), jnp.float32),
        "w_up": scatter_about(key_list[10], (9, CH, CH), (9 * CH) ** -0.5, 0.09375),
        "b_up": scatter_about(key_list[11], (CH,), 0.5, 3.0, (), jnp.float32),
    }


EPSILON = 1e-06

def layer_norm(values):
    widened = values.astype(jnp.float32)
    average = lax.optimization_barrier(jnp.mean(widened, axis=-1, keepdims=True))
    centred = widened - average
    variance = lax.optimization_barrier(jnp.mean(centred * centred, axis=-1, keepdims=True))
    return centred * lax.rsqrt(variance + EPSILON)

def attend(query, key_value):
    count = query.shape[0]
    total_keys = key_value.shape[0]
    query_heads = query.reshape(count, HEADS, DH).transpose(1, 0, 2)
    key_heads = key_value[:, :DA].reshape(total_keys, HEADS, DH).transpose(1, 0, 2)
    value_heads = key_value[:, DA:].reshape(total_keys, HEADS, DH).transpose(1, 0, 2)

    def one_head(head_args):
        query_head, key_head, value_head = head_args
        scores = jnp.dot(query_head, key_head.T, preferred_element_type=jnp.float32) * (1.0 / math.sqrt(DH))
        row_top = lax.optimization_barrier(jnp.max(scores, axis=1, keepdims=True))
        exponent = jnp.exp(scores - row_top)
        row_total = lax.optimization_barrier(jnp.sum(exponent, axis=1, keepdims=True))
        weights = exponent.astype(jnp.bfloat16)
        numerator = jnp.dot(weights, value_head, preferred_element_type=jnp.float32)
        return numerator / row_total
    heads_out = lax.map(one_head, (query_heads, key_heads, value_heads))
    return heads_out.transpose(1, 0, 2).reshape(count, DA).astype(jnp.bfloat16)

def convolve(padded, weights, out_rows, out_cols):
    total = jnp.zeros((out_rows, out_cols, weights.shape[-1]), jnp.float32)
    for offset_row in range(3):
        for offset_col in range(3):
            window = padded[offset_row:offset_row + out_rows, offset_col:offset_col + out_cols]
            total = total + jnp.dot(window, weights[offset_row * 3 + offset_col], preferred_element_type=jnp.float32)
    return total

def reference(tokens, stale_kv, w_qkv, w_out, block_table, time_table, t_index, w_final, w_in, b_in, w_up, b_up):
    time_row = lax.dynamic_index_in_dim(time_table, t_index[0].astype(jnp.int32), 0, keepdims=False)
    state = tokens
    for block_index in range(BLK):
        shift_vec = time_row[0] + block_table[block_index, 0]
        scale_vec = time_row[1] + block_table[block_index, 1]
        gate_vec = time_row[2] + block_table[block_index, 2]
        kv_table = stale_kv[block_index]
        for micro_index in range(MICRO):
            block_input = state[micro_index]
            modulated = (layer_norm(block_input) * (1.0 + scale_vec) + shift_vec).astype(jnp.bfloat16)
            projected = jnp.dot(modulated, w_qkv[block_index], preferred_element_type=jnp.float32)
            query = projected[:, :DA].astype(jnp.bfloat16)
            fresh = projected[:, DA:].astype(jnp.bfloat16)
            kv_table = kv_table.at[micro_index].set(fresh)
            attended = attend(query, kv_table.reshape(MICRO * TOK_MB, 2 * DA))
            branch = jnp.dot(attended, w_out[block_index], preferred_element_type=jnp.float32)
            x_next = (block_input.astype(jnp.float32) + gate_vec * branch).astype(jnp.bfloat16)
            state = state.at[micro_index].set(x_next)
    final_input = (layer_norm(state) * (1.0 + time_row[4]) + time_row[3]).astype(jnp.bfloat16)
    patch_values = jnp.dot(final_input.reshape(MICRO * TOK_MB, D), w_final, preferred_element_type=jnp.float32).astype(jnp.bfloat16)
    latent_image = patch_values.reshape(MICRO, RPM, TC, 2, 2, LATC).transpose(0, 1, 3, 2, 4, 5).reshape(LH, LW, LATC)
    padded_latent = jnp.pad(latent_image, ((1, 1), (1, 1), (0, 0)))
    activation = convolve(padded_latent, w_in.reshape(9, LATC, CH), LH, LW) + b_in
    features = jax.nn.silu(activation).astype(jnp.bfloat16)
    upsampled = jnp.repeat(jnp.repeat(features, 2, axis=0), 2, axis=1)
    padded_up = jnp.pad(upsampled, ((1, 1), (1, 1), (0, 0)))
    decoded = convolve(padded_up, w_up, 2 * LH, 2 * LW) + b_up
    return decoded.astype(jnp.bfloat16)
```

```python
import math

import jax
import jax.numpy as jnp
import numpy as np
from jax import lax
from jax.sharding import PartitionSpec as P

D = 1152
DH = 72
HEADS = 8
CH = 512
LATC = 4
TC = 256
DA = 576

EPSILON = 1e-06


def layer_norm(values):
    widened = values.astype(jnp.float32)
    average = jnp.mean(widened, axis=-1, keepdims=True)
    centred = widened - average
    variance = jnp.mean(centred * centred, axis=-1, keepdims=True)
    return centred * lax.rsqrt(variance + EPSILON)


def modulate(values, scale, shift):
    return (layer_norm(values) * (1.0 + scale) + shift).astype(jnp.bfloat16)


def attend(query, first, second):
    count = query.shape[0]
    total_keys = first.shape[0] + second.shape[0]
    key_value = jnp.concatenate([first, second], axis=0)
    keys = key_value[:, :DA].reshape(total_keys, HEADS, DH).transpose(1, 0, 2)
    values = key_value[:, DA:].reshape(total_keys, HEADS, DH).transpose(1, 0, 2)
    queries = query.reshape(count, HEADS, DH).transpose(1, 0, 2)

    def one_head(args):
        q, k, v = args
        scores = jnp.dot(q, k.T, preferred_element_type=jnp.float32) * (1.0 / math.sqrt(DH))
        exponent = jnp.exp(scores - jnp.max(scores, axis=1, keepdims=True))
        total = jnp.sum(exponent, axis=1, keepdims=True)
        return jnp.dot(exponent.astype(jnp.bfloat16), v, preferred_element_type=jnp.float32) / total

    if count * total_keys <= 256 * 512:
        heads = jnp.stack([one_head((queries[h], keys[h], values[h])) for h in range(HEADS)])
    else:
        heads = lax.map(one_head, (queries, keys, values))
    return heads.transpose(1, 0, 2).reshape(count, DA).astype(jnp.bfloat16)


def convolve(padded, weights, out_rows, out_cols):
    total = jnp.zeros((out_rows, out_cols, weights.shape[-1]), jnp.float32)
    for offset_row in range(3):
        for offset_col in range(3):
            window = padded[offset_row : offset_row + out_rows, offset_col : offset_col + out_cols]
            total = total + jnp.dot(
                window, weights[offset_row * 3 + offset_col], preferred_element_type=jnp.float32
            )
    return total


def patch_selector():
    sel = np.zeros((3, 3, 2, 2, LATC, 2, 2, 9 * LATC), np.float32)
    for dr in range(3):
        for ds in range(3):
            for pp in range(2):
                for qq in range(2):
                    for p in range(2):
                        for q in range(2):
                            dy = 2 * (dr - 1) + pp - p
                            dx = 2 * (ds - 1) + qq - q
                            if abs(dy) <= 1 and abs(dx) <= 1:
                                tap = (dy + 1) * 3 + dx + 1
                                for c in range(LATC):
                                    sel[dr, ds, pp, qq, c, p, q, tap * LATC + c] = 1.0
    return sel.reshape(-1, 9 * LATC)


def local(
    tokens,
    stale_kv,
    w_qkv,
    w_out,
    block_table,
    time_table,
    t_index,
    w_final,
    w_in,
    b_in,
    w_up,
    b_up,
):
    section = lax.axis_index("pipe")
    tile = lax.axis_index("patch")
    n_tiles = lax.axis_size("patch")
    swap = [(0, 1), (1, 0)]
    first_core = section == 0

    time_row = lax.dynamic_index_in_dim(time_table, t_index[0], 0, keepdims=False)
    own_tokens = lax.dynamic_index_in_dim(tokens, section, 0, keepdims=False)
    gathered = lax.all_gather(
        jnp.stack([own_tokens, stale_kv[0, 1]]), "patch", axis=1, tiled=True
    )
    x, stale = gathered[0], gathered[1]
    w_qkv_other = lax.ppermute(w_qkv[0], "pipe", swap)
    w_out_other = lax.ppermute(w_out[0], "pipe", swap)
    table_other = lax.ppermute(block_table[0], "pipe", swap)

    def of_block(block, own, other):
        return jnp.where(section == block, own, other)

    count = x.shape[0]
    rows = count // TC
    cols = TC // n_tiles
    wanted = None
    for block in range(2):
        table = of_block(block, block_table[0], table_other)
        w_block = of_block(block, w_qkv[0], w_qkv_other)
        wo_block = of_block(block, w_out[0], w_out_other)
        shift, scale, gate = (time_row[i] + table[i] for i in range(3))
        modulated = modulate(x, scale, shift)
        fresh = jnp.dot(modulated, w_block[:, DA:], preferred_element_type=jnp.float32).astype(
            jnp.bfloat16
        )
        if block == 0:
            got = lax.ppermute(fresh, "pipe", [(0, 1)])
            second = jnp.where(first_core, stale, got)
            asking, asking_x = modulated, x
        else:
            second = lax.ppermute(jnp.where(first_core, fresh, stale), "pipe", swap)

            def tile_of(a):
                grid = jnp.pad(a.reshape(rows, TC, D), ((0, 0), (1, 1), (0, 0)))
                cut = lax.dynamic_slice_in_dim(grid, tile * cols, cols + 2, 1)
                return cut.reshape(rows * (cols + 2), D)

            asking, asking_x = tile_of(modulated), tile_of(x)
        query = jnp.dot(asking, w_block[:, :DA], preferred_element_type=jnp.float32).astype(
            jnp.bfloat16
        )
        attended = attend(query, fresh, second)
        branch = jnp.dot(attended, wo_block, preferred_element_type=jnp.float32)
        x = (asking_x.astype(jnp.float32) + gate * branch).astype(jnp.bfloat16)

    final_input = modulate(x, time_row[4], time_row[3])
    patches = jnp.dot(final_input, w_final, preferred_element_type=jnp.float32).astype(jnp.bfloat16)
    patches = patches.reshape(rows, cols + 2, 4 * LATC)
    col_ids = tile * cols + jnp.arange(cols + 2) - 1
    inside = (col_ids >= 0) & (col_ids < TC)
    patches = jnp.where(inside[None, :, None], patches, jnp.zeros_like(patches))
    edge = jnp.where(first_core, patches[rows - 1], patches[0])
    got = lax.ppermute(edge, "pipe", swap)
    nothing = jnp.zeros_like(got)
    rim = jnp.concatenate(
        [
            jnp.where(first_core, nothing, got)[None],
            patches,
            jnp.where(first_core, got, nothing)[None],
        ],
        axis=0,
    )

    w_patch = (
        jnp.dot(jnp.asarray(patch_selector(), jnp.bfloat16), w_in, preferred_element_type=jnp.float32)
        .astype(jnp.bfloat16)
        .reshape(9 * 4 * LATC, 4 * CH)
    )
    wide = jnp.pad(rim, ((1, 1), (1, 1), (0, 0)))
    around = jnp.concatenate(
        [wide[i : i + rows + 2, j : j + cols + 2] for i in range(3) for j in range(3)], axis=-1
    )
    activation = jnp.dot(
        around.reshape((rows + 2) * (cols + 2), 9 * 4 * LATC), w_patch, preferred_element_type=jnp.float32
    ).reshape(rows + 2, cols + 2, 2, 2, CH)
    features = jax.nn.silu(activation + b_in).astype(jnp.bfloat16)
    features = features.transpose(0, 2, 1, 3, 4).reshape(2 * rows + 4, 2 * cols + 4, CH)[1:-1, 1:-1]
    row_ids = section * 2 * rows + jnp.arange(2 * rows + 2) - 1
    pixel_ids = tile * 2 * cols + jnp.arange(2 * cols + 2) - 1
    inside_rows = (row_ids >= 0) & (row_ids < 4 * rows)
    inside_cols = (pixel_ids >= 0) & (pixel_ids < 2 * TC)
    features = jnp.where(
        (inside_rows[:, None] & inside_cols[None, :])[:, :, None], features, jnp.zeros_like(features)
    )
    upsampled = jnp.repeat(jnp.repeat(features, 2, axis=0), 2, axis=1)[1:-1, 1:-1]
    decoded = convolve(upsampled, w_up, 4 * rows, 4 * cols) + b_up
    return decoded.astype(jnp.bfloat16)


def solution(mesh):
    placed = (
        P(None, ("grp", "patch"), None),
        P("pipe", None, ("grp", "patch"), None),
        P("pipe", None, None),
        P("pipe", None, None),
        P("pipe", None, None),
        P(),
        P("grp"),
        P(),
        P(),
        P(),
        P(),
        P(),
    )
    return jax.shard_map(
        local,
        mesh=mesh,
        in_specs=placed,
        out_specs=P(("grp", "pipe"), "patch", None),
        check_vma=False,
    )
```

```python
import math

import jax
import jax.numpy as jnp
import numpy as np
from jax import lax
from jax.sharding import PartitionSpec as P

D = 1152
DH = 72
HEADS = 8
CH = 512
LATC = 4
TC = 256
DA = 576

EPSILON = 1e-06


def layer_norm(values):
    widened = values.astype(jnp.float32)
    average = jnp.mean(widened, axis=-1, keepdims=True)
    centred = widened - average
    variance = jnp.mean(centred * centred, axis=-1, keepdims=True)
    return centred * lax.rsqrt(variance + EPSILON)


def modulate(values, scale, shift):
    return (layer_norm(values) * (1.0 + scale) + shift).astype(jnp.bfloat16)


def attend(query, first, second):
    count = query.shape[0]
    total_keys = first.shape[0] + second.shape[0]
    key_value = jnp.concatenate([first, second], axis=0)
    keys = key_value[:, :DA].reshape(total_keys, HEADS, DH).transpose(1, 0, 2)
    values = key_value[:, DA:].reshape(total_keys, HEADS, DH).transpose(1, 0, 2)
    queries = query.reshape(count, HEADS, DH).transpose(1, 0, 2)

    def one_head(args):
        q, k, v = args
        scores = jnp.dot(q, k.T, preferred_element_type=jnp.float32) * (1.0 / math.sqrt(DH))
        exponent = jnp.exp(scores - jnp.max(scores, axis=1, keepdims=True))
        total = jnp.sum(exponent, axis=1, keepdims=True)
        return jnp.dot(exponent.astype(jnp.bfloat16), v, preferred_element_type=jnp.float32) / total

    if count * total_keys <= 256 * 512:
        heads = jnp.stack([one_head((queries[h], keys[h], values[h])) for h in range(HEADS)])
    else:
        heads = lax.map(one_head, (queries, keys, values))
    return heads.transpose(1, 0, 2).reshape(count, DA).astype(jnp.bfloat16)


def convolve(padded, weights, out_rows, out_cols):
    total = jnp.zeros((out_rows, out_cols, weights.shape[-1]), jnp.float32)
    for offset_row in range(3):
        for offset_col in range(3):
            window = padded[offset_row : offset_row + out_rows, offset_col : offset_col + out_cols]
            total = total + jnp.dot(
                window, weights[offset_row * 3 + offset_col], preferred_element_type=jnp.float32
            )
    return total


def patch_selector():
    sel = np.zeros((3, 3, 2, 2, LATC, 2, 2, 9 * LATC), np.float32)
    for dr in range(3):
        for ds in range(3):
            for pp in range(2):
                for qq in range(2):
                    for p in range(2):
                        for q in range(2):
                            dy = 2 * (dr - 1) + pp - p
                            dx = 2 * (ds - 1) + qq - q
                            if abs(dy) <= 1 and abs(dx) <= 1:
                                tap = (dy + 1) * 3 + dx + 1
                                for c in range(LATC):
                                    sel[dr, ds, pp, qq, c, p, q, tap * LATC + c] = 1.0
    return sel.reshape(-1, 9 * LATC)


def in_order(pieces, first):
    count = len(pieces)
    twice = jnp.concatenate([jnp.stack(pieces)] * 2, axis=0)
    return lax.dynamic_slice_in_dim(twice, (count - first) % count, count, 0)


def gather_patch(own):
    n = lax.axis_size("patch")
    inner = 2 ** (int(math.log2(n)) // 2)
    outer = n // inner
    here = lax.axis_index("patch")

    def shifted(block, k_outer, k_inner):
        route = []
        for i in range(n):
            o, e = divmod(i, inner)
            route.append(((o + k_outer) % outer * inner + (e + k_inner) % inner, i))
        return lax.ppermute(block, "patch", route)

    column = in_order([own] + [shifted(own, k, 0) for k in range(1, outer)], here // inner)
    pieces = [column] + [shifted(column, 0, k) for k in range(1, inner)]
    both = in_order(pieces, here % inner)
    return both.transpose(1, 0, 2, 3).reshape(n * own.shape[0], own.shape[1])


def local(
    tokens,
    stale_kv,
    w_qkv,
    w_out,
    block_table,
    time_table,
    t_index,
    w_final,
    w_in,
    b_in,
    w_up,
    b_up,
):
    section = lax.axis_index("pipe")
    tile = lax.axis_index("patch")
    n_tiles = lax.axis_size("patch")
    swap = [(0, 1), (1, 0)]
    first_core = section == 0

    time_row = lax.dynamic_index_in_dim(time_table, t_index[0], 0, keepdims=False)
    own_tokens = lax.dynamic_index_in_dim(tokens, section, 0, keepdims=False)
    x = gather_patch(own_tokens)
    stale = gather_patch(stale_kv[0, 1])
    w_qkv_other = lax.ppermute(w_qkv[0], "pipe", swap)
    w_out_other = lax.ppermute(w_out[0], "pipe", swap)
    table_other = lax.ppermute(block_table[0], "pipe", swap)

    def of_block(block, own, other):
        return jnp.where(section == block, own, other)

    count = x.shape[0]
    rows = count // TC
    cols = TC // n_tiles
    wanted = None
    for block in range(2):
        table = of_block(block, block_table[0], table_other)
        w_block = of_block(block, w_qkv[0], w_qkv_other)
        wo_block = of_block(block, w_out[0], w_out_other)
        shift, scale, gate = (time_row[i] + table[i] for i in range(3))
        modulated = modulate(x, scale, shift)
        fresh = jnp.dot(modulated, w_block[:, DA:], preferred_element_type=jnp.float32).astype(
            jnp.bfloat16
        )
        if block == 0:
            got = lax.ppermute(fresh, "pipe", [(0, 1)])
            second = jnp.where(first_core, stale, got)
            asking, asking_x = modulated, x
        else:
            second = lax.ppermute(jnp.where(first_core, fresh, stale), "pipe", swap)

            def tile_of(a):
                grid = jnp.pad(a.reshape(rows, TC, D), ((0, 0), (1, 1), (0, 0)))
                cut = lax.dynamic_slice_in_dim(grid, tile * cols, cols + 2, 1)
                return cut.reshape(rows * (cols + 2), D)

            asking, asking_x = tile_of(modulated), tile_of(x)
        query = jnp.dot(asking, w_block[:, :DA], preferred_element_type=jnp.float32).astype(
            jnp.bfloat16
        )
        attended = attend(query, fresh, second)
        branch = jnp.dot(attended, wo_block, preferred_element_type=jnp.float32)
        x = (asking_x.astype(jnp.float32) + gate * branch).astype(jnp.bfloat16)

    final_input = modulate(x, time_row[4], time_row[3])
    patches = jnp.dot(final_input, w_final, preferred_element_type=jnp.float32).astype(jnp.bfloat16)
    patches = patches.reshape(rows, cols + 2, 4 * LATC)
    col_ids = tile * cols + jnp.arange(cols + 2) - 1
    inside = (col_ids >= 0) & (col_ids < TC)
    patches = jnp.where(inside[None, :, None], patches, jnp.zeros_like(patches))
    edge = jnp.where(first_core, patches[rows - 1], patches[0])
    got = lax.ppermute(edge, "pipe", swap)
    nothing = jnp.zeros_like(got)
    rim = jnp.concatenate(
        [
            jnp.where(first_core, nothing, got)[None],
            patches,
            jnp.where(first_core, got, nothing)[None],
        ],
        axis=0,
    )

    w_patch = (
        jnp.dot(jnp.asarray(patch_selector(), jnp.bfloat16), w_in, preferred_element_type=jnp.float32)
        .astype(jnp.bfloat16)
        .reshape(9 * 4 * LATC, 4 * CH)
    )
    wide = jnp.pad(rim, ((1, 1), (1, 1), (0, 0)))
    around = jnp.concatenate(
        [wide[i : i + rows + 2, j : j + cols + 2] for i in range(3) for j in range(3)], axis=-1
    )
    activation = jnp.dot(
        around.reshape((rows + 2) * (cols + 2), 9 * 4 * LATC), w_patch, preferred_element_type=jnp.float32
    ).reshape(rows + 2, cols + 2, 2, 2, CH)
    features = jax.nn.silu(activation + b_in).astype(jnp.bfloat16)
    features = features.transpose(0, 2, 1, 3, 4).reshape(2 * rows + 4, 2 * cols + 4, CH)[1:-1, 1:-1]
    row_ids = section * 2 * rows + jnp.arange(2 * rows + 2) - 1
    pixel_ids = tile * 2 * cols + jnp.arange(2 * cols + 2) - 1
    inside_rows = (row_ids >= 0) & (row_ids < 4 * rows)
    inside_cols = (pixel_ids >= 0) & (pixel_ids < 2 * TC)
    features = jnp.where(
        (inside_rows[:, None] & inside_cols[None, :])[:, :, None], features, jnp.zeros_like(features)
    )
    upsampled = jnp.repeat(jnp.repeat(features, 2, axis=0), 2, axis=1)[1:-1, 1:-1]
    decoded = convolve(upsampled, w_up, 4 * rows, 4 * cols) + b_up
    return decoded.astype(jnp.bfloat16)


def solution(mesh):
    placed = (
        P(None, ("grp", "patch"), None),
        P("pipe", None, ("grp", "patch"), None),
        P("pipe", None, None),
        P("pipe", None, None),
        P("pipe", None, None),
        P(),
        P("grp"),
        P(),
        P(),
        P(),
        P(),
        P(),
    )
    return jax.shard_map(
        local,
        mesh=mesh,
        in_specs=placed,
        out_specs=P(("grp", "pipe"), "patch", None),
        check_vma=False,
    )
```

```python
import functools
import math

import jax
import jax.numpy as jnp
import numpy as np
from jax import lax
from jax.experimental import pallas as pl
from jax.experimental.pallas import tpu as pltpu
from jax.sharding import PartitionSpec as P

D = 1152
DH = 72
HEADS = 8
CH = 512
LATC = 4
TC = 256
DA = 576
DP = 640
EPSILON = 1e-06
QUERY_SCALE = math.log2(math.e) / math.sqrt(DH)
BLOCK = 256
SMALL_BLOCK = 64
LANES = 128
VMEM_LIMIT = 56 * 1024 * 1024

F32 = jnp.float32
BF16 = jnp.bfloat16
VMEM = pl.BlockSpec(memory_space=pltpu.VMEM)
ANY = pl.BlockSpec(memory_space=pl.ANY)


def dot(a, b):
    return jnp.dot(a, b, preferred_element_type=F32)


def dot_t(a, b):
    return lax.dot_general(a, b, (((1,), (1,)), ((), ())), preferred_element_type=F32)


def normed(values, scale, shift):
    average = jnp.mean(values, axis=-1, keepdims=True)
    centred = values - average
    variance = jnp.mean(centred * centred, axis=-1, keepdims=True)
    return (centred * lax.rsqrt(variance + EPSILON) * scale + shift).astype(BF16)


def scaled_query(projected):
    return (projected * QUERY_SCALE).astype(BF16)


def window(head):
    first = head * DH // LANES * LANES
    last = -(-(head + 1) * DH // LANES) * LANES
    return first, last


def attend(query, k_ref, v_ref):
    count = query.shape[0]
    pieces = [None] * (DP // LANES)
    for head in range(HEADS):
        first, last = window(head)
        lane = lax.broadcasted_iota(jnp.int32, (count, last - first), 1) + first
        own = (lane >= head * DH) & (lane < (head + 1) * DH)
        q = jnp.where(own, query[:, first:last], jnp.zeros((), BF16))
        scores = dot_t(q, k_ref[:, first:last])
        exponent = jnp.exp2(scores - jnp.max(scores, axis=1, keepdims=True))
        total = jnp.sum(exponent, axis=1, keepdims=True)
        numerator = dot(exponent.astype(BF16), v_ref[:, first:last])
        out = jnp.where(own, numerator * (1.0 / total), 0.0)
        for i in range((last - first) // LANES):
            at = first // LANES + i
            part = out[:, i * LANES : (i + 1) * LANES]
            pieces[at] = part if pieces[at] is None else pieces[at] + part
    return jnp.concatenate(pieces, axis=1)


def each_block(count, body):
    if count <= BLOCK:
        body(0, count)
    else:

        @pl.loop(0, count // SMALL_BLOCK)
        def _(i):
            body(pl.multiple_of(i * SMALL_BLOCK, SMALL_BLOCK), SMALL_BLOCK)


def copy_of(block, own, other, target, sem):
    section = lax.axis_index("pipe")

    @pl.when(section == block)
    def _():
        pltpu.make_async_copy(own, target, sem).start()

    @pl.when(section != block)
    def _():
        pltpu.make_async_copy(other, target, sem).start()

    return pltpu.make_async_copy(own, target, sem)


QKV_CUTS = (0, 512, 1024, 1536, 3 * DA)


def project_kernel(n_pieces, *refs):
    piece_refs = refs[:n_pieces]
    vec_ref, own_ref, other_ref, x_ref, q_ref, kv_ref, w_ref, all_ref, sems = refs[n_pieces:]
    cuts = list(zip(QKV_CUTS[:-1], QKV_CUTS[1:]))
    copies = [
        copy_of(0, own_ref.at[0, :, a:b], other_ref.at[0, :, a:b], w_ref.at[:, a:b], sems.at[i])
        for i, (a, b) in enumerate(cuts)
    ]
    at = 0
    for ref in piece_refs:
        rows = ref.shape[0]
        x_ref[at : at + rows] = ref[...]
        at += rows
    waited = [False] * len(cuts)

    def body(start, size):
        values = x_ref[pl.ds(start, size)].astype(F32)
        modulated = normed(values, vec_ref[1:2], vec_ref[0:1])
        for i, (a, b) in enumerate(cuts):
            if not waited[i]:
                copies[i].wait()
            projected = dot(modulated, w_ref[:, a:b])
            if a < DA:
                lane = lax.broadcasted_iota(jnp.int32, projected.shape, 1) + a
                projected = projected * jnp.where(lane < DA, QUERY_SCALE, 1.0)
            all_ref[:, a:b] = projected.astype(BF16)
        rows = pl.ds(start, size)
        q_ref[rows, :DA] = all_ref[:, :DA]
        q_ref[rows, DA:] = jnp.zeros((size, DP - DA), BF16)
        kv_ref[0, rows] = all_ref[:, DA : 2 * DA]
        kv_ref[1, rows] = all_ref[:, 2 * DA :]

    if x_ref.shape[0] > BLOCK:
        for i, copy in enumerate(copies):
            copy.wait()
            waited[i] = True
    each_block(x_ref.shape[0], body)


def project(pieces, vecs, w_own, w_other):
    count = sum(piece.shape[0] for piece in pieces)
    return pl.pallas_call(
        functools.partial(project_kernel, len(pieces)),
        out_shape=(
            jax.ShapeDtypeStruct((count, D), BF16),
            jax.ShapeDtypeStruct((count, DP), BF16),
            jax.ShapeDtypeStruct((2, count, DA), BF16),
        ),
        in_specs=[VMEM] * (len(pieces) + 1) + [ANY] * 2,
        out_specs=(VMEM,) * 3,
        scratch_shapes=[
            pltpu.VMEM((D, 3 * DA), BF16),
            pltpu.VMEM((count if count <= BLOCK else SMALL_BLOCK, 3 * DA), BF16),
            pltpu.SemaphoreType.DMA((len(QKV_CUTS) - 1,)),
        ],
        compiler_params=pltpu.CompilerParams(vmem_limit_bytes=VMEM_LIMIT),
        name="layer_norm_and_projections",
    )(*pieces, vecs, w_own, w_other)


def fill(k_ref, v_ref, at, key, value):
    rows = pl.ds(at, key.shape[0])
    pad = jnp.zeros((key.shape[0], DP - DA), BF16)
    k_ref[rows, :DA] = key
    k_ref[rows, DA:] = pad
    v_ref[rows, :DA] = value
    v_ref[rows, DA:] = pad


def block_kernel(n_pieces, *refs):
    stale_refs = refs[:n_pieces]
    (
        x_ref, q_ref, kv_ref, got_ref, idx_ref, vec_ref, w_own, w_other, wo_own, wo_other,
        xt_ref, qt_ref, kv1_ref, w_ref, wo_ref, k_ref, v_ref, pick_ref, sems,
    ) = refs[n_pieces:]
    count = x_ref.shape[0]
    out_copy = copy_of(0, wo_own.at[0], wo_other.at[0], wo_ref, sems.at[0])
    in_copy = copy_of(1, w_own.at[0], w_other.at[0], w_ref, sems.at[1])
    first_core = lax.axis_index("pipe") == 0
    fill(k_ref, v_ref, 0, kv_ref[0], kv_ref[1])
    at = 0
    for ref in stale_refs:
        rows = ref.shape[0]
        stale = ref[...]
        key = jnp.where(first_core, stale[:, :DA], got_ref[0, at : at + rows])
        value = jnp.where(first_core, stale[:, DA:], got_ref[1, at : at + rows])
        fill(k_ref, v_ref, count + at, key, value)
        at += rows
    pick_ref[...] = jnp.zeros_like(pick_ref)
    tile_rows = idx_ref.shape[0]
    if count > BLOCK:
        out_copy.wait()
        in_copy.wait()

    def body(start, size):
        rows = pl.ds(start, size)
        attended = attend(q_ref[rows], k_ref, v_ref).astype(BF16)
        if count <= BLOCK:
            out_copy.wait()
        branch = dot(attended[:, :DA], wo_ref[...])
        x1 = (x_ref[rows].astype(F32) + vec_ref[2:3] * branch).astype(BF16)
        modulated = normed(x1.astype(F32), vec_ref[4:5], vec_ref[3:4])
        if count <= BLOCK:
            in_copy.wait()
        fresh = dot(modulated, w_ref[:, 512:])
        kv1_ref[0, rows] = fresh[:, DA - 512 : 2 * DA - 512].astype(BF16)
        kv1_ref[1, rows] = fresh[:, 2 * DA - 512 :].astype(BF16)
        lane = lax.broadcasted_iota(jnp.int32, (tile_rows, size), 1) + start
        chosen = (lane == idx_ref[:, :1]).astype(F32).astype(BF16)
        pick_ref[0] += dot(chosen, x1)
        pick_ref[1] += dot(chosen, modulated)

    each_block(count, body)
    xt_ref[...] = pick_ref[0].astype(BF16)
    projected = dot(pick_ref[1].astype(BF16), w_ref[:, :DP])
    query = scaled_query(projected)
    lane = lax.broadcasted_iota(jnp.int32, query.shape, 1)
    qt_ref[...] = jnp.where(lane < DA, query, jnp.zeros((), BF16))


def first_block(stale_pieces, x, q, kv, got, idx, vecs, w_own, w_other, wo_own, wo_other):
    count = x.shape[0]
    tile_rows = idx.shape[0]
    return pl.pallas_call(
        functools.partial(block_kernel, len(stale_pieces)),
        out_shape=(
            jax.ShapeDtypeStruct((tile_rows, D), BF16),
            jax.ShapeDtypeStruct((tile_rows, DP), BF16),
            jax.ShapeDtypeStruct((2, count, DA), BF16),
        ),
        in_specs=[VMEM] * (len(stale_pieces) + 6) + [ANY] * 4,
        out_specs=(VMEM,) * 3,
        scratch_shapes=[
            pltpu.VMEM((D, 3 * DA), BF16),
            pltpu.VMEM((DA, D), BF16),
            pltpu.VMEM((2 * count, DP), BF16),
            pltpu.VMEM((2 * count, DP), BF16),
            pltpu.VMEM((2, tile_rows, D), F32),
            pltpu.SemaphoreType.DMA((2,)),
        ],
        compiler_params=pltpu.CompilerParams(vmem_limit_bytes=VMEM_LIMIT),
        name="attention_and_next_keys",
    )(*stale_pieces, x, q, kv, got, idx, vecs, w_own, w_other, wo_own, wo_other)


def tile_kernel(
    x_ref, q_ref, kv_ref, got_ref, idx_ref, vec_ref, wf_ref, wo_own, wo_other, patch_ref, wo_ref, k_ref, v_ref, sems
):
    count = kv_ref.shape[1]
    out_copy = copy_of(1, wo_own.at[0], wo_other.at[0], wo_ref, sems.at[0])
    fill(k_ref, v_ref, 0, kv_ref[0], kv_ref[1])
    fill(k_ref, v_ref, count, got_ref[0], got_ref[1])
    attended = attend(q_ref[...], k_ref, v_ref).astype(BF16)
    out_copy.wait()
    branch = dot(attended[:, :DA], wo_ref[...])
    x2 = (x_ref[...].astype(F32) + vec_ref[5:6] * branch).astype(BF16)
    final = normed(x2.astype(F32), vec_ref[7:8], vec_ref[6:7])
    patches = dot(final, wf_ref[...]).astype(BF16).astype(F32)
    patch_ref[...] = jnp.where(idx_ref[:, :1] >= 0, patches, 0.0)


def tile_block(x, q, kv, got, idx, vecs, w_final, wo_own, wo_other):
    count = kv.shape[1]
    return pl.pallas_call(
        tile_kernel,
        out_shape=jax.ShapeDtypeStruct((x.shape[0], LANES), F32),
        in_specs=[VMEM] * 7 + [ANY] * 2,
        out_specs=VMEM,
        scratch_shapes=[
            pltpu.VMEM((DA, D), BF16),
            pltpu.VMEM((2 * count, DP), BF16),
            pltpu.VMEM((2 * count, DP), BF16),
            pltpu.SemaphoreType.DMA((1,)),
        ],
        compiler_params=pltpu.CompilerParams(vmem_limit_bytes=VMEM_LIMIT),
        name="tile_attention_and_patches",
    )(x, q, kv, got, idx, vecs, w_final, wo_own, wo_other)


def decode_kernel(
    rows, cols, pitch, patch_ref, got_ref, idx_ref, wp_ref, bin_ref, bup_ref, w_any, out_ref, w_ref, u_ref, ub_ref, sems
):
    copies = [pltpu.make_async_copy(w_any.at[t], w_ref.at[t], sems.at[t]) for t in range(9)]
    order = [3, 4, 5, 0, 1, 2, 6, 7, 8]
    for t in order:
        copies[t].start()
    first_core = lax.axis_index("pipe") == 0
    got = got_ref[...]
    above = jnp.where(first_core, 0.0, got)
    below = jnp.where(first_core, got, 0.0)
    rim = [above] + [patch_ref[r * pitch : (r + 1) * pitch] for r in range(rows)] + [below]
    column_in = idx_ref[:pitch, :1] >= 0
    shifted = [[pltpu.roll(p, (-ds) % pitch, 0) if ds else p for ds in (-1, 0, 1)] for p in rim]
    for r in range(rows + 2):
        low, high = None, None
        for dr in (-1, 0, 1):
            if not 0 <= r + dr < rows + 2:
                continue
            for ds in range(3):
                tap = (dr + 1) * 3 + ds
                piece = shifted[r + dr][ds]
                if tap == 8:
                    high = piece
                else:
                    piece = pltpu.roll(piece, 4 * LATC * tap, 1) if tap else piece
                    low = piece if low is None else low + piece
        high = jnp.zeros_like(low) if high is None else high
        around = jnp.concatenate([low, high], axis=1).astype(BF16)
        for p in range(2):
            y = 2 * (r - 1) + p + 1
            if not 0 <= y < 2 * rows + 2:
                continue
            for q in range(2):
                at = (2 * p + q) * CH
                act = dot(around, wp_ref[:, at : at + CH]) + bin_ref[...]
                feature = act / (1.0 + jnp.exp(-act))
                keep = column_in
                if y == 0:
                    keep = keep & jnp.logical_not(first_core)
                if y == 2 * rows + 1:
                    keep = keep & first_core
                feature = jnp.where(keep, feature, 0.0)
                for c in range(CH // LANES):
                    part = feature[:, c * LANES : (c + 1) * LANES]
                    u_ref[y, c, pl.ds(2 * q, pitch, stride=4), :] = part
                    u_ref[y, c, pl.ds(2 * q + 1, pitch, stride=4), :] = part
    wide = 4 * cols
    for y in range(2 * rows + 2):
        for dx in range(3):
            for c in range(CH // LANES):
                ub_ref[dx, y * wide : (y + 1) * wide, c * LANES : (c + 1) * LANES] = u_ref[
                    y, c, 3 + dx : 3 + dx + wide, :
                ].astype(BF16)

    def tap_row(dy, y_first, y_count):
        total = None
        for dx in range(3):
            copies[3 * dy + dx].wait()
            part = dot(ub_ref[dx, y_first * wide : (y_first + y_count) * wide], w_ref[3 * dy + dx])
            total = part if total is None else total + part
        return total

    def rows_of(total, y):
        return total[y * wide : (y + 1) * wide]

    middle = tap_row(1, 1, 2 * rows) + bup_ref[...]
    before = tap_row(0, 0, 2 * rows + 1)
    after = tap_row(2, 1, 2 * rows + 1)
    for y in range(2 * rows):
        own = rows_of(middle, y)
        out_ref[2 * y] = (own + rows_of(before, y) + rows_of(after, y)).astype(BF16)
        out_ref[2 * y + 1] = (own + rows_of(before, y + 1) + rows_of(after, y + 1)).astype(BF16)


def decode(rows, cols, pitch, patches, got, idx, w_patch, b_in, b_up, w_up):
    return pl.pallas_call(
        functools.partial(decode_kernel, rows, cols, pitch),
        out_shape=jax.ShapeDtypeStruct((4 * rows, 4 * cols, CH), BF16),
        in_specs=[VMEM] * 6 + [ANY],
        out_specs=VMEM,
        scratch_shapes=[
            pltpu.VMEM((9, CH, CH), BF16),
            pltpu.VMEM((2 * rows + 2, CH // LANES, 4 * pitch, LANES), F32),
            pltpu.VMEM((3, (2 * rows + 2) * 4 * cols, CH), BF16),
            pltpu.SemaphoreType.DMA((9,)),
        ],
        compiler_params=pltpu.CompilerParams(vmem_limit_bytes=VMEM_LIMIT),
        name="decoder_convolutions",
    )(patches, got, idx, w_patch, b_in, b_up, w_up)


def patch_selector():
    sel = np.zeros((3, 3, 2, 2, LATC, 2, 2, 9 * LATC), np.float32)
    for dr, ds, pp, qq, p, q in np.ndindex(3, 3, 2, 2, 2, 2):
        dy = 2 * (dr - 1) + pp - p
        dx = 2 * (ds - 1) + qq - q
        if abs(dy) <= 1 and abs(dx) <= 1:
            tap = (dy + 1) * 3 + dx + 1
            for c in range(LATC):
                sel[dr, ds, pp, qq, c, p, q, tap * LATC + c] = 1.0
    return sel.reshape(-1, 9 * LATC)


def split_of(n):
    inner = 2 ** (int(math.log2(n)) // 2)
    return n // inner, inner


def gather_patch(own):
    n = lax.axis_size("patch")
    outer, inner = split_of(n)

    def shifted(block, k_outer, k_inner):
        route = []
        for i in range(n):
            o, e = divmod(i, inner)
            route.append(((o + k_outer) % outer * inner + (e + k_inner) % inner, i))
        return lax.ppermute(block, "patch", route)

    column = jnp.concatenate([own] + [shifted(own, k, 0) for k in range(1, outer)], axis=0)
    return [column] + [shifted(column, 0, k) for k in range(1, inner)]


def local(
    tokens,
    stale_kv,
    w_qkv,
    w_out,
    block_table,
    time_table,
    t_index,
    w_final,
    w_in,
    b_in,
    w_up,
    b_up,
):
    section = lax.axis_index("pipe")
    tile = lax.axis_index("patch")
    n_tiles = lax.axis_size("patch")
    swap = [(0, 1), (1, 0)]
    first_core = section == 0
    own_count = tokens.shape[1]
    count = own_count * n_tiles
    rows = count // TC
    cols = TC // n_tiles
    pitch = -(-(cols + 3) // 8) * 8
    outer, inner = split_of(n_tiles)

    own_tokens = lax.dynamic_index_in_dim(tokens, section, 0, keepdims=False)
    x_pieces = gather_patch(own_tokens)
    stale_pieces = gather_patch(stale_kv[0, 1])
    w_qkv_other = lax.ppermute(w_qkv, "pipe", swap)
    w_out_other = lax.ppermute(w_out, "pipe", swap)
    table_other = lax.ppermute(block_table[0], "pipe", swap)

    time_row = lax.dynamic_index_in_dim(time_table, t_index[0], 0, keepdims=False)
    table = block_table[0]
    table_0 = jnp.where(first_core, table, table_other)
    table_1 = jnp.where(first_core, table_other, table)
    ones = jnp.asarray([[0.0], [1.0], [0.0]], F32)
    vecs = jnp.concatenate(
        [
            time_row[:3] + table_0 + ones,
            time_row[:3] + table_1 + ones,
            time_row[3:5] + ones[:2],
        ],
        axis=0,
    )

    padded_rows = -(-rows * pitch // 16) * 16
    place = jnp.arange(padded_rows)
    column = place % pitch - 1 + tile * cols
    inside = (place % pitch < cols + 2) & (place < rows * pitch) & (column >= 0) & (column < TC)
    token = place // pitch * TC + jnp.clip(column, 0, TC - 1)
    source = token // own_count
    k_outer = (source // inner - tile // inner) % outer
    k_inner = (source % inner - tile % inner) % inner
    spot = (k_inner * outer + k_outer) * own_count + token % own_count
    idx = jnp.broadcast_to(jnp.where(inside, spot, -1)[:, None], (padded_rows, LANES)).astype(jnp.int32)

    w_patch = (
        dot(jnp.asarray(patch_selector(), BF16), w_in).astype(BF16).reshape(9 * 4 * LATC, 4 * CH)
    )
    w_patch = jnp.pad(w_patch, ((0, 2 * LANES - 9 * 4 * LATC), (0, 0)))
    w_final = jnp.pad(w_final, ((0, 0), (0, LANES - 4 * LATC)))

    x, query, fresh = project(x_pieces, vecs, w_qkv, w_qkv_other)
    got = lax.ppermute(fresh, "pipe", [(0, 1)])
    x_tile, q_tile, fresh = first_block(
        stale_pieces, x, query, fresh, got, idx, vecs, w_qkv, w_qkv_other, w_out, w_out_other
    )
    stale = jnp.concatenate(stale_pieces, axis=0)
    stale = jnp.stack([stale[:, :DA], stale[:, DA:]])
    got = lax.ppermute(jnp.where(first_core, fresh, stale), "pipe", swap)
    patches = tile_block(x_tile, q_tile, fresh, got, idx, vecs, w_final, w_out, w_out_other)
    patches = patches[: rows * pitch]
    edge = jnp.where(first_core, patches[(rows - 1) * pitch :], patches[:pitch])
    got = lax.ppermute(edge, "pipe", swap)
    return decode(rows, cols, pitch, patches, got, idx, w_patch, b_in[None], b_up[None], w_up)


def solution(mesh):
    placed = (
        P(None, ("grp", "patch"), None),
        P("pipe", None, ("grp", "patch"), None),
        P("pipe", None, None),
        P("pipe", None, None),
        P("pipe", None, None),
        P(),
        P("grp"),
        P(),
        P(),
        P(),
        P(),
        P(),
    )
    return jax.shard_map(
        local,
        mesh=mesh,
        in_specs=placed,
        out_specs=P(("grp", "pipe"), "patch", None),
        check_vma=False,
    )
```

```python
import functools
import math

import jax
import jax.numpy as jnp
import numpy as np
from jax import lax
from jax.experimental import pallas as pl
from jax.experimental.pallas import tpu as pltpu
from jax.sharding import PartitionSpec as P

D = 1152
DH = 72
HEADS = 8
CH = 512
LATC = 4
TC = 256
DA = 576
DP = 640
SHIFT = 64
EPSILON = 1e-06
QUERY_SCALE = math.log2(math.e) / math.sqrt(DH)
BLOCK = 256
SMALL_BLOCK = 64
LANES = 128

F32 = jnp.float32
BF16 = jnp.bfloat16
VMEM = pl.BlockSpec(memory_space=pltpu.VMEM)
ANY = pl.BlockSpec(memory_space=pl.ANY)


def dot(a, b):
    return jnp.dot(a, b, preferred_element_type=F32)


def dot_t(a, b):
    return lax.dot_general(a, b, (((1,), (1,)), ((), ())), preferred_element_type=F32)


def normed(values, scale, shift):
    average = jnp.mean(values, axis=-1, keepdims=True)
    centred = values - average
    variance = jnp.mean(centred * centred, axis=-1, keepdims=True)
    return (centred * lax.rsqrt(variance + EPSILON) * scale + shift).astype(BF16)


def lane_window(start):
    return start // LANES * LANES, -(-(start + DH) // LANES) * LANES


def attend(query, kv_ref):
    count = query.shape[0]
    pieces = [None] * (DP // LANES)
    for head in range(HEADS):
        first, last = lane_window(head * DH)
        lane = lax.broadcasted_iota(jnp.int32, (count, last - first), 1) + first
        own = (lane >= head * DH) & (lane < (head + 1) * DH)
        q = jnp.where(own, query[:, first:last], jnp.zeros((), BF16))
        scores = dot_t(q, kv_ref[:, first:last])
        exponent = jnp.exp2(scores - jnp.max(scores, axis=1, keepdims=True))
        total = jnp.sum(exponent, axis=1, keepdims=True)
        start = DA + head * DH
        first, last = lane_window(start)
        numerator = dot(exponent.astype(BF16), kv_ref[:, first:last])
        lane = lax.broadcasted_iota(jnp.int32, (count, last - first), 1) + first
        own = (lane >= start) & (lane < start + DH)
        out = jnp.where(own, numerator * (1.0 / total), 0.0)
        for i in range((last - first) // LANES):
            at = (first - (DA - SHIFT)) // LANES + i
            part = out[:, i * LANES : (i + 1) * LANES]
            pieces[at] = part if pieces[at] is None else pieces[at] + part
    return jnp.concatenate(pieces, axis=1)


def each_block(count, body):
    if count <= BLOCK:
        body(0, count)
    else:

        @pl.loop(0, count // SMALL_BLOCK)
        def _(i):
            body(pl.multiple_of(i * SMALL_BLOCK, SMALL_BLOCK), SMALL_BLOCK)


def params(count):
    return pltpu.CompilerParams(vmem_limit_bytes=(24 if count <= BLOCK else 56) * 1024 * 1024)


def copy_of(block, own, other, target, sem):
    section = lax.axis_index("pipe")

    @pl.when(section == block)
    def _():
        pltpu.make_async_copy(own, target, sem).start()

    @pl.when(section != block)
    def _():
        pltpu.make_async_copy(other, target, sem).start()

    return pltpu.make_async_copy(own, target, sem)


def copy_qkv(block, own_ref, other_ref, w_ref, sems):
    return [
        copy_of(block, own_ref.at[0, a:b], other_ref.at[0, a:b], w_ref.at[a:b], sems.at[i])
        for i, (a, b) in enumerate(((0, DA), (DA, 3 * DA)))
    ]


def copy_out(block, own_ref, other_ref, wo_ref, sem):
    return copy_of(block, own_ref.at[0], other_ref.at[0], wo_ref.at[SHIFT:DP], sem)


def query_of(modulated, w_ref):
    projected = dot_t(modulated, w_ref[:DP]) * QUERY_SCALE
    lane = lax.broadcasted_iota(jnp.int32, projected.shape, 1)
    return jnp.where(lane < DA, projected, 0.0).astype(BF16)


def project_kernel(n_pieces, *refs):
    piece_refs = refs[:n_pieces]
    vec_ref, own_ref, other_ref, x_ref, q_ref, kv_ref, w_ref, sems = refs[n_pieces:]
    count = x_ref.shape[0]
    copies = copy_qkv(0, own_ref, other_ref, w_ref, sems)
    at = 0
    for ref in piece_refs:
        rows = ref.shape[0]
        x_ref[at : at + rows] = ref[...]
        at += rows
    if count > BLOCK:
        for copy in copies:
            copy.wait()

    def body(start, size):
        rows = pl.ds(start, size)
        modulated = normed(x_ref[rows].astype(F32), vec_ref[1:2], vec_ref[0:1])
        if count <= BLOCK:
            copies[0].wait()
            copies[1].wait()
        kv_ref[rows] = dot_t(modulated, w_ref[DA:]).astype(BF16)
        q_ref[rows] = query_of(modulated, w_ref)

    each_block(count, body)


def project(pieces, vecs, w_own, w_other):
    count = sum(piece.shape[0] for piece in pieces)
    return pl.pallas_call(
        functools.partial(project_kernel, len(pieces)),
        out_shape=(
            jax.ShapeDtypeStruct((count, D), BF16),
            jax.ShapeDtypeStruct((count, DP), BF16),
            jax.ShapeDtypeStruct((count, 2 * DA), BF16),
        ),
        in_specs=[VMEM] * (len(pieces) + 1) + [ANY] * 2,
        out_specs=(VMEM,) * 3,
        scratch_shapes=[
            pltpu.VMEM((3 * DA, D), BF16),
            pltpu.SemaphoreType.DMA((2,)),
        ],
        compiler_params=params(count),
        name="layer_norm_and_projections",
    )(*pieces, vecs, w_own, w_other)


def block_kernel(n_pieces, *refs):
    stale_refs = refs[:n_pieces]
    (
        x_ref, q_ref, kv_ref, got_ref, idx_ref, vec_ref, w_own, w_other, wo_own, wo_other,
        xt_ref, qt_ref, kv1_ref, send_ref, w_ref, wo_ref, all_ref, pick_ref, sems,
    ) = refs[n_pieces:]
    count = x_ref.shape[0]
    out_copy = copy_out(0, wo_own, wo_other, wo_ref, sems.at[2])
    in_copies = copy_qkv(1, w_own, w_other, w_ref, sems)
    first_core = lax.axis_index("pipe") == 0
    wo_ref[:SHIFT] = jnp.zeros((SHIFT, D), BF16)
    all_ref[:count] = kv_ref[...]
    at = 0
    for ref in stale_refs:
        rows = ref.shape[0]
        all_ref[count + at : count + at + rows] = jnp.where(first_core, ref[...], got_ref[at : at + rows])
        send_ref[at : at + rows] = ref[...]
        at += rows
    pick_ref[...] = jnp.zeros_like(pick_ref)
    tile_rows = idx_ref.shape[0]
    waits = [out_copy] + in_copies
    if count > BLOCK:
        for copy in waits:
            copy.wait()

    def body(start, size):
        rows = pl.ds(start, size)
        attended = attend(q_ref[rows], all_ref).astype(BF16)
        if count <= BLOCK:
            for copy in waits:
                copy.wait()
        branch = dot(attended, wo_ref[...])
        x1 = (x_ref[rows].astype(F32) + vec_ref[2:3] * branch).astype(BF16)
        modulated = normed(x1.astype(F32), vec_ref[4:5], vec_ref[3:4])
        fresh = dot_t(modulated, w_ref[DA:]).astype(BF16)
        kv1_ref[rows] = fresh

        @pl.when(first_core)
        def _():
            send_ref[rows] = fresh

        lane = lax.broadcasted_iota(jnp.int32, (tile_rows, size), 1) + start
        chosen = (lane == idx_ref[:, :1]).astype(F32).astype(BF16)
        pick_ref[0] += dot(chosen, x1)
        pick_ref[1] += dot(chosen, modulated)

    each_block(count, body)
    xt_ref[...] = pick_ref[0].astype(BF16)
    qt_ref[...] = query_of(pick_ref[1].astype(BF16), w_ref)


def first_block(stale_pieces, x, q, kv, got, idx, vecs, w_own, w_other, wo_own, wo_other):
    count = x.shape[0]
    tile_rows = idx.shape[0]
    return pl.pallas_call(
        functools.partial(block_kernel, len(stale_pieces)),
        out_shape=(
            jax.ShapeDtypeStruct((tile_rows, D), BF16),
            jax.ShapeDtypeStruct((tile_rows, DP), BF16),
            jax.ShapeDtypeStruct((count, 2 * DA), BF16),
            jax.ShapeDtypeStruct((count, 2 * DA), BF16),
        ),
        in_specs=[VMEM] * (len(stale_pieces) + 6) + [ANY] * 4,
        out_specs=(VMEM,) * 4,
        scratch_shapes=[
            pltpu.VMEM((3 * DA, D), BF16),
            pltpu.VMEM((DP, D), BF16),
            pltpu.VMEM((2 * count, 2 * DA), BF16),
            pltpu.VMEM((2, tile_rows, D), F32),
            pltpu.SemaphoreType.DMA((3,)),
        ],
        compiler_params=params(count),
        name="attention_and_next_keys",
    )(*stale_pieces, x, q, kv, got, idx, vecs, w_own, w_other, wo_own, wo_other)


def tile_kernel(
    x_ref, q_ref, kv_ref, got_ref, idx_ref, vec_ref, wf_ref, wo_own, wo_other, patch_ref, wo_ref, all_ref, sems
):
    count = kv_ref.shape[0]
    out_copy = copy_out(1, wo_own, wo_other, wo_ref, sems.at[0])
    wo_ref[:SHIFT] = jnp.zeros((SHIFT, D), BF16)
    all_ref[:count] = kv_ref[...]
    all_ref[count:] = got_ref[...]
    attended = attend(q_ref[...], all_ref).astype(BF16)
    out_copy.wait()
    branch = dot(attended, wo_ref[...])
    x2 = (x_ref[...].astype(F32) + vec_ref[5:6] * branch).astype(BF16)
    final = normed(x2.astype(F32), vec_ref[7:8], vec_ref[6:7])
    patches = dot_t(final, wf_ref[...]).astype(BF16).astype(F32)
    patch_ref[...] = jnp.zeros_like(patch_ref)
    patch_ref[:, : 4 * LATC] = jnp.where(idx_ref[:, :1] >= 0, patches, 0.0)


def tile_block(x, q, kv, got, idx, vecs, w_final, wo_own, wo_other):
    count = kv.shape[0]
    return pl.pallas_call(
        tile_kernel,
        out_shape=jax.ShapeDtypeStruct((x.shape[0], LANES), F32),
        in_specs=[VMEM] * 7 + [ANY] * 2,
        out_specs=VMEM,
        scratch_shapes=[
            pltpu.VMEM((DP, D), BF16),
            pltpu.VMEM((2 * count, 2 * DA), BF16),
            pltpu.SemaphoreType.DMA((1,)),
        ],
        compiler_params=params(count),
        name="tile_attention_and_patches",
    )(x, q, kv, got, idx, vecs, w_final, wo_own, wo_other)


def decode_kernel(
    rows, cols, pitch, patch_ref, got_ref, idx_ref, wp_ref, bin_ref, bup_ref, w_any, out_ref, w_ref, u_ref, ub_ref, sems
):
    copies = [pltpu.make_async_copy(w_any.at[t], w_ref.at[t], sems.at[t]) for t in range(9)]
    order = [3, 4, 5, 0, 1, 2, 6, 7, 8]
    for t in order:
        copies[t].start()
    first_core = lax.axis_index("pipe") == 0
    got = got_ref[:pitch]
    above = jnp.where(first_core, 0.0, got)
    below = jnp.where(first_core, got, 0.0)
    rim = [above] + [patch_ref[r * pitch : (r + 1) * pitch] for r in range(rows)] + [below]
    column_in = idx_ref[:pitch, :1] >= 0
    shifted = [[pltpu.roll(p, (-ds) % pitch, 0) if ds else p for ds in (-1, 0, 1)] for p in rim]
    for r in range(rows + 2):
        low, high = None, None
        for dr in (-1, 0, 1):
            if not 0 <= r + dr < rows + 2:
                continue
            for ds in range(3):
                tap = (dr + 1) * 3 + ds
                piece = shifted[r + dr][ds]
                if tap == 8:
                    high = piece
                else:
                    piece = pltpu.roll(piece, 4 * LATC * tap, 1) if tap else piece
                    low = piece if low is None else low + piece
        high = jnp.zeros_like(low) if high is None else high
        around = jnp.concatenate([low, high], axis=1).astype(BF16)
        for p in range(2):
            y = 2 * (r - 1) + p + 1
            if not 0 <= y < 2 * rows + 2:
                continue
            for q in range(2):
                at = (2 * p + q) * 2 * LANES
                act = dot(around, wp_ref[at : at + 2 * LANES]) + bin_ref[...]
                feature = act / (1.0 + jnp.exp(-act))
                keep = column_in
                if y == 0:
                    keep = keep & jnp.logical_not(first_core)
                if y == 2 * rows + 1:
                    keep = keep & first_core
                feature = jnp.where(keep, feature, 0.0)
                for c in range(CH // LANES):
                    part = feature[:, c * LANES : (c + 1) * LANES]
                    u_ref[y, c, pl.ds(2 * q, pitch, stride=4), :] = part
                    u_ref[y, c, pl.ds(2 * q + 1, pitch, stride=4), :] = part
    wide = 4 * cols
    for y in range(2 * rows + 2):
        for dx in range(3):
            for c in range(CH // LANES):
                ub_ref[dx, y * wide : (y + 1) * wide, c * LANES : (c + 1) * LANES] = u_ref[
                    y, c, 3 + dx : 3 + dx + wide, :
                ].astype(BF16)

    def tap_row(dy, y_first, y_count):
        total = None
        for dx in range(3):
            copies[3 * dy + dx].wait()
            part = dot(ub_ref[dx, y_first * wide : (y_first + y_count) * wide], w_ref[3 * dy + dx])
            total = part if total is None else total + part
        return total

    def rows_of(total, y):
        return total[y * wide : (y + 1) * wide]

    middle = tap_row(1, 1, 2 * rows) + bup_ref[...]
    before = tap_row(0, 0, 2 * rows + 1)
    after = tap_row(2, 1, 2 * rows + 1)
    for y in range(2 * rows):
        own = rows_of(middle, y)
        out_ref[2 * y] = (own + rows_of(before, y) + rows_of(after, y)).astype(BF16)
        out_ref[2 * y + 1] = (own + rows_of(before, y + 1) + rows_of(after, y + 1)).astype(BF16)


def decode(rows, cols, pitch, patches, got, idx, w_patch, b_in, b_up, w_up):
    return pl.pallas_call(
        functools.partial(decode_kernel, rows, cols, pitch),
        out_shape=jax.ShapeDtypeStruct((4 * rows, 4 * cols, CH), BF16),
        in_specs=[VMEM] * 6 + [ANY],
        out_specs=VMEM,
        scratch_shapes=[
            pltpu.VMEM((9, CH, CH), BF16),
            pltpu.VMEM((2 * rows + 2, CH // LANES, 4 * pitch, LANES), F32),
            pltpu.VMEM((3, (2 * rows + 2) * 4 * cols, CH), BF16),
            pltpu.SemaphoreType.DMA((9,)),
        ],
        compiler_params=params(0),
        name="decoder_convolutions",
    )(patches, got, idx, w_patch, b_in, b_up, w_up)


def patch_selector():
    sel = np.zeros((2, 2, 3, 3, 2, 2, LATC, 9 * LATC), np.float32)
    for p, q, dr, ds, pp, qq in np.ndindex(2, 2, 3, 3, 2, 2):
        dy = 2 * (dr - 1) + pp - p
        dx = 2 * (ds - 1) + qq - q
        if abs(dy) <= 1 and abs(dx) <= 1:
            tap = (dy + 1) * 3 + dx + 1
            for c in range(LATC):
                sel[p, q, dr, ds, pp, qq, c, tap * LATC + c] = 1.0
    sel = sel.reshape(4, 9 * 4 * LATC, 9 * LATC)
    return np.pad(sel, ((0, 0), (0, 2 * LANES - 9 * 4 * LATC), (0, 0))).reshape(-1, 9 * LATC)


def split_of(n):
    inner = 2 ** (int(math.log2(n)) // 2)
    return n // inner, inner


def shifted(block, k_outer, k_inner):
    n = lax.axis_size("patch")
    outer, inner = split_of(n)
    route = []
    for i in range(n):
        o, e = divmod(i, inner)
        route.append(((o + k_outer) % outer * inner + (e + k_inner) % inner, i))
    return lax.ppermute(block, "patch", route)


def gather_outer(own, outer):
    return jnp.concatenate([own] + [shifted(own, k, 0) for k in range(1, outer)], axis=0)


def gather_inner(column, inner):
    return [column] + [shifted(column, 0, k) for k in range(1, inner)]


def local(
    tokens,
    stale_kv,
    w_qkv,
    w_out,
    block_table,
    time_table,
    t_index,
    w_final,
    w_in,
    b_in,
    w_up,
    b_up,
):
    section = lax.axis_index("pipe")
    tile = lax.axis_index("patch")
    n_tiles = lax.axis_size("patch")
    swap = [(0, 1), (1, 0)]
    first_core = section == 0
    own_count = tokens.shape[1]
    count = own_count * n_tiles
    rows = count // TC
    cols = TC // n_tiles
    pitch = -(-(cols + 3) // 8) * 8
    outer, inner = split_of(n_tiles)

    own_tokens = lax.dynamic_index_in_dim(tokens, section, 0, keepdims=False)
    w_qkv = jnp.swapaxes(w_qkv, 1, 2)
    w_qkv_other = lax.ppermute(w_qkv, "pipe", swap)
    x_column = gather_outer(own_tokens, outer)
    x_column, own_stale = lax.optimization_barrier((x_column, stale_kv[0, 1]))
    x_pieces = gather_inner(x_column, inner)
    stale_pieces = gather_inner(gather_outer(own_stale, outer), inner)
    w_out_other = lax.ppermute(w_out, "pipe", swap)
    table_other = lax.ppermute(block_table[0], "pipe", swap)

    time_row = lax.dynamic_index_in_dim(time_table, t_index[0], 0, keepdims=False)
    table = block_table[0]
    table_0 = jnp.where(first_core, table, table_other)
    table_1 = jnp.where(first_core, table_other, table)
    ones = jnp.asarray([[0.0], [1.0], [0.0]], F32)
    vecs = jnp.concatenate(
        [
            time_row[:3] + table_0 + ones,
            time_row[:3] + table_1 + ones,
            time_row[3:5] + ones[:2],
        ],
        axis=0,
    )

    padded_rows = -(-rows * pitch // 16) * 16
    place = jnp.arange(padded_rows)
    column = place % pitch - 1 + tile * cols
    inside = (place % pitch < cols + 2) & (place < rows * pitch) & (column >= 0) & (column < TC)
    token = place // pitch * TC + jnp.clip(column, 0, TC - 1)
    source = token // own_count
    k_outer = (source // inner - tile // inner) % outer
    k_inner = (source % inner - tile % inner) % inner
    spot = (k_inner * outer + k_outer) * own_count + token % own_count
    idx = jnp.broadcast_to(jnp.where(inside, spot, -1)[:, None], (padded_rows, LANES)).astype(jnp.int32)

    w_patch = dot(jnp.asarray(patch_selector(), BF16), w_in).astype(BF16)
    x_pieces, w_patch, idx = lax.optimization_barrier((x_pieces, w_patch, idx))

    x, query, fresh = project(x_pieces, vecs, w_qkv, w_qkv_other)
    got = lax.ppermute(fresh, "pipe", [(0, 1)])
    x_tile, q_tile, fresh, send = first_block(
        stale_pieces, x, query, fresh, got, idx, vecs, w_qkv, w_qkv_other, w_out, w_out_other
    )
    got = lax.ppermute(send, "pipe", swap)
    patches = tile_block(x_tile, q_tile, fresh, got, idx, vecs, w_final.T, w_out, w_out_other)
    edge = patches
    if rows > 1:
        edge = jnp.where(first_core, patches[(rows - 1) * pitch : rows * pitch], patches[:pitch])
    got = lax.ppermute(edge, "pipe", swap)
    return decode(rows, cols, pitch, patches, got, idx, w_patch, b_in[None], b_up[None], w_up)


def solution(mesh):
    placed = (
        P(None, ("grp", "patch"), None),
        P("pipe", None, ("grp", "patch"), None),
        P("pipe", None, None),
        P("pipe", None, None),
        P("pipe", None, None),
        P(),
        P("grp"),
        P(),
        P(),
        P(),
        P(),
        P(),
    )
    return jax.shard_map(
        local,
        mesh=mesh,
        in_specs=placed,
        out_specs=P(("grp", "pipe"), "patch", None),
        check_vma=False,
    )
```

```python
import functools
import math

import jax
import jax.numpy as jnp
import numpy as np
from jax import lax
from jax.experimental import pallas as pl
from jax.experimental.pallas import tpu as pltpu
from jax.sharding import PartitionSpec as P

D = 1152
DH = 72
HEADS = 8
CH = 512
LATC = 4
TC = 256
DA = 576
DP = 640
SHIFT = 64
EPSILON = 1e-06
QUERY_SCALE = math.log2(math.e) / math.sqrt(DH)
BLOCK = 256
SMALL_BLOCK = 64
LANES = 128

F32 = jnp.float32
BF16 = jnp.bfloat16
VMEM = pl.BlockSpec(memory_space=pltpu.VMEM)
ANY = pl.BlockSpec(memory_space=pl.ANY)


def dot(a, b):
    return jnp.dot(a, b, preferred_element_type=F32)


def dot_t(a, b):
    return lax.dot_general(a, b, (((1,), (1,)), ((), ())), preferred_element_type=F32)


def normed(values, scale, shift):
    average = jnp.mean(values, axis=-1, keepdims=True)
    centred = values - average
    variance = jnp.mean(centred * centred, axis=-1, keepdims=True)
    return (centred * lax.rsqrt(variance + EPSILON) * scale + shift).astype(BF16)


def lane_window(start):
    return start // LANES * LANES, -(-(start + DH) // LANES) * LANES


def attend(query, kv_ref):
    count = query.shape[0]
    pieces = [None] * (DP // LANES)
    for head in range(HEADS):
        first, last = lane_window(head * DH)
        lane = lax.broadcasted_iota(jnp.int32, (count, last - first), 1) + first
        own = (lane >= head * DH) & (lane < (head + 1) * DH)
        q = jnp.where(own, query[:, first:last], jnp.zeros((), BF16))
        scores = dot_t(q, kv_ref[:, first:last])
        exponent = jnp.exp2(scores - jnp.max(scores, axis=1, keepdims=True))
        total = jnp.sum(exponent, axis=1, keepdims=True)
        start = DA + head * DH
        first, last = lane_window(start)
        numerator = dot(exponent.astype(BF16), kv_ref[:, first:last])
        lane = lax.broadcasted_iota(jnp.int32, (count, last - first), 1) + first
        own = (lane >= start) & (lane < start + DH)
        out = jnp.where(own, numerator * (1.0 / total), 0.0)
        for i in range((last - first) // LANES):
            at = (first - (DA - SHIFT)) // LANES + i
            part = out[:, i * LANES : (i + 1) * LANES]
            pieces[at] = part if pieces[at] is None else pieces[at] + part
    return jnp.concatenate(pieces, axis=1)


def each_block(count, body):
    if count <= BLOCK:
        body(0, count)
    else:

        @pl.loop(0, count // SMALL_BLOCK)
        def _(i):
            body(pl.multiple_of(i * SMALL_BLOCK, SMALL_BLOCK), SMALL_BLOCK)


def params(count):
    return pltpu.CompilerParams(vmem_limit_bytes=(24 if count <= BLOCK else 56) * 1024 * 1024)


def copy_of(block, own, other, target, sem):
    section = lax.axis_index("pipe")

    @pl.when(section == block)
    def _():
        pltpu.make_async_copy(own, target, sem).start()

    @pl.when(section != block)
    def _():
        pltpu.make_async_copy(other, target, sem).start()

    return pltpu.make_async_copy(own, target, sem)


def copy_qkv(block, own_ref, other_ref, w_ref, sems):
    return [
        copy_of(block, own_ref.at[0, a:b], other_ref.at[0, a:b], w_ref.at[a:b], sems.at[i])
        for i, (a, b) in enumerate(((0, DA), (DA, 3 * DA)))
    ]


def copy_out(block, own_ref, other_ref, wo_ref, sem):
    return copy_of(block, own_ref.at[0], other_ref.at[0], wo_ref.at[SHIFT:DP], sem)


def query_of(modulated, w_ref):
    projected = dot_t(modulated, w_ref[:DP]) * QUERY_SCALE
    lane = lax.broadcasted_iota(jnp.int32, projected.shape, 1)
    return jnp.where(lane < DA, projected, 0.0).astype(BF16)


def project_kernel(n_pieces, *refs):
    piece_refs = refs[:n_pieces]
    vec_ref, own_ref, other_ref, x_ref, q_ref, kv_ref, w_ref, sems = refs[n_pieces:]
    count = x_ref.shape[0]
    copies = copy_qkv(0, own_ref, other_ref, w_ref, sems)
    at = 0
    for ref in piece_refs:
        rows = ref.shape[0]
        x_ref[at : at + rows] = ref[...]
        at += rows
    if count > BLOCK:
        for copy in copies:
            copy.wait()

    def body(start, size):
        rows = pl.ds(start, size)
        modulated = normed(x_ref[rows].astype(F32), vec_ref[1:2], vec_ref[0:1])
        if count <= BLOCK:
            copies[0].wait()
            copies[1].wait()
        kv_ref[rows] = dot_t(modulated, w_ref[DA:]).astype(BF16)
        q_ref[rows] = query_of(modulated, w_ref)

    each_block(count, body)


def project(pieces, vecs, w_own, w_other):
    count = sum(piece.shape[0] for piece in pieces)
    return pl.pallas_call(
        functools.partial(project_kernel, len(pieces)),
        out_shape=(
            jax.ShapeDtypeStruct((count, D), BF16),
            jax.ShapeDtypeStruct((count, DP), BF16),
            jax.ShapeDtypeStruct((count, 2 * DA), BF16),
        ),
        in_specs=[VMEM] * (len(pieces) + 1) + [ANY] * 2,
        out_specs=(VMEM,) * 3,
        scratch_shapes=[
            pltpu.VMEM((3 * DA, D), BF16),
            pltpu.SemaphoreType.DMA((2,)),
        ],
        compiler_params=params(count),
        name="layer_norm_and_projections",
    )(*pieces, vecs, w_own, w_other)


def gather_keys(all_ref, kv_ref, stale_refs, got_ref):
    count = kv_ref.shape[0]
    first_core = lax.axis_index("pipe") == 0
    all_ref[:count] = kv_ref[...]
    at = 0
    for ref in stale_refs:
        rows = ref.shape[0]
        all_ref[count + at : count + at + rows] = jnp.where(first_core, ref[...], got_ref[at : at + rows])
        at += rows


def block_kernel(n_pieces, *refs):
    stale_refs = refs[:n_pieces]
    (
        x_ref, q_ref, kv_ref, got_ref, idx_ref, vec_ref, w_own, w_other, wo_own, wo_other,
        xt_ref, qt_ref, kv1_ref, w_ref, wo_ref, all_ref, pick_ref, sems,
    ) = refs[n_pieces:]
    count = x_ref.shape[0]
    out_copy = copy_out(0, wo_own, wo_other, wo_ref, sems.at[2])
    in_copies = copy_qkv(1, w_own, w_other, w_ref, sems)
    wo_ref[:SHIFT] = jnp.zeros((SHIFT, D), BF16)
    gather_keys(all_ref, kv_ref, stale_refs, got_ref)
    pick_ref[...] = jnp.zeros_like(pick_ref)
    tile_rows = idx_ref.shape[0]
    waits = [out_copy] + in_copies
    if count > BLOCK:
        for copy in waits:
            copy.wait()

    def body(start, size):
        rows = pl.ds(start, size)
        attended = attend(q_ref[rows], all_ref).astype(BF16)
        if count <= BLOCK:
            for copy in waits:
                copy.wait()
        branch = dot(attended, wo_ref[...])
        x1 = (x_ref[rows].astype(F32) + vec_ref[2:3] * branch).astype(BF16)
        modulated = normed(x1.astype(F32), vec_ref[4:5], vec_ref[3:4])
        fresh = dot_t(modulated, w_ref[DA:]).astype(BF16)
        kv1_ref[rows] = fresh
        lane = lax.broadcasted_iota(jnp.int32, (tile_rows, size), 1) + start
        chosen = (lane == idx_ref[:, :1]).astype(F32).astype(BF16)
        pick_ref[0] += dot(chosen, x1)
        pick_ref[1] += dot(chosen, modulated)

    each_block(count, body)
    xt_ref[...] = pick_ref[0].astype(BF16)
    qt_ref[...] = query_of(pick_ref[1].astype(BF16), w_ref)


def first_block(stale_pieces, x, q, kv, got, idx, vecs, w_own, w_other, wo_own, wo_other):
    count = x.shape[0]
    tile_rows = idx.shape[0]
    return pl.pallas_call(
        functools.partial(block_kernel, len(stale_pieces)),
        out_shape=(
            jax.ShapeDtypeStruct((tile_rows, D), BF16),
            jax.ShapeDtypeStruct((tile_rows, DP), BF16),
            jax.ShapeDtypeStruct((count, 2 * DA), BF16),
        ),
        in_specs=[VMEM] * (len(stale_pieces) + 6) + [ANY] * 4,
        out_specs=(VMEM,) * 3,
        scratch_shapes=[
            pltpu.VMEM((3 * DA, D), BF16),
            pltpu.VMEM((DP, D), BF16),
            pltpu.VMEM((2 * count, 2 * DA), BF16),
            pltpu.VMEM((2, tile_rows, D), F32),
            pltpu.SemaphoreType.DMA((3,)),
        ],
        compiler_params=params(count),
        name="attention_and_next_keys",
    )(*stale_pieces, x, q, kv, got, idx, vecs, w_own, w_other, wo_own, wo_other)


def tile_kernel(n_pieces, *refs):
    stale_refs = refs[:n_pieces]
    (
        x_ref, q_ref, kv_ref, got_ref, idx_ref, vec_ref, wf_ref, wo_own, wo_other,
        patch_ref, wo_ref, all_ref, sems,
    ) = refs[n_pieces:]
    out_copy = copy_out(1, wo_own, wo_other, wo_ref, sems.at[0])
    wo_ref[:SHIFT] = jnp.zeros((SHIFT, D), BF16)
    gather_keys(all_ref, kv_ref, stale_refs, got_ref)
    attended = attend(q_ref[...], all_ref).astype(BF16)
    out_copy.wait()
    branch = dot(attended, wo_ref[...])
    x2 = (x_ref[...].astype(F32) + vec_ref[5:6] * branch).astype(BF16)
    final = normed(x2.astype(F32), vec_ref[7:8], vec_ref[6:7])
    patches = dot_t(final, wf_ref[...]).astype(BF16).astype(F32)
    patch_ref[...] = jnp.zeros_like(patch_ref)
    patch_ref[:, : 4 * LATC] = jnp.where(idx_ref[:, :1] >= 0, patches, 0.0)


def tile_block(stale_pieces, x, q, kv, got, idx, vecs, w_final, wo_own, wo_other):
    count = kv.shape[0]
    return pl.pallas_call(
        functools.partial(tile_kernel, len(stale_pieces)),
        out_shape=jax.ShapeDtypeStruct((x.shape[0], LANES), F32),
        in_specs=[VMEM] * (len(stale_pieces) + 7) + [ANY] * 2,
        out_specs=VMEM,
        scratch_shapes=[
            pltpu.VMEM((DP, D), BF16),
            pltpu.VMEM((2 * count, 2 * DA), BF16),
            pltpu.SemaphoreType.DMA((1,)),
        ],
        compiler_params=params(count),
        name="tile_attention_and_patches",
    )(*stale_pieces, x, q, kv, got, idx, vecs, w_final, wo_own, wo_other)


def decode_kernel(
    rows, cols, pitch, patch_ref, got_ref, idx_ref, wp_ref, bin_ref, bup_ref, w_any, out_ref, w_ref, u_ref, ub_ref, sems
):
    copies = [pltpu.make_async_copy(w_any.at[t], w_ref.at[t], sems.at[t]) for t in range(9)]
    order = [3, 4, 5, 0, 1, 2, 6, 7, 8]
    for t in order:
        copies[t].start()
    first_core = lax.axis_index("pipe") == 0
    got = got_ref[:pitch]
    above = jnp.where(first_core, 0.0, got)
    below = jnp.where(first_core, got, 0.0)
    rim = [above] + [patch_ref[r * pitch : (r + 1) * pitch] for r in range(rows)] + [below]
    column_in = idx_ref[:pitch, :1] >= 0
    shifted = [[pltpu.roll(p, (-ds) % pitch, 0) if ds else p for ds in (-1, 0, 1)] for p in rim]
    for r in range(rows + 2):
        low, high = None, None
        for dr in (-1, 0, 1):
            if not 0 <= r + dr < rows + 2:
                continue
            for ds in range(3):
                tap = (dr + 1) * 3 + ds
                piece = shifted[r + dr][ds]
                if tap == 8:
                    high = piece
                else:
                    piece = pltpu.roll(piece, 4 * LATC * tap, 1) if tap else piece
                    low = piece if low is None else low + piece
        high = jnp.zeros_like(low) if high is None else high
        around = jnp.concatenate([low, high], axis=1).astype(BF16)
        for p in range(2):
            y = 2 * (r - 1) + p + 1
            if not 0 <= y < 2 * rows + 2:
                continue
            for q in range(2):
                at = (2 * p + q) * 2 * LANES
                act = dot(around, wp_ref[at : at + 2 * LANES]) + bin_ref[...]
                feature = act / (1.0 + jnp.exp(-act))
                keep = column_in
                if y == 0:
                    keep = keep & jnp.logical_not(first_core)
                if y == 2 * rows + 1:
                    keep = keep & first_core
                feature = jnp.where(keep, feature, 0.0)
                for c in range(CH // LANES):
                    part = feature[:, c * LANES : (c + 1) * LANES]
                    u_ref[y, c, pl.ds(2 * q, pitch, stride=4), :] = part
                    u_ref[y, c, pl.ds(2 * q + 1, pitch, stride=4), :] = part
    wide = 4 * cols
    for y in range(2 * rows + 2):
        for dx in range(3):
            for c in range(CH // LANES):
                ub_ref[dx, y * wide : (y + 1) * wide, c * LANES : (c + 1) * LANES] = u_ref[
                    y, c, 3 + dx : 3 + dx + wide, :
                ].astype(BF16)

    def tap_row(dy, y_first, y_count):
        total = None
        for dx in range(3):
            copies[3 * dy + dx].wait()
            part = dot(ub_ref[dx, y_first * wide : (y_first + y_count) * wide], w_ref[3 * dy + dx])
            total = part if total is None else total + part
        return total

    def rows_of(total, y):
        return total[y * wide : (y + 1) * wide]

    middle = tap_row(1, 1, 2 * rows) + bup_ref[...]
    before = tap_row(0, 0, 2 * rows + 1)
    after = tap_row(2, 1, 2 * rows + 1)
    for y in range(2 * rows):
        own = rows_of(middle, y)
        out_ref[2 * y] = (own + rows_of(before, y) + rows_of(after, y)).astype(BF16)
        out_ref[2 * y + 1] = (own + rows_of(before, y + 1) + rows_of(after, y + 1)).astype(BF16)


def decode(rows, cols, pitch, patches, got, idx, w_patch, b_in, b_up, w_up):
    return pl.pallas_call(
        functools.partial(decode_kernel, rows, cols, pitch),
        out_shape=jax.ShapeDtypeStruct((4 * rows, 4 * cols, CH), BF16),
        in_specs=[VMEM] * 6 + [ANY],
        out_specs=VMEM,
        scratch_shapes=[
            pltpu.VMEM((9, CH, CH), BF16),
            pltpu.VMEM((2 * rows + 2, CH // LANES, 4 * pitch, LANES), F32),
            pltpu.VMEM((3, (2 * rows + 2) * 4 * cols, CH), BF16),
            pltpu.SemaphoreType.DMA((9,)),
        ],
        compiler_params=params(0),
        name="decoder_convolutions",
    )(patches, got, idx, w_patch, b_in, b_up, w_up)


def patch_selector():
    sel = np.zeros((2, 2, 3, 3, 2, 2, LATC, 9 * LATC), np.float32)
    for p, q, dr, ds, pp, qq in np.ndindex(2, 2, 3, 3, 2, 2):
        dy = 2 * (dr - 1) + pp - p
        dx = 2 * (ds - 1) + qq - q
        if abs(dy) <= 1 and abs(dx) <= 1:
            tap = (dy + 1) * 3 + dx + 1
            for c in range(LATC):
                sel[p, q, dr, ds, pp, qq, c, tap * LATC + c] = 1.0
    sel = sel.reshape(4, 9 * 4 * LATC, 9 * LATC)
    return np.pad(sel, ((0, 0), (0, 2 * LANES - 9 * 4 * LATC), (0, 0))).reshape(-1, 9 * LATC)


def split_of(n):
    inner = 2 ** (int(math.log2(n)) // 2)
    return n // inner, inner


def shifted(block, k_outer, k_inner):
    n = lax.axis_size("patch")
    outer, inner = split_of(n)
    route = []
    for i in range(n):
        o, e = divmod(i, inner)
        route.append(((o + k_outer) % outer * inner + (e + k_inner) % inner, i))
    return lax.ppermute(block, "patch", route)


def doubled(column, bit):
    route = [(i ^ bit, i) for i in range(lax.axis_size("patch"))]
    return [column, lax.ppermute(column, ("pipe", "patch"), route)]


def stale_column(own):
    n = lax.axis_size("patch")
    outer, inner = split_of(n)
    bits = [inner << i for i in range(int(math.log2(outer)))] + [1 << i for i in range(1, int(math.log2(inner)))]
    for bit in bits:
        own = jnp.concatenate(doubled(own, bit), axis=0)
    return own


def local(
    tokens,
    stale_kv,
    w_qkv,
    w_out,
    block_table,
    time_table,
    t_index,
    w_final,
    w_in,
    b_in,
    w_up,
    b_up,
):
    section = lax.axis_index("pipe")
    tile = lax.axis_index("patch")
    n_tiles = lax.axis_size("patch")
    swap = [(0, 1), (1, 0)]
    first_core = section == 0
    own_count = tokens.shape[1]
    count = own_count * n_tiles
    rows = count // TC
    cols = TC // n_tiles
    pitch = -(-(cols + 3) // 8) * 8
    outer, inner = split_of(n_tiles)

    own_tokens = lax.dynamic_index_in_dim(tokens, section, 0, keepdims=False)
    w_qkv = jnp.swapaxes(w_qkv, 1, 2)
    w_qkv_other = lax.ppermute(w_qkv, "pipe", swap)
    x_column = [shifted(own_tokens, k, 0) for k in range(1, outer)]
    x_own_inner = [shifted(own_tokens, 0, k) for k in range(1, inner)]
    x_own_inner[0], own_stale = lax.optimization_barrier((x_own_inner[0], stale_kv[0, 1]))
    x_others = jnp.concatenate(x_column, axis=0)
    x_others, w_in = lax.optimization_barrier((x_others, w_in))
    x_pieces = [own_tokens, x_others]
    for k in range(1, inner):
        x_pieces += [x_own_inner[k - 1], shifted(x_others, 0, k)]
    later_stale = lax.ppermute(own_stale, "pipe", [(1, 0)])
    stale = stale_column(own_stale)
    w_out_other = lax.ppermute(w_out, "pipe", swap)
    table_other = lax.ppermute(block_table[0], "pipe", swap)

    time_row = lax.dynamic_index_in_dim(time_table, t_index[0], 0, keepdims=False)
    table = block_table[0]
    table_0 = jnp.where(first_core, table, table_other)
    table_1 = jnp.where(first_core, table_other, table)
    ones = jnp.asarray([[0.0], [1.0], [0.0]], F32)
    vecs = jnp.concatenate(
        [
            time_row[:3] + table_0 + ones,
            time_row[:3] + table_1 + ones,
            time_row[3:5] + ones[:2],
        ],
        axis=0,
    )

    padded_rows = -(-rows * pitch // 16) * 16
    place = jnp.arange(padded_rows)
    column = place % pitch - 1 + tile * cols
    inside = (place % pitch < cols + 2) & (place < rows * pitch) & (column >= 0) & (column < TC)
    token = place // pitch * TC + jnp.clip(column, 0, TC - 1)
    source = token // own_count
    k_outer = (source // inner - tile // inner) % outer
    k_inner = (source % inner - tile % inner) % inner
    spot = (k_inner * outer + k_outer) * own_count + token % own_count
    idx = jnp.broadcast_to(jnp.where(inside, spot, -1)[:, None], (padded_rows, LANES)).astype(jnp.int32)

    w_patch = dot(jnp.asarray(patch_selector(), BF16), w_in).astype(BF16)
    x_pieces, w_patch, idx, stale = lax.optimization_barrier((x_pieces, w_patch, idx, stale))
    stale_pieces = doubled(stale, 1)

    x, query, fresh = project(x_pieces, vecs, w_qkv, w_qkv_other)
    got = lax.ppermute(fresh, "pipe", [(0, 1)])
    later_stale, x = lax.optimization_barrier((later_stale, x))
    later_pieces = doubled(stale_column(later_stale), 1)
    x_tile, q_tile, fresh = first_block(
        stale_pieces, x, query, fresh, got, idx, vecs, w_qkv, w_qkv_other, w_out, w_out_other
    )
    got = lax.ppermute(fresh, "pipe", [(0, 1)])
    patches = tile_block(later_pieces, x_tile, q_tile, fresh, got, idx, vecs, w_final.T, w_out, w_out_other)
    edge = patches
    if rows > 1:
        edge = jnp.where(first_core, patches[(rows - 1) * pitch : rows * pitch], patches[:pitch])
    got = lax.ppermute(edge, "pipe", swap)
    return decode(rows, cols, pitch, patches, got, idx, w_patch, b_in[None], b_up[None], w_up)


def solution(mesh):
    placed = (
        P(None, ("grp", "patch"), None),
        P("pipe", None, ("grp", "patch"), None),
        P("pipe", None, None),
        P("pipe", None, None),
        P("pipe", None, None),
        P(),
        P("grp"),
        P(),
        P(),
        P(),
        P(),
        P(),
    )
    return jax.shard_map(
        local,
        mesh=mesh,
        in_specs=placed,
        out_specs=P(("grp", "pipe"), "patch", None),
        check_vma=False,
    )
```

```python
import functools
import math

import jax
import jax.numpy as jnp
import numpy as np
from jax import lax
from jax.experimental import pallas as pl
from jax.experimental.pallas import tpu as pltpu
from jax.sharding import PartitionSpec as P

D = 1152
DH = 72
HEADS = 8
CH = 512
LATC = 4
TC = 256
DA = 576
DP = 640
SHIFT = 64
EPSILON = 1e-06
QUERY_SCALE = math.log2(math.e) / math.sqrt(DH)
BLOCK = 256
SMALL_BLOCK = 64
LANES = 128

F32 = jnp.float32
BF16 = jnp.bfloat16
VMEM = pl.BlockSpec(memory_space=pltpu.VMEM)
ANY = pl.BlockSpec(memory_space=pl.ANY)


def dot(a, b):
    return jnp.dot(a, b, preferred_element_type=F32)


def dot_t(a, b):
    return lax.dot_general(a, b, (((1,), (1,)), ((), ())), preferred_element_type=F32)


def normed(values, scale, shift):
    average = jnp.mean(values, axis=-1, keepdims=True)
    centred = values - average
    variance = jnp.mean(centred * centred, axis=-1, keepdims=True)
    return (centred * lax.rsqrt(variance + EPSILON) * scale + shift).astype(BF16)


def lane_window(start):
    return start // LANES * LANES, -(-(start + DH) // LANES) * LANES


def attend(query, kv_ref):
    count = query.shape[0]
    pieces = [None] * (DP // LANES)
    for head in range(HEADS):
        first, last = lane_window(head * DH)
        lane = lax.broadcasted_iota(jnp.int32, (count, last - first), 1) + first
        own = (lane >= head * DH) & (lane < (head + 1) * DH)
        q = jnp.where(own, query[:, first:last], jnp.zeros((), BF16))
        scores = dot_t(q, kv_ref[:, first:last])
        exponent = jnp.exp2(scores - jnp.max(scores, axis=1, keepdims=True))
        total = jnp.sum(exponent, axis=1, keepdims=True)
        start = DA + head * DH
        first, last = lane_window(start)
        numerator = dot(exponent.astype(BF16), kv_ref[:, first:last])
        lane = lax.broadcasted_iota(jnp.int32, (count, last - first), 1) + first
        own = (lane >= start) & (lane < start + DH)
        out = jnp.where(own, numerator * (1.0 / total), 0.0)
        for i in range((last - first) // LANES):
            at = (first - (DA - SHIFT)) // LANES + i
            part = out[:, i * LANES : (i + 1) * LANES]
            pieces[at] = part if pieces[at] is None else pieces[at] + part
    return jnp.concatenate(pieces, axis=1)


def each_block(count, body):
    if count <= BLOCK:
        body(0, count)
    else:

        @pl.loop(0, count // SMALL_BLOCK)
        def _(i):
            body(pl.multiple_of(i * SMALL_BLOCK, SMALL_BLOCK), SMALL_BLOCK)


def params(count):
    return pltpu.CompilerParams(vmem_limit_bytes=(24 if count <= BLOCK else 56) * 1024 * 1024)


def copy_of(block, own, other, target, sem):
    section = lax.axis_index("pipe")

    @pl.when(section == block)
    def _():
        pltpu.make_async_copy(own, target, sem).start()

    @pl.when(section != block)
    def _():
        pltpu.make_async_copy(other, target, sem).start()

    return pltpu.make_async_copy(own, target, sem)


def copy_qkv(block, own_ref, other_ref, w_ref, sems):
    return [
        copy_of(block, own_ref.at[0, a:b], other_ref.at[0, a:b], w_ref.at[a:b], sems.at[i])
        for i, (a, b) in enumerate(((0, DA), (DA, 3 * DA)))
    ]


def copy_out(block, own_ref, other_ref, wo_ref, sem):
    return copy_of(block, own_ref.at[0], other_ref.at[0], wo_ref.at[SHIFT:DP], sem)


def query_of(modulated, w_ref):
    projected = dot_t(modulated, w_ref[:DP]) * QUERY_SCALE
    lane = lax.broadcasted_iota(jnp.int32, projected.shape, 1)
    return jnp.where(lane < DA, projected, 0.0).astype(BF16)


def project_kernel(n_pieces, *refs):
    piece_refs = refs[:n_pieces]
    vec_ref, own_ref, other_ref, x_ref, q_ref, kv_ref, w_ref, sems = refs[n_pieces:]
    count = x_ref.shape[0]
    copies = copy_qkv(0, own_ref, other_ref, w_ref, sems)
    at = 0
    for ref in piece_refs:
        rows = ref.shape[0]
        x_ref[at : at + rows] = ref[...]
        at += rows
    if count > BLOCK:
        for copy in copies:
            copy.wait()

    def body(start, size):
        rows = pl.ds(start, size)
        modulated = normed(x_ref[rows].astype(F32), vec_ref[1:2], vec_ref[0:1])
        if count <= BLOCK:
            copies[0].wait()
            copies[1].wait()
        kv_ref[rows] = dot_t(modulated, w_ref[DA:]).astype(BF16)
        q_ref[rows] = query_of(modulated, w_ref)

    each_block(count, body)


def project(pieces, vecs, w_own, w_other):
    count = sum(piece.shape[0] for piece in pieces)
    return pl.pallas_call(
        functools.partial(project_kernel, len(pieces)),
        out_shape=(
            jax.ShapeDtypeStruct((count, D), BF16),
            jax.ShapeDtypeStruct((count, DP), BF16),
            jax.ShapeDtypeStruct((count, 2 * DA), BF16),
        ),
        in_specs=[VMEM] * (len(pieces) + 1) + [ANY] * 2,
        out_specs=(VMEM,) * 3,
        scratch_shapes=[
            pltpu.VMEM((3 * DA, D), BF16),
            pltpu.SemaphoreType.DMA((2,)),
        ],
        compiler_params=params(count),
        name="layer_norm_and_projections",
    )(*pieces, vecs, w_own, w_other)


def block_kernel(n_pieces, *refs):
    stale_refs = refs[:n_pieces]
    (
        x_ref, q_ref, kv_ref, got_ref, idx_ref, vec_ref, w_own, w_other, wo_own, wo_other,
        xt_ref, qt_ref, kv1_ref, send_ref, w_ref, wo_ref, all_ref, pick_ref, sems,
    ) = refs[n_pieces:]
    count = x_ref.shape[0]
    out_copy = copy_out(0, wo_own, wo_other, wo_ref, sems.at[2])
    in_copies = copy_qkv(1, w_own, w_other, w_ref, sems)
    first_core = lax.axis_index("pipe") == 0
    wo_ref[:SHIFT] = jnp.zeros((SHIFT, D), BF16)
    all_ref[:count] = kv_ref[...]
    at = 0
    for ref in stale_refs:
        rows = ref.shape[0]
        all_ref[count + at : count + at + rows] = jnp.where(first_core, ref[...], got_ref[at : at + rows])
        send_ref[at : at + rows] = ref[...]
        at += rows
    pick_ref[...] = jnp.zeros_like(pick_ref)
    tile_rows = idx_ref.shape[0]
    waits = [out_copy] + in_copies
    if count > BLOCK:
        for copy in waits:
            copy.wait()

    def body(start, size):
        rows = pl.ds(start, size)
        attended = attend(q_ref[rows], all_ref).astype(BF16)
        if count <= BLOCK:
            for copy in waits:
                copy.wait()
        branch = dot(attended, wo_ref[...])
        x1 = (x_ref[rows].astype(F32) + vec_ref[2:3] * branch).astype(BF16)
        modulated = normed(x1.astype(F32), vec_ref[4:5], vec_ref[3:4])
        fresh = dot_t(modulated, w_ref[DA:]).astype(BF16)
        kv1_ref[rows] = fresh

        @pl.when(first_core)
        def _():
            send_ref[rows] = fresh

        lane = lax.broadcasted_iota(jnp.int32, (tile_rows, size), 1) + start
        chosen = (lane == idx_ref[:, :1]).astype(F32).astype(BF16)
        pick_ref[0] += dot(chosen, x1)
        pick_ref[1] += dot(chosen, modulated)

    each_block(count, body)
    xt_ref[...] = pick_ref[0].astype(BF16)
    qt_ref[...] = query_of(pick_ref[1].astype(BF16), w_ref)


def first_block(stale_pieces, x, q, kv, got, idx, vecs, w_own, w_other, wo_own, wo_other):
    count = x.shape[0]
    tile_rows = idx.shape[0]
    return pl.pallas_call(
        functools.partial(block_kernel, len(stale_pieces)),
        out_shape=(
            jax.ShapeDtypeStruct((tile_rows, D), BF16),
            jax.ShapeDtypeStruct((tile_rows, DP), BF16),
            jax.ShapeDtypeStruct((count, 2 * DA), BF16),
            jax.ShapeDtypeStruct((count, 2 * DA), BF16),
        ),
        in_specs=[VMEM] * (len(stale_pieces) + 6) + [ANY] * 4,
        out_specs=(VMEM,) * 4,
        scratch_shapes=[
            pltpu.VMEM((3 * DA, D), BF16),
            pltpu.VMEM((DP, D), BF16),
            pltpu.VMEM((2 * count, 2 * DA), BF16),
            pltpu.VMEM((2, tile_rows, D), F32),
            pltpu.SemaphoreType.DMA((3,)),
        ],
        compiler_params=params(count),
        name="attention_and_next_keys",
    )(*stale_pieces, x, q, kv, got, idx, vecs, w_own, w_other, wo_own, wo_other)


def tile_kernel(
    x_ref, q_ref, kv_ref, got_ref, idx_ref, vec_ref, wf_ref, wo_own, wo_other, patch_ref, wo_ref, all_ref, sems
):
    count = kv_ref.shape[0]
    out_copy = copy_out(1, wo_own, wo_other, wo_ref, sems.at[0])
    wo_ref[:SHIFT] = jnp.zeros((SHIFT, D), BF16)
    all_ref[:count] = kv_ref[...]
    all_ref[count:] = got_ref[...]
    attended = attend(q_ref[...], all_ref).astype(BF16)
    out_copy.wait()
    branch = dot(attended, wo_ref[...])
    x2 = (x_ref[...].astype(F32) + vec_ref[5:6] * branch).astype(BF16)
    final = normed(x2.astype(F32), vec_ref[7:8], vec_ref[6:7])
    patches = dot_t(final, wf_ref[...]).astype(BF16).astype(F32)
    patch_ref[...] = jnp.zeros_like(patch_ref)
    patch_ref[:, : 4 * LATC] = jnp.where(idx_ref[:, :1] >= 0, patches, 0.0)


def tile_block(x, q, kv, got, idx, vecs, w_final, wo_own, wo_other):
    count = kv.shape[0]
    return pl.pallas_call(
        tile_kernel,
        out_shape=jax.ShapeDtypeStruct((x.shape[0], LANES), F32),
        in_specs=[VMEM] * 7 + [ANY] * 2,
        out_specs=VMEM,
        scratch_shapes=[
            pltpu.VMEM((DP, D), BF16),
            pltpu.VMEM((2 * count, 2 * DA), BF16),
            pltpu.SemaphoreType.DMA((1,)),
        ],
        compiler_params=params(count),
        name="tile_attention_and_patches",
    )(x, q, kv, got, idx, vecs, w_final, wo_own, wo_other)


def decode_kernel(
    rows, cols, pitch, patch_ref, got_ref, idx_ref, wp_ref, bin_ref, bup_ref, w_any, out_ref, w_ref, u_ref, ub_ref, sems
):
    copies = [pltpu.make_async_copy(w_any.at[t], w_ref.at[t], sems.at[t]) for t in range(9)]
    order = [3, 4, 5, 0, 1, 2, 6, 7, 8]
    for t in order:
        copies[t].start()
    first_core = lax.axis_index("pipe") == 0
    got = got_ref[:pitch]
    above = jnp.where(first_core, 0.0, got)
    below = jnp.where(first_core, got, 0.0)
    rim = [above] + [patch_ref[r * pitch : (r + 1) * pitch] for r in range(rows)] + [below]
    column_in = idx_ref[:pitch, :1] >= 0
    shifted = [[pltpu.roll(p, (-ds) % pitch, 0) if ds else p for ds in (-1, 0, 1)] for p in rim]
    for r in range(rows + 2):
        low, high = None, None
        for dr in (-1, 0, 1):
            if not 0 <= r + dr < rows + 2:
                continue
            for ds in range(3):
                tap = (dr + 1) * 3 + ds
                piece = shifted[r + dr][ds]
                if tap == 8:
                    high = piece
                else:
                    piece = pltpu.roll(piece, 4 * LATC * tap, 1) if tap else piece
                    low = piece if low is None else low + piece
        high = jnp.zeros_like(low) if high is None else high
        around = jnp.concatenate([low, high], axis=1).astype(BF16)
        for p in range(2):
            y = 2 * (r - 1) + p + 1
            if not 0 <= y < 2 * rows + 2:
                continue
            for q in range(2):
                at = (2 * p + q) * 2 * LANES
                act = dot(around, wp_ref[at : at + 2 * LANES]) + bin_ref[...]
                feature = act / (1.0 + jnp.exp(-act))
                keep = column_in
                if y == 0:
                    keep = keep & jnp.logical_not(first_core)
                if y == 2 * rows + 1:
                    keep = keep & first_core
                feature = jnp.where(keep, feature, 0.0)
                for c in range(CH // LANES):
                    part = feature[:, c * LANES : (c + 1) * LANES]
                    u_ref[y, c, pl.ds(2 * q, pitch, stride=4), :] = part
                    u_ref[y, c, pl.ds(2 * q + 1, pitch, stride=4), :] = part
    wide = 4 * cols
    for y in range(2 * rows + 2):
        for dx in range(3):
            for c in range(CH // LANES):
                ub_ref[dx, y * wide : (y + 1) * wide, c * LANES : (c + 1) * LANES] = u_ref[
                    y, c, 3 + dx : 3 + dx + wide, :
                ].astype(BF16)

    def tap_row(dy, y_first, y_count):
        total = None
        for dx in range(3):
            copies[3 * dy + dx].wait()
            part = dot(ub_ref[dx, y_first * wide : (y_first + y_count) * wide], w_ref[3 * dy + dx])
            total = part if total is None else total + part
        return total

    def rows_of(total, y):
        return total[y * wide : (y + 1) * wide]

    middle = tap_row(1, 1, 2 * rows) + bup_ref[...]
    before = tap_row(0, 0, 2 * rows + 1)
    after = tap_row(2, 1, 2 * rows + 1)
    for y in range(2 * rows):
        own = rows_of(middle, y)
        out_ref[2 * y] = (own + rows_of(before, y) + rows_of(after, y)).astype(BF16)
        out_ref[2 * y + 1] = (own + rows_of(before, y + 1) + rows_of(after, y + 1)).astype(BF16)


def decode(rows, cols, pitch, patches, got, idx, w_patch, b_in, b_up, w_up):
    return pl.pallas_call(
        functools.partial(decode_kernel, rows, cols, pitch),
        out_shape=jax.ShapeDtypeStruct((4 * rows, 4 * cols, CH), BF16),
        in_specs=[VMEM] * 6 + [ANY],
        out_specs=VMEM,
        scratch_shapes=[
            pltpu.VMEM((9, CH, CH), BF16),
            pltpu.VMEM((2 * rows + 2, CH // LANES, 4 * pitch, LANES), F32),
            pltpu.VMEM((3, (2 * rows + 2) * 4 * cols, CH), BF16),
            pltpu.SemaphoreType.DMA((9,)),
        ],
        compiler_params=params(0),
        name="decoder_convolutions",
    )(patches, got, idx, w_patch, b_in, b_up, w_up)


def patch_selector():
    sel = np.zeros((2, 2, 3, 3, 2, 2, LATC, 9 * LATC), np.float32)
    for p, q, dr, ds, pp, qq in np.ndindex(2, 2, 3, 3, 2, 2):
        dy = 2 * (dr - 1) + pp - p
        dx = 2 * (ds - 1) + qq - q
        if abs(dy) <= 1 and abs(dx) <= 1:
            tap = (dy + 1) * 3 + dx + 1
            for c in range(LATC):
                sel[p, q, dr, ds, pp, qq, c, tap * LATC + c] = 1.0
    sel = sel.reshape(4, 9 * 4 * LATC, 9 * LATC)
    return np.pad(sel, ((0, 0), (0, 2 * LANES - 9 * 4 * LATC), (0, 0))).reshape(-1, 9 * LATC)


def gather_patch(own):
    n = lax.axis_size("patch")
    pieces = lax.all_to_all(jnp.broadcast_to(own[None], (n,) + own.shape), "patch", 0, 0, tiled=True)
    return [pieces.reshape(n * own.shape[0], own.shape[1])]


def local(
    tokens,
    stale_kv,
    w_qkv,
    w_out,
    block_table,
    time_table,
    t_index,
    w_final,
    w_in,
    b_in,
    w_up,
    b_up,
):
    section = lax.axis_index("pipe")
    tile = lax.axis_index("patch")
    n_tiles = lax.axis_size("patch")
    swap = [(0, 1), (1, 0)]
    first_core = section == 0
    own_count = tokens.shape[1]
    count = own_count * n_tiles
    rows = count // TC
    cols = TC // n_tiles
    pitch = -(-(cols + 3) // 8) * 8

    own_tokens = lax.dynamic_index_in_dim(tokens, section, 0, keepdims=False)
    w_qkv = jnp.swapaxes(w_qkv, 1, 2)
    w_qkv_other = lax.ppermute(w_qkv, "pipe", swap)
    x_pieces = gather_patch(own_tokens)
    stale_pieces = gather_patch(stale_kv[0, 1])
    w_out_other = lax.ppermute(w_out, "pipe", swap)
    table_other = lax.ppermute(block_table[0], "pipe", swap)

    time_row = lax.dynamic_index_in_dim(time_table, t_index[0], 0, keepdims=False)
    table = block_table[0]
    table_0 = jnp.where(first_core, table, table_other)
    table_1 = jnp.where(first_core, table_other, table)
    ones = jnp.asarray([[0.0], [1.0], [0.0]], F32)
    vecs = jnp.concatenate(
        [
            time_row[:3] + table_0 + ones,
            time_row[:3] + table_1 + ones,
            time_row[3:5] + ones[:2],
        ],
        axis=0,
    )

    padded_rows = -(-rows * pitch // 16) * 16
    place = jnp.arange(padded_rows)
    column = place % pitch - 1 + tile * cols
    inside = (place % pitch < cols + 2) & (place < rows * pitch) & (column >= 0) & (column < TC)
    token = place // pitch * TC + jnp.clip(column, 0, TC - 1)
    idx = jnp.broadcast_to(jnp.where(inside, token, -1)[:, None], (padded_rows, LANES)).astype(jnp.int32)

    w_patch = dot(jnp.asarray(patch_selector(), BF16), w_in).astype(BF16)
    x_pieces, w_patch, idx = lax.optimization_barrier((x_pieces, w_patch, idx))

    x, query, fresh = project(x_pieces, vecs, w_qkv, w_qkv_other)
    got = lax.ppermute(fresh, "pipe", [(0, 1)])
    x_tile, q_tile, fresh, send = first_block(
        stale_pieces, x, query, fresh, got, idx, vecs, w_qkv, w_qkv_other, w_out, w_out_other
    )
    got = lax.ppermute(send, "pipe", swap)
    patches = tile_block(x_tile, q_tile, fresh, got, idx, vecs, w_final.T, w_out, w_out_other)
    edge = patches
    if rows > 1:
        edge = jnp.where(first_core, patches[(rows - 1) * pitch : rows * pitch], patches[:pitch])
    got = lax.ppermute(edge, "pipe", swap)
    return decode(rows, cols, pitch, patches, got, idx, w_patch, b_in[None], b_up[None], w_up)


def solution(mesh):
    placed = (
        P(None, ("grp", "patch"), None),
        P("pipe", None, ("grp", "patch"), None),
        P("pipe", None, None),
        P("pipe", None, None),
        P("pipe", None, None),
        P(),
        P("grp"),
        P(),
        P(),
        P(),
        P(),
        P(),
    )
    return jax.shard_map(
        local,
        mesh=mesh,
        in_specs=placed,
        out_specs=P(("grp", "pipe"), "patch", None),
        check_vma=False,
    )
```

```python
import functools
import math

import jax
import jax.numpy as jnp
import numpy as np
from jax import lax
from jax.experimental import pallas as pl
from jax.experimental.pallas import tpu as pltpu
from jax.sharding import PartitionSpec as P

D = 1152
DH = 72
HEADS = 8
CH = 512
LATC = 4
TC = 256
DA = 576
DP = 640
SHIFT = 64
EPSILON = 1e-06
QUERY_SCALE = math.log2(math.e) / math.sqrt(DH)
BLOCK = 256
SMALL_BLOCK = 64
LANES = 128

F32 = jnp.float32
BF16 = jnp.bfloat16
VMEM = pl.BlockSpec(memory_space=pltpu.VMEM)
HBM = pl.BlockSpec(memory_space=pltpu.HBM)


def dot(a, b):
    return jnp.dot(a, b, preferred_element_type=F32)


def dot_t(a, b):
    return lax.dot_general(a, b, (((1,), (1,)), ((), ())), preferred_element_type=F32)


def normed(values, scale, shift):
    average = jnp.mean(values, axis=-1, keepdims=True)
    centred = values - average
    variance = jnp.mean(centred * centred, axis=-1, keepdims=True)
    return (centred * lax.rsqrt(variance + EPSILON) * scale + shift).astype(BF16)


def lane_window(start):
    return start // LANES * LANES, -(-(start + DH) // LANES) * LANES


def attend(query, kv_ref):
    count = query.shape[0]
    pieces = [None] * (DP // LANES)
    for head in range(HEADS):
        first, last = lane_window(head * DH)
        lane = lax.broadcasted_iota(jnp.int32, (count, last - first), 1) + first
        own = (lane >= head * DH) & (lane < (head + 1) * DH)
        q = jnp.where(own, query[:, first:last], jnp.zeros((), BF16))
        scores = dot_t(q, kv_ref[:, first:last])
        exponent = jnp.exp2(scores - jnp.max(scores, axis=1, keepdims=True))
        total = jnp.sum(exponent, axis=1, keepdims=True)
        start = DA + head * DH
        first, last = lane_window(start)
        numerator = dot(exponent.astype(BF16), kv_ref[:, first:last])
        lane = lax.broadcasted_iota(jnp.int32, (count, last - first), 1) + first
        own = (lane >= start) & (lane < start + DH)
        out = jnp.where(own, numerator * (1.0 / total), 0.0)
        for i in range((last - first) // LANES):
            at = (first - (DA - SHIFT)) // LANES + i
            part = out[:, i * LANES : (i + 1) * LANES]
            pieces[at] = part if pieces[at] is None else pieces[at] + part
    return jnp.concatenate(pieces, axis=1)


def each_block(count, body):
    if count <= BLOCK:
        body(0, count)
    else:

        @pl.loop(0, count // SMALL_BLOCK)
        def _(i):
            body(pl.multiple_of(i * SMALL_BLOCK, SMALL_BLOCK), SMALL_BLOCK)


def params(count):
    return pltpu.CompilerParams(vmem_limit_bytes=(24 if count <= BLOCK else 56) * 1024 * 1024)


def copy_of(block, own, other, target, sem):
    section = lax.axis_index("pipe")

    @pl.when(section == block)
    def _():
        pltpu.make_async_copy(own, target, sem).start()

    @pl.when(section != block)
    def _():
        pltpu.make_async_copy(other, target, sem).start()

    return pltpu.make_async_copy(own, target, sem)


def copy_qkv(block, own_ref, other_ref, w_ref, sems):
    return [
        copy_of(block, own_ref.at[0, a:b], other_ref.at[0, a:b], w_ref.at[a:b], sems.at[i])
        for i, (a, b) in enumerate(((0, DA), (DA, 3 * DA)))
    ]


def copy_out(block, own_ref, other_ref, wo_ref, sem):
    return copy_of(block, own_ref.at[0], other_ref.at[0], wo_ref.at[SHIFT:DP], sem)


def query_of(modulated, w_ref):
    projected = dot_t(modulated, w_ref[:DP]) * QUERY_SCALE
    lane = lax.broadcasted_iota(jnp.int32, projected.shape, 1)
    return jnp.where(lane < DA, projected, 0.0).astype(BF16)


def project_kernel(n_pieces, *refs):
    piece_refs = refs[:n_pieces]
    vec_ref, own_ref, other_ref, x_ref, q_ref, kv_ref, w_ref, sems = refs[n_pieces:]
    count = x_ref.shape[0]
    copies = copy_qkv(0, own_ref, other_ref, w_ref, sems)
    at = 0
    for ref in piece_refs:
        rows = ref.shape[0]
        x_ref[at : at + rows] = ref[...]
        at += rows
    if count > BLOCK:
        for copy in copies:
            copy.wait()

    def body(start, size):
        rows = pl.ds(start, size)
        modulated = normed(x_ref[rows].astype(F32), vec_ref[1:2], vec_ref[0:1])
        if count <= BLOCK:
            copies[0].wait()
            copies[1].wait()
        kv_ref[rows] = dot_t(modulated, w_ref[DA:]).astype(BF16)
        q_ref[rows] = query_of(modulated, w_ref)

    each_block(count, body)


def project(pieces, vecs, w_own, w_other):
    count = sum(piece.shape[0] for piece in pieces)
    return pl.pallas_call(
        functools.partial(project_kernel, len(pieces)),
        out_shape=(
            jax.ShapeDtypeStruct((count, D), BF16),
            jax.ShapeDtypeStruct((count, DP), BF16),
            jax.ShapeDtypeStruct((count, 2 * DA), BF16),
        ),
        in_specs=[VMEM] * (len(pieces) + 1) + [HBM] * 2,
        out_specs=(VMEM,) * 3,
        scratch_shapes=[
            pltpu.VMEM((3 * DA, D), BF16),
            pltpu.SemaphoreType.DMA((2,)),
        ],
        compiler_params=params(count),
        name="layer_norm_and_projections",
    )(*pieces, vecs, w_own, w_other)


def block_kernel(n_pieces, *refs):
    stale_refs = refs[:n_pieces]
    (
        x_ref, q_ref, kv_ref, got_ref, idx_ref, vec_ref, w_own, w_other, wo_own, wo_other,
        xt_ref, qt_ref, kv1_ref, send_ref, w_ref, wo_ref, all_ref, pick_ref, sems,
    ) = refs[n_pieces:]
    count = x_ref.shape[0]
    out_copy = copy_out(0, wo_own, wo_other, wo_ref, sems.at[2])
    in_copies = copy_qkv(1, w_own, w_other, w_ref, sems)
    first_core = lax.axis_index("pipe") == 0
    wo_ref[:SHIFT] = jnp.zeros((SHIFT, D), BF16)
    all_ref[:count] = kv_ref[...]
    at = 0
    for ref in stale_refs:
        rows = ref.shape[0]
        all_ref[count + at : count + at + rows] = jnp.where(first_core, ref[...], got_ref[at : at + rows])
        send_ref[at : at + rows] = ref[...]
        at += rows
    pick_ref[...] = jnp.zeros_like(pick_ref)
    tile_rows = idx_ref.shape[0]
    waits = [out_copy] + in_copies
    if count > BLOCK:
        for copy in waits:
            copy.wait()

    def body(start, size):
        rows = pl.ds(start, size)
        attended = attend(q_ref[rows], all_ref).astype(BF16)
        if count <= BLOCK:
            for copy in waits:
                copy.wait()
        branch = dot(attended, wo_ref[...])
        x1 = (x_ref[rows].astype(F32) + vec_ref[2:3] * branch).astype(BF16)
        modulated = normed(x1.astype(F32), vec_ref[4:5], vec_ref[3:4])
        fresh = dot_t(modulated, w_ref[DA:]).astype(BF16)
        kv1_ref[rows] = fresh

        @pl.when(first_core)
        def _():
            send_ref[rows] = fresh

        lane = lax.broadcasted_iota(jnp.int32, (tile_rows, size), 1) + start
        chosen = (lane == idx_ref[:, :1]).astype(F32).astype(BF16)
        pick_ref[0] += dot(chosen, x1)
        pick_ref[1] += dot(chosen, modulated)

    each_block(count, body)
    xt_ref[...] = pick_ref[0].astype(BF16)
    qt_ref[...] = query_of(pick_ref[1].astype(BF16), w_ref)


def first_block(stale_pieces, x, q, kv, got, idx, vecs, w_own, w_other, wo_own, wo_other):
    count = x.shape[0]
    tile_rows = idx.shape[0]
    return pl.pallas_call(
        functools.partial(block_kernel, len(stale_pieces)),
        out_shape=(
            jax.ShapeDtypeStruct((tile_rows, D), BF16),
            jax.ShapeDtypeStruct((tile_rows, DP), BF16),
            jax.ShapeDtypeStruct((count, 2 * DA), BF16),
            jax.ShapeDtypeStruct((count, 2 * DA), BF16),
        ),
        in_specs=[VMEM] * (len(stale_pieces) + 6) + [HBM] * 4,
        out_specs=(VMEM,) * 4,
        scratch_shapes=[
            pltpu.VMEM((3 * DA, D), BF16),
            pltpu.VMEM((DP, D), BF16),
            pltpu.VMEM((2 * count, 2 * DA), BF16),
            pltpu.VMEM((2, tile_rows, D), F32),
            pltpu.SemaphoreType.DMA((3,)),
        ],
        compiler_params=params(count),
        name="attention_and_next_keys",
    )(*stale_pieces, x, q, kv, got, idx, vecs, w_own, w_other, wo_own, wo_other)


def tile_kernel(
    x_ref, q_ref, kv_ref, got_ref, idx_ref, vec_ref, wf_ref, wo_own, wo_other, patch_ref, wo_ref, all_ref, sems
):
    count = kv_ref.shape[0]
    out_copy = copy_out(1, wo_own, wo_other, wo_ref, sems.at[0])
    wo_ref[:SHIFT] = jnp.zeros((SHIFT, D), BF16)
    all_ref[:count] = kv_ref[...]
    all_ref[count:] = got_ref[...]
    attended = attend(q_ref[...], all_ref).astype(BF16)
    out_copy.wait()
    branch = dot(attended, wo_ref[...])
    x2 = (x_ref[...].astype(F32) + vec_ref[5:6] * branch).astype(BF16)
    final = normed(x2.astype(F32), vec_ref[7:8], vec_ref[6:7])
    patches = dot_t(final, wf_ref[...]).astype(BF16).astype(F32)
    patch_ref[...] = jnp.zeros_like(patch_ref)
    patch_ref[:, : 4 * LATC] = jnp.where(idx_ref[:, :1] >= 0, patches, 0.0)


def tile_block(x, q, kv, got, idx, vecs, w_final, wo_own, wo_other):
    count = kv.shape[0]
    return pl.pallas_call(
        tile_kernel,
        out_shape=jax.ShapeDtypeStruct((x.shape[0], LANES), F32),
        in_specs=[VMEM] * 7 + [HBM] * 2,
        out_specs=VMEM,
        scratch_shapes=[
            pltpu.VMEM((DP, D), BF16),
            pltpu.VMEM((2 * count, 2 * DA), BF16),
            pltpu.SemaphoreType.DMA((1,)),
        ],
        compiler_params=params(count),
        name="tile_attention_and_patches",
    )(x, q, kv, got, idx, vecs, w_final, wo_own, wo_other)


def decode_kernel(
    rows, cols, pitch, patch_ref, got_ref, idx_ref, wp_ref, bin_ref, bup_ref, w_any, out_ref, w_ref, u_ref, ub_ref, sems
):
    copies = [pltpu.make_async_copy(w_any.at[t], w_ref.at[t], sems.at[t]) for t in range(9)]
    order = [3, 4, 5, 0, 1, 2, 6, 7, 8]
    for t in order:
        copies[t].start()
    first_core = lax.axis_index("pipe") == 0
    got = got_ref[:pitch]
    above = jnp.where(first_core, 0.0, got)
    below = jnp.where(first_core, got, 0.0)
    rim = [above] + [patch_ref[r * pitch : (r + 1) * pitch] for r in range(rows)] + [below]
    column_in = idx_ref[:pitch, :1] >= 0
    shifted = [[pltpu.roll(p, (-ds) % pitch, 0) if ds else p for ds in (-1, 0, 1)] for p in rim]
    for r in range(rows + 2):
        low, high = None, None
        for dr in (-1, 0, 1):
            if not 0 <= r + dr < rows + 2:
                continue
            for ds in range(3):
                tap = (dr + 1) * 3 + ds
                piece = shifted[r + dr][ds]
                if tap == 8:
                    high = piece
                else:
                    piece = pltpu.roll(piece, 4 * LATC * tap, 1) if tap else piece
                    low = piece if low is None else low + piece
        high = jnp.zeros_like(low) if high is None else high
        around = jnp.concatenate([low, high], axis=1).astype(BF16)
        for p in range(2):
            y = 2 * (r - 1) + p + 1
            if not 0 <= y < 2 * rows + 2:
                continue
            for q in range(2):
                at = (2 * p + q) * 2 * LANES
                act = dot(around, wp_ref[at : at + 2 * LANES]) + bin_ref[...]
                feature = act / (1.0 + jnp.exp(-act))
                keep = column_in
                if y == 0:
                    keep = keep & jnp.logical_not(first_core)
                if y == 2 * rows + 1:
                    keep = keep & first_core
                feature = jnp.where(keep, feature, 0.0)
                for c in range(CH // LANES):
                    part = feature[:, c * LANES : (c + 1) * LANES]
                    u_ref[y, c, pl.ds(2 * q, pitch, stride=4), :] = part
                    u_ref[y, c, pl.ds(2 * q + 1, pitch, stride=4), :] = part
    wide = 4 * cols
    for y in range(2 * rows + 2):
        for dx in range(3):
            for c in range(CH // LANES):
                ub_ref[dx, y * wide : (y + 1) * wide, c * LANES : (c + 1) * LANES] = u_ref[
                    y, c, 3 + dx : 3 + dx + wide, :
                ].astype(BF16)

    def tap_row(dy, y_first, y_count):
        total = None
        for dx in range(3):
            copies[3 * dy + dx].wait()
            part = dot(ub_ref[dx, y_first * wide : (y_first + y_count) * wide], w_ref[3 * dy + dx])
            total = part if total is None else total + part
        return total

    def rows_of(total, y):
        return total[y * wide : (y + 1) * wide]

    middle = tap_row(1, 1, 2 * rows) + bup_ref[...]
    before = tap_row(0, 0, 2 * rows + 1)
    after = tap_row(2, 1, 2 * rows + 1)
    for y in range(2 * rows):
        own = rows_of(middle, y)
        out_ref[2 * y] = (own + rows_of(before, y) + rows_of(after, y)).astype(BF16)
        out_ref[2 * y + 1] = (own + rows_of(before, y + 1) + rows_of(after, y + 1)).astype(BF16)


def decode(rows, cols, pitch, patches, got, idx, w_patch, b_in, b_up, w_up):
    return pl.pallas_call(
        functools.partial(decode_kernel, rows, cols, pitch),
        out_shape=jax.ShapeDtypeStruct((4 * rows, 4 * cols, CH), BF16),
        in_specs=[VMEM] * 6 + [HBM],
        out_specs=VMEM,
        scratch_shapes=[
            pltpu.VMEM((9, CH, CH), BF16),
            pltpu.VMEM((2 * rows + 2, CH // LANES, 4 * pitch, LANES), F32),
            pltpu.VMEM((3, (2 * rows + 2) * 4 * cols, CH), BF16),
            pltpu.SemaphoreType.DMA((9,)),
        ],
        compiler_params=params(0),
        name="decoder_convolutions",
    )(patches, got, idx, w_patch, b_in, b_up, w_up)


def patch_selector():
    sel = np.zeros((2, 2, 3, 3, 2, 2, LATC, 9 * LATC), np.float32)
    for p, q, dr, ds, pp, qq in np.ndindex(2, 2, 3, 3, 2, 2):
        dy = 2 * (dr - 1) + pp - p
        dx = 2 * (ds - 1) + qq - q
        if abs(dy) <= 1 and abs(dx) <= 1:
            tap = (dy + 1) * 3 + dx + 1
            for c in range(LATC):
                sel[p, q, dr, ds, pp, qq, c, tap * LATC + c] = 1.0
    sel = sel.reshape(4, 9 * 4 * LATC, 9 * LATC)
    return np.pad(sel, ((0, 0), (0, 2 * LANES - 9 * 4 * LATC), (0, 0))).reshape(-1, 9 * LATC)


def split_of(n):
    inner = 2 ** (int(math.log2(n)) // 2)
    return n // inner, inner


def shifted(block, k_outer, k_inner):
    n = lax.axis_size("patch")
    outer, inner = split_of(n)
    route = []
    for i in range(n):
        o, e = divmod(i, inner)
        route.append(((o + k_outer) % outer * inner + (e + k_inner) % inner, i))
    return lax.ppermute(block, "patch", route)


def local(
    tokens,
    stale_kv,
    w_qkv,
    w_out,
    block_table,
    time_table,
    t_index,
    w_final,
    w_in,
    b_in,
    w_up,
    b_up,
):
    section = lax.axis_index("pipe")
    tile = lax.axis_index("patch")
    n_tiles = lax.axis_size("patch")
    swap = [(0, 1), (1, 0)]
    first_core = section == 0
    own_count = tokens.shape[1]
    count = own_count * n_tiles
    rows = count // TC
    cols = TC // n_tiles
    pitch = -(-(cols + 3) // 8) * 8
    outer, inner = split_of(n_tiles)

    own_tokens = lax.dynamic_index_in_dim(tokens, section, 0, keepdims=False)
    w_qkv = jnp.swapaxes(w_qkv, 1, 2)
    w_qkv_other = lax.ppermute(w_qkv, "pipe", swap)
    tables = lax.all_gather(block_table[0], "pipe")
    x_column = [shifted(own_tokens, k, 0) for k in range(1, outer)]
    x_own_inner = [shifted(own_tokens, 0, k) for k in range(1, inner)]
    own_stale = stale_kv[0, 1]
    x_column, x_own_inner, w_qkv_other, own_stale, w_in = lax.optimization_barrier(
        (x_column, x_own_inner, w_qkv_other, own_stale, w_in)
    )
    x_pieces = [own_tokens] + x_column
    for k in range(1, inner):
        x_pieces += [x_own_inner[k - 1]] + [shifted(piece, 0, k) for piece in x_column]
    stale_column = [own_stale] + [shifted(own_stale, k, 0) for k in range(1, outer)]

    time_row = lax.dynamic_index_in_dim(time_table, t_index[0], 0, keepdims=False)
    ones = jnp.asarray([[0.0], [1.0], [0.0]], F32)
    vecs = jnp.concatenate(
        [
            time_row[:3] + tables[0] + ones,
            time_row[:3] + tables[1] + ones,
            time_row[3:5] + ones[:2],
        ],
        axis=0,
    )

    padded_rows = -(-rows * pitch // 16) * 16
    place = jnp.arange(padded_rows)
    column = place % pitch - 1 + tile * cols
    inside = (place % pitch < cols + 2) & (place < rows * pitch) & (column >= 0) & (column < TC)
    token = place // pitch * TC + jnp.clip(column, 0, TC - 1)
    source = token // own_count
    k_outer = (source // inner - tile // inner) % outer
    k_inner = (source % inner - tile % inner) % inner
    spot = (k_inner * outer + k_outer) * own_count + token % own_count
    idx = jnp.broadcast_to(jnp.where(inside, spot, -1)[:, None], (padded_rows, LANES)).astype(jnp.int32)

    w_patch = dot(jnp.asarray(patch_selector(), BF16), w_in).astype(BF16)
    x_pieces, w_patch, idx, stale_column, w_out = lax.optimization_barrier(
        (x_pieces, w_patch, idx, stale_column, w_out)
    )
    w_out_other = lax.ppermute(w_out, "pipe", swap)
    stale_pieces = stale_column + [shifted(piece, 0, k) for k in range(1, inner) for piece in stale_column]

    x, query, fresh = project(x_pieces, vecs, w_qkv, w_qkv_other)
    got = lax.ppermute(fresh, "pipe", [(0, 1)])
    x_tile, q_tile, fresh, send = first_block(
        stale_pieces, x, query, fresh, got, idx, vecs, w_qkv, w_qkv_other, w_out, w_out_other
    )
    got = lax.ppermute(send, "pipe", swap)
    patches = tile_block(x_tile, q_tile, fresh, got, idx, vecs, w_final.T, w_out, w_out_other)
    edge = patches
    if rows > 1:
        edge = jnp.where(first_core, patches[(rows - 1) * pitch : rows * pitch], patches[:pitch])
    got = lax.ppermute(edge, "pipe", swap)
    return decode(rows, cols, pitch, patches, got, idx, w_patch, b_in[None], b_up[None], w_up)


def solution(mesh):
    placed = (
        P(None, ("grp", "patch"), None),
        P("pipe", None, ("grp", "patch"), None),
        P("pipe", None, None),
        P("pipe", None, None),
        P("pipe", None, None),
        P(),
        P("grp"),
        P(),
        P(),
        P(),
        P(),
        P(),
    )
    return jax.shard_map(
        local,
        mesh=mesh,
        in_specs=placed,
        out_specs=P(("grp", "pipe"), "patch", None),
        check_vma=False,
    )
```

```python
import functools
import math

import jax
import jax.numpy as jnp
import numpy as np
from jax import lax
from jax.experimental import pallas as pl
from jax.experimental.pallas import tpu as pltpu
from jax.sharding import PartitionSpec as P

D = 1152
DH = 72
HEADS = 8
CH = 512
LATC = 4
TC = 256
DA = 576
DP = 640
SHIFT = 64
EPSILON = 1e-06
QUERY_SCALE = math.log2(math.e) / math.sqrt(DH)
BLOCK = 256
SMALL_BLOCK = 64
LANES = 128

F32 = jnp.float32
BF16 = jnp.bfloat16
VMEM = pl.BlockSpec(memory_space=pltpu.VMEM)
ANY = pl.BlockSpec(memory_space=pl.ANY)


def dot(a, b):
    return jnp.dot(a, b, preferred_element_type=F32)


def dot_t(a, b):
    return lax.dot_general(a, b, (((1,), (1,)), ((), ())), preferred_element_type=F32)


def normed(values, scale, shift):
    average = jnp.mean(values, axis=-1, keepdims=True)
    centred = values - average
    variance = jnp.mean(centred * centred, axis=-1, keepdims=True)
    return (centred * lax.rsqrt(variance + EPSILON) * scale + shift).astype(BF16)


def lane_window(start):
    return start // LANES * LANES, -(-(start + DH) // LANES) * LANES


def attend(query, kv_ref):
    count = query.shape[0]
    pieces = [None] * (DP // LANES)
    for head in range(HEADS):
        first, last = lane_window(head * DH)
        lane = lax.broadcasted_iota(jnp.int32, (count, last - first), 1) + first
        own = (lane >= head * DH) & (lane < (head + 1) * DH)
        q = jnp.where(own, query[:, first:last], jnp.zeros((), BF16))
        scores = dot_t(q, kv_ref[:, first:last])
        exponent = jnp.exp2(scores - jnp.max(scores, axis=1, keepdims=True))
        total = jnp.sum(exponent, axis=1, keepdims=True)
        start = DA + head * DH
        first, last = lane_window(start)
        numerator = dot(exponent.astype(BF16), kv_ref[:, first:last])
        lane = lax.broadcasted_iota(jnp.int32, (count, last - first), 1) + first
        own = (lane >= start) & (lane < start + DH)
        out = jnp.where(own, numerator * (1.0 / total), 0.0)
        for i in range((last - first) // LANES):
            at = (first - (DA - SHIFT)) // LANES + i
            part = out[:, i * LANES : (i + 1) * LANES]
            pieces[at] = part if pieces[at] is None else pieces[at] + part
    return jnp.concatenate(pieces, axis=1)


def each_block(count, body):
    if count <= BLOCK:
        body(0, count)
    else:

        @pl.loop(0, count // SMALL_BLOCK)
        def _(i):
            body(pl.multiple_of(i * SMALL_BLOCK, SMALL_BLOCK), SMALL_BLOCK)


def params(count):
    return pltpu.CompilerParams(vmem_limit_bytes=(24 if count <= BLOCK else 56) * 1024 * 1024)


def copy_of(block, own, other, target, sem):
    section = lax.axis_index("pipe")

    @pl.when(section == block)
    def _():
        pltpu.make_async_copy(own, target, sem).start()

    @pl.when(section != block)
    def _():
        pltpu.make_async_copy(other, target, sem).start()

    return pltpu.make_async_copy(own, target, sem)


def copy_qkv(block, own_ref, other_ref, w_ref, sems):
    return [
        copy_of(block, own_ref.at[0, a:b], other_ref.at[0, a:b], w_ref.at[a:b], sems.at[i])
        for i, (a, b) in enumerate(((0, DA), (DA, 3 * DA)))
    ]


def copy_out(block, own_ref, other_ref, wo_ref, sem):
    return copy_of(block, own_ref.at[0], other_ref.at[0], wo_ref.at[SHIFT:DP], sem)


def query_of(modulated, w_ref):
    projected = dot_t(modulated, w_ref[:DP]) * QUERY_SCALE
    lane = lax.broadcasted_iota(jnp.int32, projected.shape, 1)
    return jnp.where(lane < DA, projected, 0.0).astype(BF16)


def join(refs, target):
    at = 0
    for ref in refs:
        rows = ref.shape[0]
        target[at : at + rows] = ref[...]
        at += rows


def chunks(first, last, step=256):
    return [(at, min(at + step, last)) for at in range(first, last, step)]


KV_CUTS = chunks(DA, 3 * DA)
QUERY_CUTS = chunks(0, DA)


def project_kernel(n_pieces, n_stale, *refs):
    piece_refs = refs[:n_pieces]
    stale_refs = refs[n_pieces : n_pieces + n_stale]
    vec_ref, own_ref, other_ref, x_ref, q_ref, kv_ref, stale_ref, w_ref, sems = refs[n_pieces + n_stale :]
    count = x_ref.shape[0]
    copies = [
        copy_of(0, own_ref.at[0, a:b], other_ref.at[0, a:b], w_ref.at[a:b], sems.at[i])
        for i, (a, b) in enumerate(KV_CUTS + QUERY_CUTS)
    ]
    join(piece_refs, x_ref)
    join(stale_refs, stale_ref)
    if count > BLOCK:
        for copy in copies:
            copy.wait()

    def body(start, size):
        rows = pl.ds(start, size)
        modulated = normed(x_ref[rows].astype(F32), vec_ref[1:2], vec_ref[0:1])
        for i, (a, b) in enumerate(KV_CUTS):
            if count <= BLOCK:
                copies[i].wait()
            kv_ref[rows, a - DA : b - DA] = dot_t(modulated, w_ref[a:b]).astype(BF16)
        if count <= BLOCK:
            for copy in copies[len(KV_CUTS) :]:
                copy.wait()
        q_ref[rows] = query_of(modulated, w_ref)

    each_block(count, body)


def project(pieces, stale_pieces, vecs, w_own, w_other):
    count = sum(piece.shape[0] for piece in pieces)
    stale_count = sum(piece.shape[0] for piece in stale_pieces)
    return pl.pallas_call(
        functools.partial(project_kernel, len(pieces), len(stale_pieces)),
        out_shape=(
            jax.ShapeDtypeStruct((count, D), BF16),
            jax.ShapeDtypeStruct((count, DP), BF16),
            jax.ShapeDtypeStruct((count, 2 * DA), BF16),
            jax.ShapeDtypeStruct((stale_count, 2 * DA), BF16),
        ),
        in_specs=[VMEM] * (len(pieces) + len(stale_pieces) + 1) + [ANY] * 2,
        out_specs=(VMEM,) * 4,
        scratch_shapes=[
            pltpu.VMEM((3 * DA, D), BF16),
            pltpu.SemaphoreType.DMA((len(KV_CUTS) + len(QUERY_CUTS),)),
        ],
        compiler_params=params(count),
        name="layer_norm_and_projections",
    )(*pieces, *stale_pieces, vecs, in_hbm(w_own), w_other)


def in_hbm(array):
    return pltpu.with_memory_space_constraint(array, pltpu.HBM)


def block_kernel(n_pieces, *refs):
    stale_refs = refs[:n_pieces]
    (
        x_ref, q_ref, kv_ref, got_ref, idx_ref, vec_ref, w_own, w_other, wo_own, wo_other,
        xt_ref, qt_ref, kv1_ref, send_ref, w_ref, wo_ref, all_ref, pick_ref, sems,
    ) = refs[n_pieces:]
    count = x_ref.shape[0]
    out_copy = copy_out(0, wo_own, wo_other, wo_ref, sems.at[2])
    in_copies = copy_qkv(1, w_own, w_other, w_ref, sems)
    first_core = lax.axis_index("pipe") == 0
    wo_ref[:SHIFT] = jnp.zeros((SHIFT, D), BF16)
    all_ref[:count] = kv_ref[...]
    at = 0
    for ref in stale_refs:
        rows = ref.shape[0]
        all_ref[count + at : count + at + rows] = jnp.where(first_core, ref[...], got_ref[at : at + rows])
        send_ref[at : at + rows] = ref[...]
        at += rows
    pick_ref[...] = jnp.zeros_like(pick_ref)
    tile_rows = idx_ref.shape[0]
    waits = [out_copy] + in_copies
    if count > BLOCK:
        for copy in waits:
            copy.wait()

    def body(start, size):
        rows = pl.ds(start, size)
        attended = attend(q_ref[rows], all_ref).astype(BF16)
        if count <= BLOCK:
            for copy in waits:
                copy.wait()
        branch = dot(attended, wo_ref[...])
        x1 = (x_ref[rows].astype(F32) + vec_ref[2:3] * branch).astype(BF16)
        modulated = normed(x1.astype(F32), vec_ref[4:5], vec_ref[3:4])
        fresh = dot_t(modulated, w_ref[DA:]).astype(BF16)
        kv1_ref[rows] = fresh

        @pl.when(first_core)
        def _():
            send_ref[rows] = fresh

        lane = lax.broadcasted_iota(jnp.int32, (tile_rows, size), 1) + start
        chosen = (lane == idx_ref[:, :1]).astype(F32).astype(BF16)
        pick_ref[0] += dot(chosen, x1)
        pick_ref[1] += dot(chosen, modulated)

    each_block(count, body)
    xt_ref[...] = pick_ref[0].astype(BF16)
    qt_ref[...] = query_of(pick_ref[1].astype(BF16), w_ref)


def first_block(stale_pieces, x, q, kv, got, idx, vecs, w_own, w_other, wo_own, wo_other):
    count = x.shape[0]
    tile_rows = idx.shape[0]
    return pl.pallas_call(
        functools.partial(block_kernel, len(stale_pieces)),
        out_shape=(
            jax.ShapeDtypeStruct((tile_rows, D), BF16),
            jax.ShapeDtypeStruct((tile_rows, DP), BF16),
            jax.ShapeDtypeStruct((count, 2 * DA), BF16),
            jax.ShapeDtypeStruct((count, 2 * DA), BF16),
        ),
        in_specs=[VMEM] * (len(stale_pieces) + 6) + [ANY] * 4,
        out_specs=(VMEM,) * 4,
        scratch_shapes=[
            pltpu.VMEM((3 * DA, D), BF16),
            pltpu.VMEM((DP, D), BF16),
            pltpu.VMEM((2 * count, 2 * DA), BF16),
            pltpu.VMEM((2, tile_rows, D), F32),
            pltpu.SemaphoreType.DMA((3,)),
        ],
        compiler_params=params(count),
        name="attention_and_next_keys",
    )(
        *stale_pieces, x, q, kv, got, idx, vecs, in_hbm(w_own), w_other, in_hbm(wo_own), wo_other
    )


def tile_kernel(
    x_ref, q_ref, kv_ref, got_ref, idx_ref, vec_ref, wf_ref, wo_own, wo_other, patch_ref, wo_ref, all_ref, sems
):
    count = kv_ref.shape[0]
    out_copy = copy_out(1, wo_own, wo_other, wo_ref, sems.at[0])
    wo_ref[:SHIFT] = jnp.zeros((SHIFT, D), BF16)
    all_ref[:count] = kv_ref[...]
    all_ref[count:] = got_ref[...]
    attended = attend(q_ref[...], all_ref).astype(BF16)
    out_copy.wait()
    branch = dot(attended, wo_ref[...])
    x2 = (x_ref[...].astype(F32) + vec_ref[5:6] * branch).astype(BF16)
    final = normed(x2.astype(F32), vec_ref[7:8], vec_ref[6:7])
    patches = dot_t(final, wf_ref[...]).astype(BF16).astype(F32)
    patch_ref[...] = jnp.zeros_like(patch_ref)
    patch_ref[:, : 4 * LATC] = jnp.where(idx_ref[:, :1] >= 0, patches, 0.0)


def tile_block(x, q, kv, got, idx, vecs, w_final, wo_own, wo_other):
    count = kv.shape[0]
    return pl.pallas_call(
        tile_kernel,
        out_shape=jax.ShapeDtypeStruct((x.shape[0], LANES), F32),
        in_specs=[VMEM] * 7 + [ANY] * 2,
        out_specs=VMEM,
        scratch_shapes=[
            pltpu.VMEM((DP, D), BF16),
            pltpu.VMEM((2 * count, 2 * DA), BF16),
            pltpu.SemaphoreType.DMA((1,)),
        ],
        compiler_params=params(count),
        name="tile_attention_and_patches",
    )(x, q, kv, got, idx, vecs, w_final, in_hbm(wo_own), wo_other)


def decode_kernel(
    rows, cols, pitch, patch_ref, got_ref, idx_ref, wp_ref, bin_ref, bup_ref, w_any, out_ref, w_ref, u_ref, ub_ref, sems
):
    copies = [pltpu.make_async_copy(w_any.at[t], w_ref.at[t], sems.at[t]) for t in range(9)]
    order = [3, 4, 5, 0, 1, 2, 6, 7, 8]
    for t in order:
        copies[t].start()
    first_core = lax.axis_index("pipe") == 0
    got = got_ref[:pitch]
    above = jnp.where(first_core, 0.0, got)
    below = jnp.where(first_core, got, 0.0)
    rim = [above] + [patch_ref[r * pitch : (r + 1) * pitch] for r in range(rows)] + [below]
    column_in = idx_ref[:pitch, :1] >= 0
    shifted = [[pltpu.roll(p, (-ds) % pitch, 0) if ds else p for ds in (-1, 0, 1)] for p in rim]
    for r in range(rows + 2):
        low, high = None, None
        for dr in (-1, 0, 1):
            if not 0 <= r + dr < rows + 2:
                continue
            for ds in range(3):
                tap = (dr + 1) * 3 + ds
                piece = shifted[r + dr][ds]
                if tap == 8:
                    high = piece
                else:
                    piece = pltpu.roll(piece, 4 * LATC * tap, 1) if tap else piece
                    low = piece if low is None else low + piece
        high = jnp.zeros_like(low) if high is None else high
        around = jnp.concatenate([low, high], axis=1).astype(BF16)
        for p in range(2):
            y = 2 * (r - 1) + p + 1
            if not 0 <= y < 2 * rows + 2:
                continue
            for q in range(2):
                at = (2 * p + q) * 2 * LANES
                act = dot(around, wp_ref[at : at + 2 * LANES]) + bin_ref[...]
                feature = act / (1.0 + jnp.exp(-act))
                keep = column_in
                if y == 0:
                    keep = keep & jnp.logical_not(first_core)
                if y == 2 * rows + 1:
                    keep = keep & first_core
                feature = jnp.where(keep, feature, 0.0)
                for c in range(CH // LANES):
                    part = feature[:, c * LANES : (c + 1) * LANES]
                    u_ref[y, c, pl.ds(2 * q, pitch, stride=4), :] = part
                    u_ref[y, c, pl.ds(2 * q + 1, pitch, stride=4), :] = part
    wide = 4 * cols
    for y in range(2 * rows + 2):
        for dx in range(3):
            for c in range(CH // LANES):
                ub_ref[dx, y * wide : (y + 1) * wide, c * LANES : (c + 1) * LANES] = u_ref[
                    y, c, 3 + dx : 3 + dx + wide, :
                ].astype(BF16)

    def tap_row(dy, y_first, y_count):
        total = None
        for dx in range(3):
            copies[3 * dy + dx].wait()
            part = dot(ub_ref[dx, y_first * wide : (y_first + y_count) * wide], w_ref[3 * dy + dx])
            total = part if total is None else total + part
        return total

    def rows_of(total, y):
        return total[y * wide : (y + 1) * wide]

    middle = tap_row(1, 1, 2 * rows) + bup_ref[...]
    before = tap_row(0, 0, 2 * rows + 1)
    after = tap_row(2, 1, 2 * rows + 1)
    for y in range(2 * rows):
        own = rows_of(middle, y)
        out_ref[2 * y] = (own + rows_of(before, y) + rows_of(after, y)).astype(BF16)
        out_ref[2 * y + 1] = (own + rows_of(before, y + 1) + rows_of(after, y + 1)).astype(BF16)


def decode(rows, cols, pitch, patches, got, idx, w_patch, b_in, b_up, w_up):
    return pl.pallas_call(
        functools.partial(decode_kernel, rows, cols, pitch),
        out_shape=jax.ShapeDtypeStruct((4 * rows, 4 * cols, CH), BF16),
        in_specs=[VMEM] * 6 + [ANY],
        out_specs=VMEM,
        scratch_shapes=[
            pltpu.VMEM((9, CH, CH), BF16),
            pltpu.VMEM((2 * rows + 2, CH // LANES, 4 * pitch, LANES), F32),
            pltpu.VMEM((3, (2 * rows + 2) * 4 * cols, CH), BF16),
            pltpu.SemaphoreType.DMA((9,)),
        ],
        compiler_params=params(0),
        name="decoder_convolutions",
    )(patches, got, idx, w_patch, b_in, b_up, w_up)


def patch_selector():
    sel = np.zeros((2, 2, 3, 3, 2, 2, LATC, 9 * LATC), np.float32)
    for p, q, dr, ds, pp, qq in np.ndindex(2, 2, 3, 3, 2, 2):
        dy = 2 * (dr - 1) + pp - p
        dx = 2 * (ds - 1) + qq - q
        if abs(dy) <= 1 and abs(dx) <= 1:
            tap = (dy + 1) * 3 + dx + 1
            for c in range(LATC):
                sel[p, q, dr, ds, pp, qq, c, tap * LATC + c] = 1.0
    sel = sel.reshape(4, 9 * 4 * LATC, 9 * LATC)
    return np.pad(sel, ((0, 0), (0, 2 * LANES - 9 * 4 * LATC), (0, 0))).reshape(-1, 9 * LATC)


def split_of(n):
    inner = 2 ** (int(math.log2(n)) // 2)
    return n // inner, inner


def shifted(block, k_outer, k_inner):
    n = lax.axis_size("patch")
    outer, inner = split_of(n)
    route = []
    for i in range(n):
        o, e = divmod(i, inner)
        route.append(((o + k_outer) % outer * inner + (e + k_inner) % inner, i))
    return lax.ppermute(block, "patch", route)


def local(
    tokens,
    stale_kv,
    w_qkv,
    w_out,
    block_table,
    time_table,
    t_index,
    w_final,
    w_in,
    b_in,
    w_up,
    b_up,
):
    section = lax.axis_index("pipe")
    tile = lax.axis_index("patch")
    n_tiles = lax.axis_size("patch")
    swap = [(0, 1), (1, 0)]
    first_core = section == 0
    own_count = tokens.shape[1]
    count = own_count * n_tiles
    rows = count // TC
    cols = TC // n_tiles
    pitch = -(-(cols + 3) // 8) * 8
    outer, inner = split_of(n_tiles)

    own_tokens = lax.dynamic_index_in_dim(tokens, section, 0, keepdims=False)
    w_qkv = jnp.swapaxes(w_qkv, 1, 2)
    w_qkv_other = lax.ppermute(w_qkv, "pipe", swap)
    w_out_other = lax.ppermute(w_out, "pipe", swap)
    tables = lax.all_gather(block_table[0], "pipe")
    x_column = [shifted(own_tokens, k, 0) for k in range(1, outer)]

    time_row = lax.dynamic_index_in_dim(time_table, t_index[0], 0, keepdims=False)
    ones = jnp.asarray([[0.0], [1.0], [0.0]], F32)
    vecs = jnp.concatenate(
        [
            time_row[:3] + tables[0] + ones,
            time_row[:3] + tables[1] + ones,
            time_row[3:5] + ones[:2],
        ],
        axis=0,
    )

    padded_rows = -(-rows * pitch // 16) * 16
    place = jnp.arange(padded_rows)
    column = place % pitch - 1 + tile * cols
    inside = (place % pitch < cols + 2) & (place < rows * pitch) & (column >= 0) & (column < TC)
    token = place // pitch * TC + jnp.clip(column, 0, TC - 1)
    source = token // own_count
    k_outer = (source // inner - tile // inner) % outer
    k_inner = (source % inner - tile % inner) % inner
    spot = (k_inner * outer + k_outer) * own_count + token % own_count
    idx = jnp.broadcast_to(jnp.where(inside, spot, -1)[:, None], (padded_rows, LANES)).astype(jnp.int32)

    w_patch = dot(jnp.asarray(patch_selector(), BF16), w_in).astype(BF16)

    x_column, w_qkv_other, w_out_other, vecs, w_patch, idx, own_stale = lax.optimization_barrier(
        (x_column, w_qkv_other, w_out_other, vecs, w_patch, idx, stale_kv[0, 1])
    )
    x_column = jnp.concatenate([own_tokens] + x_column, axis=0)
    x_pieces = [x_column] + [shifted(x_column, 0, k) for k in range(1, inner)]
    stale_column = [own_stale] + [shifted(own_stale, k, 0) for k in range(1, outer)]
    x, query, fresh, stale_column = project(x_pieces, stale_column, vecs, w_qkv, w_qkv_other)
    got = lax.ppermute(fresh, "pipe", [(0, 1)])
    stale_pieces = [stale_column] + [shifted(stale_column, 0, k) for k in range(1, inner)]
    x_tile, q_tile, fresh, send = first_block(
        stale_pieces, x, query, fresh, got, idx, vecs, w_qkv, w_qkv_other, w_out, w_out_other
    )
    got = lax.ppermute(send, "pipe", swap)
    patches = tile_block(x_tile, q_tile, fresh, got, idx, vecs, w_final.T, w_out, w_out_other)
    edge = patches
    if rows > 1:
        edge = jnp.where(first_core, patches[(rows - 1) * pitch : rows * pitch], patches[:pitch])
    got = lax.ppermute(edge, "pipe", swap)
    return decode(rows, cols, pitch, patches, got, idx, w_patch, b_in[None], b_up[None], w_up)


def solution(mesh):
    placed = (
        P(None, ("grp", "patch"), None),
        P("pipe", None, ("grp", "patch"), None),
        P("pipe", None, None),
        P("pipe", None, None),
        P("pipe", None, None),
        P(),
        P("grp"),
        P(),
        P(),
        P(),
        P(),
        P(),
    )
    return jax.shard_map(
        local,
        mesh=mesh,
        in_specs=placed,
        out_specs=P(("grp", "pipe"), "patch", None),
        check_vma=False,
    )
```

```python
import functools
import math

import jax
import jax.numpy as jnp
import numpy as np
from jax import lax
from jax.experimental import pallas as pl
from jax.experimental.pallas import tpu as pltpu
from jax.sharding import PartitionSpec as P

D = 1152
DH = 72
HEADS = 8
CH = 512
LATC = 4
TC = 256
DA = 576
DP = 640
SHIFT = 64
EPSILON = 1e-06
QUERY_SCALE = math.log2(math.e) / math.sqrt(DH)
BLOCK = 256
SMALL_BLOCK = 64
LANES = 128

F32 = jnp.float32
BF16 = jnp.bfloat16
VMEM = pl.BlockSpec(memory_space=pltpu.VMEM)
ANY = pl.BlockSpec(memory_space=pl.ANY)


def dot(a, b):
    return jnp.dot(a, b, preferred_element_type=F32)


def dot_t(a, b):
    return lax.dot_general(a, b, (((1,), (1,)), ((), ())), preferred_element_type=F32)


def normed(values, scale, shift):
    average = jnp.mean(values, axis=-1, keepdims=True)
    centred = values - average
    variance = jnp.mean(centred * centred, axis=-1, keepdims=True)
    return (centred * lax.rsqrt(variance + EPSILON) * scale + shift).astype(BF16)


def lane_window(start):
    return start // LANES * LANES, -(-(start + DH) // LANES) * LANES


def attend(query, kv_ref):
    count = query.shape[0]
    pieces = [None] * (DP // LANES)
    for head in range(HEADS):
        first, last = lane_window(head * DH)
        lane = lax.broadcasted_iota(jnp.int32, (count, last - first), 1) + first
        own = (lane >= head * DH) & (lane < (head + 1) * DH)
        q = jnp.where(own, query[:, first:last], jnp.zeros((), BF16))
        scores = dot_t(q, kv_ref[:, first:last])
        exponent = jnp.exp2(scores - jnp.max(scores, axis=1, keepdims=True))
        total = jnp.sum(exponent, axis=1, keepdims=True)
        start = DA + head * DH
        first, last = lane_window(start)
        numerator = dot(exponent.astype(BF16), kv_ref[:, first:last])
        lane = lax.broadcasted_iota(jnp.int32, (count, last - first), 1) + first
        own = (lane >= start) & (lane < start + DH)
        out = jnp.where(own, numerator * (1.0 / total), 0.0)
        for i in range((last - first) // LANES):
            at = (first - (DA - SHIFT)) // LANES + i
            part = out[:, i * LANES : (i + 1) * LANES]
            pieces[at] = part if pieces[at] is None else pieces[at] + part
    return jnp.concatenate(pieces, axis=1)


def each_block(count, body):
    if count <= BLOCK:
        body(0, count)
    else:

        @pl.loop(0, count // SMALL_BLOCK)
        def _(i):
            body(pl.multiple_of(i * SMALL_BLOCK, SMALL_BLOCK), SMALL_BLOCK)


def params(count):
    return pltpu.CompilerParams(vmem_limit_bytes=(24 if count <= BLOCK else 56) * 1024 * 1024)


def weights_kernel(own_ref, other_ref, wo_own, wo_other, w0_ref, w1_ref, wo0_ref, wo1_ref, sems):
    first = lax.axis_index("pipe") == 0
    pad = jnp.zeros((SHIFT, D), BF16)
    wo0_ref[:SHIFT] = pad
    wo1_ref[:SHIFT] = pad
    outs = (wo0_ref.at[SHIFT:], wo1_ref.at[SHIFT:])
    copies = []
    for i, (in_place, arrived, targets) in enumerate(
        ((own_ref.at[0], other_ref.at[0], (w0_ref, w1_ref)), (wo_own.at[0], wo_other.at[0], outs))
    ):
        for block in range(2):
            own = (first if block == 0 else jnp.logical_not(first))
            sem = sems.at[2 * i + block]
            copies.append(pltpu.make_async_copy(in_place, targets[block], sem))

            @pl.when(own)
            def _():
                pltpu.make_async_copy(in_place, targets[block], sem).start()

            @pl.when(jnp.logical_not(own))
            def _():
                pltpu.make_async_copy(arrived, targets[block], sem).start()

    for copy in copies:
        copy.wait()


def weights_in_vmem(w_own, w_other, wo_own, wo_other):
    return pl.pallas_call(
        weights_kernel,
        out_shape=(jax.ShapeDtypeStruct((3 * DA, D), BF16),) * 2 + (jax.ShapeDtypeStruct((DP, D), BF16),) * 2,
        in_specs=[ANY] * 4,
        out_specs=(VMEM,) * 4,
        scratch_shapes=[pltpu.SemaphoreType.DMA((4,))],
        compiler_params=params(0),
        name="weights_by_block",
    )(in_hbm(w_own), w_other, in_hbm(wo_own), wo_other)


def query_of(modulated, w_ref):
    projected = dot_t(modulated, w_ref[:DP]) * QUERY_SCALE
    lane = lax.broadcasted_iota(jnp.int32, projected.shape, 1)
    return jnp.where(lane < DA, projected, 0.0).astype(BF16)


def join(refs, target):
    at = 0
    for ref in refs:
        rows = ref.shape[0]
        target[at : at + rows] = ref[...]
        at += rows


def project_kernel(n_pieces, *refs):
    piece_refs = refs[:n_pieces]
    vec_ref, w_ref, x_ref, q_ref, kv_ref = refs[n_pieces:]
    join(piece_refs, x_ref)

    def body(start, size):
        rows = pl.ds(start, size)
        modulated = normed(x_ref[rows].astype(F32), vec_ref[1:2], vec_ref[0:1])
        kv_ref[rows] = dot_t(modulated, w_ref[DA:]).astype(BF16)
        q_ref[rows] = query_of(modulated, w_ref)

    each_block(x_ref.shape[0], body)


def project(pieces, vecs, weights):
    count = sum(piece.shape[0] for piece in pieces)
    return pl.pallas_call(
        functools.partial(project_kernel, len(pieces)),
        out_shape=(
            jax.ShapeDtypeStruct((count, D), BF16),
            jax.ShapeDtypeStruct((count, DP), BF16),
            jax.ShapeDtypeStruct((count, 2 * DA), BF16),
        ),
        in_specs=[VMEM] * (len(pieces) + 2),
        out_specs=(VMEM,) * 3,
        compiler_params=params(count),
        name="layer_norm_and_projections",
    )(*pieces, vecs, weights)


def in_hbm(array):
    return pltpu.with_memory_space_constraint(array, pltpu.HBM)


def block_kernel(n_pieces, n_got, *refs):
    stale_refs = refs[:n_pieces]
    got_refs = refs[n_pieces : n_pieces + n_got]
    (
        x_ref, q_ref, kv_ref, idx_ref, vec_ref, w0_ref, w1_ref, wo_ref,
        xt_ref, qt_ref, kv1_ref, send_ref, all_ref, pick_ref,
    ) = refs[n_pieces + n_got :]
    count = x_ref.shape[0]
    first_core = lax.axis_index("pipe") == 0
    all_ref[:count] = kv_ref[...]
    join(stale_refs, send_ref)

    @pl.when(first_core)
    def _():
        join(stale_refs, all_ref.at[count:])

    @pl.when(jnp.logical_not(first_core))
    def _():
        at = count
        for ref in got_refs:

            def body(start, size):
                modulated = normed(ref[pl.ds(start, size)].astype(F32), vec_ref[1:2], vec_ref[0:1])
                all_ref[pl.ds(at + start, size)] = dot_t(modulated, w0_ref[DA:]).astype(BF16)

            each_block(ref.shape[0], body)
            at += ref.shape[0]

    pick_ref[...] = jnp.zeros_like(pick_ref)
    tile_rows = idx_ref.shape[0]

    def body(start, size):
        rows = pl.ds(start, size)
        attended = attend(q_ref[rows], all_ref).astype(BF16)
        branch = dot(attended, wo_ref[...])
        x1 = (x_ref[rows].astype(F32) + vec_ref[2:3] * branch).astype(BF16)
        modulated = normed(x1.astype(F32), vec_ref[4:5], vec_ref[3:4])
        fresh = dot_t(modulated, w1_ref[DA:]).astype(BF16)
        kv1_ref[rows] = fresh

        @pl.when(first_core)
        def _():
            send_ref[rows] = fresh

        lane = lax.broadcasted_iota(jnp.int32, (tile_rows, size), 1) + start
        chosen = (lane == idx_ref[:, :1]).astype(F32).astype(BF16)
        pick_ref[0] += dot(chosen, x1)
        pick_ref[1] += dot(chosen, modulated)

    each_block(count, body)
    xt_ref[...] = pick_ref[0].astype(BF16)
    qt_ref[...] = query_of(pick_ref[1].astype(BF16), w1_ref)


def first_block(stale_pieces, got_pieces, x, q, kv, idx, vecs, w_block, w_next, wo_block):
    count = x.shape[0]
    tile_rows = idx.shape[0]
    return pl.pallas_call(
        functools.partial(block_kernel, len(stale_pieces), len(got_pieces)),
        out_shape=(
            jax.ShapeDtypeStruct((tile_rows, D), BF16),
            jax.ShapeDtypeStruct((tile_rows, DP), BF16),
            jax.ShapeDtypeStruct((count, 2 * DA), BF16),
            jax.ShapeDtypeStruct((count, 2 * DA), BF16),
        ),
        in_specs=[VMEM] * (len(stale_pieces) + len(got_pieces) + 8),
        out_specs=(VMEM,) * 4,
        scratch_shapes=[
            pltpu.VMEM((2 * count, 2 * DA), BF16),
            pltpu.VMEM((2, tile_rows, D), F32),
        ],
        compiler_params=params(count),
        name="attention_and_next_keys",
    )(*stale_pieces, *got_pieces, x, q, kv, idx, vecs, w_block, w_next, wo_block)


def tile_kernel(x_ref, q_ref, kv_ref, got_ref, idx_ref, vec_ref, wf_ref, wo_ref, patch_ref, all_ref):
    count = kv_ref.shape[0]
    all_ref[:count] = kv_ref[...]
    all_ref[count:] = got_ref[...]
    attended = attend(q_ref[...], all_ref).astype(BF16)
    branch = dot(attended, wo_ref[...])
    x2 = (x_ref[...].astype(F32) + vec_ref[5:6] * branch).astype(BF16)
    final = normed(x2.astype(F32), vec_ref[7:8], vec_ref[6:7])
    patches = dot_t(final, wf_ref[...]).astype(BF16).astype(F32)
    patch_ref[...] = jnp.zeros_like(patch_ref)
    patch_ref[:, : 4 * LATC] = jnp.where(idx_ref[:, :1] >= 0, patches, 0.0)


def tile_block(x, q, kv, got, idx, vecs, w_final, wo_block):
    count = kv.shape[0]
    return pl.pallas_call(
        tile_kernel,
        out_shape=jax.ShapeDtypeStruct((x.shape[0], LANES), F32),
        in_specs=[VMEM] * 8,
        out_specs=VMEM,
        scratch_shapes=[pltpu.VMEM((2 * count, 2 * DA), BF16)],
        compiler_params=params(count),
        name="tile_attention_and_patches",
    )(x, q, kv, got, idx, vecs, w_final, wo_block)


def decode_kernel(
    rows, cols, pitch, patch_ref, got_ref, idx_ref, wp_ref, bin_ref, bup_ref, w_ref, out_ref, u_ref, ub_ref
):
    first_core = lax.axis_index("pipe") == 0
    got = got_ref[:pitch]
    above = jnp.where(first_core, 0.0, got)
    below = jnp.where(first_core, got, 0.0)
    rim = [above] + [patch_ref[r * pitch : (r + 1) * pitch] for r in range(rows)] + [below]
    column_in = idx_ref[:pitch, :1] >= 0
    shifted = [[pltpu.roll(p, (-ds) % pitch, 0) if ds else p for ds in (-1, 0, 1)] for p in rim]
    for r in range(rows + 2):
        low, high = None, None
        for dr in (-1, 0, 1):
            if not 0 <= r + dr < rows + 2:
                continue
            for ds in range(3):
                tap = (dr + 1) * 3 + ds
                piece = shifted[r + dr][ds]
                if tap == 8:
                    high = piece
                else:
                    piece = pltpu.roll(piece, 4 * LATC * tap, 1) if tap else piece
                    low = piece if low is None else low + piece
        high = jnp.zeros_like(low) if high is None else high
        around = jnp.concatenate([low, high], axis=1).astype(BF16)
        for p in range(2):
            y = 2 * (r - 1) + p + 1
            if not 0 <= y < 2 * rows + 2:
                continue
            for q in range(2):
                at = (2 * p + q) * 2 * LANES
                act = dot(around, wp_ref[at : at + 2 * LANES]) + bin_ref[...]
                feature = act / (1.0 + jnp.exp(-act))
                keep = column_in
                if y == 0:
                    keep = keep & jnp.logical_not(first_core)
                if y == 2 * rows + 1:
                    keep = keep & first_core
                feature = jnp.where(keep, feature, 0.0)
                for c in range(CH // LANES):
                    part = feature[:, c * LANES : (c + 1) * LANES]
                    u_ref[y, c, pl.ds(2 * q, pitch, stride=4), :] = part
                    u_ref[y, c, pl.ds(2 * q + 1, pitch, stride=4), :] = part
    wide = 4 * cols
    for y in range(2 * rows + 2):
        for dx in range(3):
            for c in range(CH // LANES):
                ub_ref[dx, y * wide : (y + 1) * wide, c * LANES : (c + 1) * LANES] = u_ref[
                    y, c, 3 + dx : 3 + dx + wide, :
                ].astype(BF16)

    def tap_row(dy, y_first, y_count):
        total = None
        for dx in range(3):
            part = dot(ub_ref[dx, y_first * wide : (y_first + y_count) * wide], w_ref[3 * dy + dx])
            total = part if total is None else total + part
        return total

    def rows_of(total, y):
        return total[y * wide : (y + 1) * wide]

    middle = tap_row(1, 1, 2 * rows) + bup_ref[...]
    before = tap_row(0, 0, 2 * rows + 1)
    after = tap_row(2, 1, 2 * rows + 1)
    for y in range(2 * rows):
        own = rows_of(middle, y)
        out_ref[2 * y] = (own + rows_of(before, y) + rows_of(after, y)).astype(BF16)
        out_ref[2 * y + 1] = (own + rows_of(before, y + 1) + rows_of(after, y + 1)).astype(BF16)


def decode(rows, cols, pitch, patches, got, idx, w_patch, b_in, b_up, w_up):
    return pl.pallas_call(
        functools.partial(decode_kernel, rows, cols, pitch),
        out_shape=jax.ShapeDtypeStruct((4 * rows, 4 * cols, CH), BF16),
        in_specs=[VMEM] * 7,
        out_specs=VMEM,
        scratch_shapes=[
            pltpu.VMEM((2 * rows + 2, CH // LANES, 4 * pitch, LANES), F32),
            pltpu.VMEM((3, (2 * rows + 2) * 4 * cols, CH), BF16),
        ],
        compiler_params=params(0),
        name="decoder_convolutions",
    )(patches, got, idx, w_patch, b_in, b_up, w_up)


def patch_selector():
    sel = np.zeros((2, 2, 3, 3, 2, 2, LATC, 9 * LATC), np.float32)
    for p, q, dr, ds, pp, qq in np.ndindex(2, 2, 3, 3, 2, 2):
        dy = 2 * (dr - 1) + pp - p
        dx = 2 * (ds - 1) + qq - q
        if abs(dy) <= 1 and abs(dx) <= 1:
            tap = (dy + 1) * 3 + dx + 1
            for c in range(LATC):
                sel[p, q, dr, ds, pp, qq, c, tap * LATC + c] = 1.0
    sel = sel.reshape(4, 9 * 4 * LATC, 9 * LATC)
    return np.pad(sel, ((0, 0), (0, 2 * LANES - 9 * 4 * LATC), (0, 0))).reshape(-1, 9 * LATC)


def split_of(n):
    inner = 2 ** (int(math.log2(n)) // 2)
    return n // inner, inner


def shifted(block, k_outer, k_inner):
    n = lax.axis_size("patch")
    outer, inner = split_of(n)
    route = []
    for i in range(n):
        o, e = divmod(i, inner)
        route.append(((o + k_outer) % outer * inner + (e + k_inner) % inner, i))
    return lax.ppermute(block, "patch", route)


def local(
    tokens,
    stale_kv,
    w_qkv,
    w_out,
    block_table,
    time_table,
    t_index,
    w_final,
    w_in,
    b_in,
    w_up,
    b_up,
):
    section = lax.axis_index("pipe")
    tile = lax.axis_index("patch")
    n_tiles = lax.axis_size("patch")
    swap = [(0, 1), (1, 0)]
    first_core = section == 0
    own_count = tokens.shape[1]
    count = own_count * n_tiles
    rows = count // TC
    cols = TC // n_tiles
    pitch = -(-(cols + 3) // 8) * 8
    outer, inner = split_of(n_tiles)

    own_tokens = lax.dynamic_index_in_dim(tokens, section, 0, keepdims=False)
    w_qkv = jnp.swapaxes(w_qkv, 1, 2)
    w_qkv_other = lax.ppermute(w_qkv, "pipe", swap)
    tables = lax.all_gather(block_table[0], "pipe")
    x_column = [shifted(own_tokens, k, 0) for k in range(1, outer)]

    time_row = lax.dynamic_index_in_dim(time_table, t_index[0], 0, keepdims=False)
    ones = jnp.asarray([[0.0], [1.0], [0.0]], F32)
    vecs = jnp.concatenate(
        [
            time_row[:3] + tables[0] + ones,
            time_row[:3] + tables[1] + ones,
            time_row[3:5] + ones[:2],
        ],
        axis=0,
    )

    padded_rows = -(-rows * pitch // 16) * 16
    place = jnp.arange(padded_rows)
    column = place % pitch - 1 + tile * cols
    inside = (place % pitch < cols + 2) & (place < rows * pitch) & (column >= 0) & (column < TC)
    token = place // pitch * TC + jnp.clip(column, 0, TC - 1)
    source = token // own_count
    k_outer = (source // inner - tile // inner) % outer
    k_inner = (source % inner - tile % inner) % inner
    spot = (k_inner * outer + k_outer) * own_count + token % own_count
    idx = jnp.broadcast_to(jnp.where(inside, spot, -1)[:, None], (padded_rows, LANES)).astype(jnp.int32)

    x_column, w_qkv_other, vecs, idx, own_stale, w_in, w_out = lax.optimization_barrier(
        (x_column, w_qkv_other, vecs, idx, stale_kv[0, 1], w_in, w_out)
    )
    w_patch = dot(jnp.asarray(patch_selector(), BF16), w_in).astype(BF16)
    x_column = jnp.concatenate([own_tokens] + x_column, axis=0)
    x_column, own_stale, w_out = lax.optimization_barrier((x_column, own_stale, w_out))
    x_pieces = [x_column] + [shifted(x_column, 0, k) for k in range(1, inner)]
    stale_column = [own_stale] + [shifted(own_stale, k, 0) for k in range(1, outer)]
    w_out_other = lax.ppermute(w_out, "pipe", swap)
    w_0, w_1, wo_0, wo_1 = weights_in_vmem(w_qkv, w_qkv_other, w_out, w_out_other)
    x_pieces, stale_column, w_patch, w_0 = lax.optimization_barrier((x_pieces, stale_column, w_patch, w_0))
    stale_column = jnp.concatenate(stale_column, axis=0)
    x_pieces, stale_column, w_patch = lax.optimization_barrier((x_pieces, stale_column, w_patch))
    got_pieces = [lax.ppermute(piece, "pipe", [(0, 1)]) for piece in x_pieces]
    x, query, fresh = project(x_pieces, vecs, w_0)
    stale_pieces = [stale_column] + [shifted(stale_column, 0, k) for k in range(1, inner)]
    x_tile, q_tile, fresh, send = first_block(
        stale_pieces, got_pieces, x, query, fresh, idx, vecs, w_0, w_1, wo_0
    )
    got = lax.ppermute(send, "pipe", swap)
    patches = tile_block(x_tile, q_tile, fresh, got, idx, vecs, w_final.T, wo_1)
    edge = patches
    if rows > 1:
        edge = jnp.where(first_core, patches[(rows - 1) * pitch : rows * pitch], patches[:pitch])
    got = lax.ppermute(edge, "pipe", swap)
    return decode(rows, cols, pitch, patches, got, idx, w_patch, b_in[None], b_up[None], w_up)


def solution(mesh):
    placed = (
        P(None, ("grp", "patch"), None),
        P("pipe", None, ("grp", "patch"), None),
        P("pipe", None, None),
        P("pipe", None, None),
        P("pipe", None, None),
        P(),
        P("grp"),
        P(),
        P(),
        P(),
        P(),
        P(),
    )
    return jax.shard_map(
        local,
        mesh=mesh,
        in_specs=placed,
        out_specs=P(("grp", "pipe"), "patch", None),
        check_vma=False,
    )
```

```python
import functools
import math

import jax
import jax.numpy as jnp
import numpy as np
from jax import lax
from jax.experimental import pallas as pl
from jax.experimental.pallas import tpu as pltpu
from jax.sharding import PartitionSpec as P

D = 1152
DH = 72
HEADS = 8
CH = 512
LATC = 4
TC = 256
DA = 576
DP = 640
SHIFT = 64
EPSILON = 1e-06
QUERY_SCALE = math.log2(math.e) / math.sqrt(DH)
BLOCK = 256
SMALL_BLOCK = 64
LANES = 128

F32 = jnp.float32
BF16 = jnp.bfloat16
VMEM = pl.BlockSpec(memory_space=pltpu.VMEM)
ANY = pl.BlockSpec(memory_space=pl.ANY)


def dot(a, b):
    return jnp.dot(a, b, preferred_element_type=F32)


def dot_t(a, b):
    return lax.dot_general(a, b, (((1,), (1,)), ((), ())), preferred_element_type=F32)


def normed(values, scale, shift):
    average = jnp.mean(values, axis=-1, keepdims=True)
    centred = values - average
    variance = jnp.mean(centred * centred, axis=-1, keepdims=True)
    return (centred * lax.rsqrt(variance + EPSILON) * scale + shift).astype(BF16)


def lane_window(start):
    return start // LANES * LANES, -(-(start + DH) // LANES) * LANES


def attend(query, kv_ref):
    count = query.shape[0]
    pieces = [None] * (DP // LANES)
    for head in range(HEADS):
        first, last = lane_window(head * DH)
        lane = lax.broadcasted_iota(jnp.int32, (count, last - first), 1) + first
        own = (lane >= head * DH) & (lane < (head + 1) * DH)
        q = jnp.where(own, query[:, first:last], jnp.zeros((), BF16))
        scores = dot_t(q, kv_ref[:, first:last])
        exponent = jnp.exp2(scores - jnp.max(scores, axis=1, keepdims=True))
        total = jnp.sum(exponent, axis=1, keepdims=True)
        start = DA + head * DH
        first, last = lane_window(start)
        numerator = dot(exponent.astype(BF16), kv_ref[:, first:last])
        lane = lax.broadcasted_iota(jnp.int32, (count, last - first), 1) + first
        own = (lane >= start) & (lane < start + DH)
        out = jnp.where(own, numerator * (1.0 / total), 0.0)
        for i in range((last - first) // LANES):
            at = (first - (DA - SHIFT)) // LANES + i
            part = out[:, i * LANES : (i + 1) * LANES]
            pieces[at] = part if pieces[at] is None else pieces[at] + part
    return jnp.concatenate(pieces, axis=1)


def each_block(count, body):
    if count <= BLOCK:
        body(0, count)
    else:

        @pl.loop(0, count // SMALL_BLOCK)
        def _(i):
            body(pl.multiple_of(i * SMALL_BLOCK, SMALL_BLOCK), SMALL_BLOCK)


def params(count):
    return pltpu.CompilerParams(vmem_limit_bytes=(24 if count <= BLOCK else 56) * 1024 * 1024)


def weights_kernel(own_ref, other_ref, wo_own, w0_ref, w1_ref, wo_ref, sems):
    first = lax.axis_index("pipe") == 0
    copies = [
        pltpu.make_async_copy(own_ref.at[0], w0_ref, sems.at[0]),
        pltpu.make_async_copy(own_ref.at[0], w1_ref, sems.at[1]),
        pltpu.make_async_copy(wo_own.at[0], wo_ref, sems.at[2]),
    ]
    copies[2].start()

    @pl.when(first)
    def _():
        copies[0].start()
        pltpu.make_async_copy(other_ref.at[0], w1_ref, sems.at[1]).start()

    @pl.when(jnp.logical_not(first))
    def _():
        copies[1].start()
        pltpu.make_async_copy(other_ref.at[0], w0_ref, sems.at[0]).start()

    for copy in copies:
        copy.wait()


def weights_in_vmem(w_own, w_other, wo_own):
    return pl.pallas_call(
        weights_kernel,
        out_shape=(jax.ShapeDtypeStruct((3 * DA, D), BF16),) * 2 + (jax.ShapeDtypeStruct((DA, D), BF16),),
        in_specs=[ANY] * 3,
        out_specs=(VMEM,) * 3,
        scratch_shapes=[pltpu.SemaphoreType.DMA((3,))],
        compiler_params=params(0),
        name="weights_by_block",
    )(in_hbm(w_own), w_other, in_hbm(wo_own))


def choose_out(block, own_ref, other_ref, wo_ref):
    mine = lax.axis_index("pipe") == block
    wo_ref[:SHIFT] = jnp.zeros((SHIFT, D), BF16)

    @pl.when(mine)
    def _():
        wo_ref[SHIFT:] = own_ref[...]

    @pl.when(jnp.logical_not(mine))
    def _():
        wo_ref[SHIFT:] = other_ref[0]


def query_of(modulated, w_ref):
    projected = dot_t(modulated, w_ref[:DP]) * QUERY_SCALE
    lane = lax.broadcasted_iota(jnp.int32, projected.shape, 1)
    return jnp.where(lane < DA, projected, 0.0).astype(BF16)


def join(refs, target):
    at = 0
    for ref in refs:
        rows = ref.shape[0]
        target[at : at + rows] = ref[...]
        at += rows


def project_kernel(x_ref, vec_ref, w_ref, q_ref, kv_ref):
    def body(start, size):
        rows = pl.ds(start, size)
        modulated = normed(x_ref[rows].astype(F32), vec_ref[1:2], vec_ref[0:1])
        kv_ref[rows] = dot_t(modulated, w_ref[DA:]).astype(BF16)
        q_ref[rows] = query_of(modulated, w_ref)

    each_block(x_ref.shape[0], body)


def project(x, vecs, weights):
    count = x.shape[0]
    return pl.pallas_call(
        project_kernel,
        out_shape=(
            jax.ShapeDtypeStruct((count, DP), BF16),
            jax.ShapeDtypeStruct((count, 2 * DA), BF16),
        ),
        in_specs=[VMEM] * 3,
        out_specs=(VMEM,) * 2,
        compiler_params=params(count),
        name="layer_norm_and_projections",
    )(x, vecs, weights)


def in_hbm(array):
    return pltpu.with_memory_space_constraint(array, pltpu.HBM)


def block_kernel(n_pieces, *refs):
    stale_refs = refs[:n_pieces]
    (
        got_ref, x_ref, q_ref, kv_ref, idx_ref, vec_ref, w0_ref, w1_ref, wo_own, wo_other,
        xt_ref, qt_ref, kv1_ref, all_ref, pick_ref, wo_ref,
    ) = refs[n_pieces:]
    count = x_ref.shape[0]
    first_core = lax.axis_index("pipe") == 0
    all_ref[:count] = kv_ref[...]
    choose_out(0, wo_own, wo_other, wo_ref)

    @pl.when(first_core)
    def _():
        join(stale_refs, all_ref.at[count:])

    @pl.when(jnp.logical_not(first_core))
    def _():
        def body(start, size):
            modulated = normed(got_ref[pl.ds(start, size)].astype(F32), vec_ref[1:2], vec_ref[0:1])
            all_ref[pl.ds(count + start, size)] = dot_t(modulated, w0_ref[DA:]).astype(BF16)

        each_block(count, body)

    pick_ref[...] = jnp.zeros_like(pick_ref)
    tile_rows = idx_ref.shape[0]

    def body(start, size):
        rows = pl.ds(start, size)
        attended = attend(q_ref[rows], all_ref).astype(BF16)
        branch = dot(attended, wo_ref[...])
        x1 = (x_ref[rows].astype(F32) + vec_ref[2:3] * branch).astype(BF16)
        modulated = normed(x1.astype(F32), vec_ref[4:5], vec_ref[3:4])
        fresh = dot_t(modulated, w1_ref[DA:]).astype(BF16)
        kv1_ref[rows] = fresh
        lane = lax.broadcasted_iota(jnp.int32, (tile_rows, size), 1) + start
        chosen = (lane == idx_ref[:, :1]).astype(F32).astype(BF16)
        pick_ref[0] += dot(chosen, x1)
        pick_ref[1] += dot(chosen, modulated)

    each_block(count, body)
    xt_ref[...] = pick_ref[0].astype(BF16)
    qt_ref[...] = query_of(pick_ref[1].astype(BF16), w1_ref)


def first_block(stale_pieces, got_x, x, q, kv, idx, vecs, w_block, w_next, wo_own, wo_other):
    count = x.shape[0]
    tile_rows = idx.shape[0]
    return pl.pallas_call(
        functools.partial(block_kernel, len(stale_pieces)),
        out_shape=(
            jax.ShapeDtypeStruct((tile_rows, D), BF16),
            jax.ShapeDtypeStruct((tile_rows, DP), BF16),
            jax.ShapeDtypeStruct((count, 2 * DA), BF16),
        ),
        in_specs=[VMEM] * (len(stale_pieces) + 10),
        out_specs=(VMEM,) * 3,
        scratch_shapes=[
            pltpu.VMEM((2 * count, 2 * DA), BF16),
            pltpu.VMEM((2, tile_rows, D), F32),
            pltpu.VMEM((DP, D), BF16),
        ],
        compiler_params=params(count),
        name="attention_and_next_keys",
    )(*stale_pieces, got_x, x, q, kv, idx, vecs, w_block, w_next, wo_own, wo_other)


def attend_at_once(query, kv_ref):
    count = query.shape[0]
    lane = lax.broadcasted_iota(jnp.int32, (count, DP), 1)
    masked = [
        jnp.where((lane >= h * DH) & (lane < (h + 1) * DH), query, jnp.zeros((), BF16)) for h in range(HEADS)
    ]
    scores = dot_t(jnp.concatenate(masked, axis=0), kv_ref[:, :DP])
    exponent = jnp.exp2(scores - jnp.max(scores, axis=1, keepdims=True))
    total = jnp.sum(exponent, axis=1, keepdims=True)
    numerator = dot(exponent.astype(BF16), kv_ref[:, DA - SHIFT :]) * (1.0 / total)
    out = None
    for h in range(HEADS):
        own = (lane >= SHIFT + h * DH) & (lane < SHIFT + (h + 1) * DH)
        part = jnp.where(own, numerator[h * count : (h + 1) * count], 0.0)
        out = part if out is None else out + part
    return out


def tile_kernel(
    x_ref, q_ref, kv_ref, got_ref, idx_ref, vec_ref, wf_ref, wo_own, wo_other, patch_ref, all_ref, wo_ref
):
    count = kv_ref.shape[0]
    all_ref[:count] = kv_ref[...]
    all_ref[count:] = got_ref[...]
    choose_out(1, wo_own, wo_other, wo_ref)
    attended = (attend_at_once if count <= BLOCK else attend)(q_ref[...], all_ref).astype(BF16)
    branch = dot(attended, wo_ref[...])
    x2 = (x_ref[...].astype(F32) + vec_ref[5:6] * branch).astype(BF16)
    final = normed(x2.astype(F32), vec_ref[7:8], vec_ref[6:7])
    patches = dot_t(final, wf_ref[...]).astype(BF16).astype(F32)
    patch_ref[...] = jnp.zeros_like(patch_ref)
    patch_ref[:, : 4 * LATC] = jnp.where(idx_ref[:, :1] >= 0, patches, 0.0)


def tile_block(x, q, kv, got, idx, vecs, w_final, wo_own, wo_other):
    count = kv.shape[0]
    return pl.pallas_call(
        tile_kernel,
        out_shape=jax.ShapeDtypeStruct((x.shape[0], LANES), F32),
        in_specs=[VMEM] * 9,
        out_specs=VMEM,
        scratch_shapes=[pltpu.VMEM((2 * count, 2 * DA), BF16), pltpu.VMEM((DP, D), BF16)],
        compiler_params=params(count),
        name="tile_attention_and_patches",
    )(x, q, kv, got, idx, vecs, w_final, wo_own, wo_other)


def decode_kernel(
    rows, cols, pitch, patch_ref, got_ref, idx_ref, wp_ref, bin_ref, bup_ref, w_ref, out_ref, u_ref, ub_ref
):
    first_core = lax.axis_index("pipe") == 0
    got = got_ref[:pitch]
    above = jnp.where(first_core, 0.0, got)
    below = jnp.where(first_core, got, 0.0)
    rim = [above] + [patch_ref[r * pitch : (r + 1) * pitch] for r in range(rows)] + [below]
    column_in = idx_ref[:pitch, :1] >= 0
    shifted = [[pltpu.roll(p, (-ds) % pitch, 0) if ds else p for ds in (-1, 0, 1)] for p in rim]
    for r in range(rows + 2):
        low, high = None, None
        for dr in (-1, 0, 1):
            if not 0 <= r + dr < rows + 2:
                continue
            for ds in range(3):
                tap = (dr + 1) * 3 + ds
                piece = shifted[r + dr][ds]
                if tap == 8:
                    high = piece
                else:
                    piece = pltpu.roll(piece, 4 * LATC * tap, 1) if tap else piece
                    low = piece if low is None else low + piece
        high = jnp.zeros_like(low) if high is None else high
        around = jnp.concatenate([low, high], axis=1).astype(BF16)
        for p in range(2):
            y = 2 * (r - 1) + p + 1
            if not 0 <= y < 2 * rows + 2:
                continue
            for q in range(2):
                at = (2 * p + q) * 2 * LANES
                act = dot(around, wp_ref[at : at + 2 * LANES]) + bin_ref[...]
                feature = act / (1.0 + jnp.exp(-act))
                keep = column_in
                if y == 0:
                    keep = keep & jnp.logical_not(first_core)
                if y == 2 * rows + 1:
                    keep = keep & first_core
                feature = jnp.where(keep, feature, 0.0)
                for c in range(CH // LANES):
                    part = feature[:, c * LANES : (c + 1) * LANES]
                    u_ref[y, c, pl.ds(2 * q, pitch, stride=4), :] = part
                    u_ref[y, c, pl.ds(2 * q + 1, pitch, stride=4), :] = part
    wide = 4 * cols
    for y in range(2 * rows + 2):
        for dx in range(3):
            for c in range(CH // LANES):
                ub_ref[dx, y * wide : (y + 1) * wide, c * LANES : (c + 1) * LANES] = u_ref[
                    y, c, 3 + dx : 3 + dx + wide, :
                ].astype(BF16)

    def tap_row(dy, y_first, y_count):
        total = None
        for dx in range(3):
            part = dot(ub_ref[dx, y_first * wide : (y_first + y_count) * wide], w_ref[3 * dy + dx])
            total = part if total is None else total + part
        return total

    def rows_of(total, y):
        return total[y * wide : (y + 1) * wide]

    middle = tap_row(1, 1, 2 * rows) + bup_ref[...]
    before = tap_row(0, 0, 2 * rows + 1)
    after = tap_row(2, 1, 2 * rows + 1)
    for y in range(2 * rows):
        own = rows_of(middle, y)
        out_ref[2 * y] = (own + rows_of(before, y) + rows_of(after, y)).astype(BF16)
        out_ref[2 * y + 1] = (own + rows_of(before, y + 1) + rows_of(after, y + 1)).astype(BF16)


def decode(rows, cols, pitch, patches, got, idx, w_patch, b_in, b_up, w_up):
    return pl.pallas_call(
        functools.partial(decode_kernel, rows, cols, pitch),
        out_shape=jax.ShapeDtypeStruct((4 * rows, 4 * cols, CH), BF16),
        in_specs=[VMEM] * 7,
        out_specs=VMEM,
        scratch_shapes=[
            pltpu.VMEM((2 * rows + 2, CH // LANES, 4 * pitch, LANES), F32),
            pltpu.VMEM((3, (2 * rows + 2) * 4 * cols, CH), BF16),
        ],
        compiler_params=params(0),
        name="decoder_convolutions",
    )(patches, got, idx, w_patch, b_in, b_up, w_up)


def patch_selector():
    sel = np.zeros((2, 2, 3, 3, 2, 2, LATC, 9 * LATC), np.float32)
    for p, q, dr, ds, pp, qq in np.ndindex(2, 2, 3, 3, 2, 2):
        dy = 2 * (dr - 1) + pp - p
        dx = 2 * (ds - 1) + qq - q
        if abs(dy) <= 1 and abs(dx) <= 1:
            tap = (dy + 1) * 3 + dx + 1
            for c in range(LATC):
                sel[p, q, dr, ds, pp, qq, c, tap * LATC + c] = 1.0
    sel = sel.reshape(4, 9 * 4 * LATC, 9 * LATC)
    return np.pad(sel, ((0, 0), (0, 2 * LANES - 9 * 4 * LATC), (0, 0))).reshape(-1, 9 * LATC)


def split_of(n):
    inner = 2 ** (int(math.log2(n)) // 2)
    return n // inner, inner


def shifted(block, k_outer, k_inner, cores=(0, 1)):
    n = lax.axis_size("patch")
    outer, inner = split_of(n)
    route = []
    for core in cores:
        for i in range(n):
            o, e = divmod(i, inner)
            source = (o + k_outer) % outer * inner + (e + k_inner) % inner
            route.append((core * n + source, core * n + i))
    return lax.ppermute(block, ("pipe", "patch"), route)


def local(
    tokens,
    stale_kv,
    w_qkv,
    w_out,
    block_table,
    time_table,
    t_index,
    w_final,
    w_in,
    b_in,
    w_up,
    b_up,
):
    section = lax.axis_index("pipe")
    tile = lax.axis_index("patch")
    n_tiles = lax.axis_size("patch")
    swap = [(0, 1), (1, 0)]
    first_core = section == 0
    own_count = tokens.shape[1]
    count = own_count * n_tiles
    rows = count // TC
    cols = TC // n_tiles
    pitch = -(-(cols + 3) // 8) * 8
    outer, inner = split_of(n_tiles)

    own_tokens = lax.dynamic_index_in_dim(tokens, section, 0, keepdims=False)
    w_qkv = jnp.swapaxes(w_qkv, 1, 2)
    w_qkv_other = lax.ppermute(w_qkv, "pipe", swap)
    tables = lax.all_gather(block_table[0], "pipe")
    w_out_other = lax.ppermute(w_out, "pipe", swap)
    x_others = jnp.concatenate([shifted(own_tokens, k, 0) for k in range(1, outer)], axis=0)
    x_own_inner = [shifted(own_tokens, 0, k) for k in range(1, inner)]

    time_row = lax.dynamic_index_in_dim(time_table, t_index[0], 0, keepdims=False)
    ones = jnp.asarray([[0.0], [1.0], [0.0]], F32)
    vecs = jnp.concatenate(
        [
            time_row[:3] + tables[0] + ones,
            time_row[:3] + tables[1] + ones,
            time_row[3:5] + ones[:2],
        ],
        axis=0,
    )

    padded_rows = -(-rows * pitch // 16) * 16
    place = jnp.arange(padded_rows)
    column = place % pitch - 1 + tile * cols
    inside = (place % pitch < cols + 2) & (place < rows * pitch) & (column >= 0) & (column < TC)
    token = place // pitch * TC + jnp.clip(column, 0, TC - 1)
    source = token // own_count
    k_outer = (source // inner - tile // inner) % outer
    k_inner = (source % inner - tile % inner) % inner
    spot = (k_inner * outer + k_outer) * own_count + token % own_count
    idx = jnp.broadcast_to(jnp.where(inside, spot, -1)[:, None], (padded_rows, LANES)).astype(jnp.int32)

    x_others, x_own_inner, w_qkv_other, w_out_other, vecs, idx, own_stale = lax.optimization_barrier(
        (x_others, x_own_inner, w_qkv_other, w_out_other, vecs, idx, stale_kv[0, 1])
    )
    x_late = [shifted(x_others, 0, k) for k in range(1, inner)]
    stale_column = [own_stale] + [shifted(own_stale, k, 0) for k in range(1, outer)]
    w_0, w_1, w_out_own = weights_in_vmem(w_qkv, w_qkv_other, w_out)
    x_late, stale_column, w_0 = lax.optimization_barrier((x_late, stale_column, w_0))
    stale_column = jnp.concatenate(stale_column, axis=0)
    x_pieces = [own_tokens, x_others]
    for k in range(1, inner):
        x_pieces += [x_own_inner[k - 1], x_late[k - 1]]
    x = jnp.concatenate(x_pieces, axis=0)
    x, stale_column = lax.optimization_barrier((x, stale_column))
    got_x = lax.ppermute(x, "pipe", [(0, 1)])
    stale_pieces = [stale_column] + [shifted(stale_column, 0, k, (0,)) for k in range(1, inner)]
    query, fresh = project(x, vecs, w_0)
    fresh, own_column = lax.optimization_barrier((fresh, stale_column))
    next_pieces = [own_column] + [shifted(own_column, 0, k, (1,)) for k in range(1, inner)]
    x_tile, q_tile, fresh = first_block(
        stale_pieces, got_x, x, query, fresh, idx, vecs, w_0, w_1, w_out_own, w_out_other
    )
    send = jnp.where(first_core, fresh, jnp.concatenate(next_pieces, axis=0))
    send, w_in = lax.optimization_barrier((send, w_in))
    got = lax.ppermute(send, "pipe", swap)
    w_patch = dot(jnp.asarray(patch_selector(), BF16), w_in).astype(BF16)
    got, w_patch = lax.optimization_barrier((got, w_patch))
    patches = tile_block(x_tile, q_tile, fresh, got, idx, vecs, w_final.T, w_out_own, w_out_other)
    edge = patches
    if rows > 1:
        edge = jnp.where(first_core, patches[(rows - 1) * pitch : rows * pitch], patches[:pitch])
    got = lax.ppermute(edge, "pipe", swap)
    return decode(rows, cols, pitch, patches, got, idx, w_patch, b_in[None], b_up[None], w_up)


def solution(mesh):
    placed = (
        P(None, ("grp", "patch"), None),
        P("pipe", None, ("grp", "patch"), None),
        P("pipe", None, None),
        P("pipe", None, None),
        P("pipe", None, None),
        P(),
        P("grp"),
        P(),
        P(),
        P(),
        P(),
        P(),
    )
    return jax.shard_map(
        local,
        mesh=mesh,
        in_specs=placed,
        out_specs=P(("grp", "pipe"), "patch", None),
        check_vma=False,
    )
```

```python
import functools
import math

import jax
import jax.numpy as jnp
import numpy as np
from jax import lax
from jax.experimental import pallas as pl
from jax.experimental.pallas import tpu as pltpu
from jax.sharding import PartitionSpec as P

D = 1152
DH = 72
HEADS = 8
CH = 512
LATC = 4
TC = 256
DA = 576
DP = 640
SHIFT = 64
EPSILON = 1e-06
QUERY_SCALE = math.log2(math.e) / math.sqrt(DH)
BLOCK = 256
SMALL_BLOCK = 64
LANES = 128

F32 = jnp.float32
BF16 = jnp.bfloat16
VMEM = pl.BlockSpec(memory_space=pltpu.VMEM)
ANY = pl.BlockSpec(memory_space=pl.ANY)


def dot(a, b):
    return jnp.dot(a, b, preferred_element_type=F32)


def dot_t(a, b):
    return lax.dot_general(a, b, (((1,), (1,)), ((), ())), preferred_element_type=F32)


def normed(values, scale, shift):
    average = jnp.mean(values, axis=-1, keepdims=True)
    centred = values - average
    variance = jnp.mean(centred * centred, axis=-1, keepdims=True)
    return (centred * lax.rsqrt(variance + EPSILON) * scale + shift).astype(BF16)


def lane_window(start):
    return start // LANES * LANES, -(-(start + DH) // LANES) * LANES


def attend(query, kv_ref):
    count = query.shape[0]
    pieces = [None] * (DP // LANES)
    for head in range(HEADS):
        first, last = lane_window(head * DH)
        lane = lax.broadcasted_iota(jnp.int32, (count, last - first), 1) + first
        own = (lane >= head * DH) & (lane < (head + 1) * DH)
        q = jnp.where(own, query[:, first:last], jnp.zeros((), BF16))
        scores = dot_t(q, kv_ref[:, first:last])
        exponent = jnp.exp2(scores - jnp.max(scores, axis=1, keepdims=True))
        total = jnp.sum(exponent, axis=1, keepdims=True)
        start = DA + head * DH
        first, last = lane_window(start)
        numerator = dot(exponent.astype(BF16), kv_ref[:, first:last])
        lane = lax.broadcasted_iota(jnp.int32, (count, last - first), 1) + first
        own = (lane >= start) & (lane < start + DH)
        out = jnp.where(own, numerator * (1.0 / total), 0.0)
        for i in range((last - first) // LANES):
            at = (first - (DA - SHIFT)) // LANES + i
            part = out[:, i * LANES : (i + 1) * LANES]
            pieces[at] = part if pieces[at] is None else pieces[at] + part
    return jnp.concatenate(pieces, axis=1)


def each_block(count, body):
    if count <= BLOCK:
        body(0, count)
    else:

        @pl.loop(0, count // SMALL_BLOCK)
        def _(i):
            body(pl.multiple_of(i * SMALL_BLOCK, SMALL_BLOCK), SMALL_BLOCK)


def params(count):
    return pltpu.CompilerParams(vmem_limit_bytes=(24 if count <= BLOCK else 56) * 1024 * 1024)


def weights_kernel(own_ref, other_ref, wo_own, wo_other, w0_ref, w1_ref, wo0_ref, wo1_ref, sems):
    first = lax.axis_index("pipe") == 0
    pad = jnp.zeros((SHIFT, D), BF16)
    wo0_ref[:SHIFT] = pad
    wo1_ref[:SHIFT] = pad
    outs = (wo0_ref.at[SHIFT:], wo1_ref.at[SHIFT:])
    copies = []
    for i, (in_place, arrived, targets) in enumerate(
        ((own_ref.at[0], other_ref.at[0], (w0_ref, w1_ref)), (wo_own.at[0], wo_other.at[0], outs))
    ):
        for block in range(2):
            own = (first if block == 0 else jnp.logical_not(first))
            sem = sems.at[2 * i + block]
            copies.append(pltpu.make_async_copy(in_place, targets[block], sem))

            @pl.when(own)
            def _():
                pltpu.make_async_copy(in_place, targets[block], sem).start()

            @pl.when(jnp.logical_not(own))
            def _():
                pltpu.make_async_copy(arrived, targets[block], sem).start()

    for copy in copies:
        copy.wait()


def weights_in_vmem(w_own, w_other, wo_own, wo_other):
    return pl.pallas_call(
        weights_kernel,
        out_shape=(jax.ShapeDtypeStruct((3 * DA, D), BF16),) * 2 + (jax.ShapeDtypeStruct((DP, D), BF16),) * 2,
        in_specs=[ANY] * 4,
        out_specs=(VMEM,) * 4,
        scratch_shapes=[pltpu.SemaphoreType.DMA((4,))],
        compiler_params=params(0),
        name="weights_by_block",
    )(in_hbm(w_own), w_other, in_hbm(wo_own), wo_other)


def query_of(modulated, w_ref):
    projected = dot_t(modulated, w_ref[:DP]) * QUERY_SCALE
    lane = lax.broadcasted_iota(jnp.int32, projected.shape, 1)
    return jnp.where(lane < DA, projected, 0.0).astype(BF16)


def join(refs, target):
    at = 0
    for ref in refs:
        rows = ref.shape[0]
        target[at : at + rows] = ref[...]
        at += rows


def project_kernel(n_pieces, *refs):
    piece_refs = refs[:n_pieces]
    vec_ref, w_ref, x_ref, q_ref, kv_ref = refs[n_pieces:]
    join(piece_refs, x_ref)

    def body(start, size):
        rows = pl.ds(start, size)
        modulated = normed(x_ref[rows].astype(F32), vec_ref[1:2], vec_ref[0:1])
        kv_ref[rows] = dot_t(modulated, w_ref[DA:]).astype(BF16)
        q_ref[rows] = query_of(modulated, w_ref)

    each_block(x_ref.shape[0], body)


def project(pieces, vecs, weights):
    count = sum(piece.shape[0] for piece in pieces)
    return pl.pallas_call(
        functools.partial(project_kernel, len(pieces)),
        out_shape=(
            jax.ShapeDtypeStruct((count, D), BF16),
            jax.ShapeDtypeStruct((count, DP), BF16),
            jax.ShapeDtypeStruct((count, 2 * DA), BF16),
        ),
        in_specs=[VMEM] * (len(pieces) + 2),
        out_specs=(VMEM,) * 3,
        compiler_params=params(count),
        name="layer_norm_and_projections",
    )(*pieces, vecs, weights)


def in_hbm(array):
    return pltpu.with_memory_space_constraint(array, pltpu.HBM)


def gather_keys(all_ref, kv_ref, stale_refs, got_ref):
    count = kv_ref.shape[0]
    first_core = lax.axis_index("pipe") == 0
    all_ref[:count] = kv_ref[...]

    @pl.when(first_core)
    def _():
        join(stale_refs, all_ref.at[count:])

    @pl.when(jnp.logical_not(first_core))
    def _():
        all_ref[count:] = got_ref[...]


def block_kernel(n_pieces, *refs):
    stale_refs = refs[:n_pieces]
    (
        got_ref, x_ref, q_ref, kv_ref, idx_ref, vec_ref, w1_ref, wo_ref,
        xt_ref, qt_ref, kv1_ref, all_ref, pick_ref,
    ) = refs[n_pieces:]
    count = x_ref.shape[0]
    gather_keys(all_ref, kv_ref, stale_refs, got_ref)
    pick_ref[...] = jnp.zeros_like(pick_ref)
    tile_rows = idx_ref.shape[0]

    def body(start, size):
        rows = pl.ds(start, size)
        attended = attend(q_ref[rows], all_ref).astype(BF16)
        branch = dot(attended, wo_ref[...])
        x1 = (x_ref[rows].astype(F32) + vec_ref[2:3] * branch).astype(BF16)
        modulated = normed(x1.astype(F32), vec_ref[4:5], vec_ref[3:4])
        fresh = dot_t(modulated, w1_ref[DA:]).astype(BF16)
        kv1_ref[rows] = fresh
        lane = lax.broadcasted_iota(jnp.int32, (tile_rows, size), 1) + start
        chosen = (lane == idx_ref[:, :1]).astype(F32).astype(BF16)
        pick_ref[0] += dot(chosen, x1)
        pick_ref[1] += dot(chosen, modulated)

    each_block(count, body)
    xt_ref[...] = pick_ref[0].astype(BF16)
    qt_ref[...] = query_of(pick_ref[1].astype(BF16), w1_ref)


def first_block(stale_pieces, got, x, q, kv, idx, vecs, w_next, wo_block):
    count = x.shape[0]
    tile_rows = idx.shape[0]
    return pl.pallas_call(
        functools.partial(block_kernel, len(stale_pieces)),
        out_shape=(
            jax.ShapeDtypeStruct((tile_rows, D), BF16),
            jax.ShapeDtypeStruct((tile_rows, DP), BF16),
            jax.ShapeDtypeStruct((count, 2 * DA), BF16),
        ),
        in_specs=[VMEM] * (len(stale_pieces) + 8),
        out_specs=(VMEM,) * 3,
        scratch_shapes=[
            pltpu.VMEM((2 * count, 2 * DA), BF16),
            pltpu.VMEM((2, tile_rows, D), F32),
        ],
        compiler_params=params(count),
        name="attention_and_next_keys",
    )(*stale_pieces, got, x, q, kv, idx, vecs, w_next, wo_block)


def tile_kernel(n_pieces, *refs):
    stale_refs = refs[:n_pieces]
    x_ref, q_ref, kv_ref, got_ref, idx_ref, vec_ref, wf_ref, wo_ref, patch_ref, all_ref = refs[n_pieces:]
    gather_keys(all_ref, kv_ref, stale_refs, got_ref)
    attended = attend(q_ref[...], all_ref).astype(BF16)
    branch = dot(attended, wo_ref[...])
    x2 = (x_ref[...].astype(F32) + vec_ref[5:6] * branch).astype(BF16)
    final = normed(x2.astype(F32), vec_ref[7:8], vec_ref[6:7])
    patches = dot_t(final, wf_ref[...]).astype(BF16).astype(F32)
    patch_ref[...] = jnp.zeros_like(patch_ref)
    patch_ref[:, : 4 * LATC] = jnp.where(idx_ref[:, :1] >= 0, patches, 0.0)


def tile_block(stale_pieces, x, q, kv, got, idx, vecs, w_final, wo_block):
    count = kv.shape[0]
    return pl.pallas_call(
        functools.partial(tile_kernel, len(stale_pieces)),
        out_shape=jax.ShapeDtypeStruct((x.shape[0], LANES), F32),
        in_specs=[VMEM] * (len(stale_pieces) + 8),
        out_specs=VMEM,
        scratch_shapes=[pltpu.VMEM((2 * count, 2 * DA), BF16)],
        compiler_params=params(count),
        name="tile_attention_and_patches",
    )(*stale_pieces, x, q, kv, got, idx, vecs, w_final, wo_block)


def decode_kernel(
    rows, cols, pitch, patch_ref, got_ref, idx_ref, wp_ref, bin_ref, bup_ref, w_ref, out_ref, u_ref, ub_ref
):
    first_core = lax.axis_index("pipe") == 0
    got = got_ref[:pitch]
    above = jnp.where(first_core, 0.0, got)
    below = jnp.where(first_core, got, 0.0)
    rim = [above] + [patch_ref[r * pitch : (r + 1) * pitch] for r in range(rows)] + [below]
    column_in = idx_ref[:pitch, :1] >= 0
    shifted = [[pltpu.roll(p, (-ds) % pitch, 0) if ds else p for ds in (-1, 0, 1)] for p in rim]
    for r in range(rows + 2):
        low, high = None, None
        for dr in (-1, 0, 1):
            if not 0 <= r + dr < rows + 2:
                continue
            for ds in range(3):
                tap = (dr + 1) * 3 + ds
                piece = shifted[r + dr][ds]
                if tap == 8:
                    high = piece
                else:
                    piece = pltpu.roll(piece, 4 * LATC * tap, 1) if tap else piece
                    low = piece if low is None else low + piece
        high = jnp.zeros_like(low) if high is None else high
        around = jnp.concatenate([low, high], axis=1).astype(BF16)
        for p in range(2):
            y = 2 * (r - 1) + p + 1
            if not 0 <= y < 2 * rows + 2:
                continue
            for q in range(2):
                at = (2 * p + q) * 2 * LANES
                act = dot(around, wp_ref[at : at + 2 * LANES]) + bin_ref[...]
                feature = act / (1.0 + jnp.exp(-act))
                keep = column_in
                if y == 0:
                    keep = keep & jnp.logical_not(first_core)
                if y == 2 * rows + 1:
                    keep = keep & first_core
                feature = jnp.where(keep, feature, 0.0)
                for c in range(CH // LANES):
                    part = feature[:, c * LANES : (c + 1) * LANES]
                    u_ref[y, c, pl.ds(2 * q, pitch, stride=4), :] = part
                    u_ref[y, c, pl.ds(2 * q + 1, pitch, stride=4), :] = part
    wide = 4 * cols
    for y in range(2 * rows + 2):
        for dx in range(3):
            for c in range(CH // LANES):
                ub_ref[dx, y * wide : (y + 1) * wide, c * LANES : (c + 1) * LANES] = u_ref[
                    y, c, 3 + dx : 3 + dx + wide, :
                ].astype(BF16)

    def tap_row(dy, y_first, y_count):
        total = None
        for dx in range(3):
            part = dot(ub_ref[dx, y_first * wide : (y_first + y_count) * wide], w_ref[3 * dy + dx])
            total = part if total is None else total + part
        return total

    def rows_of(total, y):
        return total[y * wide : (y + 1) * wide]

    middle = tap_row(1, 1, 2 * rows) + bup_ref[...]
    before = tap_row(0, 0, 2 * rows + 1)
    after = tap_row(2, 1, 2 * rows + 1)
    for y in range(2 * rows):
        own = rows_of(middle, y)
        out_ref[2 * y] = (own + rows_of(before, y) + rows_of(after, y)).astype(BF16)
        out_ref[2 * y + 1] = (own + rows_of(before, y + 1) + rows_of(after, y + 1)).astype(BF16)


def decode(rows, cols, pitch, patches, got, idx, w_patch, b_in, b_up, w_up):
    return pl.pallas_call(
        functools.partial(decode_kernel, rows, cols, pitch),
        out_shape=jax.ShapeDtypeStruct((4 * rows, 4 * cols, CH), BF16),
        in_specs=[VMEM] * 7,
        out_specs=VMEM,
        scratch_shapes=[
            pltpu.VMEM((2 * rows + 2, CH // LANES, 4 * pitch, LANES), F32),
            pltpu.VMEM((3, (2 * rows + 2) * 4 * cols, CH), BF16),
        ],
        compiler_params=params(0),
        name="decoder_convolutions",
    )(patches, got, idx, w_patch, b_in, b_up, w_up)


def patch_selector():
    sel = np.zeros((2, 2, 3, 3, 2, 2, LATC, 9 * LATC), np.float32)
    for p, q, dr, ds, pp, qq in np.ndindex(2, 2, 3, 3, 2, 2):
        dy = 2 * (dr - 1) + pp - p
        dx = 2 * (ds - 1) + qq - q
        if abs(dy) <= 1 and abs(dx) <= 1:
            tap = (dy + 1) * 3 + dx + 1
            for c in range(LATC):
                sel[p, q, dr, ds, pp, qq, c, tap * LATC + c] = 1.0
    sel = sel.reshape(4, 9 * 4 * LATC, 9 * LATC)
    return np.pad(sel, ((0, 0), (0, 2 * LANES - 9 * 4 * LATC), (0, 0))).reshape(-1, 9 * LATC)


def split_of(n):
    inner = 2 ** (int(math.log2(n)) // 2)
    return n // inner, inner


def shifted(block, k_outer, k_inner, cores=(0, 1)):
    n = lax.axis_size("patch")
    outer, inner = split_of(n)
    route = []
    for core in cores:
        for i in range(n):
            o, e = divmod(i, inner)
            source = (o + k_outer) % outer * inner + (e + k_inner) % inner
            route.append((core * n + source, core * n + i))
    return lax.ppermute(block, ("pipe", "patch"), route)


def local(
    tokens,
    stale_kv,
    w_qkv,
    w_out,
    block_table,
    time_table,
    t_index,
    w_final,
    w_in,
    b_in,
    w_up,
    b_up,
):
    section = lax.axis_index("pipe")
    tile = lax.axis_index("patch")
    n_tiles = lax.axis_size("patch")
    swap = [(0, 1), (1, 0)]
    first_core = section == 0
    own_count = tokens.shape[1]
    count = own_count * n_tiles
    rows = count // TC
    cols = TC // n_tiles
    pitch = -(-(cols + 3) // 8) * 8
    outer, inner = split_of(n_tiles)

    own_tokens = lax.dynamic_index_in_dim(tokens, section, 0, keepdims=False)
    w_qkv = jnp.swapaxes(w_qkv, 1, 2)
    w_qkv_other = lax.ppermute(w_qkv, "pipe", swap)
    tables = lax.all_gather(block_table[0], "pipe")
    x_column = [shifted(own_tokens, k, 0) for k in range(1, outer)]
    own_stale = stale_kv[0, 1]
    both_stale = jnp.concatenate([own_stale, lax.ppermute(own_stale, "pipe", [(1, 0)])], axis=0)
    lines = [both_stale] + [shifted(both_stale, 0, k, (0,)) for k in range(1, inner)]

    time_row = lax.dynamic_index_in_dim(time_table, t_index[0], 0, keepdims=False)
    ones = jnp.asarray([[0.0], [1.0], [0.0]], F32)
    vecs = jnp.concatenate(
        [
            time_row[:3] + tables[0] + ones,
            time_row[:3] + tables[1] + ones,
            time_row[3:5] + ones[:2],
        ],
        axis=0,
    )

    padded_rows = -(-rows * pitch // 16) * 16
    place = jnp.arange(padded_rows)
    column = place % pitch - 1 + tile * cols
    inside = (place % pitch < cols + 2) & (place < rows * pitch) & (column >= 0) & (column < TC)
    token = place // pitch * TC + jnp.clip(column, 0, TC - 1)
    source = token // own_count
    k_outer = (source // inner - tile // inner) % outer
    k_inner = (source % inner - tile % inner) % inner
    spot = (k_inner * outer + k_outer) * own_count + token % own_count
    idx = jnp.broadcast_to(jnp.where(inside, spot, -1)[:, None], (padded_rows, LANES)).astype(jnp.int32)

    x_column, lines, w_qkv_other, vecs, idx, w_out = lax.optimization_barrier(
        (x_column, lines, w_qkv_other, vecs, idx, w_out)
    )
    x_column = jnp.concatenate([own_tokens] + x_column, axis=0)
    stale_line = jnp.concatenate([line[:own_count] for line in lines], axis=0)
    next_line = jnp.concatenate([line[own_count:] for line in lines], axis=0)
    x_column, stale_line, next_line, w_out = lax.optimization_barrier((x_column, stale_line, next_line, w_out))
    x_pieces = [x_column] + [shifted(x_column, 0, k) for k in range(1, inner)]
    stale_pieces = [stale_line] + [shifted(stale_line, k, 0, (0,)) for k in range(1, outer)]
    w_out_other = lax.ppermute(w_out, "pipe", swap)
    w_0, w_1, wo_0, wo_1 = weights_in_vmem(w_qkv, w_qkv_other, w_out, w_out_other)
    x_pieces, stale_pieces, w_0 = lax.optimization_barrier((x_pieces, stale_pieces, w_0))
    x, query, fresh = project(x_pieces, vecs, w_0)
    got = lax.ppermute(fresh, "pipe", [(0, 1)])
    fresh, next_line = lax.optimization_barrier((fresh, next_line))
    next_pieces = [next_line] + [shifted(next_line, k, 0, (0,)) for k in range(1, outer)]
    x_tile, q_tile, fresh = first_block(stale_pieces, got, x, query, fresh, idx, vecs, w_1, wo_0)
    fresh, next_pieces, w_in = lax.optimization_barrier((fresh, next_pieces, w_in))
    got = lax.ppermute(fresh, "pipe", [(0, 1)])
    w_patch = dot(jnp.asarray(patch_selector(), BF16), w_in).astype(BF16)
    got, w_patch = lax.optimization_barrier((got, w_patch))
    patches = tile_block(next_pieces, x_tile, q_tile, fresh, got, idx, vecs, w_final.T, wo_1)
    edge = patches
    if rows > 1:
        edge = jnp.where(first_core, patches[(rows - 1) * pitch : rows * pitch], patches[:pitch])
    got = lax.ppermute(edge, "pipe", swap)
    return decode(rows, cols, pitch, patches, got, idx, w_patch, b_in[None], b_up[None], w_up)


def solution(mesh):
    placed = (
        P(None, ("grp", "patch"), None),
        P("pipe", None, ("grp", "patch"), None),
        P("pipe", None, None),
        P("pipe", None, None),
        P("pipe", None, None),
        P(),
        P("grp"),
        P(),
        P(),
        P(),
        P(),
        P(),
    )
    return jax.shard_map(
        local,
        mesh=mesh,
        in_specs=placed,
        out_specs=P(("grp", "pipe"), "patch", None),
        check_vma=False,
    )
```

```python
import functools
import math

import jax
import jax.numpy as jnp
import numpy as np
from jax import lax
from jax.experimental import pallas as pl
from jax.experimental.pallas import tpu as pltpu
from jax.sharding import PartitionSpec as P

D = 1152
DH = 72
HEADS = 8
CH = 512
LATC = 4
TC = 256
DA = 576
DP = 640
SHIFT = 64
EPSILON = 1e-06
QUERY_SCALE = math.log2(math.e) / math.sqrt(DH)
BLOCK = 256
SMALL_BLOCK = 64
LANES = 128

F32 = jnp.float32
BF16 = jnp.bfloat16
VMEM = pl.BlockSpec(memory_space=pltpu.VMEM)
ANY = pl.BlockSpec(memory_space=pl.ANY)


def dot(a, b):
    return jnp.dot(a, b, preferred_element_type=F32)


def dot_t(a, b):
    return lax.dot_general(a, b, (((1,), (1,)), ((), ())), preferred_element_type=F32)


def normed(values, scale, shift):
    average = jnp.mean(values, axis=-1, keepdims=True)
    centred = values - average
    variance = jnp.mean(centred * centred, axis=-1, keepdims=True)
    return (centred * lax.rsqrt(variance + EPSILON) * scale + shift).astype(BF16)


def lane_window(start):
    return start // LANES * LANES, -(-(start + DH) // LANES) * LANES


def attend(query, kv_ref):
    count = query.shape[0]
    pieces = [None] * (DP // LANES)
    for head in range(HEADS):
        first, last = lane_window(head * DH)
        lane = lax.broadcasted_iota(jnp.int32, (count, last - first), 1) + first
        own = (lane >= head * DH) & (lane < (head + 1) * DH)
        q = jnp.where(own, query[:, first:last], jnp.zeros((), BF16))
        scores = dot_t(q, kv_ref[:, first:last])
        exponent = jnp.exp2(scores - jnp.max(scores, axis=1, keepdims=True))
        total = jnp.sum(exponent, axis=1, keepdims=True)
        start = DA + head * DH
        first, last = lane_window(start)
        numerator = dot(exponent.astype(BF16), kv_ref[:, first:last])
        lane = lax.broadcasted_iota(jnp.int32, (count, last - first), 1) + first
        own = (lane >= start) & (lane < start + DH)
        out = jnp.where(own, numerator * (1.0 / total), 0.0)
        for i in range((last - first) // LANES):
            at = (first - (DA - SHIFT)) // LANES + i
            part = out[:, i * LANES : (i + 1) * LANES]
            pieces[at] = part if pieces[at] is None else pieces[at] + part
    return jnp.concatenate(pieces, axis=1)


def each_block(count, body):
    if count <= BLOCK:
        body(0, count)
    else:

        @pl.loop(0, count // SMALL_BLOCK)
        def _(i):
            body(pl.multiple_of(i * SMALL_BLOCK, SMALL_BLOCK), SMALL_BLOCK)


def params(count):
    return pltpu.CompilerParams(vmem_limit_bytes=(24 if count <= BLOCK else 56) * 1024 * 1024)


def weights_kernel(own_ref, other_ref, wo_own, wo_other, w0_ref, w1_ref, wo0_ref, wo1_ref, sems):
    first = lax.axis_index("pipe") == 0
    pad = jnp.zeros((SHIFT, D), BF16)
    wo0_ref[:SHIFT] = pad
    wo1_ref[:SHIFT] = pad
    outs = (wo0_ref.at[SHIFT:], wo1_ref.at[SHIFT:])
    copies = []
    for i, (in_place, arrived, targets) in enumerate(
        ((own_ref.at[0], other_ref.at[0], (w0_ref, w1_ref)), (wo_own.at[0], wo_other.at[0], outs))
    ):
        for block in range(2):
            own = (first if block == 0 else jnp.logical_not(first))
            sem = sems.at[2 * i + block]
            copies.append(pltpu.make_async_copy(in_place, targets[block], sem))

            @pl.when(own)
            def _():
                pltpu.make_async_copy(in_place, targets[block], sem).start()

            @pl.when(jnp.logical_not(own))
            def _():
                pltpu.make_async_copy(arrived, targets[block], sem).start()

    for copy in copies:
        copy.wait()


def weights_in_vmem(w_own, w_other, wo_own, wo_other):
    return pl.pallas_call(
        weights_kernel,
        out_shape=(jax.ShapeDtypeStruct((3 * DA, D), BF16),) * 2 + (jax.ShapeDtypeStruct((DP, D), BF16),) * 2,
        in_specs=[ANY] * 4,
        out_specs=(VMEM,) * 4,
        scratch_shapes=[pltpu.SemaphoreType.DMA((4,))],
        compiler_params=params(0),
        name="weights_by_block",
    )(in_hbm(w_own), w_other, in_hbm(wo_own), wo_other)


def query_of(modulated, w_ref):
    projected = dot_t(modulated, w_ref[:DP]) * QUERY_SCALE
    lane = lax.broadcasted_iota(jnp.int32, projected.shape, 1)
    return jnp.where(lane < DA, projected, 0.0).astype(BF16)


def join(refs, target):
    at = 0
    for ref in refs:
        rows = ref.shape[0]
        target[at : at + rows] = ref[...]
        at += rows


def project_kernel(n_pieces, *refs):
    piece_refs = refs[:n_pieces]
    vec_ref, w_ref, x_ref, q_ref, kv_ref = refs[n_pieces : n_pieces + 5]
    part_refs = refs[n_pieces + 5 :]
    join(piece_refs, x_ref)

    def body(start, size):
        rows = pl.ds(start, size)
        modulated = normed(x_ref[rows].astype(F32), vec_ref[1:2], vec_ref[0:1])
        kv_ref[rows] = dot_t(modulated, w_ref[DA:]).astype(BF16)
        q_ref[rows] = query_of(modulated, w_ref)

    each_block(x_ref.shape[0], body)
    at = 0
    for ref in part_refs:
        rows = ref.shape[0]
        ref[...] = kv_ref[at : at + rows]
        at += rows


def project(pieces, vecs, weights):
    count = sum(piece.shape[0] for piece in pieces)
    step = 3 * count // 8
    parts = (step, step, count - 2 * step)
    return pl.pallas_call(
        functools.partial(project_kernel, len(pieces)),
        out_shape=(
            jax.ShapeDtypeStruct((count, D), BF16),
            jax.ShapeDtypeStruct((count, DP), BF16),
            jax.ShapeDtypeStruct((count, 2 * DA), BF16),
        )
        + tuple(jax.ShapeDtypeStruct((part, 2 * DA), BF16) for part in parts),
        in_specs=[VMEM] * (len(pieces) + 2),
        out_specs=(VMEM,) * 6,
        compiler_params=params(count),
        name="layer_norm_and_projections",
    )(*pieces, vecs, weights)


def in_hbm(array):
    return pltpu.with_memory_space_constraint(array, pltpu.HBM)


def gather_keys(all_ref, kv_ref, stale_refs, got_refs):
    count = kv_ref.shape[0]
    first_core = lax.axis_index("pipe") == 0
    all_ref[:count] = kv_ref[...]

    @pl.when(first_core)
    def _():
        join(stale_refs, all_ref.at[count:])

    @pl.when(jnp.logical_not(first_core))
    def _():
        join(got_refs, all_ref.at[count:])


def block_kernel(n_pieces, n_got, *refs):
    stale_refs = refs[:n_pieces]
    got_refs = refs[n_pieces : n_pieces + n_got]
    (
        x_ref, q_ref, kv_ref, idx_ref, vec_ref, w1_ref, wo_ref,
        xt_ref, qt_ref, kv1_ref, send_ref, all_ref, pick_ref,
    ) = refs[n_pieces + n_got :]
    count = x_ref.shape[0]
    first_core = lax.axis_index("pipe") == 0
    gather_keys(all_ref, kv_ref, stale_refs, got_refs)
    join(stale_refs, send_ref)
    pick_ref[...] = jnp.zeros_like(pick_ref)
    tile_rows = idx_ref.shape[0]

    def body(start, size):
        rows = pl.ds(start, size)
        attended = attend(q_ref[rows], all_ref).astype(BF16)
        branch = dot(attended, wo_ref[...])
        x1 = (x_ref[rows].astype(F32) + vec_ref[2:3] * branch).astype(BF16)
        modulated = normed(x1.astype(F32), vec_ref[4:5], vec_ref[3:4])
        fresh = dot_t(modulated, w1_ref[DA:]).astype(BF16)
        kv1_ref[rows] = fresh

        @pl.when(first_core)
        def _():
            send_ref[rows] = fresh

        lane = lax.broadcasted_iota(jnp.int32, (tile_rows, size), 1) + start
        chosen = (lane == idx_ref[:, :1]).astype(F32).astype(BF16)
        pick_ref[0] += dot(chosen, x1)
        pick_ref[1] += dot(chosen, modulated)

    each_block(count, body)
    xt_ref[...] = pick_ref[0].astype(BF16)
    qt_ref[...] = query_of(pick_ref[1].astype(BF16), w1_ref)


def first_block(stale_pieces, got_pieces, x, q, kv, idx, vecs, w_next, wo_block):
    count = x.shape[0]
    tile_rows = idx.shape[0]
    return pl.pallas_call(
        functools.partial(block_kernel, len(stale_pieces), len(got_pieces)),
        out_shape=(
            jax.ShapeDtypeStruct((tile_rows, D), BF16),
            jax.ShapeDtypeStruct((tile_rows, DP), BF16),
            jax.ShapeDtypeStruct((count, 2 * DA), BF16),
            jax.ShapeDtypeStruct((count, 2 * DA), BF16),
        ),
        in_specs=[VMEM] * (len(stale_pieces) + len(got_pieces) + 7),
        out_specs=(VMEM,) * 4,
        scratch_shapes=[
            pltpu.VMEM((2 * count, 2 * DA), BF16),
            pltpu.VMEM((2, tile_rows, D), F32),
        ],
        compiler_params=params(count),
        name="attention_and_next_keys",
    )(*stale_pieces, *got_pieces, x, q, kv, idx, vecs, w_next, wo_block)


def tile_kernel(x_ref, q_ref, kv_ref, got_ref, idx_ref, vec_ref, wf_ref, wo_ref, patch_ref, all_ref):
    count = kv_ref.shape[0]
    all_ref[:count] = kv_ref[...]
    all_ref[count:] = got_ref[...]
    attended = attend(q_ref[...], all_ref).astype(BF16)
    branch = dot(attended, wo_ref[...])
    x2 = (x_ref[...].astype(F32) + vec_ref[5:6] * branch).astype(BF16)
    final = normed(x2.astype(F32), vec_ref[7:8], vec_ref[6:7])
    patches = dot_t(final, wf_ref[...]).astype(BF16).astype(F32)
    patch_ref[...] = jnp.zeros_like(patch_ref)
    patch_ref[:, : 4 * LATC] = jnp.where(idx_ref[:, :1] >= 0, patches, 0.0)


def tile_block(x, q, kv, got, idx, vecs, w_final, wo_block):
    count = kv.shape[0]
    return pl.pallas_call(
        tile_kernel,
        out_shape=jax.ShapeDtypeStruct((x.shape[0], LANES), F32),
        in_specs=[VMEM] * 8,
        out_specs=VMEM,
        scratch_shapes=[pltpu.VMEM((2 * count, 2 * DA), BF16)],
        compiler_params=params(count),
        name="tile_attention_and_patches",
    )(x, q, kv, got, idx, vecs, w_final, wo_block)


def decode_kernel(
    rows, cols, pitch, patch_ref, got_ref, idx_ref, wp_ref, bin_ref, bup_ref, w_ref, out_ref, u_ref, ub_ref
):
    first_core = lax.axis_index("pipe") == 0
    got = got_ref[:pitch]
    above = jnp.where(first_core, 0.0, got)
    below = jnp.where(first_core, got, 0.0)
    rim = [above] + [patch_ref[r * pitch : (r + 1) * pitch] for r in range(rows)] + [below]
    column_in = idx_ref[:pitch, :1] >= 0
    shifted = [[pltpu.roll(p, (-ds) % pitch, 0) if ds else p for ds in (-1, 0, 1)] for p in rim]
    for r in range(rows + 2):
        low, high = None, None
        for dr in (-1, 0, 1):
            if not 0 <= r + dr < rows + 2:
                continue
            for ds in range(3):
                tap = (dr + 1) * 3 + ds
                piece = shifted[r + dr][ds]
                if tap == 8:
                    high = piece
                else:
                    piece = pltpu.roll(piece, 4 * LATC * tap, 1) if tap else piece
                    low = piece if low is None else low + piece
        high = jnp.zeros_like(low) if high is None else high
        around = jnp.concatenate([low, high], axis=1).astype(BF16)
        for p in range(2):
            y = 2 * (r - 1) + p + 1
            if not 0 <= y < 2 * rows + 2:
                continue
            for q in range(2):
                at = (2 * p + q) * 2 * LANES
                act = dot(around, wp_ref[at : at + 2 * LANES]) + bin_ref[...]
                feature = act / (1.0 + jnp.exp(-act))
                keep = column_in
                if y == 0:
                    keep = keep & jnp.logical_not(first_core)
                if y == 2 * rows + 1:
                    keep = keep & first_core
                feature = jnp.where(keep, feature, 0.0)
                for c in range(CH // LANES):
                    part = feature[:, c * LANES : (c + 1) * LANES]
                    u_ref[y, c, pl.ds(2 * q, pitch, stride=4), :] = part
                    u_ref[y, c, pl.ds(2 * q + 1, pitch, stride=4), :] = part
    wide = 4 * cols
    for y in range(2 * rows + 2):
        for dx in range(3):
            for c in range(CH // LANES):
                ub_ref[dx, y * wide : (y + 1) * wide, c * LANES : (c + 1) * LANES] = u_ref[
                    y, c, 3 + dx : 3 + dx + wide, :
                ].astype(BF16)

    def tap_row(dy, y_first, y_count):
        total = None
        for dx in range(3):
            part = dot(ub_ref[dx, y_first * wide : (y_first + y_count) * wide], w_ref[3 * dy + dx])
            total = part if total is None else total + part
        return total

    def rows_of(total, y):
        return total[y * wide : (y + 1) * wide]

    middle = tap_row(1, 1, 2 * rows) + bup_ref[...]
    before = tap_row(0, 0, 2 * rows + 1)
    after = tap_row(2, 1, 2 * rows + 1)
    for y in range(2 * rows):
        own = rows_of(middle, y)
        out_ref[2 * y] = (own + rows_of(before, y) + rows_of(after, y)).astype(BF16)
        out_ref[2 * y + 1] = (own + rows_of(before, y + 1) + rows_of(after, y + 1)).astype(BF16)


def decode(rows, cols, pitch, patches, got, idx, w_patch, b_in, b_up, w_up):
    return pl.pallas_call(
        functools.partial(decode_kernel, rows, cols, pitch),
        out_shape=jax.ShapeDtypeStruct((4 * rows, 4 * cols, CH), BF16),
        in_specs=[VMEM] * 7,
        out_specs=VMEM,
        scratch_shapes=[
            pltpu.VMEM((2 * rows + 2, CH // LANES, 4 * pitch, LANES), F32),
            pltpu.VMEM((3, (2 * rows + 2) * 4 * cols, CH), BF16),
        ],
        compiler_params=params(0),
        name="decoder_convolutions",
    )(patches, got, idx, w_patch, b_in, b_up, w_up)


def patch_selector():
    sel = np.zeros((2, 2, 3, 3, 2, 2, LATC, 9 * LATC), np.float32)
    for p, q, dr, ds, pp, qq in np.ndindex(2, 2, 3, 3, 2, 2):
        dy = 2 * (dr - 1) + pp - p
        dx = 2 * (ds - 1) + qq - q
        if abs(dy) <= 1 and abs(dx) <= 1:
            tap = (dy + 1) * 3 + dx + 1
            for c in range(LATC):
                sel[p, q, dr, ds, pp, qq, c, tap * LATC + c] = 1.0
    sel = sel.reshape(4, 9 * 4 * LATC, 9 * LATC)
    return np.pad(sel, ((0, 0), (0, 2 * LANES - 9 * 4 * LATC), (0, 0))).reshape(-1, 9 * LATC)


def split_of(n):
    inner = 2 ** (int(math.log2(n)) // 2)
    return n // inner, inner


def shifted(block, k_outer, k_inner, cores=(0, 1)):
    n = lax.axis_size("patch")
    outer, inner = split_of(n)
    route = []
    for core in cores:
        for i in range(n):
            o, e = divmod(i, inner)
            source = (o + k_outer) % outer * inner + (e + k_inner) % inner
            route.append((core * n + source, core * n + i))
    return lax.ppermute(block, ("pipe", "patch"), route)


def local(
    tokens,
    stale_kv,
    w_qkv,
    w_out,
    block_table,
    time_table,
    t_index,
    w_final,
    w_in,
    b_in,
    w_up,
    b_up,
):
    section = lax.axis_index("pipe")
    tile = lax.axis_index("patch")
    n_tiles = lax.axis_size("patch")
    swap = [(0, 1), (1, 0)]
    first_core = section == 0
    own_count = tokens.shape[1]
    count = own_count * n_tiles
    rows = count // TC
    cols = TC // n_tiles
    pitch = -(-(cols + 3) // 8) * 8
    outer, inner = split_of(n_tiles)

    own_tokens = lax.dynamic_index_in_dim(tokens, section, 0, keepdims=False)
    w_qkv = jnp.swapaxes(w_qkv, 1, 2)
    w_qkv_other = lax.ppermute(w_qkv, "pipe", swap)
    tables = lax.all_gather(block_table[0], "pipe")
    x_column = [shifted(own_tokens, k, 0) for k in range(1, outer)]

    time_row = lax.dynamic_index_in_dim(time_table, t_index[0], 0, keepdims=False)
    ones = jnp.asarray([[0.0], [1.0], [0.0]], F32)
    vecs = jnp.concatenate(
        [
            time_row[:3] + tables[0] + ones,
            time_row[:3] + tables[1] + ones,
            time_row[3:5] + ones[:2],
        ],
        axis=0,
    )

    padded_rows = -(-rows * pitch // 16) * 16
    place = jnp.arange(padded_rows)
    column = place % pitch - 1 + tile * cols
    inside = (place % pitch < cols + 2) & (place < rows * pitch) & (column >= 0) & (column < TC)
    token = place // pitch * TC + jnp.clip(column, 0, TC - 1)
    source = token // own_count
    k_outer = (source // inner - tile // inner) % outer
    k_inner = (source % inner - tile % inner) % inner
    spot = (k_inner * outer + k_outer) * own_count + token % own_count
    idx = jnp.broadcast_to(jnp.where(inside, spot, -1)[:, None], (padded_rows, LANES)).astype(jnp.int32)

    x_column, w_qkv_other, vecs, idx, own_stale, w_out = lax.optimization_barrier(
        (x_column, w_qkv_other, vecs, idx, stale_kv[0, 1], w_out)
    )
    x_column = jnp.concatenate([own_tokens] + x_column, axis=0)
    x_column, own_stale, w_out = lax.optimization_barrier((x_column, own_stale, w_out))
    x_pieces = [x_column] + [shifted(x_column, 0, k) for k in range(1, inner)]
    stale_column = [own_stale] + [shifted(own_stale, k, 0) for k in range(1, outer)]
    w_out_other = lax.ppermute(w_out, "pipe", swap)
    w_0, w_1, wo_0, wo_1 = weights_in_vmem(w_qkv, w_qkv_other, w_out, w_out_other)
    x_pieces, stale_column, w_0 = lax.optimization_barrier((x_pieces, stale_column, w_0))
    stale_column = jnp.concatenate(stale_column, axis=0)
    x_pieces, stale_column = lax.optimization_barrier((x_pieces, stale_column))
    stale_pieces = [stale_column] + [shifted(stale_column, 0, k) for k in range(1, inner)]
    x, query, fresh, *parts = project(x_pieces, vecs, w_0)
    got_pieces = [lax.ppermute(part, "pipe", [(0, 1)]) for part in parts]
    x_tile, q_tile, fresh, send = first_block(
        stale_pieces, got_pieces, x, query, fresh, idx, vecs, w_1, wo_0
    )
    send, w_in = lax.optimization_barrier((send, w_in))
    got = lax.ppermute(send, "pipe", swap)
    w_patch = dot(jnp.asarray(patch_selector(), BF16), w_in).astype(BF16)
    got, w_patch = lax.optimization_barrier((got, w_patch))
    patches = tile_block(x_tile, q_tile, fresh, got, idx, vecs, w_final.T, wo_1)
    edge = patches
    if rows > 1:
        edge = jnp.where(first_core, patches[(rows - 1) * pitch : rows * pitch], patches[:pitch])
    got = lax.ppermute(edge, "pipe", swap)
    return decode(rows, cols, pitch, patches, got, idx, w_patch, b_in[None], b_up[None], w_up)


def solution(mesh):
    placed = (
        P(None, ("grp", "patch"), None),
        P("pipe", None, ("grp", "patch"), None),
        P("pipe", None, None),
        P("pipe", None, None),
        P("pipe", None, None),
        P(),
        P("grp"),
        P(),
        P(),
        P(),
        P(),
        P(),
    )
    return jax.shard_map(
        local,
        mesh=mesh,
        in_specs=placed,
        out_specs=P(("grp", "pipe"), "patch", None),
        check_vma=False,
    )
```

```python
import functools
import math

import jax
import jax.numpy as jnp
import numpy as np
from jax import lax
from jax.experimental import pallas as pl
from jax.experimental.pallas import tpu as pltpu
from jax.sharding import PartitionSpec as P

D = 1152
DH = 72
HEADS = 8
CH = 512
LATC = 4
TC = 256
DA = 576
DP = 640
SHIFT = 64
EPSILON = 1e-06
QUERY_SCALE = math.log2(math.e) / math.sqrt(DH)
BLOCK = 256
SMALL_BLOCK = 64
LANES = 128

F32 = jnp.float32
BF16 = jnp.bfloat16
VMEM = pl.BlockSpec(memory_space=pltpu.VMEM)
ANY = pl.BlockSpec(memory_space=pl.ANY)


def dot(a, b):
    return jnp.dot(a, b, preferred_element_type=F32)


def dot_t(a, b):
    return lax.dot_general(a, b, (((1,), (1,)), ((), ())), preferred_element_type=F32)


def normed(values, scale, shift):
    average = jnp.mean(values, axis=-1, keepdims=True)
    centred = values - average
    variance = jnp.mean(centred * centred, axis=-1, keepdims=True)
    return (centred * lax.rsqrt(variance + EPSILON) * scale + shift).astype(BF16)


def lane_window(start):
    return start // LANES * LANES, -(-(start + DH) // LANES) * LANES


def attend(query, kv_ref):
    count = query.shape[0]
    pieces = [None] * (DP // LANES)
    for head in range(HEADS):
        first, last = lane_window(head * DH)
        lane = lax.broadcasted_iota(jnp.int32, (count, last - first), 1) + first
        own = (lane >= head * DH) & (lane < (head + 1) * DH)
        q = jnp.where(own, query[:, first:last], jnp.zeros((), BF16))
        scores = dot_t(q, kv_ref[:, first:last])
        exponent = jnp.exp2(scores - jnp.max(scores, axis=1, keepdims=True))
        total = jnp.sum(exponent, axis=1, keepdims=True)
        start = DA + head * DH
        first, last = lane_window(start)
        numerator = dot(exponent.astype(BF16), kv_ref[:, first:last])
        lane = lax.broadcasted_iota(jnp.int32, (count, last - first), 1) + first
        own = (lane >= start) & (lane < start + DH)
        out = jnp.where(own, numerator * (1.0 / total), 0.0)
        for i in range((last - first) // LANES):
            at = (first - (DA - SHIFT)) // LANES + i
            part = out[:, i * LANES : (i + 1) * LANES]
            pieces[at] = part if pieces[at] is None else pieces[at] + part
    return jnp.concatenate(pieces, axis=1)


def each_block(count, body):
    if count <= BLOCK:
        body(0, count)
    else:

        @pl.loop(0, count // SMALL_BLOCK)
        def _(i):
            body(pl.multiple_of(i * SMALL_BLOCK, SMALL_BLOCK), SMALL_BLOCK)


def params(count):
    return pltpu.CompilerParams(vmem_limit_bytes=(24 if count <= BLOCK else 56) * 1024 * 1024)


def weights_kernel(own_ref, other_ref, wo_own, wo_other, w0_ref, w1_ref, wo0_ref, wo1_ref, sems):
    first = lax.axis_index("pipe") == 0
    pad = jnp.zeros((SHIFT, D), BF16)
    wo0_ref[:SHIFT] = pad
    wo1_ref[:SHIFT] = pad
    outs = (wo0_ref.at[SHIFT:], wo1_ref.at[SHIFT:])
    copies = []
    for i, (in_place, arrived, targets) in enumerate(
        ((own_ref.at[0], other_ref.at[0], (w0_ref, w1_ref)), (wo_own.at[0], wo_other.at[0], outs))
    ):
        for block in range(2):
            own = (first if block == 0 else jnp.logical_not(first))
            sem = sems.at[2 * i + block]
            copies.append(pltpu.make_async_copy(in_place, targets[block], sem))

            @pl.when(own)
            def _():
                pltpu.make_async_copy(in_place, targets[block], sem).start()

            @pl.when(jnp.logical_not(own))
            def _():
                pltpu.make_async_copy(arrived, targets[block], sem).start()

    for copy in copies:
        copy.wait()


def weights_in_vmem(w_own, w_other, wo_own, wo_other):
    return pl.pallas_call(
        weights_kernel,
        out_shape=(jax.ShapeDtypeStruct((3 * DA, D), BF16),) * 2 + (jax.ShapeDtypeStruct((DP, D), BF16),) * 2,
        in_specs=[ANY] * 4,
        out_specs=(VMEM,) * 4,
        scratch_shapes=[pltpu.SemaphoreType.DMA((4,))],
        compiler_params=params(0),
        name="weights_by_block",
    )(in_hbm(w_own), w_other, in_hbm(wo_own), wo_other)


def query_of(modulated, w_ref):
    projected = dot_t(modulated, w_ref[:DP]) * QUERY_SCALE
    lane = lax.broadcasted_iota(jnp.int32, projected.shape, 1)
    return jnp.where(lane < DA, projected, 0.0).astype(BF16)


def join(refs, target):
    at = 0
    for ref in refs:
        rows = ref.shape[0]
        target[at : at + rows] = ref[...]
        at += rows


def project_kernel(n_pieces, *refs):
    piece_refs = refs[:n_pieces]
    vec_ref, w_ref, x_ref, q_ref, kv_ref = refs[n_pieces : n_pieces + 5]
    part_refs = refs[n_pieces + 5 :]
    join(piece_refs, x_ref)

    def body(start, size):
        rows = pl.ds(start, size)
        modulated = normed(x_ref[rows].astype(F32), vec_ref[1:2], vec_ref[0:1])
        kv_ref[rows] = dot_t(modulated, w_ref[DA:]).astype(BF16)
        q_ref[rows] = query_of(modulated, w_ref)

    each_block(x_ref.shape[0], body)
    at = 0
    for ref in part_refs:
        rows = ref.shape[0]
        ref[...] = kv_ref[at : at + rows]
        at += rows


def project(pieces, vecs, weights):
    count = sum(piece.shape[0] for piece in pieces)
    step = 3 * count // 8
    parts = (step, step, count - 2 * step)
    return pl.pallas_call(
        functools.partial(project_kernel, len(pieces)),
        out_shape=(
            jax.ShapeDtypeStruct((count, D), BF16),
            jax.ShapeDtypeStruct((count, DP), BF16),
            jax.ShapeDtypeStruct((count, 2 * DA), BF16),
        )
        + tuple(jax.ShapeDtypeStruct((part, 2 * DA), BF16) for part in parts),
        in_specs=[VMEM] * (len(pieces) + 2),
        out_specs=(VMEM,) * 6,
        compiler_params=params(count),
        name="layer_norm_and_projections",
    )(*pieces, vecs, weights)


def in_hbm(array):
    return pltpu.with_memory_space_constraint(array, pltpu.HBM)


def gather_keys(all_ref, kv_ref, stale_refs, got_refs):
    count = kv_ref.shape[0]
    first_core = lax.axis_index("pipe") == 0
    all_ref[:count] = kv_ref[...]

    @pl.when(first_core)
    def _():
        join(stale_refs, all_ref.at[count:])

    @pl.when(jnp.logical_not(first_core))
    def _():
        join(got_refs, all_ref.at[count:])


def block_kernel(n_pieces, n_got, *refs):
    stale_refs = refs[:n_pieces]
    got_refs = refs[n_pieces : n_pieces + n_got]
    (
        x_ref, q_ref, kv_ref, idx_ref, vec_ref, w1_ref, wo_ref,
        xt_ref, qt_ref, kv1_ref, send_ref, all_ref, pick_ref,
    ) = refs[n_pieces + n_got :]
    count = x_ref.shape[0]
    first_core = lax.axis_index("pipe") == 0
    gather_keys(all_ref, kv_ref, stale_refs, got_refs)
    join(stale_refs, send_ref)
    pick_ref[...] = jnp.zeros_like(pick_ref)
    tile_rows = idx_ref.shape[0]

    def body(start, size):
        rows = pl.ds(start, size)
        attended = attend(q_ref[rows], all_ref).astype(BF16)
        branch = dot(attended, wo_ref[...])
        x1 = (x_ref[rows].astype(F32) + vec_ref[2:3] * branch).astype(BF16)
        modulated = normed(x1.astype(F32), vec_ref[4:5], vec_ref[3:4])
        fresh = dot_t(modulated, w1_ref[DA:]).astype(BF16)
        kv1_ref[rows] = fresh

        @pl.when(first_core)
        def _():
            send_ref[rows] = fresh

        lane = lax.broadcasted_iota(jnp.int32, (tile_rows, size), 1) + start
        chosen = (lane == idx_ref[:, :1]).astype(F32).astype(BF16)
        pick_ref[0] += dot(chosen, x1)
        pick_ref[1] += dot(chosen, modulated)

    each_block(count, body)
    xt_ref[...] = pick_ref[0].astype(BF16)
    qt_ref[...] = query_of(pick_ref[1].astype(BF16), w1_ref)


def first_block(stale_pieces, got_pieces, x, q, kv, idx, vecs, w_next, wo_block):
    count = x.shape[0]
    tile_rows = idx.shape[0]
    return pl.pallas_call(
        functools.partial(block_kernel, len(stale_pieces), len(got_pieces)),
        out_shape=(
            jax.ShapeDtypeStruct((tile_rows, D), BF16),
            jax.ShapeDtypeStruct((tile_rows, DP), BF16),
            jax.ShapeDtypeStruct((count, 2 * DA), BF16),
            jax.ShapeDtypeStruct((count, 2 * DA), BF16),
        ),
        in_specs=[VMEM] * (len(stale_pieces) + len(got_pieces) + 7),
        out_specs=(VMEM,) * 4,
        scratch_shapes=[
            pltpu.VMEM((2 * count, 2 * DA), BF16),
            pltpu.VMEM((2, tile_rows, D), F32),
        ],
        compiler_params=params(count),
        name="attention_and_next_keys",
    )(*stale_pieces, *got_pieces, x, q, kv, idx, vecs, w_next, wo_block)


def tile_kernel(x_ref, q_ref, kv_ref, got_ref, idx_ref, vec_ref, wf_ref, wo_ref, patch_ref, all_ref):
    count = kv_ref.shape[0]
    all_ref[:count] = kv_ref[...]
    all_ref[count:] = got_ref[...]
    attended = attend(q_ref[...], all_ref).astype(BF16)
    branch = dot(attended, wo_ref[...])
    x2 = (x_ref[...].astype(F32) + vec_ref[5:6] * branch).astype(BF16)
    final = normed(x2.astype(F32), vec_ref[7:8], vec_ref[6:7])
    patches = dot_t(final, wf_ref[...]).astype(BF16).astype(F32)
    patch_ref[...] = jnp.zeros_like(patch_ref)
    patch_ref[:, : 4 * LATC] = jnp.where(idx_ref[:, :1] >= 0, patches, 0.0)


def tile_block(x, q, kv, got, idx, vecs, w_final, wo_block):
    count = kv.shape[0]
    return pl.pallas_call(
        tile_kernel,
        out_shape=jax.ShapeDtypeStruct((x.shape[0], LANES), F32),
        in_specs=[VMEM] * 8,
        out_specs=VMEM,
        scratch_shapes=[pltpu.VMEM((2 * count, 2 * DA), BF16)],
        compiler_params=params(count),
        name="tile_attention_and_patches",
    )(x, q, kv, got, idx, vecs, w_final, wo_block)


def decode_kernel(
    rows, cols, pitch, patch_ref, got_ref, idx_ref, wp_ref, bin_ref, bup_ref, w_ref, out_ref, u_ref, ub_ref
):
    first_core = lax.axis_index("pipe") == 0
    got = got_ref[:pitch]
    above = jnp.where(first_core, 0.0, got)
    below = jnp.where(first_core, got, 0.0)
    rim = [above] + [patch_ref[r * pitch : (r + 1) * pitch] for r in range(rows)] + [below]
    column_in = idx_ref[:pitch, :1] >= 0
    shifted = [[pltpu.roll(p, (-ds) % pitch, 0) if ds else p for ds in (-1, 0, 1)] for p in rim]
    for r in range(rows + 2):
        low, high = None, None
        for dr in (-1, 0, 1):
            if not 0 <= r + dr < rows + 2:
                continue
            for ds in range(3):
                tap = (dr + 1) * 3 + ds
                piece = shifted[r + dr][ds]
                if tap == 8:
                    high = piece
                else:
                    piece = pltpu.roll(piece, 4 * LATC * tap, 1) if tap else piece
                    low = piece if low is None else low + piece
        high = jnp.zeros_like(low) if high is None else high
        around = jnp.concatenate([low, high], axis=1).astype(BF16)
        for p in range(2):
            y = 2 * (r - 1) + p + 1
            if not 0 <= y < 2 * rows + 2:
                continue
            for q in range(2):
                at = (2 * p + q) * 2 * LANES
                act = dot(around, wp_ref[at : at + 2 * LANES]) + bin_ref[...]
                feature = act / (1.0 + jnp.exp(-act))
                keep = column_in
                if y == 0:
                    keep = keep & jnp.logical_not(first_core)
                if y == 2 * rows + 1:
                    keep = keep & first_core
                feature = jnp.where(keep, feature, 0.0)
                for c in range(CH // LANES):
                    part = feature[:, c * LANES : (c + 1) * LANES]
                    u_ref[y, c, pl.ds(2 * q, pitch, stride=4), :] = part
                    u_ref[y, c, pl.ds(2 * q + 1, pitch, stride=4), :] = part
    wide = 4 * cols
    for y in range(2 * rows + 2):
        for dx in range(3):
            for c in range(CH // LANES):
                ub_ref[dx, y * wide : (y + 1) * wide, c * LANES : (c + 1) * LANES] = u_ref[
                    y, c, 3 + dx : 3 + dx + wide, :
                ].astype(BF16)

    def tap_row(dy, y_first, y_count):
        total = None
        for dx in range(3):
            part = dot(ub_ref[dx, y_first * wide : (y_first + y_count) * wide], w_ref[3 * dy + dx])
            total = part if total is None else total + part
        return total

    def rows_of(total, y):
        return total[y * wide : (y + 1) * wide]

    middle = tap_row(1, 1, 2 * rows) + bup_ref[...]
    before = tap_row(0, 0, 2 * rows + 1)
    after = tap_row(2, 1, 2 * rows + 1)
    for y in range(2 * rows):
        own = rows_of(middle, y)
        out_ref[2 * y] = (own + rows_of(before, y) + rows_of(after, y)).astype(BF16)
        out_ref[2 * y + 1] = (own + rows_of(before, y + 1) + rows_of(after, y + 1)).astype(BF16)


def decode(rows, cols, pitch, patches, got, idx, w_patch, b_in, b_up, w_up):
    return pl.pallas_call(
        functools.partial(decode_kernel, rows, cols, pitch),
        out_shape=jax.ShapeDtypeStruct((4 * rows, 4 * cols, CH), BF16),
        in_specs=[VMEM] * 7,
        out_specs=VMEM,
        scratch_shapes=[
            pltpu.VMEM((2 * rows + 2, CH // LANES, 4 * pitch, LANES), F32),
            pltpu.VMEM((3, (2 * rows + 2) * 4 * cols, CH), BF16),
        ],
        compiler_params=params(0),
        name="decoder_convolutions",
    )(patches, got, idx, w_patch, b_in, b_up, w_up)


def patch_selector():
    sel = np.zeros((2, 2, 3, 3, 2, 2, LATC, 9 * LATC), np.float32)
    for p, q, dr, ds, pp, qq in np.ndindex(2, 2, 3, 3, 2, 2):
        dy = 2 * (dr - 1) + pp - p
        dx = 2 * (ds - 1) + qq - q
        if abs(dy) <= 1 and abs(dx) <= 1:
            tap = (dy + 1) * 3 + dx + 1
            for c in range(LATC):
                sel[p, q, dr, ds, pp, qq, c, tap * LATC + c] = 1.0
    sel = sel.reshape(4, 9 * 4 * LATC, 9 * LATC)
    return np.pad(sel, ((0, 0), (0, 2 * LANES - 9 * 4 * LATC), (0, 0))).reshape(-1, 9 * LATC)


def split_of(n):
    inner = 2 ** (int(math.log2(n)) // 2)
    return n // inner, inner


def swapped(block, k_outer, k_inner):
    n = lax.axis_size("patch")
    _, inner = split_of(n)
    return lax.ppermute(block, "patch", [(i ^ (k_outer * inner + k_inner), i) for i in range(n)])


def local(
    tokens,
    stale_kv,
    w_qkv,
    w_out,
    block_table,
    time_table,
    t_index,
    w_final,
    w_in,
    b_in,
    w_up,
    b_up,
):
    section = lax.axis_index("pipe")
    tile = lax.axis_index("patch")
    n_tiles = lax.axis_size("patch")
    swap = [(0, 1), (1, 0)]
    first_core = section == 0
    own_count = tokens.shape[1]
    count = own_count * n_tiles
    rows = count // TC
    cols = TC // n_tiles
    pitch = -(-(cols + 3) // 8) * 8
    outer, inner = split_of(n_tiles)

    own_tokens = lax.dynamic_index_in_dim(tokens, section, 0, keepdims=False)
    w_qkv = jnp.swapaxes(w_qkv, 1, 2)
    w_qkv_other = lax.ppermute(w_qkv, "pipe", swap)
    tables = lax.all_gather(block_table[0], "pipe")
    x_column = [swapped(own_tokens, k, 0) for k in range(1, outer)]

    time_row = lax.dynamic_index_in_dim(time_table, t_index[0], 0, keepdims=False)
    ones = jnp.asarray([[0.0], [1.0], [0.0]], F32)
    vecs = jnp.concatenate(
        [
            time_row[:3] + tables[0] + ones,
            time_row[:3] + tables[1] + ones,
            time_row[3:5] + ones[:2],
        ],
        axis=0,
    )

    padded_rows = -(-rows * pitch // 16) * 16
    place = jnp.arange(padded_rows)
    column = place % pitch - 1 + tile * cols
    inside = (place % pitch < cols + 2) & (place < rows * pitch) & (column >= 0) & (column < TC)
    token = place // pitch * TC + jnp.clip(column, 0, TC - 1)
    source = token // own_count
    k_outer = (source // inner) ^ (tile // inner)
    k_inner = (source % inner) ^ (tile % inner)
    spot = (k_inner * outer + k_outer) * own_count + token % own_count
    idx = jnp.broadcast_to(jnp.where(inside, spot, -1)[:, None], (padded_rows, LANES)).astype(jnp.int32)

    x_column, w_qkv_other, vecs, idx, own_stale, w_out = lax.optimization_barrier(
        (x_column, w_qkv_other, vecs, idx, stale_kv[0, 1], w_out)
    )
    x_column = jnp.concatenate([own_tokens] + x_column, axis=0)
    x_column, own_stale, w_out = lax.optimization_barrier((x_column, own_stale, w_out))
    x_pieces = [x_column] + [swapped(x_column, 0, k) for k in range(1, inner)]
    stale_column = [own_stale] + [swapped(own_stale, k, 0) for k in range(1, outer)]
    w_out_other = lax.ppermute(w_out, "pipe", swap)
    w_0, w_1, wo_0, wo_1 = weights_in_vmem(w_qkv, w_qkv_other, w_out, w_out_other)
    x_pieces, stale_column, w_0 = lax.optimization_barrier((x_pieces, stale_column, w_0))
    stale_column = jnp.concatenate(stale_column, axis=0)
    x_pieces, stale_column = lax.optimization_barrier((x_pieces, stale_column))
    stale_pieces = [stale_column] + [swapped(stale_column, 0, k) for k in range(1, inner)]
    x, query, fresh, *parts = project(x_pieces, vecs, w_0)
    got_pieces = [lax.ppermute(part, "pipe", swap) for part in parts]
    x_tile, q_tile, fresh, send = first_block(
        stale_pieces, got_pieces, x, query, fresh, idx, vecs, w_1, wo_0
    )
    send, w_in = lax.optimization_barrier((send, w_in))
    got = lax.ppermute(send, "pipe", swap)
    w_patch = dot(jnp.asarray(patch_selector(), BF16), w_in).astype(BF16)
    got, w_patch = lax.optimization_barrier((got, w_patch))
    patches = tile_block(x_tile, q_tile, fresh, got, idx, vecs, w_final.T, wo_1)
    edge = patches
    if rows > 1:
        edge = jnp.where(first_core, patches[(rows - 1) * pitch : rows * pitch], patches[:pitch])
    got = lax.ppermute(edge, "pipe", swap)
    return decode(rows, cols, pitch, patches, got, idx, w_patch, b_in[None], b_up[None], w_up)


def solution(mesh):
    placed = (
        P(None, ("grp", "patch"), None),
        P("pipe", None, ("grp", "patch"), None),
        P("pipe", None, None),
        P("pipe", None, None),
        P("pipe", None, None),
        P(),
        P("grp"),
        P(),
        P(),
        P(),
        P(),
        P(),
    )
    return jax.shard_map(
        local,
        mesh=mesh,
        in_specs=placed,
        out_specs=P(("grp", "pipe"), "patch", None),
        check_vma=False,
    )
```

```python
import functools
import math

import jax
import jax.numpy as jnp
import numpy as np
from jax import lax
from jax.experimental import pallas as pl
from jax.experimental.pallas import tpu as pltpu
from jax.sharding import PartitionSpec as P

D = 1152
DH = 72
HEADS = 8
CH = 512
LATC = 4
TC = 256
DA = 576
DP = 640
SHIFT = 64
EPSILON = 1e-06
QUERY_SCALE = math.log2(math.e) / math.sqrt(DH)
BLOCK = 256
SMALL_BLOCK = 64
LANES = 128

F32 = jnp.float32
BF16 = jnp.bfloat16
VMEM = pl.BlockSpec(memory_space=pltpu.VMEM)
ANY = pl.BlockSpec(memory_space=pl.ANY)


def dot(a, b):
    return jnp.dot(a, b, preferred_element_type=F32)


def dot_t(a, b):
    return lax.dot_general(a, b, (((1,), (1,)), ((), ())), preferred_element_type=F32)


def normed(values, scale, shift):
    average = jnp.mean(values, axis=-1, keepdims=True)
    centred = values - average
    variance = jnp.mean(centred * centred, axis=-1, keepdims=True)
    return (centred * lax.rsqrt(variance + EPSILON) * scale + shift).astype(BF16)


def lane_window(start):
    return start // LANES * LANES, -(-(start + DH) // LANES) * LANES


def head_scores(query, kv_ref, head):
    first, last = lane_window(head * DH)
    lane = lax.broadcasted_iota(jnp.int32, (query.shape[0], last - first), 1) + first
    own = (lane >= head * DH) & (lane < (head + 1) * DH)
    return dot_t(jnp.where(own, query[:, first:last], jnp.zeros((), BF16)), kv_ref[:, first:last])


def value_window(head):
    return lane_window(DA + head * DH)


def weigh(exponent, kv_ref, head):
    first, last = value_window(head)
    return dot(exponent.astype(BF16), kv_ref[:, first:last])


def spread(outs):
    pieces = [None] * (DP // LANES)
    for head, out in enumerate(outs):
        first, last = value_window(head)
        start = DA + head * DH
        lane = lax.broadcasted_iota(jnp.int32, out.shape, 1) + first
        out = jnp.where((lane >= start) & (lane < start + DH), out, 0.0)
        for i in range((last - first) // LANES):
            at = (first - (DA - SHIFT)) // LANES + i
            part = out[:, i * LANES : (i + 1) * LANES]
            pieces[at] = part if pieces[at] is None else pieces[at] + part
    return jnp.concatenate(pieces, axis=1)


def attend(query, kv_ref):
    outs = []
    for head in range(HEADS):
        scores = head_scores(query, kv_ref, head)
        exponent = jnp.exp2(scores - jnp.max(scores, axis=1, keepdims=True))
        total = jnp.sum(exponent, axis=1, keepdims=True)
        outs.append(weigh(exponent, kv_ref, head) * (1.0 / total))
    return spread(outs)


def attend_begin(query, kv_ref):
    outs = []
    lane = lax.broadcasted_iota(jnp.int32, (query.shape[0], LANES), 1)
    state = jnp.zeros((query.shape[0], LANES), F32)
    for head in range(HEADS):
        scores = head_scores(query, kv_ref, head)
        top = jnp.max(scores, axis=1, keepdims=True)
        exponent = jnp.exp2(scores - top)
        total = jnp.sum(exponent, axis=1, keepdims=True)
        outs.append(weigh(exponent, kv_ref, head))
        state = jnp.where(lane == head, top, jnp.where(lane == HEADS + head, total, state))
    return spread(outs), state


def attend_end(query, kv_ref, sums, state):
    outs = []
    for head in range(HEADS):
        scores = head_scores(query, kv_ref, head)
        before, total = state[:, head : head + 1], state[:, HEADS + head : HEADS + head + 1]
        top = jnp.maximum(before, jnp.max(scores, axis=1, keepdims=True))
        exponent = jnp.exp2(scores - top)
        keep = jnp.exp2(before - top)
        total = keep * total + jnp.sum(exponent, axis=1, keepdims=True)
        first, last = value_window(head)
        earlier = sums[:, first - (DA - SHIFT) : last - (DA - SHIFT)]
        outs.append((keep * earlier + weigh(exponent, kv_ref, head)) * (1.0 / total))
    return spread(outs)


def each_block(count, body):
    if count <= BLOCK:
        body(0, count)
    else:

        @pl.loop(0, count // SMALL_BLOCK)
        def _(i):
            body(pl.multiple_of(i * SMALL_BLOCK, SMALL_BLOCK), SMALL_BLOCK)


def params(count):
    return pltpu.CompilerParams(vmem_limit_bytes=(24 if count <= BLOCK else 56) * 1024 * 1024)


def weights_kernel(own_ref, other_ref, wo_own, wo_other, w0_ref, w1_ref, wo0_ref, wo1_ref, sems):
    first = lax.axis_index("pipe") == 0
    pad = jnp.zeros((SHIFT, D), BF16)
    wo0_ref[:SHIFT] = pad
    wo1_ref[:SHIFT] = pad
    outs = (wo0_ref.at[SHIFT:], wo1_ref.at[SHIFT:])
    copies = []
    for i, (in_place, arrived, targets) in enumerate(
        ((own_ref.at[0], other_ref.at[0], (w0_ref, w1_ref)), (wo_own.at[0], wo_other.at[0], outs))
    ):
        for block in range(2):
            own = (first if block == 0 else jnp.logical_not(first))
            sem = sems.at[2 * i + block]
            copies.append(pltpu.make_async_copy(in_place, targets[block], sem))

            @pl.when(own)
            def _():
                pltpu.make_async_copy(in_place, targets[block], sem).start()

            @pl.when(jnp.logical_not(own))
            def _():
                pltpu.make_async_copy(arrived, targets[block], sem).start()

    for copy in copies:
        copy.wait()


def weights_in_vmem(w_own, w_other, wo_own, wo_other):
    return pl.pallas_call(
        weights_kernel,
        out_shape=(jax.ShapeDtypeStruct((3 * DA, D), BF16),) * 2 + (jax.ShapeDtypeStruct((DP, D), BF16),) * 2,
        in_specs=[ANY] * 4,
        out_specs=(VMEM,) * 4,
        scratch_shapes=[pltpu.SemaphoreType.DMA((4,))],
        compiler_params=params(0),
        name="weights_by_block",
    )(in_hbm(w_own), w_other, in_hbm(wo_own), wo_other)


def query_of(modulated, w_ref):
    projected = dot_t(modulated, w_ref[:DP]) * QUERY_SCALE
    lane = lax.broadcasted_iota(jnp.int32, projected.shape, 1)
    return jnp.where(lane < DA, projected, 0.0).astype(BF16)


def join(refs, target):
    at = 0
    for ref in refs:
        rows = ref.shape[0]
        target[at : at + rows] = ref[...]
        at += rows


def project_kernel(n_pieces, *refs):
    piece_refs = refs[:n_pieces]
    vec_ref, w_ref, x_ref, q_ref, kv_ref = refs[n_pieces : n_pieces + 5]
    part_refs = refs[n_pieces + 5 :]
    join(piece_refs, x_ref)

    def body(start, size):
        rows = pl.ds(start, size)
        modulated = normed(x_ref[rows].astype(F32), vec_ref[1:2], vec_ref[0:1])
        kv_ref[rows] = dot_t(modulated, w_ref[DA:]).astype(BF16)
        q_ref[rows] = query_of(modulated, w_ref)

    each_block(x_ref.shape[0], body)
    at = 0
    for ref in part_refs:
        rows = ref.shape[0]
        ref[...] = kv_ref[at : at + rows]
        at += rows


def project(pieces, vecs, weights):
    count = sum(piece.shape[0] for piece in pieces)
    parts = (count // 4,) * 4
    return pl.pallas_call(
        functools.partial(project_kernel, len(pieces)),
        out_shape=(
            jax.ShapeDtypeStruct((count, D), BF16),
            jax.ShapeDtypeStruct((count, DP), BF16),
            jax.ShapeDtypeStruct((count, 2 * DA), BF16),
        )
        + tuple(jax.ShapeDtypeStruct((part, 2 * DA), BF16) for part in parts),
        in_specs=[VMEM] * (len(pieces) + 2),
        out_specs=(VMEM,) * 7,
        compiler_params=params(count),
        name="layer_norm_and_projections",
    )(*pieces, vecs, weights)


def in_hbm(array):
    return pltpu.with_memory_space_constraint(array, pltpu.HBM)


def fresh_kernel(q_ref, kv_ref, sum_ref, state_ref):
    def body(start, size):
        rows = pl.ds(start, size)
        sums, state = attend_begin(q_ref[rows], kv_ref)
        sum_ref[rows] = sums
        state_ref[rows] = state

    each_block(q_ref.shape[0], body)


def attend_fresh(q, kv):
    count = q.shape[0]
    return pl.pallas_call(
        fresh_kernel,
        out_shape=(jax.ShapeDtypeStruct((count, DP), F32), jax.ShapeDtypeStruct((count, LANES), F32)),
        in_specs=[VMEM] * 2,
        out_specs=(VMEM,) * 2,
        compiler_params=params(count),
        name="attention_over_own_keys",
    )(q, kv)


def block_kernel(n_pieces, n_got, *refs):
    stale_refs = refs[:n_pieces]
    got_refs = refs[n_pieces : n_pieces + n_got]
    (
        x_ref, q_ref, sum_ref, state_ref, idx_ref, vec_ref, w1_ref, wo_ref,
        xt_ref, qt_ref, kv1_ref, send_ref, other_ref, pick_ref,
    ) = refs[n_pieces + n_got :]
    count = x_ref.shape[0]
    first_core = lax.axis_index("pipe") == 0
    join(stale_refs, send_ref)

    @pl.when(first_core)
    def _():
        join(stale_refs, other_ref)

    @pl.when(jnp.logical_not(first_core))
    def _():
        join(got_refs, other_ref)

    pick_ref[...] = jnp.zeros_like(pick_ref)
    tile_rows = idx_ref.shape[0]

    def body(start, size):
        rows = pl.ds(start, size)
        attended = attend_end(q_ref[rows], other_ref, sum_ref[rows], state_ref[rows]).astype(BF16)
        branch = dot(attended, wo_ref[...])
        x1 = (x_ref[rows].astype(F32) + vec_ref[2:3] * branch).astype(BF16)
        modulated = normed(x1.astype(F32), vec_ref[4:5], vec_ref[3:4])
        fresh = dot_t(modulated, w1_ref[DA:]).astype(BF16)
        kv1_ref[rows] = fresh

        @pl.when(first_core)
        def _():
            send_ref[rows] = fresh

        lane = lax.broadcasted_iota(jnp.int32, (tile_rows, size), 1) + start
        chosen = (lane == idx_ref[:, :1]).astype(F32).astype(BF16)
        pick_ref[0] += dot(chosen, x1)
        pick_ref[1] += dot(chosen, modulated)

    each_block(count, body)
    xt_ref[...] = pick_ref[0].astype(BF16)
    qt_ref[...] = query_of(pick_ref[1].astype(BF16), w1_ref)


def first_block(stale_pieces, got_pieces, x, q, sums, state, idx, vecs, w_next, wo_block):
    count = x.shape[0]
    tile_rows = idx.shape[0]
    return pl.pallas_call(
        functools.partial(block_kernel, len(stale_pieces), len(got_pieces)),
        out_shape=(
            jax.ShapeDtypeStruct((tile_rows, D), BF16),
            jax.ShapeDtypeStruct((tile_rows, DP), BF16),
            jax.ShapeDtypeStruct((count, 2 * DA), BF16),
            jax.ShapeDtypeStruct((count, 2 * DA), BF16),
        ),
        in_specs=[VMEM] * (len(stale_pieces) + len(got_pieces) + 8),
        out_specs=(VMEM,) * 4,
        scratch_shapes=[
            pltpu.VMEM((count, 2 * DA), BF16),
            pltpu.VMEM((2, tile_rows, D), F32),
        ],
        compiler_params=params(count),
        name="attention_and_next_keys",
    )(*stale_pieces, *got_pieces, x, q, sums, state, idx, vecs, w_next, wo_block)


def tile_kernel(x_ref, q_ref, kv_ref, got_ref, idx_ref, vec_ref, wf_ref, wo_ref, patch_ref, all_ref):
    count = kv_ref.shape[0]
    all_ref[:count] = kv_ref[...]
    all_ref[count:] = got_ref[...]
    attended = attend(q_ref[...], all_ref).astype(BF16)
    branch = dot(attended, wo_ref[...])
    x2 = (x_ref[...].astype(F32) + vec_ref[5:6] * branch).astype(BF16)
    final = normed(x2.astype(F32), vec_ref[7:8], vec_ref[6:7])
    patches = dot_t(final, wf_ref[...]).astype(BF16).astype(F32)
    patch_ref[...] = jnp.zeros_like(patch_ref)
    patch_ref[:, : 4 * LATC] = jnp.where(idx_ref[:, :1] >= 0, patches, 0.0)


def tile_block(x, q, kv, got, idx, vecs, w_final, wo_block):
    count = kv.shape[0]
    return pl.pallas_call(
        tile_kernel,
        out_shape=jax.ShapeDtypeStruct((x.shape[0], LANES), F32),
        in_specs=[VMEM] * 8,
        out_specs=VMEM,
        scratch_shapes=[pltpu.VMEM((2 * count, 2 * DA), BF16)],
        compiler_params=params(count),
        name="tile_attention_and_patches",
    )(x, q, kv, got, idx, vecs, w_final, wo_block)


def decode_kernel(
    rows, cols, pitch, patch_ref, got_ref, idx_ref, wp_ref, bin_ref, bup_ref, w_ref, out_ref, u_ref, ub_ref
):
    first_core = lax.axis_index("pipe") == 0
    got = got_ref[:pitch]
    above = jnp.where(first_core, 0.0, got)
    below = jnp.where(first_core, got, 0.0)
    rim = [above] + [patch_ref[r * pitch : (r + 1) * pitch] for r in range(rows)] + [below]
    column_in = idx_ref[:pitch, :1] >= 0
    shifted = [[pltpu.roll(p, (-ds) % pitch, 0) if ds else p for ds in (-1, 0, 1)] for p in rim]
    for r in range(rows + 2):
        low, high = None, None
        for dr in (-1, 0, 1):
            if not 0 <= r + dr < rows + 2:
                continue
            for ds in range(3):
                tap = (dr + 1) * 3 + ds
                piece = shifted[r + dr][ds]
                if tap == 8:
                    high = piece
                else:
                    piece = pltpu.roll(piece, 4 * LATC * tap, 1) if tap else piece
                    low = piece if low is None else low + piece
        high = jnp.zeros_like(low) if high is None else high
        around = jnp.concatenate([low, high], axis=1).astype(BF16)
        for p in range(2):
            y = 2 * (r - 1) + p + 1
            if not 0 <= y < 2 * rows + 2:
                continue
            for q in range(2):
                at = (2 * p + q) * 2 * LANES
                act = dot(around, wp_ref[at : at + 2 * LANES]) + bin_ref[...]
                feature = act / (1.0 + jnp.exp(-act))
                keep = column_in
                if y == 0:
                    keep = keep & jnp.logical_not(first_core)
                if y == 2 * rows + 1:
                    keep = keep & first_core
                feature = jnp.where(keep, feature, 0.0)
                for c in range(CH // LANES):
                    part = feature[:, c * LANES : (c + 1) * LANES]
                    u_ref[y, c, pl.ds(2 * q, pitch, stride=4), :] = part
                    u_ref[y, c, pl.ds(2 * q + 1, pitch, stride=4), :] = part
    wide = 4 * cols
    for y in range(2 * rows + 2):
        for dx in range(3):
            for c in range(CH // LANES):
                ub_ref[dx, y * wide : (y + 1) * wide, c * LANES : (c + 1) * LANES] = u_ref[
                    y, c, 3 + dx : 3 + dx + wide, :
                ].astype(BF16)

    def tap_row(dy, y_first, y_count):
        total = None
        for dx in range(3):
            part = dot(ub_ref[dx, y_first * wide : (y_first + y_count) * wide], w_ref[3 * dy + dx])
            total = part if total is None else total + part
        return total

    def rows_of(total, y):
        return total[y * wide : (y + 1) * wide]

    middle = tap_row(1, 1, 2 * rows) + bup_ref[...]
    before = tap_row(0, 0, 2 * rows + 1)
    after = tap_row(2, 1, 2 * rows + 1)
    for y in range(2 * rows):
        own = rows_of(middle, y)
        out_ref[2 * y] = (own + rows_of(before, y) + rows_of(after, y)).astype(BF16)
        out_ref[2 * y + 1] = (own + rows_of(before, y + 1) + rows_of(after, y + 1)).astype(BF16)


def decode(rows, cols, pitch, patches, got, idx, w_patch, b_in, b_up, w_up):
    return pl.pallas_call(
        functools.partial(decode_kernel, rows, cols, pitch),
        out_shape=jax.ShapeDtypeStruct((4 * rows, 4 * cols, CH), BF16),
        in_specs=[VMEM] * 7,
        out_specs=VMEM,
        scratch_shapes=[
            pltpu.VMEM((2 * rows + 2, CH // LANES, 4 * pitch, LANES), F32),
            pltpu.VMEM((3, (2 * rows + 2) * 4 * cols, CH), BF16),
        ],
        compiler_params=params(0),
        name="decoder_convolutions",
    )(patches, got, idx, w_patch, b_in, b_up, w_up)


def patch_selector():
    sel = np.zeros((2, 2, 3, 3, 2, 2, LATC, 9 * LATC), np.float32)
    for p, q, dr, ds, pp, qq in np.ndindex(2, 2, 3, 3, 2, 2):
        dy = 2 * (dr - 1) + pp - p
        dx = 2 * (ds - 1) + qq - q
        if abs(dy) <= 1 and abs(dx) <= 1:
            tap = (dy + 1) * 3 + dx + 1
            for c in range(LATC):
                sel[p, q, dr, ds, pp, qq, c, tap * LATC + c] = 1.0
    sel = sel.reshape(4, 9 * 4 * LATC, 9 * LATC)
    return np.pad(sel, ((0, 0), (0, 2 * LANES - 9 * 4 * LATC), (0, 0))).reshape(-1, 9 * LATC)


def split_of(n):
    inner = 2 ** (int(math.log2(n)) // 2)
    return n // inner, inner


def swapped(block, k_outer, k_inner):
    n = lax.axis_size("patch")
    _, inner = split_of(n)
    return lax.ppermute(block, "patch", [(i ^ (k_outer * inner + k_inner), i) for i in range(n)])


def local(
    tokens,
    stale_kv,
    w_qkv,
    w_out,
    block_table,
    time_table,
    t_index,
    w_final,
    w_in,
    b_in,
    w_up,
    b_up,
):
    section = lax.axis_index("pipe")
    tile = lax.axis_index("patch")
    n_tiles = lax.axis_size("patch")
    swap = [(0, 1), (1, 0)]
    first_core = section == 0
    own_count = tokens.shape[1]
    count = own_count * n_tiles
    rows = count // TC
    cols = TC // n_tiles
    pitch = -(-(cols + 3) // 8) * 8
    outer, inner = split_of(n_tiles)

    own_tokens = lax.dynamic_index_in_dim(tokens, section, 0, keepdims=False)
    w_qkv = jnp.swapaxes(w_qkv, 1, 2)
    w_qkv_other = lax.ppermute(w_qkv, "pipe", swap)
    tables = lax.all_gather(block_table[0], "pipe")
    x_column = [swapped(own_tokens, k, 0) for k in range(1, outer)]
    own_stale = stale_kv[0, 1]
    stale_line = [swapped(own_stale, 0, k) for k in range(1, inner)]

    time_row = lax.dynamic_index_in_dim(time_table, t_index[0], 0, keepdims=False)
    ones = jnp.asarray([[0.0], [1.0], [0.0]], F32)
    vecs = jnp.concatenate(
        [
            time_row[:3] + tables[0] + ones,
            time_row[:3] + tables[1] + ones,
            time_row[3:5] + ones[:2],
        ],
        axis=0,
    )

    padded_rows = -(-rows * pitch // 16) * 16
    place = jnp.arange(padded_rows)
    column = place % pitch - 1 + tile * cols
    inside = (place % pitch < cols + 2) & (place < rows * pitch) & (column >= 0) & (column < TC)
    token = place // pitch * TC + jnp.clip(column, 0, TC - 1)
    source = token // own_count
    k_outer = (source // inner) ^ (tile // inner)
    k_inner = (source % inner) ^ (tile % inner)
    spot = (k_inner * outer + k_outer) * own_count + token % own_count
    idx = jnp.broadcast_to(jnp.where(inside, spot, -1)[:, None], (padded_rows, LANES)).astype(jnp.int32)

    x_column, w_qkv_other, vecs, idx, own_stale, stale_line, w_out = lax.optimization_barrier(
        (x_column, w_qkv_other, vecs, idx, own_stale, stale_line, w_out)
    )
    x_column = jnp.concatenate([own_tokens] + x_column, axis=0)
    x_column, own_stale, w_out = lax.optimization_barrier((x_column, own_stale, w_out))
    x_pieces = [x_column] + [swapped(x_column, 0, k) for k in range(1, inner)]
    stale_column = [swapped(own_stale, k, 0) for k in range(1, outer)]
    w_out_other = lax.ppermute(w_out, "pipe", swap)
    w_0, w_1, wo_0, wo_1 = weights_in_vmem(w_qkv, w_qkv_other, w_out, w_out_other)
    x_pieces, stale_column, w_0 = lax.optimization_barrier((x_pieces, stale_column, w_0))
    stale_column = jnp.concatenate(stale_column, axis=0)
    x_pieces, stale_column = lax.optimization_barrier((x_pieces, stale_column))
    stale_pieces = [own_stale, stale_column] + stale_line + [swapped(stale_column, 0, k) for k in range(1, inner)]
    x, query, fresh, *parts = project(x_pieces, vecs, w_0)
    got_pieces = [lax.ppermute(part, "pipe", swap) for part in parts]
    sums, state = attend_fresh(query, fresh)
    x_tile, q_tile, fresh, send = first_block(
        stale_pieces, got_pieces, x, query, sums, state, idx, vecs, w_1, wo_0
    )
    send, w_in = lax.optimization_barrier((send, w_in))
    got = lax.ppermute(send, "pipe", swap)
    w_patch = dot(jnp.asarray(patch_selector(), BF16), w_in).astype(BF16)
    got, w_patch = lax.optimization_barrier((got, w_patch))
    patches = tile_block(x_tile, q_tile, fresh, got, idx, vecs, w_final.T, wo_1)
    edge = patches
    if rows > 1:
        edge = jnp.where(first_core, patches[(rows - 1) * pitch : rows * pitch], patches[:pitch])
    got = lax.ppermute(edge, "pipe", swap)
    return decode(rows, cols, pitch, patches, got, idx, w_patch, b_in[None], b_up[None], w_up)


def solution(mesh):
    placed = (
        P(None, ("grp", "patch"), None),
        P("pipe", None, ("grp", "patch"), None),
        P("pipe", None, None),
        P("pipe", None, None),
        P("pipe", None, None),
        P(),
        P("grp"),
        P(),
        P(),
        P(),
        P(),
        P(),
    )
    return jax.shard_map(
        local,
        mesh=mesh,
        in_specs=placed,
        out_specs=P(("grp", "pipe"), "patch", None),
        check_vma=False,
    )
```

```python
import functools
import math

import jax
import jax.numpy as jnp
import numpy as np
from jax import lax
from jax.experimental import pallas as pl
from jax.experimental.pallas import tpu as pltpu
from jax.sharding import PartitionSpec as P

D = 1152
DH = 72
HEADS = 8
CH = 512
LATC = 4
TC = 256
DA = 576
DP = 640
SHIFT = 64
EPSILON = 1e-06
QUERY_SCALE = math.log2(math.e) / math.sqrt(DH)
BLOCK = 256
SMALL_BLOCK = 64
LANES = 128

F32 = jnp.float32
BF16 = jnp.bfloat16
VMEM = pl.BlockSpec(memory_space=pltpu.VMEM)
ANY = pl.BlockSpec(memory_space=pl.ANY)


def dot(a, b):
    return jnp.dot(a, b, preferred_element_type=F32)


def dot_t(a, b):
    return lax.dot_general(a, b, (((1,), (1,)), ((), ())), preferred_element_type=F32)


def normed(values, scale, shift):
    average = jnp.mean(values, axis=-1, keepdims=True)
    centred = values - average
    variance = jnp.mean(centred * centred, axis=-1, keepdims=True)
    return (centred * lax.rsqrt(variance + EPSILON) * scale + shift).astype(BF16)


def lane_window(start):
    return start // LANES * LANES, -(-(start + DH) // LANES) * LANES


def head_scores(query, kv_ref, head):
    first, last = lane_window(head * DH)
    lane = lax.broadcasted_iota(jnp.int32, (query.shape[0], last - first), 1) + first
    own = (lane >= head * DH) & (lane < (head + 1) * DH)
    return dot_t(jnp.where(own, query[:, first:last], jnp.zeros((), BF16)), kv_ref[:, first:last])


def value_window(head):
    return lane_window(DA + head * DH)


def weigh(exponent, kv_ref, head):
    first, last = value_window(head)
    return dot(exponent.astype(BF16), kv_ref[:, first:last])


def spread(outs):
    pieces = [None] * (DP // LANES)
    for head, out in enumerate(outs):
        first, last = value_window(head)
        start = DA + head * DH
        lane = lax.broadcasted_iota(jnp.int32, out.shape, 1) + first
        out = jnp.where((lane >= start) & (lane < start + DH), out, 0.0)
        for i in range((last - first) // LANES):
            at = (first - (DA - SHIFT)) // LANES + i
            part = out[:, i * LANES : (i + 1) * LANES]
            pieces[at] = part if pieces[at] is None else pieces[at] + part
    return jnp.concatenate(pieces, axis=1)


def attend(query, kv_ref):
    outs = []
    for head in range(HEADS):
        scores = head_scores(query, kv_ref, head)
        exponent = jnp.exp2(scores - jnp.max(scores, axis=1, keepdims=True))
        total = jnp.sum(exponent, axis=1, keepdims=True)
        outs.append(weigh(exponent, kv_ref, head) * (1.0 / total))
    return spread(outs)


def attend_begin(query, kv_ref):
    outs = []
    lane = lax.broadcasted_iota(jnp.int32, (query.shape[0], LANES), 1)
    state = jnp.zeros((query.shape[0], LANES), F32)
    for head in range(HEADS):
        scores = head_scores(query, kv_ref, head)
        top = jnp.max(scores, axis=1, keepdims=True)
        exponent = jnp.exp2(scores - top)
        total = jnp.sum(exponent, axis=1, keepdims=True)
        outs.append(weigh(exponent, kv_ref, head))
        state = jnp.where(lane == head, top, jnp.where(lane == HEADS + head, total, state))
    return spread(outs), state


def attend_end(query, kv_ref, sums, state):
    outs = []
    for head in range(HEADS):
        scores = head_scores(query, kv_ref, head)
        before, total = state[:, head : head + 1], state[:, HEADS + head : HEADS + head + 1]
        top = jnp.maximum(before, jnp.max(scores, axis=1, keepdims=True))
        exponent = jnp.exp2(scores - top)
        keep = jnp.exp2(before - top)
        total = keep * total + jnp.sum(exponent, axis=1, keepdims=True)
        first, last = value_window(head)
        earlier = sums[:, first - (DA - SHIFT) : last - (DA - SHIFT)]
        outs.append((keep * earlier + weigh(exponent, kv_ref, head)) * (1.0 / total))
    return spread(outs)


def each_block(count, body):
    if count <= BLOCK:
        body(0, count)
    else:

        @pl.loop(0, count // SMALL_BLOCK)
        def _(i):
            body(pl.multiple_of(i * SMALL_BLOCK, SMALL_BLOCK), SMALL_BLOCK)


def params(count):
    return pltpu.CompilerParams(vmem_limit_bytes=(24 if count <= BLOCK else 56) * 1024 * 1024)


def weights_kernel(own_ref, other_ref, wo_own, wo_other, w0_ref, w1_ref, wo0_ref, wo1_ref, sems):
    first = lax.axis_index("pipe") == 0
    pad = jnp.zeros((SHIFT, D), BF16)
    wo0_ref[:SHIFT] = pad
    wo1_ref[:SHIFT] = pad
    outs = (wo0_ref.at[SHIFT:], wo1_ref.at[SHIFT:])
    copies = []
    for i, (in_place, arrived, targets) in enumerate(
        ((own_ref.at[0], other_ref.at[0], (w0_ref, w1_ref)), (wo_own.at[0], wo_other.at[0], outs))
    ):
        for block in range(2):
            own = (first if block == 0 else jnp.logical_not(first))
            sem = sems.at[2 * i + block]
            copies.append(pltpu.make_async_copy(in_place, targets[block], sem))

            @pl.when(own)
            def _():
                pltpu.make_async_copy(in_place, targets[block], sem).start()

            @pl.when(jnp.logical_not(own))
            def _():
                pltpu.make_async_copy(arrived, targets[block], sem).start()

    for copy in copies:
        copy.wait()


def weights_in_vmem(w_own, w_other, wo_own, wo_other):
    return pl.pallas_call(
        weights_kernel,
        out_shape=(jax.ShapeDtypeStruct((3 * DA, D), BF16),) * 2 + (jax.ShapeDtypeStruct((DP, D), BF16),) * 2,
        in_specs=[ANY] * 4,
        out_specs=(VMEM,) * 4,
        scratch_shapes=[pltpu.SemaphoreType.DMA((4,))],
        compiler_params=params(0),
        name="weights_by_block",
    )(in_hbm(w_own), w_other, in_hbm(wo_own), wo_other)


def query_of(modulated, w_ref):
    projected = dot_t(modulated, w_ref[:DP]) * QUERY_SCALE
    lane = lax.broadcasted_iota(jnp.int32, projected.shape, 1)
    return jnp.where(lane < DA, projected, 0.0).astype(BF16)


def join(refs, target):
    at = 0
    for ref in refs:
        rows = ref.shape[0]
        target[at : at + rows] = ref[...]
        at += rows


def project_kernel(n_pieces, *refs):
    piece_refs = refs[:n_pieces]
    vec_ref, w_ref, x_ref, q_ref, kv_ref = refs[n_pieces : n_pieces + 5]
    part_refs = refs[n_pieces + 5 :]
    join(piece_refs, x_ref)

    def body(start, size):
        rows = pl.ds(start, size)
        modulated = normed(x_ref[rows].astype(F32), vec_ref[1:2], vec_ref[0:1])
        kv_ref[rows] = dot_t(modulated, w_ref[DA:]).astype(BF16)
        q_ref[rows] = query_of(modulated, w_ref)

    each_block(x_ref.shape[0], body)
    at = 0
    for ref in part_refs:
        rows = ref.shape[0]
        ref[...] = kv_ref[at : at + rows]
        at += rows


def project(pieces, vecs, weights):
    count = sum(piece.shape[0] for piece in pieces)
    parts = (count // 4,) * 4
    return pl.pallas_call(
        functools.partial(project_kernel, len(pieces)),
        out_shape=(
            jax.ShapeDtypeStruct((count, D), BF16),
            jax.ShapeDtypeStruct((count, DP), BF16),
            jax.ShapeDtypeStruct((count, 2 * DA), BF16),
        )
        + tuple(jax.ShapeDtypeStruct((part, 2 * DA), BF16) for part in parts),
        in_specs=[VMEM] * (len(pieces) + 2),
        out_specs=(VMEM,) * 7,
        compiler_params=params(count),
        name="layer_norm_and_projections",
    )(*pieces, vecs, weights)


def in_hbm(array):
    return pltpu.with_memory_space_constraint(array, pltpu.HBM)


def fresh_kernel(q_ref, kv_ref, sum_ref, state_ref):
    def body(start, size):
        rows = pl.ds(start, size)
        sums, state = attend_begin(q_ref[rows], kv_ref)
        sum_ref[rows] = sums
        state_ref[rows] = state

    each_block(q_ref.shape[0], body)


def attend_fresh(q, kv):
    count = q.shape[0]
    return pl.pallas_call(
        fresh_kernel,
        out_shape=(jax.ShapeDtypeStruct((count, DP), F32), jax.ShapeDtypeStruct((count, LANES), F32)),
        in_specs=[VMEM] * 2,
        out_specs=(VMEM,) * 2,
        compiler_params=params(kv.shape[0]),
        name="attention_over_own_keys",
    )(q, kv)


def block_kernel(n_pieces, n_got, *refs):
    stale_refs = refs[:n_pieces]
    got_refs = refs[n_pieces : n_pieces + n_got]
    (
        x_ref, q_ref, kv_ref, idx_ref, vec_ref, w1_ref, wo_ref,
        xt_ref, qt_ref, kv1_ref, send_ref, all_ref, pick_ref,
    ) = refs[n_pieces + n_got :]
    count = x_ref.shape[0]
    first_core = lax.axis_index("pipe") == 0
    join(stale_refs, send_ref)
    all_ref[:count] = kv_ref[...]

    @pl.when(first_core)
    def _():
        join(stale_refs, all_ref.at[count:])

    @pl.when(jnp.logical_not(first_core))
    def _():
        join(got_refs, all_ref.at[count:])

    pick_ref[...] = jnp.zeros_like(pick_ref)
    tile_rows = idx_ref.shape[0]

    def body(start, size):
        rows = pl.ds(start, size)
        attended = attend(q_ref[rows], all_ref).astype(BF16)
        branch = dot(attended, wo_ref[...])
        x1 = (x_ref[rows].astype(F32) + vec_ref[2:3] * branch).astype(BF16)
        modulated = normed(x1.astype(F32), vec_ref[4:5], vec_ref[3:4])
        fresh = dot_t(modulated, w1_ref[DA:]).astype(BF16)
        kv1_ref[rows] = fresh

        @pl.when(first_core)
        def _():
            send_ref[rows] = fresh

        lane = lax.broadcasted_iota(jnp.int32, (tile_rows, size), 1) + start
        chosen = (lane == idx_ref[:, :1]).astype(F32).astype(BF16)
        pick_ref[0] += dot(chosen, x1)
        pick_ref[1] += dot(chosen, modulated)

    each_block(count, body)
    xt_ref[...] = pick_ref[0].astype(BF16)
    qt_ref[...] = query_of(pick_ref[1].astype(BF16), w1_ref)


def first_block(stale_pieces, got_pieces, x, q, kv, idx, vecs, w_next, wo_block):
    count = x.shape[0]
    tile_rows = idx.shape[0]
    return pl.pallas_call(
        functools.partial(block_kernel, len(stale_pieces), len(got_pieces)),
        out_shape=(
            jax.ShapeDtypeStruct((tile_rows, D), BF16),
            jax.ShapeDtypeStruct((tile_rows, DP), BF16),
            jax.ShapeDtypeStruct((count, 2 * DA), BF16),
            jax.ShapeDtypeStruct((count, 2 * DA), BF16),
        ),
        in_specs=[VMEM] * (len(stale_pieces) + len(got_pieces) + 7),
        out_specs=(VMEM,) * 4,
        scratch_shapes=[
            pltpu.VMEM((2 * count, 2 * DA), BF16),
            pltpu.VMEM((2, tile_rows, D), F32),
        ],
        compiler_params=params(count),
        name="attention_and_next_keys",
    )(*stale_pieces, *got_pieces, x, q, kv, idx, vecs, w_next, wo_block)


def tile_kernel(x_ref, q_ref, sum_ref, state_ref, got_ref, idx_ref, vec_ref, wf_ref, wo_ref, patch_ref):
    attended = attend_end(q_ref[...], got_ref, sum_ref[...], state_ref[...]).astype(BF16)
    branch = dot(attended, wo_ref[...])
    x2 = (x_ref[...].astype(F32) + vec_ref[5:6] * branch).astype(BF16)
    final = normed(x2.astype(F32), vec_ref[7:8], vec_ref[6:7])
    patches = dot_t(final, wf_ref[...]).astype(BF16).astype(F32)
    patch_ref[...] = jnp.zeros_like(patch_ref)
    patch_ref[:, : 4 * LATC] = jnp.where(idx_ref[:, :1] >= 0, patches, 0.0)


def tile_block(x, q, sums, state, got, idx, vecs, w_final, wo_block):
    return pl.pallas_call(
        tile_kernel,
        out_shape=jax.ShapeDtypeStruct((x.shape[0], LANES), F32),
        in_specs=[VMEM] * 9,
        out_specs=VMEM,
        compiler_params=params(got.shape[0]),
        name="tile_attention_and_patches",
    )(x, q, sums, state, got, idx, vecs, w_final, wo_block)


def decode_kernel(
    rows, cols, pitch, patch_ref, got_ref, idx_ref, wp_ref, bin_ref, bup_ref, w_ref, out_ref, u_ref, ub_ref
):
    first_core = lax.axis_index("pipe") == 0
    got = got_ref[:pitch]
    above = jnp.where(first_core, 0.0, got)
    below = jnp.where(first_core, got, 0.0)
    rim = [above] + [patch_ref[r * pitch : (r + 1) * pitch] for r in range(rows)] + [below]
    column_in = idx_ref[:pitch, :1] >= 0
    shifted = [[pltpu.roll(p, (-ds) % pitch, 0) if ds else p for ds in (-1, 0, 1)] for p in rim]
    for r in range(rows + 2):
        low, high = None, None
        for dr in (-1, 0, 1):
            if not 0 <= r + dr < rows + 2:
                continue
            for ds in range(3):
                tap = (dr + 1) * 3 + ds
                piece = shifted[r + dr][ds]
                if tap == 8:
                    high = piece
                else:
                    piece = pltpu.roll(piece, 4 * LATC * tap, 1) if tap else piece
                    low = piece if low is None else low + piece
        high = jnp.zeros_like(low) if high is None else high
        around = jnp.concatenate([low, high], axis=1).astype(BF16)
        for p in range(2):
            y = 2 * (r - 1) + p + 1
            if not 0 <= y < 2 * rows + 2:
                continue
            for q in range(2):
                at = (2 * p + q) * 2 * LANES
                act = dot(around, wp_ref[at : at + 2 * LANES]) + bin_ref[...]
                feature = act / (1.0 + jnp.exp(-act))
                keep = column_in
                if y == 0:
                    keep = keep & jnp.logical_not(first_core)
                if y == 2 * rows + 1:
                    keep = keep & first_core
                feature = jnp.where(keep, feature, 0.0)
                for c in range(CH // LANES):
                    part = feature[:, c * LANES : (c + 1) * LANES]
                    u_ref[y, c, pl.ds(2 * q, pitch, stride=4), :] = part
                    u_ref[y, c, pl.ds(2 * q + 1, pitch, stride=4), :] = part
    wide = 4 * cols
    for y in range(2 * rows + 2):
        for dx in range(3):
            for c in range(CH // LANES):
                ub_ref[dx, y * wide : (y + 1) * wide, c * LANES : (c + 1) * LANES] = u_ref[
                    y, c, 3 + dx : 3 + dx + wide, :
                ].astype(BF16)

    def tap_row(dy, y_first, y_count):
        total = None
        for dx in range(3):
            part = dot(ub_ref[dx, y_first * wide : (y_first + y_count) * wide], w_ref[3 * dy + dx])
            total = part if total is None else total + part
        return total

    def rows_of(total, y):
        return total[y * wide : (y + 1) * wide]

    middle = tap_row(1, 1, 2 * rows) + bup_ref[...]
    before = tap_row(0, 0, 2 * rows + 1)
    after = tap_row(2, 1, 2 * rows + 1)
    for y in range(2 * rows):
        own = rows_of(middle, y)
        out_ref[2 * y] = (own + rows_of(before, y) + rows_of(after, y)).astype(BF16)
        out_ref[2 * y + 1] = (own + rows_of(before, y + 1) + rows_of(after, y + 1)).astype(BF16)


def decode(rows, cols, pitch, patches, got, idx, w_patch, b_in, b_up, w_up):
    return pl.pallas_call(
        functools.partial(decode_kernel, rows, cols, pitch),
        out_shape=jax.ShapeDtypeStruct((4 * rows, 4 * cols, CH), BF16),
        in_specs=[VMEM] * 7,
        out_specs=VMEM,
        scratch_shapes=[
            pltpu.VMEM((2 * rows + 2, CH // LANES, 4 * pitch, LANES), F32),
            pltpu.VMEM((3, (2 * rows + 2) * 4 * cols, CH), BF16),
        ],
        compiler_params=params(0),
        name="decoder_convolutions",
    )(patches, got, idx, w_patch, b_in, b_up, w_up)


def patch_selector():
    sel = np.zeros((2, 2, 3, 3, 2, 2, LATC, 9 * LATC), np.float32)
    for p, q, dr, ds, pp, qq in np.ndindex(2, 2, 3, 3, 2, 2):
        dy = 2 * (dr - 1) + pp - p
        dx = 2 * (ds - 1) + qq - q
        if abs(dy) <= 1 and abs(dx) <= 1:
            tap = (dy + 1) * 3 + dx + 1
            for c in range(LATC):
                sel[p, q, dr, ds, pp, qq, c, tap * LATC + c] = 1.0
    sel = sel.reshape(4, 9 * 4 * LATC, 9 * LATC)
    return np.pad(sel, ((0, 0), (0, 2 * LANES - 9 * 4 * LATC), (0, 0))).reshape(-1, 9 * LATC)


def split_of(n):
    inner = 2 ** (int(math.log2(n)) // 2)
    return n // inner, inner


def swapped(block, k_outer, k_inner):
    n = lax.axis_size("patch")
    _, inner = split_of(n)
    return lax.ppermute(block, "patch", [(i ^ (k_outer * inner + k_inner), i) for i in range(n)])


def local(
    tokens,
    stale_kv,
    w_qkv,
    w_out,
    block_table,
    time_table,
    t_index,
    w_final,
    w_in,
    b_in,
    w_up,
    b_up,
):
    section = lax.axis_index("pipe")
    tile = lax.axis_index("patch")
    n_tiles = lax.axis_size("patch")
    swap = [(0, 1), (1, 0)]
    first_core = section == 0
    own_count = tokens.shape[1]
    count = own_count * n_tiles
    rows = count // TC
    cols = TC // n_tiles
    pitch = -(-(cols + 3) // 8) * 8
    outer, inner = split_of(n_tiles)

    own_tokens = lax.dynamic_index_in_dim(tokens, section, 0, keepdims=False)
    w_qkv = jnp.swapaxes(w_qkv, 1, 2)
    w_qkv_other = lax.ppermute(w_qkv, "pipe", swap)
    tables = lax.all_gather(block_table[0], "pipe")
    x_column = [swapped(own_tokens, k, 0) for k in range(1, outer)]
    own_stale = stale_kv[0, 1]
    stale_line = [swapped(own_stale, 0, k) for k in range(1, inner)]

    time_row = lax.dynamic_index_in_dim(time_table, t_index[0], 0, keepdims=False)
    ones = jnp.asarray([[0.0], [1.0], [0.0]], F32)
    vecs = jnp.concatenate(
        [
            time_row[:3] + tables[0] + ones,
            time_row[:3] + tables[1] + ones,
            time_row[3:5] + ones[:2],
        ],
        axis=0,
    )

    padded_rows = -(-rows * pitch // 16) * 16
    place = jnp.arange(padded_rows)
    column = place % pitch - 1 + tile * cols
    inside = (place % pitch < cols + 2) & (place < rows * pitch) & (column >= 0) & (column < TC)
    token = place // pitch * TC + jnp.clip(column, 0, TC - 1)
    source = token // own_count
    k_outer = (source // inner) ^ (tile // inner)
    k_inner = (source % inner) ^ (tile % inner)
    spot = (k_inner * outer + k_outer) * own_count + token % own_count
    idx = jnp.broadcast_to(jnp.where(inside, spot, -1)[:, None], (padded_rows, LANES)).astype(jnp.int32)

    x_column, w_qkv_other, vecs, idx, own_stale, stale_line, w_out = lax.optimization_barrier(
        (x_column, w_qkv_other, vecs, idx, own_stale, stale_line, w_out)
    )
    x_column = jnp.concatenate([own_tokens] + x_column, axis=0)
    x_column, own_stale, w_out = lax.optimization_barrier((x_column, own_stale, w_out))
    x_pieces = [x_column] + [swapped(x_column, 0, k) for k in range(1, inner)]
    stale_column = [swapped(own_stale, k, 0) for k in range(1, outer)]
    w_out_other = lax.ppermute(w_out, "pipe", swap)
    w_0, w_1, wo_0, wo_1 = weights_in_vmem(w_qkv, w_qkv_other, w_out, w_out_other)
    x_pieces, stale_column, w_0 = lax.optimization_barrier((x_pieces, stale_column, w_0))
    stale_column = jnp.concatenate(stale_column, axis=0)
    x_pieces, stale_column = lax.optimization_barrier((x_pieces, stale_column))
    stale_pieces = [own_stale, stale_column] + stale_line + [swapped(stale_column, 0, k) for k in range(1, inner)]
    x, query, fresh, *parts = project(x_pieces, vecs, w_0)
    got_pieces = [lax.ppermute(part, "pipe", swap) for part in parts]
    x_tile, q_tile, fresh, send = first_block(
        stale_pieces, got_pieces, x, query, fresh, idx, vecs, w_1, wo_0
    )
    send, w_in = lax.optimization_barrier((send, w_in))
    got = lax.ppermute(send, "pipe", swap)
    w_patch = dot(jnp.asarray(patch_selector(), BF16), w_in).astype(BF16)
    sums, state = attend_fresh(q_tile, fresh)
    got, w_patch, sums, state = lax.optimization_barrier((got, w_patch, sums, state))
    patches = tile_block(x_tile, q_tile, sums, state, got, idx, vecs, w_final.T, wo_1)
    edge = patches
    if rows > 1:
        edge = jnp.where(first_core, patches[(rows - 1) * pitch : rows * pitch], patches[:pitch])
    got = lax.ppermute(edge, "pipe", swap)
    return decode(rows, cols, pitch, patches, got, idx, w_patch, b_in[None], b_up[None], w_up)


def solution(mesh):
    placed = (
        P(None, ("grp", "patch"), None),
        P("pipe", None, ("grp", "patch"), None),
        P("pipe", None, None),
        P("pipe", None, None),
        P("pipe", None, None),
        P(),
        P("grp"),
        P(),
        P(),
        P(),
        P(),
        P(),
    )
    return jax.shard_map(
        local,
        mesh=mesh,
        in_specs=placed,
        out_specs=P(("grp", "pipe"), "patch", None),
        check_vma=False,
    )
```

```python
import functools
import math

import jax
import jax.numpy as jnp
import numpy as np
from jax import lax
from jax.experimental import pallas as pl
from jax.experimental.pallas import tpu as pltpu
from jax.sharding import PartitionSpec as P

D = 1152
DH = 72
HEADS = 8
CH = 512
LATC = 4
TC = 256
DA = 576
DP = 640
SHIFT = 64
EPSILON = 1e-06
QUERY_SCALE = math.log2(math.e) / math.sqrt(DH)
BLOCK = 256
SMALL_BLOCK = 64
LANES = 128

F32 = jnp.float32
BF16 = jnp.bfloat16
VMEM = pl.BlockSpec(memory_space=pltpu.VMEM)
ANY = pl.BlockSpec(memory_space=pl.ANY)


def dot(a, b):
    return jnp.dot(a, b, preferred_element_type=F32)


def dot_t(a, b):
    return lax.dot_general(a, b, (((1,), (1,)), ((), ())), preferred_element_type=F32)


def normed(values, scale, shift):
    average = jnp.mean(values, axis=-1, keepdims=True)
    centred = values - average
    variance = jnp.mean(centred * centred, axis=-1, keepdims=True)
    return (centred * lax.rsqrt(variance + EPSILON) * scale + shift).astype(BF16)


def lane_window(start):
    return start // LANES * LANES, -(-(start + DH) // LANES) * LANES


def head_scores(query, kv_ref, head):
    first, last = lane_window(head * DH)
    lane = lax.broadcasted_iota(jnp.int32, (query.shape[0], last - first), 1) + first
    own = (lane >= head * DH) & (lane < (head + 1) * DH)
    return dot_t(jnp.where(own, query[:, first:last], jnp.zeros((), BF16)), kv_ref[:, first:last])


def value_window(head):
    return lane_window(DA + head * DH)


def weigh(exponent, kv_ref, head):
    first, last = value_window(head)
    return dot(exponent.astype(BF16), kv_ref[:, first:last])


def spread(outs):
    pieces = [None] * (DP // LANES)
    for head, out in enumerate(outs):
        first, last = value_window(head)
        start = DA + head * DH
        lane = lax.broadcasted_iota(jnp.int32, out.shape, 1) + first
        out = jnp.where((lane >= start) & (lane < start + DH), out, 0.0)
        for i in range((last - first) // LANES):
            at = (first - (DA - SHIFT)) // LANES + i
            part = out[:, i * LANES : (i + 1) * LANES]
            pieces[at] = part if pieces[at] is None else pieces[at] + part
    return jnp.concatenate(pieces, axis=1)


def attend(query, kv_ref):
    outs = []
    for head in range(HEADS):
        scores = head_scores(query, kv_ref, head)
        exponent = jnp.exp2(scores - jnp.max(scores, axis=1, keepdims=True))
        total = jnp.sum(exponent, axis=1, keepdims=True)
        outs.append(weigh(exponent, kv_ref, head) * (1.0 / total))
    return spread(outs)


def attend_begin(query, kv_ref):
    outs = []
    lane = lax.broadcasted_iota(jnp.int32, (query.shape[0], LANES), 1)
    state = jnp.zeros((query.shape[0], LANES), F32)
    for head in range(HEADS):
        scores = head_scores(query, kv_ref, head)
        top = jnp.max(scores, axis=1, keepdims=True)
        exponent = jnp.exp2(scores - top)
        total = jnp.sum(exponent, axis=1, keepdims=True)
        outs.append(weigh(exponent, kv_ref, head))
        state = jnp.where(lane == head, top, jnp.where(lane == HEADS + head, total, state))
    return spread(outs), state


def attend_end(query, kv_ref, sums, state):
    outs = []
    for head in range(HEADS):
        scores = head_scores(query, kv_ref, head)
        before, total = state[:, head : head + 1], state[:, HEADS + head : HEADS + head + 1]
        top = jnp.maximum(before, jnp.max(scores, axis=1, keepdims=True))
        exponent = jnp.exp2(scores - top)
        keep = jnp.exp2(before - top)
        total = keep * total + jnp.sum(exponent, axis=1, keepdims=True)
        first, last = value_window(head)
        earlier = sums[:, first - (DA - SHIFT) : last - (DA - SHIFT)]
        outs.append((keep * earlier + weigh(exponent, kv_ref, head)) * (1.0 / total))
    return spread(outs)


def each_block(count, body):
    if count <= BLOCK:
        body(0, count)
    else:

        @pl.loop(0, count // SMALL_BLOCK)
        def _(i):
            body(pl.multiple_of(i * SMALL_BLOCK, SMALL_BLOCK), SMALL_BLOCK)


def params(count):
    return pltpu.CompilerParams(vmem_limit_bytes=(24 if count <= BLOCK else 56) * 1024 * 1024)


def weights_kernel(own_ref, other_ref, wo_own, wo_other, w0_ref, w1_ref, wo0_ref, wo1_ref, sems):
    first = lax.axis_index("pipe") == 0
    pad = jnp.zeros((SHIFT, D), BF16)
    wo0_ref[:SHIFT] = pad
    wo1_ref[:SHIFT] = pad
    outs = (wo0_ref.at[SHIFT:], wo1_ref.at[SHIFT:])
    copies = []
    for i, (in_place, arrived, targets) in enumerate(
        ((own_ref.at[0], other_ref.at[0], (w0_ref, w1_ref)), (wo_own.at[0], wo_other.at[0], outs))
    ):
        for block in range(2):
            own = (first if block == 0 else jnp.logical_not(first))
            sem = sems.at[2 * i + block]
            copies.append(pltpu.make_async_copy(in_place, targets[block], sem))

            @pl.when(own)
            def _():
                pltpu.make_async_copy(in_place, targets[block], sem).start()

            @pl.when(jnp.logical_not(own))
            def _():
                pltpu.make_async_copy(arrived, targets[block], sem).start()

    for copy in copies:
        copy.wait()


def weights_in_vmem(w_own, w_other, wo_own, wo_other):
    return pl.pallas_call(
        weights_kernel,
        out_shape=(jax.ShapeDtypeStruct((3 * DA, D), BF16),) * 2 + (jax.ShapeDtypeStruct((DP, D), BF16),) * 2,
        in_specs=[ANY] * 4,
        out_specs=(VMEM,) * 4,
        scratch_shapes=[pltpu.SemaphoreType.DMA((4,))],
        compiler_params=params(0),
        name="weights_by_block",
    )(in_hbm(w_own), w_other, in_hbm(wo_own), wo_other)


def query_of(modulated, w_ref):
    projected = dot_t(modulated, w_ref[:DP]) * QUERY_SCALE
    lane = lax.broadcasted_iota(jnp.int32, projected.shape, 1)
    return jnp.where(lane < DA, projected, 0.0).astype(BF16)


def join(refs, target):
    at = 0
    for ref in refs:
        rows = ref.shape[0]
        target[at : at + rows] = ref[...]
        at += rows


def project_kernel(n_pieces, *refs):
    piece_refs = refs[:n_pieces]
    vec_ref, w_ref, x_ref, q_ref, kv_ref = refs[n_pieces : n_pieces + 5]
    part_refs = refs[n_pieces + 5 :]
    join(piece_refs, x_ref)

    def body(start, size):
        rows = pl.ds(start, size)
        modulated = normed(x_ref[rows].astype(F32), vec_ref[1:2], vec_ref[0:1])
        kv_ref[rows] = dot_t(modulated, w_ref[DA:]).astype(BF16)
        q_ref[rows] = query_of(modulated, w_ref)

    each_block(x_ref.shape[0], body)
    at = 0
    for ref in part_refs:
        rows = ref.shape[0]
        ref[...] = kv_ref[at : at + rows]
        at += rows


def project(pieces, vecs, weights):
    count = sum(piece.shape[0] for piece in pieces)
    parts = (count // 4,) * 4
    return pl.pallas_call(
        functools.partial(project_kernel, len(pieces)),
        out_shape=(
            jax.ShapeDtypeStruct((count, D), BF16),
            jax.ShapeDtypeStruct((count, DP), BF16),
            jax.ShapeDtypeStruct((count, 2 * DA), BF16),
        )
        + tuple(jax.ShapeDtypeStruct((part, 2 * DA), BF16) for part in parts),
        in_specs=[VMEM] * (len(pieces) + 2),
        out_specs=(VMEM,) * 7,
        compiler_params=params(count),
        name="layer_norm_and_projections",
    )(*pieces, vecs, weights)


def in_hbm(array):
    return pltpu.with_memory_space_constraint(array, pltpu.HBM)


def fresh_kernel(x_ref, mod_ref, kv_ref, idx_ref, w_ref, xt_ref, qt_ref, sum_ref, state_ref, pick_ref):
    tile_rows = idx_ref.shape[0]
    pick_ref[...] = jnp.zeros_like(pick_ref)

    def body(start, size):
        rows = pl.ds(start, size)
        lane = lax.broadcasted_iota(jnp.int32, (tile_rows, size), 1) + start
        chosen = (lane == idx_ref[:, :1]).astype(F32).astype(BF16)
        pick_ref[0] += dot(chosen, mod_ref[rows])
        pick_ref[1] += dot(chosen, x_ref[rows])

    each_block(x_ref.shape[0], body)
    query = query_of(pick_ref[0].astype(BF16), w_ref)
    sum_ref[...], state_ref[...] = attend_begin(query, kv_ref)
    qt_ref[...] = query
    xt_ref[...] = pick_ref[1].astype(BF16)


def attend_fresh(x, modulated, kv, idx, w_block):
    rows = idx.shape[0]
    return pl.pallas_call(
        fresh_kernel,
        out_shape=(
            jax.ShapeDtypeStruct((rows, D), BF16),
            jax.ShapeDtypeStruct((rows, DP), BF16),
            jax.ShapeDtypeStruct((rows, DP), F32),
            jax.ShapeDtypeStruct((rows, LANES), F32),
        ),
        in_specs=[VMEM] * 5,
        out_specs=(VMEM,) * 4,
        scratch_shapes=[pltpu.VMEM((2, rows, D), F32)],
        compiler_params=params(kv.shape[0]),
        name="tile_attention_over_own_keys",
    )(x, modulated, kv, idx, w_block)


def block_kernel(n_pieces, n_got, *refs):
    stale_refs = refs[:n_pieces]
    got_refs = refs[n_pieces : n_pieces + n_got]
    (
        x_ref, q_ref, kv_ref, vec_ref, w1_ref, wo_ref, x1_ref, mod_ref, kv1_ref, send_ref, all_ref,
    ) = refs[n_pieces + n_got :]
    count = x_ref.shape[0]
    first_core = lax.axis_index("pipe") == 0
    join(stale_refs, send_ref)
    all_ref[:count] = kv_ref[...]

    @pl.when(first_core)
    def _():
        join(stale_refs, all_ref.at[count:])

    @pl.when(jnp.logical_not(first_core))
    def _():
        join(got_refs, all_ref.at[count:])


    def body(start, size):
        rows = pl.ds(start, size)
        attended = attend(q_ref[rows], all_ref).astype(BF16)
        branch = dot(attended, wo_ref[...])
        x1 = (x_ref[rows].astype(F32) + vec_ref[2:3] * branch).astype(BF16)
        modulated = normed(x1.astype(F32), vec_ref[4:5], vec_ref[3:4])
        fresh = dot_t(modulated, w1_ref[DA:]).astype(BF16)
        kv1_ref[rows] = fresh

        @pl.when(first_core)
        def _():
            send_ref[rows] = fresh

        x1_ref[rows] = x1
        mod_ref[rows] = modulated

    each_block(count, body)


def first_block(stale_pieces, got_pieces, x, q, kv, vecs, w_next, wo_block):
    count = x.shape[0]
    return pl.pallas_call(
        functools.partial(block_kernel, len(stale_pieces), len(got_pieces)),
        out_shape=(
            jax.ShapeDtypeStruct((count, D), BF16),
            jax.ShapeDtypeStruct((count, D), BF16),
            jax.ShapeDtypeStruct((count, 2 * DA), BF16),
            jax.ShapeDtypeStruct((count, 2 * DA), BF16),
        ),
        in_specs=[VMEM] * (len(stale_pieces) + len(got_pieces) + 6),
        out_specs=(VMEM,) * 4,
        scratch_shapes=[pltpu.VMEM((2 * count, 2 * DA), BF16)],
        compiler_params=params(count),
        name="attention_and_next_keys",
    )(*stale_pieces, *got_pieces, x, q, kv, vecs, w_next, wo_block)


def tile_kernel(x_ref, q_ref, sum_ref, state_ref, got_ref, idx_ref, vec_ref, wf_ref, wo_ref, patch_ref):
    attended = attend_end(q_ref[...], got_ref, sum_ref[...], state_ref[...]).astype(BF16)
    branch = dot(attended, wo_ref[...])
    x2 = (x_ref[...].astype(F32) + vec_ref[5:6] * branch).astype(BF16)
    final = normed(x2.astype(F32), vec_ref[7:8], vec_ref[6:7])
    patches = dot_t(final, wf_ref[...]).astype(BF16).astype(F32)
    patch_ref[...] = jnp.zeros_like(patch_ref)
    patch_ref[:, : 4 * LATC] = jnp.where(idx_ref[:, :1] >= 0, patches, 0.0)


def tile_block(x, q, sums, state, got, idx, vecs, w_final, wo_block):
    return pl.pallas_call(
        tile_kernel,
        out_shape=jax.ShapeDtypeStruct((x.shape[0], LANES), F32),
        in_specs=[VMEM] * 9,
        out_specs=VMEM,
        compiler_params=params(got.shape[0]),
        name="tile_attention_and_patches",
    )(x, q, sums, state, got, idx, vecs, w_final, wo_block)


def decode_kernel(
    rows, cols, pitch, patch_ref, got_ref, idx_ref, wp_ref, bin_ref, bup_ref, w_ref, out_ref, u_ref, ub_ref
):
    first_core = lax.axis_index("pipe") == 0
    got = got_ref[:pitch]
    above = jnp.where(first_core, 0.0, got)
    below = jnp.where(first_core, got, 0.0)
    rim = [above] + [patch_ref[r * pitch : (r + 1) * pitch] for r in range(rows)] + [below]
    column_in = idx_ref[:pitch, :1] >= 0
    shifted = [[pltpu.roll(p, (-ds) % pitch, 0) if ds else p for ds in (-1, 0, 1)] for p in rim]
    around = []
    for r in range(rows + 2):
        low, high = None, None
        for dr in (-1, 0, 1):
            if not 0 <= r + dr < rows + 2:
                continue
            for ds in range(3):
                tap = (dr + 1) * 3 + ds
                piece = shifted[r + dr][ds]
                if tap == 8:
                    high = piece
                else:
                    piece = pltpu.roll(piece, 4 * LATC * tap, 1) if tap else piece
                    low = piece if low is None else low + piece
        high = jnp.zeros_like(low) if high is None else high
        around.append(jnp.concatenate([low, high], axis=1))
    for p in range(2):
        first = 1 - p
        stacked = jnp.concatenate(around[first : first + rows + 1], axis=0).astype(BF16)
        for q in range(2):
            at = (2 * p + q) * 2 * LANES
            act = dot(stacked, wp_ref[at : at + 2 * LANES]) + bin_ref[...]
            feature = act / (1.0 + jnp.exp(-act))
            for i in range(rows + 1):
                y = 2 * (first + i - 1) + p + 1
                keep = column_in
                if y == 0:
                    keep = keep & jnp.logical_not(first_core)
                if y == 2 * rows + 1:
                    keep = keep & first_core
                kept = jnp.where(keep, feature[i * pitch : (i + 1) * pitch], 0.0)
                for c in range(CH // LANES):
                    part = kept[:, c * LANES : (c + 1) * LANES]
                    u_ref[y, c, pl.ds(2 * q, pitch, stride=4), :] = part
                    u_ref[y, c, pl.ds(2 * q + 1, pitch, stride=4), :] = part
    wide = 4 * cols
    for y in range(2 * rows + 2):
        for dx in range(3):
            for c in range(CH // LANES):
                ub_ref[dx, y * wide : (y + 1) * wide, c * LANES : (c + 1) * LANES] = u_ref[
                    y, c, 3 + dx : 3 + dx + wide, :
                ].astype(BF16)

    def tap_row(dy, y_first, y_count):
        total = None
        for dx in range(3):
            part = dot(ub_ref[dx, y_first * wide : (y_first + y_count) * wide], w_ref[3 * dy + dx])
            total = part if total is None else total + part
        return total

    def rows_of(total, y):
        return total[y * wide : (y + 1) * wide]

    middle = tap_row(1, 1, 2 * rows) + bup_ref[...]
    before = tap_row(0, 0, 2 * rows + 1)
    after = tap_row(2, 1, 2 * rows + 1)
    for y in range(2 * rows):
        own = rows_of(middle, y)
        out_ref[2 * y] = (own + rows_of(before, y) + rows_of(after, y)).astype(BF16)
        out_ref[2 * y + 1] = (own + rows_of(before, y + 1) + rows_of(after, y + 1)).astype(BF16)


def decode(rows, cols, pitch, patches, got, idx, w_patch, b_in, b_up, w_up):
    return pl.pallas_call(
        functools.partial(decode_kernel, rows, cols, pitch),
        out_shape=jax.ShapeDtypeStruct((4 * rows, 4 * cols, CH), BF16),
        in_specs=[VMEM] * 7,
        out_specs=VMEM,
        scratch_shapes=[
            pltpu.VMEM((2 * rows + 2, CH // LANES, 4 * pitch, LANES), F32),
            pltpu.VMEM((3, (2 * rows + 2) * 4 * cols, CH), BF16),
        ],
        compiler_params=params(0),
        name="decoder_convolutions",
    )(patches, got, idx, w_patch, b_in, b_up, w_up)


def patch_selector():
    sel = np.zeros((2, 2, 3, 3, 2, 2, LATC, 9 * LATC), np.float32)
    for p, q, dr, ds, pp, qq in np.ndindex(2, 2, 3, 3, 2, 2):
        dy = 2 * (dr - 1) + pp - p
        dx = 2 * (ds - 1) + qq - q
        if abs(dy) <= 1 and abs(dx) <= 1:
            tap = (dy + 1) * 3 + dx + 1
            for c in range(LATC):
                sel[p, q, dr, ds, pp, qq, c, tap * LATC + c] = 1.0
    sel = sel.reshape(4, 9 * 4 * LATC, 9 * LATC)
    return np.pad(sel, ((0, 0), (0, 2 * LANES - 9 * 4 * LATC), (0, 0))).reshape(-1, 9 * LATC)


def split_of(n):
    inner = 2 ** (int(math.log2(n)) // 2)
    return n // inner, inner


def swapped(block, k_outer, k_inner):
    n = lax.axis_size("patch")
    _, inner = split_of(n)
    return lax.ppermute(block, "patch", [(i ^ (k_outer * inner + k_inner), i) for i in range(n)])


def local(
    tokens,
    stale_kv,
    w_qkv,
    w_out,
    block_table,
    time_table,
    t_index,
    w_final,
    w_in,
    b_in,
    w_up,
    b_up,
):
    section = lax.axis_index("pipe")
    tile = lax.axis_index("patch")
    n_tiles = lax.axis_size("patch")
    swap = [(0, 1), (1, 0)]
    first_core = section == 0
    own_count = tokens.shape[1]
    count = own_count * n_tiles
    rows = count // TC
    cols = TC // n_tiles
    pitch = -(-(cols + 3) // 8) * 8
    outer, inner = split_of(n_tiles)

    own_tokens = lax.dynamic_index_in_dim(tokens, section, 0, keepdims=False)
    w_qkv = jnp.swapaxes(w_qkv, 1, 2)
    w_qkv_other = lax.ppermute(w_qkv, "pipe", swap)
    tables = lax.all_gather(block_table[0], "pipe")
    x_column = [swapped(own_tokens, k, 0) for k in range(1, outer)]
    own_stale = stale_kv[0, 1]
    w_out_other = lax.ppermute(w_out, "pipe", swap)

    time_row = lax.dynamic_index_in_dim(time_table, t_index[0], 0, keepdims=False)
    ones = jnp.asarray([[0.0], [1.0], [0.0]], F32)
    vecs = jnp.concatenate(
        [
            time_row[:3] + tables[0] + ones,
            time_row[:3] + tables[1] + ones,
            time_row[3:5] + ones[:2],
        ],
        axis=0,
    )

    padded_rows = -(-rows * pitch // 16) * 16
    place = jnp.arange(padded_rows)
    column = place % pitch - 1 + tile * cols
    inside = (place % pitch < cols + 2) & (place < rows * pitch) & (column >= 0) & (column < TC)
    token = place // pitch * TC + jnp.clip(column, 0, TC - 1)
    source = token // own_count
    k_outer = (source // inner) ^ (tile // inner)
    k_inner = (source % inner) ^ (tile % inner)
    spot = (k_inner * outer + k_outer) * own_count + token % own_count
    idx = jnp.broadcast_to(jnp.where(inside, spot, -1)[:, None], (padded_rows, LANES)).astype(jnp.int32)

    x_column, w_qkv_other, w_out_other, vecs, idx, own_stale, w_in = lax.optimization_barrier(
        (x_column, w_qkv_other, w_out_other, vecs, idx, own_stale, w_in)
    )
    x_column = jnp.concatenate([own_tokens] + x_column, axis=0)
    x_column, own_stale = lax.optimization_barrier((x_column, own_stale))
    x_pieces = [x_column] + [swapped(x_column, 0, k) for k in range(1, inner)]
    stale_column = [swapped(own_stale, k, 0) for k in range(1, outer)]
    stale_line = [swapped(own_stale, 0, k) for k in range(1, inner)]
    w_patch = dot(jnp.asarray(patch_selector(), BF16), w_in).astype(BF16)
    w_0, w_1, wo_0, wo_1 = weights_in_vmem(w_qkv, w_qkv_other, w_out, w_out_other)
    x_pieces, stale_column, stale_line, w_patch, w_0 = lax.optimization_barrier(
        (x_pieces, stale_column, stale_line, w_patch, w_0)
    )
    stale_column = jnp.concatenate(stale_column, axis=0)
    x_pieces, stale_column = lax.optimization_barrier((x_pieces, stale_column))
    stale_pieces = [own_stale, stale_column] + stale_line + [swapped(stale_column, 0, k) for k in range(1, inner)]
    x, query, fresh, *parts = project(x_pieces, vecs, w_0)
    got_pieces = [lax.ppermute(part, "pipe", swap) for part in parts]
    x, modulated, fresh, send = first_block(stale_pieces, got_pieces, x, query, fresh, vecs, w_1, wo_0)
    got = lax.ppermute(send, "pipe", swap)
    x_tile, q_tile, sums, state = attend_fresh(x, modulated, fresh, idx, w_1)
    patches = tile_block(x_tile, q_tile, sums, state, got, idx, vecs, w_final.T, wo_1)
    edge = patches
    if rows > 1:
        edge = jnp.where(first_core, patches[(rows - 1) * pitch : rows * pitch], patches[:pitch])
    got = lax.ppermute(edge, "pipe", swap)
    return decode(rows, cols, pitch, patches, got, idx, w_patch, b_in[None], b_up[None], w_up)


def solution(mesh):
    placed = (
        P(None, ("grp", "patch"), None),
        P("pipe", None, ("grp", "patch"), None),
        P("pipe", None, None),
        P("pipe", None, None),
        P("pipe", None, None),
        P(),
        P("grp"),
        P(),
        P(),
        P(),
        P(),
        P(),
    )
    return jax.shard_map(
        local,
        mesh=mesh,
        in_specs=placed,
        out_specs=P(("grp", "pipe"), "patch", None),
        check_vma=False,
    )
```

```python
import functools
import math

import jax
import jax.numpy as jnp
import numpy as np
from jax import lax
from jax.experimental import pallas as pl
from jax.experimental.pallas import tpu as pltpu
from jax.sharding import PartitionSpec as P

D = 1152
DH = 72
HEADS = 8
CH = 512
LATC = 4
TC = 256
DA = 576
DP = 640
SHIFT = 64
EPSILON = 1e-06
QUERY_SCALE = math.log2(math.e) / math.sqrt(DH)
BLOCK = 256
SMALL_BLOCK = 64
LANES = 128

F32 = jnp.float32
BF16 = jnp.bfloat16
VMEM = pl.BlockSpec(memory_space=pltpu.VMEM)
ANY = pl.BlockSpec(memory_space=pl.ANY)


def dot(a, b):
    return jnp.dot(a, b, preferred_element_type=F32)


def dot_t(a, b):
    return lax.dot_general(a, b, (((1,), (1,)), ((), ())), preferred_element_type=F32)


def normed(values, scale, shift):
    average = jnp.mean(values, axis=-1, keepdims=True)
    centred = values - average
    variance = jnp.mean(centred * centred, axis=-1, keepdims=True)
    return (centred * lax.rsqrt(variance + EPSILON) * scale + shift).astype(BF16)


def lane_window(start):
    return start // LANES * LANES, -(-(start + DH) // LANES) * LANES


def head_scores(query, kv_ref, head):
    first, last = lane_window(head * DH)
    lane = lax.broadcasted_iota(jnp.int32, (query.shape[0], last - first), 1) + first
    own = (lane >= head * DH) & (lane < (head + 1) * DH)
    return dot_t(jnp.where(own, query[:, first:last], jnp.zeros((), BF16)), kv_ref[:, first:last])


def value_window(head):
    return lane_window(DA + head * DH)


def weigh(exponent, kv_ref, head):
    first, last = value_window(head)
    return dot(exponent.astype(BF16), kv_ref[:, first:last])


def spread(outs):
    pieces = [None] * (DP // LANES)
    for head, out in enumerate(outs):
        first, last = value_window(head)
        start = DA + head * DH
        lane = lax.broadcasted_iota(jnp.int32, out.shape, 1) + first
        out = jnp.where((lane >= start) & (lane < start + DH), out, 0.0)
        for i in range((last - first) // LANES):
            at = (first - (DA - SHIFT)) // LANES + i
            part = out[:, i * LANES : (i + 1) * LANES]
            pieces[at] = part if pieces[at] is None else pieces[at] + part
    return jnp.concatenate(pieces, axis=1)


def attend(query, kv_ref):
    outs = []
    for head in range(HEADS):
        scores = head_scores(query, kv_ref, head)
        exponent = jnp.exp2(scores - jnp.max(scores, axis=1, keepdims=True))
        total = jnp.sum(exponent, axis=1, keepdims=True)
        outs.append(weigh(exponent, kv_ref, head) * (1.0 / total))
    return spread(outs)


def attend_begin(query, kv_ref):
    outs = []
    lane = lax.broadcasted_iota(jnp.int32, (query.shape[0], LANES), 1)
    state = jnp.zeros((query.shape[0], LANES), F32)
    for head in range(HEADS):
        scores = head_scores(query, kv_ref, head)
        top = jnp.max(scores, axis=1, keepdims=True)
        exponent = jnp.exp2(scores - top)
        total = jnp.sum(exponent, axis=1, keepdims=True)
        outs.append(weigh(exponent, kv_ref, head))
        state = jnp.where(lane == head, top, jnp.where(lane == HEADS + head, total, state))
    return spread(outs), state


def attend_end(query, kv_ref, sums, state):
    outs = []
    for head in range(HEADS):
        scores = head_scores(query, kv_ref, head)
        before, total = state[:, head : head + 1], state[:, HEADS + head : HEADS + head + 1]
        top = jnp.maximum(before, jnp.max(scores, axis=1, keepdims=True))
        exponent = jnp.exp2(scores - top)
        keep = jnp.exp2(before - top)
        total = keep * total + jnp.sum(exponent, axis=1, keepdims=True)
        first, last = value_window(head)
        earlier = sums[:, first - (DA - SHIFT) : last - (DA - SHIFT)]
        outs.append((keep * earlier + weigh(exponent, kv_ref, head)) * (1.0 / total))
    return spread(outs)


def each_block(count, body):
    if count <= BLOCK:
        body(0, count)
    else:

        @pl.loop(0, count // SMALL_BLOCK)
        def _(i):
            body(pl.multiple_of(i * SMALL_BLOCK, SMALL_BLOCK), SMALL_BLOCK)


def params(count):
    return pltpu.CompilerParams(vmem_limit_bytes=(24 if count <= BLOCK else 56) * 1024 * 1024)


def weights_kernel(own_ref, other_ref, wo_own, wo_other, w0_ref, w1_ref, wo0_ref, wo1_ref, sems):
    first = lax.axis_index("pipe") == 0
    pad = jnp.zeros((SHIFT, D), BF16)
    wo0_ref[:SHIFT] = pad
    wo1_ref[:SHIFT] = pad
    outs = (wo0_ref.at[SHIFT:], wo1_ref.at[SHIFT:])
    copies = []
    for i, (in_place, arrived, targets) in enumerate(
        ((own_ref.at[0], other_ref.at[0], (w0_ref, w1_ref)), (wo_own.at[0], wo_other.at[0], outs))
    ):
        for block in range(2):
            own = (first if block == 0 else jnp.logical_not(first))
            sem = sems.at[2 * i + block]
            copies.append(pltpu.make_async_copy(in_place, targets[block], sem))

            @pl.when(own)
            def _():
                pltpu.make_async_copy(in_place, targets[block], sem).start()

            @pl.when(jnp.logical_not(own))
            def _():
                pltpu.make_async_copy(arrived, targets[block], sem).start()

    for copy in copies:
        copy.wait()


def weights_in_vmem(w_own, w_other, wo_own, wo_other):
    return pl.pallas_call(
        weights_kernel,
        out_shape=(jax.ShapeDtypeStruct((3 * DA, D), BF16),) * 2 + (jax.ShapeDtypeStruct((DP, D), BF16),) * 2,
        in_specs=[ANY] * 4,
        out_specs=(VMEM,) * 4,
        scratch_shapes=[pltpu.SemaphoreType.DMA((4,))],
        compiler_params=params(0),
        name="weights_by_block",
    )(in_hbm(w_own), w_other, in_hbm(wo_own), wo_other)


def query_of(modulated, w_ref):
    projected = dot_t(modulated, w_ref[:DP]) * QUERY_SCALE
    lane = lax.broadcasted_iota(jnp.int32, projected.shape, 1)
    return jnp.where(lane < DA, projected, 0.0).astype(BF16)


def join(refs, target):
    at = 0
    for ref in refs:
        rows = ref.shape[0]
        target[at : at + rows] = ref[...]
        at += rows


def project_kernel(n_pieces, *refs):
    piece_refs = refs[:n_pieces]
    vec_ref, w_ref, x_ref, q_ref, kv_ref = refs[n_pieces : n_pieces + 5]
    part_refs = refs[n_pieces + 5 :]
    join(piece_refs, x_ref)

    def body(start, size):
        rows = pl.ds(start, size)
        modulated = normed(x_ref[rows].astype(F32), vec_ref[1:2], vec_ref[0:1])
        kv_ref[rows] = dot_t(modulated, w_ref[DA:]).astype(BF16)
        q_ref[rows] = query_of(modulated, w_ref)

    each_block(x_ref.shape[0], body)
    at = 0
    for ref in part_refs:
        rows = ref.shape[0]
        ref[...] = kv_ref[at : at + rows]
        at += rows


def project(pieces, vecs, weights):
    count = sum(piece.shape[0] for piece in pieces)
    parts = (count // 4,) * 4
    return pl.pallas_call(
        functools.partial(project_kernel, len(pieces)),
        out_shape=(
            jax.ShapeDtypeStruct((count, D), BF16),
            jax.ShapeDtypeStruct((count, DP), BF16),
            jax.ShapeDtypeStruct((count, 2 * DA), BF16),
        )
        + tuple(jax.ShapeDtypeStruct((part, 2 * DA), BF16) for part in parts),
        in_specs=[VMEM] * (len(pieces) + 2),
        out_specs=(VMEM,) * 7,
        compiler_params=params(count),
        name="layer_norm_and_projections",
    )(*pieces, vecs, weights)


def in_hbm(array):
    return pltpu.with_memory_space_constraint(array, pltpu.HBM)


def fresh_kernel(x_ref, mod_ref, kv_ref, idx_ref, w_ref, xt_ref, qt_ref, sum_ref, state_ref, pick_ref):
    tile_rows = idx_ref.shape[0]
    pick_ref[...] = jnp.zeros_like(pick_ref)

    def body(start, size):
        rows = pl.ds(start, size)
        lane = lax.broadcasted_iota(jnp.int32, (tile_rows, size), 1) + start
        chosen = (lane == idx_ref[:, :1]).astype(F32).astype(BF16)
        pick_ref[0] += dot(chosen, mod_ref[rows])
        pick_ref[1] += dot(chosen, x_ref[rows])

    each_block(x_ref.shape[0], body)
    query = query_of(pick_ref[0].astype(BF16), w_ref)
    sum_ref[...], state_ref[...] = attend_begin(query, kv_ref)
    qt_ref[...] = query
    xt_ref[...] = pick_ref[1].astype(BF16)


def attend_fresh(x, modulated, kv, idx, w_block):
    rows = idx.shape[0]
    return pl.pallas_call(
        fresh_kernel,
        out_shape=(
            jax.ShapeDtypeStruct((rows, D), BF16),
            jax.ShapeDtypeStruct((rows, DP), BF16),
            jax.ShapeDtypeStruct((rows, DP), F32),
            jax.ShapeDtypeStruct((rows, LANES), F32),
        ),
        in_specs=[VMEM] * 5,
        out_specs=(VMEM,) * 4,
        scratch_shapes=[pltpu.VMEM((2, rows, D), F32)],
        compiler_params=params(kv.shape[0]),
        name="tile_attention_over_own_keys",
    )(x, modulated, kv, idx, w_block)


def block_kernel(n_pieces, n_got, *refs):
    stale_refs = refs[:n_pieces]
    got_refs = refs[n_pieces : n_pieces + n_got]
    (
        x_ref, q_ref, kv_ref, vec_ref, w1_ref, wo_ref, x1_ref, mod_ref, kv1_ref, send_ref, all_ref,
    ) = refs[n_pieces + n_got :]
    count = x_ref.shape[0]
    first_core = lax.axis_index("pipe") == 0
    join(stale_refs, send_ref)
    all_ref[:count] = kv_ref[...]

    @pl.when(first_core)
    def _():
        join(stale_refs, all_ref.at[count:])

    @pl.when(jnp.logical_not(first_core))
    def _():
        join(got_refs, all_ref.at[count:])


    def body(start, size):
        rows = pl.ds(start, size)
        attended = attend(q_ref[rows], all_ref).astype(BF16)
        branch = dot(attended, wo_ref[...])
        x1 = (x_ref[rows].astype(F32) + vec_ref[2:3] * branch).astype(BF16)
        modulated = normed(x1.astype(F32), vec_ref[4:5], vec_ref[3:4])
        fresh = dot_t(modulated, w1_ref[DA:]).astype(BF16)
        kv1_ref[rows] = fresh

        @pl.when(first_core)
        def _():
            send_ref[rows] = fresh

        x1_ref[rows] = x1
        mod_ref[rows] = modulated

    each_block(count, body)


def first_block(stale_pieces, got_pieces, x, q, kv, vecs, w_next, wo_block):
    count = x.shape[0]
    return pl.pallas_call(
        functools.partial(block_kernel, len(stale_pieces), len(got_pieces)),
        out_shape=(
            jax.ShapeDtypeStruct((count, D), BF16),
            jax.ShapeDtypeStruct((count, D), BF16),
            jax.ShapeDtypeStruct((count, 2 * DA), BF16),
            jax.ShapeDtypeStruct((count, 2 * DA), BF16),
        ),
        in_specs=[VMEM] * (len(stale_pieces) + len(got_pieces) + 6),
        out_specs=(VMEM,) * 4,
        scratch_shapes=[pltpu.VMEM((2 * count, 2 * DA), BF16)],
        compiler_params=params(count),
        name="attention_and_next_keys",
    )(*stale_pieces, *got_pieces, x, q, kv, vecs, w_next, wo_block)


def tile_kernel(x_ref, q_ref, sum_ref, state_ref, got_ref, idx_ref, vec_ref, wf_ref, wo_ref, patch_ref):
    attended = attend_end(q_ref[...], got_ref, sum_ref[...], state_ref[...]).astype(BF16)
    branch = dot(attended, wo_ref[...])
    x2 = (x_ref[...].astype(F32) + vec_ref[5:6] * branch).astype(BF16)
    final = normed(x2.astype(F32), vec_ref[7:8], vec_ref[6:7])
    patches = dot_t(final, wf_ref[...]).astype(BF16).astype(F32)
    patch_ref[...] = jnp.zeros_like(patch_ref)
    patch_ref[:, : 4 * LATC] = jnp.where(idx_ref[:, :1] >= 0, patches, 0.0)


def tile_block(x, q, sums, state, got, idx, vecs, w_final, wo_block):
    return pl.pallas_call(
        tile_kernel,
        out_shape=jax.ShapeDtypeStruct((x.shape[0], LANES), F32),
        in_specs=[VMEM] * 9,
        out_specs=VMEM,
        compiler_params=params(got.shape[0]),
        name="tile_attention_and_patches",
    )(x, q, sums, state, got, idx, vecs, w_final, wo_block)


def decode_kernel(
    rows, cols, pitch, patch_ref, got_ref, idx_ref, wp_ref, bin_ref, bup_ref, w_ref, out_ref, u_ref, ub_ref
):
    first_core = lax.axis_index("pipe") == 0
    got = got_ref[:pitch]
    above = jnp.where(first_core, 0.0, got)
    below = jnp.where(first_core, got, 0.0)
    rim = [above] + [patch_ref[r * pitch : (r + 1) * pitch] for r in range(rows)] + [below]
    column_in = idx_ref[:pitch, :1] >= 0
    shifted = [[pltpu.roll(p, (-ds) % pitch, 0) if ds else p for ds in (-1, 0, 1)] for p in rim]
    around = []
    for r in range(rows + 2):
        low, high = None, None
        for dr in (-1, 0, 1):
            if not 0 <= r + dr < rows + 2:
                continue
            for ds in range(3):
                tap = (dr + 1) * 3 + ds
                piece = shifted[r + dr][ds]
                if tap == 8:
                    high = piece
                else:
                    piece = pltpu.roll(piece, 4 * LATC * tap, 1) if tap else piece
                    low = piece if low is None else low + piece
        high = jnp.zeros_like(low) if high is None else high
        around.append(jnp.concatenate([low, high], axis=1))
    for p in range(2):
        first = 1 - p
        stacked = jnp.concatenate(around[first : first + rows + 1], axis=0).astype(BF16)
        for q in range(2):
            at = (2 * p + q) * 2 * LANES
            act = dot(stacked, wp_ref[at : at + 2 * LANES]) + bin_ref[...]
            feature = act / (1.0 + jnp.exp(-act))
            for i in range(rows + 1):
                y = 2 * (first + i - 1) + p + 1
                keep = column_in
                if y == 0:
                    keep = keep & jnp.logical_not(first_core)
                if y == 2 * rows + 1:
                    keep = keep & first_core
                kept = jnp.where(keep, feature[i * pitch : (i + 1) * pitch], 0.0)
                for c in range(CH // LANES):
                    part = kept[:, c * LANES : (c + 1) * LANES]
                    u_ref[y, c, pl.ds(2 * q, pitch, stride=4), :] = part
                    u_ref[y, c, pl.ds(2 * q + 1, pitch, stride=4), :] = part
    wide = 4 * cols
    for y in range(2 * rows + 2):
        for dx in range(3):
            for c in range(CH // LANES):
                ub_ref[dx, y * wide : (y + 1) * wide, c * LANES : (c + 1) * LANES] = u_ref[
                    y, c, 3 + dx : 3 + dx + wide, :
                ].astype(BF16)

    def tap_row(dy, y_first, y_count):
        total = None
        for dx in range(3):
            part = dot(ub_ref[dx, y_first * wide : (y_first + y_count) * wide], w_ref[3 * dy + dx])
            total = part if total is None else total + part
        return total

    def rows_of(total, y):
        return total[y * wide : (y + 1) * wide]

    middle = tap_row(1, 1, 2 * rows) + bup_ref[...]
    before = tap_row(0, 0, 2 * rows + 1)
    after = tap_row(2, 1, 2 * rows + 1)
    for y in range(2 * rows):
        own = rows_of(middle, y)
        out_ref[2 * y] = (own + rows_of(before, y) + rows_of(after, y)).astype(BF16)
        out_ref[2 * y + 1] = (own + rows_of(before, y + 1) + rows_of(after, y + 1)).astype(BF16)


def decode(rows, cols, pitch, patches, got, idx, w_patch, b_in, b_up, w_up):
    return pl.pallas_call(
        functools.partial(decode_kernel, rows, cols, pitch),
        out_shape=jax.ShapeDtypeStruct((4 * rows, 4 * cols, CH), BF16),
        in_specs=[VMEM] * 7,
        out_specs=VMEM,
        scratch_shapes=[
            pltpu.VMEM((2 * rows + 2, CH // LANES, 4 * pitch, LANES), F32),
            pltpu.VMEM((3, (2 * rows + 2) * 4 * cols, CH), BF16),
        ],
        compiler_params=params(0),
        name="decoder_convolutions",
    )(patches, got, idx, w_patch, b_in, b_up, w_up)


def patch_selector():
    sel = np.zeros((2, 2, 3, 3, 2, 2, LATC, 9 * LATC), np.float32)
    for p, q, dr, ds, pp, qq in np.ndindex(2, 2, 3, 3, 2, 2):
        dy = 2 * (dr - 1) + pp - p
        dx = 2 * (ds - 1) + qq - q
        if abs(dy) <= 1 and abs(dx) <= 1:
            tap = (dy + 1) * 3 + dx + 1
            for c in range(LATC):
                sel[p, q, dr, ds, pp, qq, c, tap * LATC + c] = 1.0
    sel = sel.reshape(4, 9 * 4 * LATC, 9 * LATC)
    return np.pad(sel, ((0, 0), (0, 2 * LANES - 9 * 4 * LATC), (0, 0))).reshape(-1, 9 * LATC)


def split_of(n):
    inner = 2 ** (int(math.log2(n)) // 2)
    return n // inner, inner


def swapped(block, k_outer, k_inner):
    n = lax.axis_size("patch")
    _, inner = split_of(n)
    return lax.ppermute(block, "patch", [(i ^ (k_outer * inner + k_inner), i) for i in range(n)])


def local(
    tokens,
    stale_kv,
    w_qkv,
    w_out,
    block_table,
    time_table,
    t_index,
    w_final,
    w_in,
    b_in,
    w_up,
    b_up,
):
    section = lax.axis_index("pipe")
    tile = lax.axis_index("patch")
    n_tiles = lax.axis_size("patch")
    swap = [(0, 1), (1, 0)]
    first_core = section == 0
    own_count = tokens.shape[1]
    count = own_count * n_tiles
    rows = count // TC
    cols = TC // n_tiles
    pitch = -(-(cols + 3) // 8) * 8
    outer, inner = split_of(n_tiles)

    own_tokens = lax.dynamic_index_in_dim(tokens, section, 0, keepdims=False)
    w_qkv = jnp.swapaxes(w_qkv, 1, 2)
    w_qkv_other = lax.ppermute(w_qkv, "pipe", swap)
    tables = lax.all_gather(block_table[0], "pipe")
    x_column = [swapped(own_tokens, k, 0) for k in range(1, outer)]
    own_stale = stale_kv[0, 1]
    w_out_other = lax.ppermute(w_out, "pipe", swap)

    time_row = lax.dynamic_index_in_dim(time_table, t_index[0], 0, keepdims=False)
    ones = jnp.asarray([[0.0], [1.0], [0.0]], F32)
    vecs = jnp.concatenate(
        [
            time_row[:3] + tables[0] + ones,
            time_row[:3] + tables[1] + ones,
            time_row[3:5] + ones[:2],
        ],
        axis=0,
    )

    padded_rows = -(-rows * pitch // 16) * 16
    place = jnp.arange(padded_rows)
    column = place % pitch - 1 + tile * cols
    inside = (place % pitch < cols + 2) & (place < rows * pitch) & (column >= 0) & (column < TC)
    token = place // pitch * TC + jnp.clip(column, 0, TC - 1)
    source = token // own_count
    k_outer = (source // inner) ^ (tile // inner)
    k_inner = (source % inner) ^ (tile % inner)
    spot = (k_inner * outer + k_outer) * own_count + token % own_count
    idx = jnp.broadcast_to(jnp.where(inside, spot, -1)[:, None], (padded_rows, LANES)).astype(jnp.int32)

    x_column, w_qkv_other, w_out_other, vecs, idx, own_stale, w_in = lax.optimization_barrier(
        (x_column, w_qkv_other, w_out_other, vecs, idx, own_stale, w_in)
    )
    x_column = jnp.concatenate([own_tokens] + x_column, axis=0)
    x_column, own_stale = lax.optimization_barrier((x_column, own_stale))
    x_pieces = [x_column] + [swapped(x_column, 0, k) for k in range(1, inner)]
    stale_column = [swapped(own_stale, k, 0) for k in range(1, outer)]
    stale_line = [swapped(own_stale, 0, k) for k in range(1, inner)]
    w_0, w_1, wo_0, wo_1 = weights_in_vmem(w_qkv, w_qkv_other, w_out, w_out_other)
    x_pieces, stale_column, stale_line, w_0 = lax.optimization_barrier((x_pieces, stale_column, stale_line, w_0))
    stale_column = jnp.concatenate(stale_column, axis=0)
    x_pieces, stale_column = lax.optimization_barrier((x_pieces, stale_column))
    stale_pieces = [own_stale, stale_column] + stale_line + [swapped(stale_column, 0, k) for k in range(1, inner)]
    x, query, fresh, *parts = project(x_pieces, vecs, w_0)
    got_pieces = [lax.ppermute(part, "pipe", swap) for part in parts]
    x, modulated, fresh, send = first_block(stale_pieces, got_pieces, x, query, fresh, vecs, w_1, wo_0)
    got = lax.ppermute(send, "pipe", swap)
    x_tile, q_tile, sums, state = attend_fresh(x, modulated, fresh, idx, w_1)
    patches = tile_block(x_tile, q_tile, sums, state, got, idx, vecs, w_final.T, wo_1)
    patches, w_in = lax.optimization_barrier((patches, w_in))
    w_patch = dot(jnp.asarray(patch_selector(), BF16), w_in).astype(BF16)
    edge = patches
    if rows > 1:
        edge = jnp.where(first_core, patches[(rows - 1) * pitch : rows * pitch], patches[:pitch])
    got = lax.ppermute(edge, "pipe", swap)
    return decode(rows, cols, pitch, patches, got, idx, w_patch, b_in[None], b_up[None], w_up)


def solution(mesh):
    placed = (
        P(None, ("grp", "patch"), None),
        P("pipe", None, ("grp", "patch"), None),
        P("pipe", None, None),
        P("pipe", None, None),
        P("pipe", None, None),
        P(),
        P("grp"),
        P(),
        P(),
        P(),
        P(),
        P(),
    )
    return jax.shard_map(
        local,
        mesh=mesh,
        in_specs=placed,
        out_specs=P(("grp", "pipe"), "patch", None),
        check_vma=False,
    )
```

```python
import functools
import math

import jax
import jax.numpy as jnp
import numpy as np
from jax import lax
from jax.experimental import pallas as pl
from jax.experimental.pallas import tpu as pltpu
from jax.sharding import PartitionSpec as P

D = 1152
DH = 72
HEADS = 8
CH = 512
LATC = 4
TC = 256
DA = 576
DP = 640
SHIFT = 64
EPSILON = 1e-06
QUERY_SCALE = math.log2(math.e) / math.sqrt(DH)
BLOCK = 256
SMALL_BLOCK = 64
LANES = 128

F32 = jnp.float32
BF16 = jnp.bfloat16
VMEM = pl.BlockSpec(memory_space=pltpu.VMEM)
ANY = pl.BlockSpec(memory_space=pl.ANY)


def dot(a, b):
    return jnp.dot(a, b, preferred_element_type=F32)


def dot_t(a, b):
    return lax.dot_general(a, b, (((1,), (1,)), ((), ())), preferred_element_type=F32)


def normed(values, scale, shift):
    average = jnp.mean(values, axis=-1, keepdims=True)
    centred = values - average
    variance = jnp.mean(centred * centred, axis=-1, keepdims=True)
    return (centred * lax.rsqrt(variance + EPSILON) * scale + shift).astype(BF16)


def lane_window(start):
    return start // LANES * LANES, -(-(start + DH) // LANES) * LANES


def head_scores(query, kv_ref, head):
    first, last = lane_window(head * DH)
    lane = lax.broadcasted_iota(jnp.int32, (query.shape[0], last - first), 1) + first
    own = (lane >= head * DH) & (lane < (head + 1) * DH)
    return dot_t(jnp.where(own, query[:, first:last], jnp.zeros((), BF16)), kv_ref[:, first:last])


def value_window(head):
    return lane_window(DA + head * DH)


def weigh(exponent, kv_ref, head):
    first, last = value_window(head)
    return dot(exponent.astype(BF16), kv_ref[:, first:last])


def spread(outs):
    pieces = [None] * (DP // LANES)
    for head, out in enumerate(outs):
        first, last = value_window(head)
        start = DA + head * DH
        lane = lax.broadcasted_iota(jnp.int32, out.shape, 1) + first
        out = jnp.where((lane >= start) & (lane < start + DH), out, 0.0)
        for i in range((last - first) // LANES):
            at = (first - (DA - SHIFT)) // LANES + i
            part = out[:, i * LANES : (i + 1) * LANES]
            pieces[at] = part if pieces[at] is None else pieces[at] + part
    return jnp.concatenate(pieces, axis=1)


def attend(query, kv_ref):
    outs = []
    for head in range(HEADS):
        scores = head_scores(query, kv_ref, head)
        exponent = jnp.exp2(scores - jnp.max(scores, axis=1, keepdims=True))
        total = jnp.sum(exponent, axis=1, keepdims=True)
        outs.append(weigh(exponent, kv_ref, head) * (1.0 / total))
    return spread(outs)


def attend_begin(query, kv_ref):
    outs = []
    lane = lax.broadcasted_iota(jnp.int32, (query.shape[0], LANES), 1)
    state = jnp.zeros((query.shape[0], LANES), F32)
    for head in range(HEADS):
        scores = head_scores(query, kv_ref, head)
        top = jnp.max(scores, axis=1, keepdims=True)
        exponent = jnp.exp2(scores - top)
        total = jnp.sum(exponent, axis=1, keepdims=True)
        outs.append(weigh(exponent, kv_ref, head))
        state = jnp.where(lane == head, top, jnp.where(lane == HEADS + head, total, state))
    return spread(outs), state


def attend_end(query, kv_ref, sums, state):
    outs = []
    for head in range(HEADS):
        scores = head_scores(query, kv_ref, head)
        before, total = state[:, head : head + 1], state[:, HEADS + head : HEADS + head + 1]
        top = jnp.maximum(before, jnp.max(scores, axis=1, keepdims=True))
        exponent = jnp.exp2(scores - top)
        keep = jnp.exp2(before - top)
        total = keep * total + jnp.sum(exponent, axis=1, keepdims=True)
        first, last = value_window(head)
        earlier = sums[:, first - (DA - SHIFT) : last - (DA - SHIFT)]
        outs.append((keep * earlier + weigh(exponent, kv_ref, head)) * (1.0 / total))
    return spread(outs)


def each_block(count, body):
    if count <= BLOCK:
        body(0, count)
    else:

        @pl.loop(0, count // SMALL_BLOCK)
        def _(i):
            body(pl.multiple_of(i * SMALL_BLOCK, SMALL_BLOCK), SMALL_BLOCK)


def params(count):
    return pltpu.CompilerParams(vmem_limit_bytes=(24 if count <= BLOCK else 56) * 1024 * 1024)


def weights_kernel(own_ref, other_ref, wo_own, wo_other, w0_ref, w1_ref, wo0_ref, wo1_ref, sems):
    first = lax.axis_index("pipe") == 0
    pad = jnp.zeros((SHIFT, D), BF16)
    wo0_ref[:SHIFT] = pad
    wo1_ref[:SHIFT] = pad
    outs = (wo0_ref.at[SHIFT:], wo1_ref.at[SHIFT:])
    copies = []
    for i, (in_place, arrived, targets) in enumerate(
        ((own_ref.at[0], other_ref.at[0], (w0_ref, w1_ref)), (wo_own.at[0], wo_other.at[0], outs))
    ):
        for block in range(2):
            own = (first if block == 0 else jnp.logical_not(first))
            sem = sems.at[2 * i + block]
            copies.append(pltpu.make_async_copy(in_place, targets[block], sem))

            @pl.when(own)
            def _():
                pltpu.make_async_copy(in_place, targets[block], sem).start()

            @pl.when(jnp.logical_not(own))
            def _():
                pltpu.make_async_copy(arrived, targets[block], sem).start()

    for copy in copies:
        copy.wait()


def weights_in_vmem(w_own, w_other, wo_own, wo_other):
    return pl.pallas_call(
        weights_kernel,
        out_shape=(jax.ShapeDtypeStruct((3 * DA, D), BF16),) * 2 + (jax.ShapeDtypeStruct((DP, D), BF16),) * 2,
        in_specs=[ANY] * 4,
        out_specs=(VMEM,) * 4,
        scratch_shapes=[pltpu.SemaphoreType.DMA((4,))],
        compiler_params=params(0),
        name="weights_by_block",
    )(in_hbm(w_own), w_other, in_hbm(wo_own), wo_other)


def query_of(modulated, w_ref):
    projected = dot_t(modulated, w_ref[:DP]) * QUERY_SCALE
    lane = lax.broadcasted_iota(jnp.int32, projected.shape, 1)
    return jnp.where(lane < DA, projected, 0.0).astype(BF16)


def join(refs, target):
    at = 0
    for ref in refs:
        rows = ref.shape[0]
        target[at : at + rows] = ref[...]
        at += rows


def project_kernel(n_pieces, *refs):
    piece_refs = refs[:n_pieces]
    vec_ref, w_ref, x_ref, q_ref, kv_ref = refs[n_pieces : n_pieces + 5]
    part_refs = refs[n_pieces + 5 :]
    join(piece_refs, x_ref)

    def body(start, size):
        rows = pl.ds(start, size)
        modulated = normed(x_ref[rows].astype(F32), vec_ref[1:2], vec_ref[0:1])
        kv_ref[rows] = dot_t(modulated, w_ref[DA:]).astype(BF16)
        q_ref[rows] = query_of(modulated, w_ref)

    each_block(x_ref.shape[0], body)
    at = 0
    for ref in part_refs:
        rows = ref.shape[0]
        ref[...] = kv_ref[at : at + rows]
        at += rows


def project(pieces, vecs, weights):
    count = sum(piece.shape[0] for piece in pieces)
    parts = (count // 4,) * 4
    return pl.pallas_call(
        functools.partial(project_kernel, len(pieces)),
        out_shape=(
            jax.ShapeDtypeStruct((count, D), BF16),
            jax.ShapeDtypeStruct((count, DP), BF16),
            jax.ShapeDtypeStruct((count, 2 * DA), BF16),
        )
        + tuple(jax.ShapeDtypeStruct((part, 2 * DA), BF16) for part in parts),
        in_specs=[VMEM] * (len(pieces) + 2),
        out_specs=(VMEM,) * 7,
        compiler_params=params(count),
        name="layer_norm_and_projections",
    )(*pieces, vecs, weights)


def in_hbm(array):
    return pltpu.with_memory_space_constraint(array, pltpu.HBM)


def fresh_kernel(x_ref, mod_ref, kv_ref, idx_ref, w_ref, xt_ref, qt_ref, sum_ref, state_ref, pick_ref):
    tile_rows = idx_ref.shape[0]
    pick_ref[...] = jnp.zeros_like(pick_ref)

    def body(start, size):
        rows = pl.ds(start, size)
        lane = lax.broadcasted_iota(jnp.int32, (tile_rows, size), 1) + start
        chosen = (lane == idx_ref[:, :1]).astype(F32).astype(BF16)
        pick_ref[0] += dot(chosen, mod_ref[rows])
        pick_ref[1] += dot(chosen, x_ref[rows])

    each_block(x_ref.shape[0], body)
    query = query_of(pick_ref[0].astype(BF16), w_ref)
    sum_ref[...], state_ref[...] = attend_begin(query, kv_ref)
    qt_ref[...] = query
    xt_ref[...] = pick_ref[1].astype(BF16)


def attend_fresh(x, modulated, kv, idx, w_block):
    rows = idx.shape[0]
    return pl.pallas_call(
        fresh_kernel,
        out_shape=(
            jax.ShapeDtypeStruct((rows, D), BF16),
            jax.ShapeDtypeStruct((rows, DP), BF16),
            jax.ShapeDtypeStruct((rows, DP), F32),
            jax.ShapeDtypeStruct((rows, LANES), F32),
        ),
        in_specs=[VMEM] * 5,
        out_specs=(VMEM,) * 4,
        scratch_shapes=[pltpu.VMEM((2, rows, D), F32)],
        compiler_params=params(kv.shape[0]),
        name="tile_attention_over_own_keys",
    )(x, modulated, kv, idx, w_block)


def block_kernel(n_pieces, n_got, *refs):
    stale_refs = refs[:n_pieces]
    got_refs = refs[n_pieces : n_pieces + n_got]
    (
        x_ref, q_ref, kv_ref, vec_ref, w1_ref, wo_ref, x1_ref, mod_ref, kv1_ref, send_ref, all_ref,
    ) = refs[n_pieces + n_got :]
    count = x_ref.shape[0]
    first_core = lax.axis_index("pipe") == 0
    join(stale_refs, send_ref)
    all_ref[:count] = kv_ref[...]

    @pl.when(first_core)
    def _():
        join(stale_refs, all_ref.at[count:])

    @pl.when(jnp.logical_not(first_core))
    def _():
        join(got_refs, all_ref.at[count:])


    def body(start, size):
        rows = pl.ds(start, size)
        attended = attend(q_ref[rows], all_ref).astype(BF16)
        branch = dot(attended, wo_ref[...])
        x1 = (x_ref[rows].astype(F32) + vec_ref[2:3] * branch).astype(BF16)
        modulated = normed(x1.astype(F32), vec_ref[4:5], vec_ref[3:4])
        fresh = dot_t(modulated, w1_ref[DA:]).astype(BF16)
        kv1_ref[rows] = fresh

        @pl.when(first_core)
        def _():
            send_ref[rows] = fresh

        x1_ref[rows] = x1
        mod_ref[rows] = modulated

    each_block(count, body)


def first_block(stale_pieces, got_pieces, x, q, kv, vecs, w_next, wo_block):
    count = x.shape[0]
    return pl.pallas_call(
        functools.partial(block_kernel, len(stale_pieces), len(got_pieces)),
        out_shape=(
            jax.ShapeDtypeStruct((count, D), BF16),
            jax.ShapeDtypeStruct((count, D), BF16),
            jax.ShapeDtypeStruct((count, 2 * DA), BF16),
            jax.ShapeDtypeStruct((count, 2 * DA), BF16),
        ),
        in_specs=[VMEM] * (len(stale_pieces) + len(got_pieces) + 6),
        out_specs=(VMEM,) * 4,
        scratch_shapes=[pltpu.VMEM((2 * count, 2 * DA), BF16)],
        compiler_params=params(count),
        name="attention_and_next_keys",
    )(*stale_pieces, *got_pieces, x, q, kv, vecs, w_next, wo_block)


def tile_kernel(x_ref, q_ref, sum_ref, state_ref, got_ref, idx_ref, vec_ref, wf_ref, wo_ref, patch_ref):
    attended = attend_end(q_ref[...], got_ref, sum_ref[...], state_ref[...]).astype(BF16)
    branch = dot(attended, wo_ref[...])
    x2 = (x_ref[...].astype(F32) + vec_ref[5:6] * branch).astype(BF16)
    final = normed(x2.astype(F32), vec_ref[7:8], vec_ref[6:7])
    patches = dot_t(final, wf_ref[...]).astype(BF16).astype(F32)
    patch_ref[...] = jnp.zeros_like(patch_ref)
    patch_ref[:, : 4 * LATC] = jnp.where(idx_ref[:, :1] >= 0, patches, 0.0)


def tile_block(x, q, sums, state, got, idx, vecs, w_final, wo_block):
    return pl.pallas_call(
        tile_kernel,
        out_shape=jax.ShapeDtypeStruct((x.shape[0], LANES), F32),
        in_specs=[VMEM] * 9,
        out_specs=VMEM,
        compiler_params=params(got.shape[0]),
        name="tile_attention_and_patches",
    )(x, q, sums, state, got, idx, vecs, w_final, wo_block)


def decode_kernel(
    rows, cols, pitch, patch_ref, got_ref, idx_ref, wp_ref, bin_ref, bup_ref, w_ref, out_ref, f_ref, fb_ref, o_ref
):
    first_core = lax.axis_index("pipe") == 0
    got = got_ref[:pitch]
    above = jnp.where(first_core, 0.0, got)
    below = jnp.where(first_core, got, 0.0)
    rim = [above] + [patch_ref[r * pitch : (r + 1) * pitch] for r in range(rows)] + [below]
    column_in = idx_ref[:pitch, :1] >= 0
    shifted = [[pltpu.roll(p, (-ds) % pitch, 0) if ds else p for ds in (-1, 0, 1)] for p in rim]
    around = []
    for r in range(rows + 2):
        low, high = None, None
        for dr in (-1, 0, 1):
            if not 0 <= r + dr < rows + 2:
                continue
            for ds in range(3):
                tap = (dr + 1) * 3 + ds
                piece = shifted[r + dr][ds]
                if tap == 8:
                    high = piece
                else:
                    piece = pltpu.roll(piece, 4 * LATC * tap, 1) if tap else piece
                    low = piece if low is None else low + piece
        high = jnp.zeros_like(low) if high is None else high
        around.append(jnp.concatenate([low, high], axis=1))
    for p in range(2):
        first = 1 - p
        stacked = jnp.concatenate(around[first : first + rows + 1], axis=0).astype(BF16)
        for q in range(2):
            at = (2 * p + q) * 2 * LANES
            act = dot(stacked, wp_ref[at : at + 2 * LANES]) + bin_ref[...]
            feature = act / (1.0 + jnp.exp(-act))
            for i in range(rows + 1):
                y = 2 * (first + i - 1) + p + 1
                keep = column_in
                if y == 0:
                    keep = keep & jnp.logical_not(first_core)
                if y == 2 * rows + 1:
                    keep = keep & first_core
                kept = jnp.where(keep, feature[i * pitch : (i + 1) * pitch], 0.0)
                for c in range(CH // LANES):
                    part = kept[:, c * LANES : (c + 1) * LANES]
                    f_ref[y, c, pl.ds(RIM - 2 + q, pitch, stride=2), :] = part
    across = 2 * cols
    wide = feature_pitch(cols)
    for y in range(2 * rows + 2):
        for c in range(CH // LANES):
            fb_ref[y * wide : (y + 1) * wide, c * LANES : (c + 1) * LANES] = f_ref[y, c, :wide, :].astype(BF16)

    def product(dy, dx, first, count):
        return dot(fb_ref[first * wide : (first + count) * wide], w_ref[3 * dy + dx])

    sums = []
    for dx in range(3):
        before = product(0, dx, 0, 2 * rows + 1)
        middle = product(1, dx, 1, 2 * rows)
        after = product(2, dx, 1, 2 * rows + 1)

        def rows_of(total, y):
            return total[y * wide : (y + 1) * wide]

        sums.append(
            [
                rows_of(middle, y) + rows_of(before, y + odd) + rows_of(after, y + odd)
                for y in range(2 * rows)
                for odd in range(2)
            ]
        )
    for row in range(4 * rows):
        left, centre, right = (sums[dx][row] for dx in range(3))
        here = slice(RIM, RIM + across)
        even = (centre + right)[here] + left[RIM - 1 : RIM - 1 + across] + bup_ref[...]
        odd = (centre + left)[here] + right[RIM + 1 : RIM + 1 + across] + bup_ref[...]
        for c in range(CH // LANES):
            lanes = slice(c * LANES, (c + 1) * LANES)
            o_ref[row, c, pl.ds(0, across, stride=2), :] = even[:, lanes]
            o_ref[row, c, pl.ds(1, across, stride=2), :] = odd[:, lanes]
            out_ref[row, :, lanes] = o_ref[row, c].astype(BF16)


RIM = 8


def feature_pitch(cols):
    return -(-(2 * cols + 2 * RIM) // 16) * 16


def decode(rows, cols, pitch, patches, got, idx, w_patch, b_in, b_up, w_up):
    return pl.pallas_call(
        functools.partial(decode_kernel, rows, cols, pitch),
        out_shape=jax.ShapeDtypeStruct((4 * rows, 4 * cols, CH), BF16),
        in_specs=[VMEM] * 7,
        out_specs=VMEM,
        scratch_shapes=[
            pltpu.VMEM((2 * rows + 2, CH // LANES, max(2 * pitch + RIM, feature_pitch(cols)), LANES), F32),
            pltpu.VMEM(((2 * rows + 2) * feature_pitch(cols), CH), BF16),
            pltpu.VMEM((4 * rows, CH // LANES, 4 * cols, LANES), F32),
        ],
        compiler_params=params(0),
        name="decoder_convolutions",
    )(patches, got, idx, w_patch, b_in, b_up, w_up)


def patch_selector():
    sel = np.zeros((2, 2, 3, 3, 2, 2, LATC, 9 * LATC), np.float32)
    for p, q, dr, ds, pp, qq in np.ndindex(2, 2, 3, 3, 2, 2):
        dy = 2 * (dr - 1) + pp - p
        dx = 2 * (ds - 1) + qq - q
        if abs(dy) <= 1 and abs(dx) <= 1:
            tap = (dy + 1) * 3 + dx + 1
            for c in range(LATC):
                sel[p, q, dr, ds, pp, qq, c, tap * LATC + c] = 1.0
    sel = sel.reshape(4, 9 * 4 * LATC, 9 * LATC)
    return np.pad(sel, ((0, 0), (0, 2 * LANES - 9 * 4 * LATC), (0, 0))).reshape(-1, 9 * LATC)


def split_of(n):
    inner = 2 ** (int(math.log2(n)) // 2)
    return n // inner, inner


def swapped(block, k_outer, k_inner):
    n = lax.axis_size("patch")
    _, inner = split_of(n)
    return lax.ppermute(block, "patch", [(i ^ (k_outer * inner + k_inner), i) for i in range(n)])


def local(
    tokens,
    stale_kv,
    w_qkv,
    w_out,
    block_table,
    time_table,
    t_index,
    w_final,
    w_in,
    b_in,
    w_up,
    b_up,
):
    section = lax.axis_index("pipe")
    tile = lax.axis_index("patch")
    n_tiles = lax.axis_size("patch")
    swap = [(0, 1), (1, 0)]
    first_core = section == 0
    own_count = tokens.shape[1]
    count = own_count * n_tiles
    rows = count // TC
    cols = TC // n_tiles
    pitch = -(-(cols + 3) // 8) * 8
    outer, inner = split_of(n_tiles)

    own_tokens = lax.dynamic_index_in_dim(tokens, section, 0, keepdims=False)
    w_qkv = jnp.swapaxes(w_qkv, 1, 2)
    w_qkv_other = lax.ppermute(w_qkv, "pipe", swap)
    tables = lax.all_gather(block_table[0], "pipe")
    x_column = [swapped(own_tokens, k, 0) for k in range(1, outer)]
    own_stale = stale_kv[0, 1]
    w_out_other = lax.ppermute(w_out, "pipe", swap)

    time_row = lax.dynamic_index_in_dim(time_table, t_index[0], 0, keepdims=False)
    ones = jnp.asarray([[0.0], [1.0], [0.0]], F32)
    vecs = jnp.concatenate(
        [
            time_row[:3] + tables[0] + ones,
            time_row[:3] + tables[1] + ones,
            time_row[3:5] + ones[:2],
        ],
        axis=0,
    )

    padded_rows = -(-rows * pitch // 16) * 16
    place = jnp.arange(padded_rows)
    column = place % pitch - 1 + tile * cols
    inside = (place % pitch < cols + 2) & (place < rows * pitch) & (column >= 0) & (column < TC)
    token = place // pitch * TC + jnp.clip(column, 0, TC - 1)
    source = token // own_count
    k_outer = (source // inner) ^ (tile // inner)
    k_inner = (source % inner) ^ (tile % inner)
    spot = (k_inner * outer + k_outer) * own_count + token % own_count
    idx = jnp.broadcast_to(jnp.where(inside, spot, -1)[:, None], (padded_rows, LANES)).astype(jnp.int32)

    x_column, w_qkv_other, w_out_other, vecs, idx, own_stale, w_in = lax.optimization_barrier(
        (x_column, w_qkv_other, w_out_other, vecs, idx, own_stale, w_in)
    )
    x_column = jnp.concatenate([own_tokens] + x_column, axis=0)
    x_column, own_stale = lax.optimization_barrier((x_column, own_stale))
    x_pieces = [x_column] + [swapped(x_column, 0, k) for k in range(1, inner)]
    stale_column = [swapped(own_stale, k, 0) for k in range(1, outer)]
    stale_line = [swapped(own_stale, 0, k) for k in range(1, inner)]
    w_0, w_1, wo_0, wo_1 = weights_in_vmem(w_qkv, w_qkv_other, w_out, w_out_other)
    x_pieces, stale_column, stale_line, w_0 = lax.optimization_barrier((x_pieces, stale_column, stale_line, w_0))
    stale_column = jnp.concatenate(stale_column, axis=0)
    x_pieces, stale_column = lax.optimization_barrier((x_pieces, stale_column))
    stale_pieces = [own_stale, stale_column] + stale_line + [swapped(stale_column, 0, k) for k in range(1, inner)]
    x, query, fresh, *parts = project(x_pieces, vecs, w_0)
    got_pieces = [lax.ppermute(part, "pipe", swap) for part in parts]
    x, modulated, fresh, send = first_block(stale_pieces, got_pieces, x, query, fresh, vecs, w_1, wo_0)
    got = lax.ppermute(send, "pipe", swap)
    x_tile, q_tile, sums, state = attend_fresh(x, modulated, fresh, idx, w_1)
    patches = tile_block(x_tile, q_tile, sums, state, got, idx, vecs, w_final.T, wo_1)
    patches, w_in = lax.optimization_barrier((patches, w_in))
    w_patch = dot(jnp.asarray(patch_selector(), BF16), w_in).astype(BF16)
    edge = patches
    if rows > 1:
        edge = jnp.where(first_core, patches[(rows - 1) * pitch : rows * pitch], patches[:pitch])
    got = lax.ppermute(edge, "pipe", swap)
    return decode(rows, cols, pitch, patches, got, idx, w_patch, b_in[None], b_up[None], w_up)


def solution(mesh):
    placed = (
        P(None, ("grp", "patch"), None),
        P("pipe", None, ("grp", "patch"), None),
        P("pipe", None, None),
        P("pipe", None, None),
        P("pipe", None, None),
        P(),
        P("grp"),
        P(),
        P(),
        P(),
        P(),
        P(),
    )
    return jax.shard_map(
        local,
        mesh=mesh,
        in_specs=placed,
        out_specs=P(("grp", "pipe"), "patch", None),
        check_vma=False,
    )
```

```python
import functools
import math

import jax
import jax.numpy as jnp
import numpy as np
from jax import lax
from jax.experimental import pallas as pl
from jax.experimental.pallas import tpu as pltpu
from jax.sharding import PartitionSpec as P

D = 1152
DH = 72
HEADS = 8
CH = 512
LATC = 4
TC = 256
DA = 576
DP = 640
SHIFT = 64
EPSILON = 1e-06
QUERY_SCALE = math.log2(math.e) / math.sqrt(DH)
BLOCK = 256
SMALL_BLOCK = 64
LANES = 128

F32 = jnp.float32
BF16 = jnp.bfloat16
VMEM = pl.BlockSpec(memory_space=pltpu.VMEM)
ANY = pl.BlockSpec(memory_space=pl.ANY)


def dot(a, b):
    return jnp.dot(a, b, preferred_element_type=F32)


def dot_t(a, b):
    return lax.dot_general(a, b, (((1,), (1,)), ((), ())), preferred_element_type=F32)


def normed(values, scale, shift):
    average = jnp.mean(values, axis=-1, keepdims=True)
    centred = values - average
    variance = jnp.mean(centred * centred, axis=-1, keepdims=True)
    return (centred * lax.rsqrt(variance + EPSILON) * scale + shift).astype(BF16)


def lane_window(start):
    return start // LANES * LANES, -(-(start + DH) // LANES) * LANES


def head_scores(query, kv_ref, head):
    first, last = lane_window(head * DH)
    lane = lax.broadcasted_iota(jnp.int32, (query.shape[0], last - first), 1) + first
    own = (lane >= head * DH) & (lane < (head + 1) * DH)
    return dot_t(jnp.where(own, query[:, first:last], jnp.zeros((), BF16)), kv_ref[:, first:last])


def value_window(head):
    return lane_window(DA + head * DH)


def weigh(exponent, kv_ref, head):
    first, last = value_window(head)
    return dot(exponent.astype(BF16), kv_ref[:, first:last])


def spread(outs):
    pieces = [None] * (DP // LANES)
    for head, out in enumerate(outs):
        first, last = value_window(head)
        start = DA + head * DH
        lane = lax.broadcasted_iota(jnp.int32, out.shape, 1) + first
        out = jnp.where((lane >= start) & (lane < start + DH), out, 0.0)
        for i in range((last - first) // LANES):
            at = (first - (DA - SHIFT)) // LANES + i
            part = out[:, i * LANES : (i + 1) * LANES]
            pieces[at] = part if pieces[at] is None else pieces[at] + part
    return jnp.concatenate(pieces, axis=1)


def attend(query, kv_ref):
    outs = []
    for head in range(HEADS):
        scores = head_scores(query, kv_ref, head)
        exponent = jnp.exp2(scores - jnp.max(scores, axis=1, keepdims=True))
        total = jnp.sum(exponent, axis=1, keepdims=True)
        outs.append(weigh(exponent, kv_ref, head) * (1.0 / total))
    return spread(outs)


def attend_begin(query, kv_ref):
    outs = []
    lane = lax.broadcasted_iota(jnp.int32, (query.shape[0], LANES), 1)
    state = jnp.zeros((query.shape[0], LANES), F32)
    for head in range(HEADS):
        scores = head_scores(query, kv_ref, head)
        top = jnp.max(scores, axis=1, keepdims=True)
        exponent = jnp.exp2(scores - top)
        total = jnp.sum(exponent, axis=1, keepdims=True)
        outs.append(weigh(exponent, kv_ref, head))
        state = jnp.where(lane == head, top, jnp.where(lane == HEADS + head, total, state))
    return spread(outs), state


def attend_end(query, kv_ref, sums, state):
    outs = []
    for head in range(HEADS):
        scores = head_scores(query, kv_ref, head)
        before, total = state[:, head : head + 1], state[:, HEADS + head : HEADS + head + 1]
        top = jnp.maximum(before, jnp.max(scores, axis=1, keepdims=True))
        exponent = jnp.exp2(scores - top)
        keep = jnp.exp2(before - top)
        total = keep * total + jnp.sum(exponent, axis=1, keepdims=True)
        first, last = value_window(head)
        earlier = sums[:, first - (DA - SHIFT) : last - (DA - SHIFT)]
        outs.append((keep * earlier + weigh(exponent, kv_ref, head)) * (1.0 / total))
    return spread(outs)


def each_block(count, body):
    if count <= BLOCK:
        body(0, count)
    else:

        @pl.loop(0, count // SMALL_BLOCK)
        def _(i):
            body(pl.multiple_of(i * SMALL_BLOCK, SMALL_BLOCK), SMALL_BLOCK)


def params(count):
    return pltpu.CompilerParams(vmem_limit_bytes=(24 if count <= BLOCK else 56) * 1024 * 1024)


def weights_kernel(own_ref, other_ref, wo_own, wo_other, w0_ref, w1_ref, wo0_ref, wo1_ref, sems):
    first = lax.axis_index("pipe") == 0
    pad = jnp.zeros((SHIFT, D), BF16)
    wo0_ref[:SHIFT] = pad
    wo1_ref[:SHIFT] = pad
    outs = (wo0_ref.at[SHIFT:], wo1_ref.at[SHIFT:])
    copies = []
    for i, (in_place, arrived, targets) in enumerate(
        ((own_ref.at[0], other_ref.at[0], (w0_ref, w1_ref)), (wo_own.at[0], wo_other.at[0], outs))
    ):
        for block in range(2):
            own = (first if block == 0 else jnp.logical_not(first))
            sem = sems.at[2 * i + block]
            copies.append(pltpu.make_async_copy(in_place, targets[block], sem))

            @pl.when(own)
            def _():
                pltpu.make_async_copy(in_place, targets[block], sem).start()

            @pl.when(jnp.logical_not(own))
            def _():
                pltpu.make_async_copy(arrived, targets[block], sem).start()

    for copy in copies:
        copy.wait()


def weights_in_vmem(w_own, w_other, wo_own, wo_other):
    return pl.pallas_call(
        weights_kernel,
        out_shape=(jax.ShapeDtypeStruct((3 * DA, D), BF16),) * 2 + (jax.ShapeDtypeStruct((DP, D), BF16),) * 2,
        in_specs=[ANY] * 4,
        out_specs=(VMEM,) * 4,
        scratch_shapes=[pltpu.SemaphoreType.DMA((4,))],
        compiler_params=params(0),
        name="weights_by_block",
    )(in_hbm(w_own), w_other, in_hbm(wo_own), wo_other)


def query_of(modulated, w_ref):
    projected = dot_t(modulated, w_ref[:DP]) * QUERY_SCALE
    lane = lax.broadcasted_iota(jnp.int32, projected.shape, 1)
    return jnp.where(lane < DA, projected, 0.0).astype(BF16)


def join(refs, target):
    at = 0
    for ref in refs:
        rows = ref.shape[0]
        target[at : at + rows] = ref[...]
        at += rows


def project_kernel(n_pieces, *refs):
    piece_refs = refs[:n_pieces]
    vec_ref, w_ref, x_ref, q_ref, kv_ref = refs[n_pieces : n_pieces + 5]
    part_refs = refs[n_pieces + 5 :]
    join(piece_refs, x_ref)

    def body(start, size):
        rows = pl.ds(start, size)
        modulated = normed(x_ref[rows].astype(F32), vec_ref[1:2], vec_ref[0:1])
        kv_ref[rows] = dot_t(modulated, w_ref[DA:]).astype(BF16)
        q_ref[rows] = query_of(modulated, w_ref)

    each_block(x_ref.shape[0], body)
    at = 0
    for ref in part_refs:
        rows = ref.shape[0]
        ref[...] = kv_ref[at : at + rows]
        at += rows


def project(pieces, vecs, weights):
    count = sum(piece.shape[0] for piece in pieces)
    parts = (count // 4,) * 4
    return pl.pallas_call(
        functools.partial(project_kernel, len(pieces)),
        out_shape=(
            jax.ShapeDtypeStruct((count, D), BF16),
            jax.ShapeDtypeStruct((count, DP), BF16),
            jax.ShapeDtypeStruct((count, 2 * DA), BF16),
        )
        + tuple(jax.ShapeDtypeStruct((part, 2 * DA), BF16) for part in parts),
        in_specs=[VMEM] * (len(pieces) + 2),
        out_specs=(VMEM,) * 7,
        compiler_params=params(count),
        name="layer_norm_and_projections",
    )(*pieces, vecs, weights)


def in_hbm(array):
    return pltpu.with_memory_space_constraint(array, pltpu.HBM)


def fresh_kernel(x_ref, mod_ref, kv_ref, idx_ref, w_ref, xt_ref, qt_ref, sum_ref, state_ref, pick_ref):
    tile_rows = idx_ref.shape[0]
    pick_ref[...] = jnp.zeros_like(pick_ref)

    def body(start, size):
        rows = pl.ds(start, size)
        lane = lax.broadcasted_iota(jnp.int32, (tile_rows, size), 1) + start
        chosen = (lane == idx_ref[:, :1]).astype(F32).astype(BF16)
        pick_ref[0] += dot(chosen, mod_ref[rows])
        pick_ref[1] += dot(chosen, x_ref[rows])

    each_block(x_ref.shape[0], body)
    query = query_of(pick_ref[0].astype(BF16), w_ref)
    sum_ref[...], state_ref[...] = attend_begin(query, kv_ref)
    qt_ref[...] = query
    xt_ref[...] = pick_ref[1].astype(BF16)


def attend_fresh(x, modulated, kv, idx, w_block):
    rows = idx.shape[0]
    return pl.pallas_call(
        fresh_kernel,
        out_shape=(
            jax.ShapeDtypeStruct((rows, D), BF16),
            jax.ShapeDtypeStruct((rows, DP), BF16),
            jax.ShapeDtypeStruct((rows, DP), F32),
            jax.ShapeDtypeStruct((rows, LANES), F32),
        ),
        in_specs=[VMEM] * 5,
        out_specs=(VMEM,) * 4,
        scratch_shapes=[pltpu.VMEM((2, rows, D), F32)],
        compiler_params=params(kv.shape[0]),
        name="tile_attention_over_own_keys",
    )(x, modulated, kv, idx, w_block)


def block_kernel(n_pieces, n_got, *refs):
    stale_refs = refs[:n_pieces]
    got_refs = refs[n_pieces : n_pieces + n_got]
    (
        x_ref, q_ref, kv_ref, vec_ref, w1_ref, wo_ref, x1_ref, mod_ref, kv1_ref, send_ref, all_ref,
    ) = refs[n_pieces + n_got :]
    count = x_ref.shape[0]
    first_core = lax.axis_index("pipe") == 0
    join(stale_refs, send_ref)
    all_ref[:count] = kv_ref[...]

    @pl.when(first_core)
    def _():
        join(stale_refs, all_ref.at[count:])

    @pl.when(jnp.logical_not(first_core))
    def _():
        join(got_refs, all_ref.at[count:])


    def body(start, size):
        rows = pl.ds(start, size)
        attended = attend(q_ref[rows], all_ref).astype(BF16)
        branch = dot(attended, wo_ref[...])
        x1 = (x_ref[rows].astype(F32) + vec_ref[2:3] * branch).astype(BF16)
        modulated = normed(x1.astype(F32), vec_ref[4:5], vec_ref[3:4])
        fresh = dot_t(modulated, w1_ref[DA:]).astype(BF16)
        kv1_ref[rows] = fresh

        @pl.when(first_core)
        def _():
            send_ref[rows] = fresh

        x1_ref[rows] = x1
        mod_ref[rows] = modulated

    each_block(count, body)


def first_block(stale_pieces, got_pieces, x, q, kv, vecs, w_next, wo_block):
    count = x.shape[0]
    return pl.pallas_call(
        functools.partial(block_kernel, len(stale_pieces), len(got_pieces)),
        out_shape=(
            jax.ShapeDtypeStruct((count, D), BF16),
            jax.ShapeDtypeStruct((count, D), BF16),
            jax.ShapeDtypeStruct((count, 2 * DA), BF16),
            jax.ShapeDtypeStruct((count, 2 * DA), BF16),
        ),
        in_specs=[VMEM] * (len(stale_pieces) + len(got_pieces) + 6),
        out_specs=(VMEM,) * 4,
        scratch_shapes=[pltpu.VMEM((2 * count, 2 * DA), BF16)],
        compiler_params=params(count),
        name="attention_and_next_keys",
    )(*stale_pieces, *got_pieces, x, q, kv, vecs, w_next, wo_block)


def tile_kernel(x_ref, q_ref, sum_ref, state_ref, got_ref, idx_ref, vec_ref, wf_ref, wo_ref, patch_ref):
    attended = attend_end(q_ref[...], got_ref, sum_ref[...], state_ref[...]).astype(BF16)
    branch = dot(attended, wo_ref[...])
    x2 = (x_ref[...].astype(F32) + vec_ref[5:6] * branch).astype(BF16)
    final = normed(x2.astype(F32), vec_ref[7:8], vec_ref[6:7])
    patches = dot_t(final, wf_ref[...]).astype(BF16).astype(F32)
    patch_ref[...] = jnp.zeros_like(patch_ref)
    patch_ref[:, : 4 * LATC] = jnp.where(idx_ref[:, :1] >= 0, patches, 0.0)


def tile_block(x, q, sums, state, got, idx, vecs, w_final, wo_block):
    return pl.pallas_call(
        tile_kernel,
        out_shape=jax.ShapeDtypeStruct((x.shape[0], LANES), F32),
        in_specs=[VMEM] * 9,
        out_specs=VMEM,
        compiler_params=params(got.shape[0]),
        name="tile_attention_and_patches",
    )(x, q, sums, state, got, idx, vecs, w_final, wo_block)


def decode_kernel(
    rows, cols, pitch, patch_ref, got_ref, idx_ref, wp_ref, bin_ref, bup_ref, w_ref, out_ref, f_ref, fb_ref, o_ref
):
    first_core = lax.axis_index("pipe") == 0
    got = got_ref[:pitch]
    above = jnp.where(first_core, 0.0, got)
    below = jnp.where(first_core, got, 0.0)
    rim = [above] + [patch_ref[r * pitch : (r + 1) * pitch] for r in range(rows)] + [below]
    column_in = idx_ref[:pitch, :1] >= 0
    shifted = [[pltpu.roll(p, (-ds) % pitch, 0) if ds else p for ds in (-1, 0, 1)] for p in rim]
    around = []
    for r in range(rows + 2):
        low, high = None, None
        for dr in (-1, 0, 1):
            if not 0 <= r + dr < rows + 2:
                continue
            for ds in range(3):
                tap = (dr + 1) * 3 + ds
                piece = shifted[r + dr][ds]
                if tap == 8:
                    high = piece
                else:
                    piece = pltpu.roll(piece, 4 * LATC * tap, 1) if tap else piece
                    low = piece if low is None else low + piece
        high = jnp.zeros_like(low) if high is None else high
        around.append(jnp.concatenate([low, high], axis=1))
    for p in range(2):
        first = 1 - p
        stacked = jnp.concatenate(around[first : first + rows + 1], axis=0).astype(BF16)
        for q in range(2):
            at = (2 * p + q) * 2 * LANES
            act = dot(stacked, wp_ref[at : at + 2 * LANES]) + bin_ref[...]
            feature = act / (1.0 + jnp.exp(-act))
            for i in range(rows + 1):
                y = 2 * (first + i - 1) + p + 1
                keep = column_in
                if y == 0:
                    keep = keep & jnp.logical_not(first_core)
                if y == 2 * rows + 1:
                    keep = keep & first_core
                kept = jnp.where(keep, feature[i * pitch : (i + 1) * pitch], 0.0)
                for c in range(CH // LANES):
                    part = kept[:, c * LANES : (c + 1) * LANES]
                    f_ref[y, c, pl.ds(RIM - 2 + q, pitch, stride=2), :] = part
    across = 2 * cols
    wide = feature_pitch(cols)
    for y in range(2 * rows + 2):
        for c in range(CH // LANES):
            fb_ref[y * wide : (y + 1) * wide, c * LANES : (c + 1) * LANES] = f_ref[y, c, :wide, :].astype(BF16)

    def product(dy, dx, first, count):
        return dot(fb_ref[first * wide : (first + count) * wide], w_ref[3 * dy + dx])

    sums = []
    for dx in range(3):
        before = product(0, dx, 0, 2 * rows + 1)
        middle = product(1, dx, 1, 2 * rows)
        after = product(2, dx, 1, 2 * rows + 1)

        def rows_of(total, y):
            return total[y * wide : (y + 1) * wide]

        sums.append(
            [
                rows_of(middle, y) + rows_of(before, y + odd) + rows_of(after, y + odd)
                for y in range(2 * rows)
                for odd in range(2)
            ]
        )
    for row in range(4 * rows):
        left, centre, right = (sums[dx][row] for dx in range(3))
        here = slice(RIM, RIM + across)
        even = (centre + right)[here] + left[RIM - 1 : RIM - 1 + across] + bup_ref[...]
        odd = (centre + left)[here] + right[RIM + 1 : RIM + 1 + across] + bup_ref[...]
        for c in range(CH // LANES):
            lanes = slice(c * LANES, (c + 1) * LANES)
            o_ref[row, c, pl.ds(0, across, stride=2), :] = even[:, lanes]
            o_ref[row, c, pl.ds(1, across, stride=2), :] = odd[:, lanes]
            out_ref[row, :, lanes] = o_ref[row, c].astype(BF16)


RIM = 8


def feature_pitch(cols):
    return -(-(2 * cols + 2 * RIM) // 16) * 16


def decode(rows, cols, pitch, patches, got, idx, w_patch, b_in, b_up, w_up):
    return pl.pallas_call(
        functools.partial(decode_kernel, rows, cols, pitch),
        out_shape=jax.ShapeDtypeStruct((4 * rows, 4 * cols, CH), BF16),
        in_specs=[VMEM] * 7,
        out_specs=VMEM,
        scratch_shapes=[
            pltpu.VMEM((2 * rows + 2, CH // LANES, max(2 * pitch + RIM, feature_pitch(cols)), LANES), F32),
            pltpu.VMEM(((2 * rows + 2) * feature_pitch(cols), CH), BF16),
            pltpu.VMEM((4 * rows, CH // LANES, 4 * cols, LANES), F32),
        ],
        compiler_params=params(0),
        name="decoder_convolutions",
    )(patches, got, idx, w_patch, b_in, b_up, w_up)


def patch_selector():
    sel = np.zeros((2, 2, 3, 3, 2, 2, LATC, 9 * LATC), np.float32)
    for p, q, dr, ds, pp, qq in np.ndindex(2, 2, 3, 3, 2, 2):
        dy = 2 * (dr - 1) + pp - p
        dx = 2 * (ds - 1) + qq - q
        if abs(dy) <= 1 and abs(dx) <= 1:
            tap = (dy + 1) * 3 + dx + 1
            for c in range(LATC):
                sel[p, q, dr, ds, pp, qq, c, tap * LATC + c] = 1.0
    sel = sel.reshape(4, 9 * 4 * LATC, 9 * LATC)
    return np.pad(sel, ((0, 0), (0, 2 * LANES - 9 * 4 * LATC), (0, 0))).reshape(-1, 9 * LATC)


def split_of(n):
    inner = 2 ** (int(math.log2(n)) // 2)
    return n // inner, inner


def swapped(block, k_outer, k_inner):
    n = lax.axis_size("patch")
    _, inner = split_of(n)
    return lax.ppermute(block, "patch", [(i ^ (k_outer * inner + k_inner), i) for i in range(n)])


def local(
    tokens,
    stale_kv,
    w_qkv,
    w_out,
    block_table,
    time_table,
    t_index,
    w_final,
    w_in,
    b_in,
    w_up,
    b_up,
):
    section = lax.axis_index("pipe")
    tile = lax.axis_index("patch")
    n_tiles = lax.axis_size("patch")
    swap = [(0, 1), (1, 0)]
    first_core = section == 0
    own_count = tokens.shape[1]
    count = own_count * n_tiles
    rows = count // TC
    cols = TC // n_tiles
    pitch = -(-(cols + 3) // 8) * 8
    outer, inner = split_of(n_tiles)

    own_tokens = lax.dynamic_index_in_dim(tokens, section, 0, keepdims=False)
    w_qkv = jnp.swapaxes(w_qkv, 1, 2)
    tables = lax.all_gather(block_table[0], "pipe")
    x_column = [swapped(own_tokens, k, 0) for k in range(1, outer)]
    own_stale = stale_kv[0, 1]
    w_out_other = lax.ppermute(w_out, "pipe", swap)
    stale_line = [swapped(own_stale, 0, k) for k in range(1, inner)]

    time_row = lax.dynamic_index_in_dim(time_table, t_index[0], 0, keepdims=False)
    ones = jnp.asarray([[0.0], [1.0], [0.0]], F32)
    vecs = jnp.concatenate(
        [
            time_row[:3] + tables[0] + ones,
            time_row[:3] + tables[1] + ones,
            time_row[3:5] + ones[:2],
        ],
        axis=0,
    )

    padded_rows = -(-rows * pitch // 16) * 16
    place = jnp.arange(padded_rows)
    column = place % pitch - 1 + tile * cols
    inside = (place % pitch < cols + 2) & (place < rows * pitch) & (column >= 0) & (column < TC)
    token = place // pitch * TC + jnp.clip(column, 0, TC - 1)
    source = token // own_count
    k_outer = (source // inner) ^ (tile // inner)
    k_inner = (source % inner) ^ (tile % inner)
    spot = (k_inner * outer + k_outer) * own_count + token % own_count
    idx = jnp.broadcast_to(jnp.where(inside, spot, -1)[:, None], (padded_rows, LANES)).astype(jnp.int32)

    x_column, stale_line, w_out_other, vecs, idx, own_stale, w_send = lax.optimization_barrier(
        (x_column, stale_line, w_out_other, vecs, idx, own_stale, w_qkv)
    )
    x_column = jnp.concatenate([own_tokens] + x_column, axis=0)
    x_column, own_stale = lax.optimization_barrier((x_column, own_stale))
    w_qkv_other = lax.ppermute(w_send, "pipe", swap)
    x_pieces = [x_column] + [swapped(x_column, 0, k) for k in range(1, inner)]
    stale_column = [swapped(own_stale, k, 0) for k in range(1, outer)]
    w_0, w_1, wo_0, wo_1 = weights_in_vmem(w_qkv, w_qkv_other, w_out, w_out_other)
    x_pieces, stale_column, w_0 = lax.optimization_barrier((x_pieces, stale_column, w_0))
    stale_column = jnp.concatenate(stale_column, axis=0)
    x_pieces, stale_column = lax.optimization_barrier((x_pieces, stale_column))
    stale_pieces = [own_stale, stale_column] + stale_line + [swapped(stale_column, 0, k) for k in range(1, inner)]
    x, query, fresh, *parts = project(x_pieces, vecs, w_0)
    got_pieces = [lax.ppermute(part, "pipe", swap) for part in parts]
    x, modulated, fresh, send = first_block(stale_pieces, got_pieces, x, query, fresh, vecs, w_1, wo_0)
    got = lax.ppermute(send, "pipe", swap)
    x_tile, q_tile, sums, state = attend_fresh(x, modulated, fresh, idx, w_1)
    patches = tile_block(x_tile, q_tile, sums, state, got, idx, vecs, w_final.T, wo_1)
    patches, w_in = lax.optimization_barrier((patches, w_in))
    w_patch = dot(jnp.asarray(patch_selector(), BF16), w_in).astype(BF16)
    edge = patches
    if rows > 1:
        edge = jnp.where(first_core, patches[(rows - 1) * pitch : rows * pitch], patches[:pitch])
    got = lax.ppermute(edge, "pipe", swap)
    return decode(rows, cols, pitch, patches, got, idx, w_patch, b_in[None], b_up[None], w_up)


def solution(mesh):
    placed = (
        P(None, ("grp", "patch"), None),
        P("pipe", None, ("grp", "patch"), None),
        P("pipe", None, None),
        P("pipe", None, None),
        P("pipe", None, None),
        P(),
        P("grp"),
        P(),
        P(),
        P(),
        P(),
        P(),
    )
    return jax.shard_map(
        local,
        mesh=mesh,
        in_specs=placed,
        out_specs=P(("grp", "pipe"), "patch", None),
        check_vma=False,
    )
```

```python
import functools
import math

import jax
import jax.numpy as jnp
import numpy as np
from jax import lax
from jax.experimental import pallas as pl
from jax.experimental.pallas import tpu as pltpu
from jax.sharding import PartitionSpec as P

D = 1152
DH = 72
HEADS = 8
CH = 512
LATC = 4
TC = 256
DA = 576
DP = 640
SHIFT = 64
EPSILON = 1e-06
QUERY_SCALE = math.log2(math.e) / math.sqrt(DH)
BLOCK = 256
SMALL_BLOCK = 64
LANES = 128

F32 = jnp.float32
BF16 = jnp.bfloat16
VMEM = pl.BlockSpec(memory_space=pltpu.VMEM)
ANY = pl.BlockSpec(memory_space=pl.ANY)


def dot(a, b):
    return jnp.dot(a, b, preferred_element_type=F32)


def dot_t(a, b):
    return lax.dot_general(a, b, (((1,), (1,)), ((), ())), preferred_element_type=F32)


def normed(values, scale, shift):
    average = jnp.mean(values, axis=-1, keepdims=True)
    centred = values - average
    variance = jnp.mean(centred * centred, axis=-1, keepdims=True)
    return (centred * lax.rsqrt(variance + EPSILON) * scale + shift).astype(BF16)


def lane_window(start):
    return start // LANES * LANES, -(-(start + DH) // LANES) * LANES


def head_scores(query, kv_ref, head):
    first, last = lane_window(head * DH)
    lane = lax.broadcasted_iota(jnp.int32, (query.shape[0], last - first), 1) + first
    own = (lane >= head * DH) & (lane < (head + 1) * DH)
    return dot_t(jnp.where(own, query[:, first:last], jnp.zeros((), BF16)), kv_ref[:, first:last])


def value_window(head):
    return lane_window(DA + head * DH)


def weigh(exponent, kv_ref, head):
    first, last = value_window(head)
    return dot(exponent.astype(BF16), kv_ref[:, first:last])


def spread(outs):
    pieces = [None] * (DP // LANES)
    for head, out in enumerate(outs):
        first, last = value_window(head)
        start = DA + head * DH
        lane = lax.broadcasted_iota(jnp.int32, out.shape, 1) + first
        out = jnp.where((lane >= start) & (lane < start + DH), out, 0.0)
        for i in range((last - first) // LANES):
            at = (first - (DA - SHIFT)) // LANES + i
            part = out[:, i * LANES : (i + 1) * LANES]
            pieces[at] = part if pieces[at] is None else pieces[at] + part
    return jnp.concatenate(pieces, axis=1)


def attend(query, kv_ref):
    outs = []
    for head in range(HEADS):
        scores = head_scores(query, kv_ref, head)
        exponent = jnp.exp2(scores - jnp.max(scores, axis=1, keepdims=True))
        total = jnp.sum(exponent, axis=1, keepdims=True)
        outs.append(weigh(exponent, kv_ref, head) * (1.0 / total))
    return spread(outs)


def attend_begin(query, kv_ref):
    outs = []
    lane = lax.broadcasted_iota(jnp.int32, (query.shape[0], LANES), 1)
    state = jnp.zeros((query.shape[0], LANES), F32)
    for head in range(HEADS):
        scores = head_scores(query, kv_ref, head)
        top = jnp.max(scores, axis=1, keepdims=True)
        exponent = jnp.exp2(scores - top)
        total = jnp.sum(exponent, axis=1, keepdims=True)
        outs.append(weigh(exponent, kv_ref, head))
        state = jnp.where(lane == head, top, jnp.where(lane == HEADS + head, total, state))
    return spread(outs), state


def attend_end(query, kv_ref, sums, state):
    outs = []
    for head in range(HEADS):
        scores = head_scores(query, kv_ref, head)
        before, total = state[:, head : head + 1], state[:, HEADS + head : HEADS + head + 1]
        top = jnp.maximum(before, jnp.max(scores, axis=1, keepdims=True))
        exponent = jnp.exp2(scores - top)
        keep = jnp.exp2(before - top)
        total = keep * total + jnp.sum(exponent, axis=1, keepdims=True)
        first, last = value_window(head)
        earlier = sums[:, first - (DA - SHIFT) : last - (DA - SHIFT)]
        outs.append((keep * earlier + weigh(exponent, kv_ref, head)) * (1.0 / total))
    return spread(outs)


def each_block(count, body):
    if count <= BLOCK:
        body(0, count)
    else:

        @pl.loop(0, count // SMALL_BLOCK)
        def _(i):
            body(pl.multiple_of(i * SMALL_BLOCK, SMALL_BLOCK), SMALL_BLOCK)


def params(count):
    return pltpu.CompilerParams(vmem_limit_bytes=(24 if count <= BLOCK else 56) * 1024 * 1024)


def weights_kernel(own_ref, other_ref, wo_own, wo_other, w0_ref, w1_ref, wo0_ref, wo1_ref, sems):
    first = lax.axis_index("pipe") == 0
    pad = jnp.zeros((SHIFT, D), BF16)
    wo0_ref[:SHIFT] = pad
    wo1_ref[:SHIFT] = pad
    outs = (wo0_ref.at[SHIFT:], wo1_ref.at[SHIFT:])
    copies = []
    for i, (in_place, arrived, targets) in enumerate(
        ((own_ref.at[0], other_ref.at[0], (w0_ref, w1_ref)), (wo_own.at[0], wo_other.at[0], outs))
    ):
        for block in range(2):
            own = (first if block == 0 else jnp.logical_not(first))
            sem = sems.at[2 * i + block]
            copies.append(pltpu.make_async_copy(in_place, targets[block], sem))

            @pl.when(own)
            def _():
                pltpu.make_async_copy(in_place, targets[block], sem).start()

            @pl.when(jnp.logical_not(own))
            def _():
                pltpu.make_async_copy(arrived, targets[block], sem).start()

    for copy in copies:
        copy.wait()


def weights_in_vmem(w_own, w_other, wo_own, wo_other):
    return pl.pallas_call(
        weights_kernel,
        out_shape=(jax.ShapeDtypeStruct((3 * DA, D), BF16),) * 2 + (jax.ShapeDtypeStruct((DP, D), BF16),) * 2,
        in_specs=[ANY] * 4,
        out_specs=(VMEM,) * 4,
        scratch_shapes=[pltpu.SemaphoreType.DMA((4,))],
        compiler_params=params(0),
        name="weights_by_block",
    )(in_hbm(w_own), w_other, in_hbm(wo_own), wo_other)


def query_of(modulated, w_ref):
    projected = dot_t(modulated, w_ref[:DP]) * QUERY_SCALE
    lane = lax.broadcasted_iota(jnp.int32, projected.shape, 1)
    return jnp.where(lane < DA, projected, 0.0).astype(BF16)


def join(refs, target):
    at = 0
    for ref in refs:
        rows = ref.shape[0]
        target[at : at + rows] = ref[...]
        at += rows


def project_kernel(n_pieces, *refs):
    piece_refs = refs[:n_pieces]
    vec_ref, w_ref, x_ref, q_ref, kv_ref = refs[n_pieces : n_pieces + 5]
    part_refs = refs[n_pieces + 5 :]
    join(piece_refs, x_ref)

    def body(start, size):
        rows = pl.ds(start, size)
        modulated = normed(x_ref[rows].astype(F32), vec_ref[1:2], vec_ref[0:1])
        kv_ref[rows] = dot_t(modulated, w_ref[DA:]).astype(BF16)
        q_ref[rows] = query_of(modulated, w_ref)

    each_block(x_ref.shape[0], body)
    at = 0
    for ref in part_refs:
        rows = ref.shape[0]
        ref[...] = kv_ref[at : at + rows]
        at += rows


def project(pieces, vecs, weights):
    count = sum(piece.shape[0] for piece in pieces)
    parts = (count // 4,) * 4
    return pl.pallas_call(
        functools.partial(project_kernel, len(pieces)),
        out_shape=(
            jax.ShapeDtypeStruct((count, D), BF16),
            jax.ShapeDtypeStruct((count, DP), BF16),
            jax.ShapeDtypeStruct((count, 2 * DA), BF16),
        )
        + tuple(jax.ShapeDtypeStruct((part, 2 * DA), BF16) for part in parts),
        in_specs=[VMEM] * (len(pieces) + 2),
        out_specs=(VMEM,) * 7,
        compiler_params=params(count),
        name="layer_norm_and_projections",
    )(*pieces, vecs, weights)


def in_hbm(array):
    return pltpu.with_memory_space_constraint(array, pltpu.HBM)


def fresh_kernel(x_ref, mod_ref, kv_ref, idx_ref, w_ref, xt_ref, qt_ref, sum_ref, state_ref, pick_ref):
    tile_rows = idx_ref.shape[0]
    pick_ref[...] = jnp.zeros_like(pick_ref)

    def body(start, size):
        rows = pl.ds(start, size)
        lane = lax.broadcasted_iota(jnp.int32, (tile_rows, size), 1) + start
        chosen = (lane == idx_ref[:, :1]).astype(F32).astype(BF16)
        pick_ref[0] += dot(chosen, mod_ref[rows])
        pick_ref[1] += dot(chosen, x_ref[rows])

    each_block(x_ref.shape[0], body)
    query = query_of(pick_ref[0].astype(BF16), w_ref)
    sum_ref[...], state_ref[...] = attend_begin(query, kv_ref)
    qt_ref[...] = query
    xt_ref[...] = pick_ref[1].astype(BF16)


def attend_fresh(x, modulated, kv, idx, w_block):
    rows = idx.shape[0]
    return pl.pallas_call(
        fresh_kernel,
        out_shape=(
            jax.ShapeDtypeStruct((rows, D), BF16),
            jax.ShapeDtypeStruct((rows, DP), BF16),
            jax.ShapeDtypeStruct((rows, DP), F32),
            jax.ShapeDtypeStruct((rows, LANES), F32),
        ),
        in_specs=[VMEM] * 5,
        out_specs=(VMEM,) * 4,
        scratch_shapes=[pltpu.VMEM((2, rows, D), F32)],
        compiler_params=params(kv.shape[0]),
        name="tile_attention_over_own_keys",
    )(x, modulated, kv, idx, w_block)


def block_kernel(n_pieces, n_got, *refs):
    stale_refs = refs[:n_pieces]
    got_refs = refs[n_pieces : n_pieces + n_got]
    (
        x_ref, q_ref, kv_ref, vec_ref, w1_ref, wo_ref, x1_ref, mod_ref, kv1_ref, send_ref, all_ref,
    ) = refs[n_pieces + n_got :]
    count = x_ref.shape[0]
    first_core = lax.axis_index("pipe") == 0
    join(stale_refs, send_ref)
    all_ref[:count] = kv_ref[...]

    @pl.when(first_core)
    def _():
        join(stale_refs, all_ref.at[count:])

    @pl.when(jnp.logical_not(first_core))
    def _():
        join(got_refs, all_ref.at[count:])


    def body(start, size):
        rows = pl.ds(start, size)
        attended = attend(q_ref[rows], all_ref).astype(BF16)
        branch = dot(attended, wo_ref[...])
        x1 = (x_ref[rows].astype(F32) + vec_ref[2:3] * branch).astype(BF16)
        modulated = normed(x1.astype(F32), vec_ref[4:5], vec_ref[3:4])
        fresh = dot_t(modulated, w1_ref[DA:]).astype(BF16)
        kv1_ref[rows] = fresh

        @pl.when(first_core)
        def _():
            send_ref[rows] = fresh

        x1_ref[rows] = x1
        mod_ref[rows] = modulated

    each_block(count, body)


def first_block(stale_pieces, got_pieces, x, q, kv, vecs, w_next, wo_block):
    count = x.shape[0]
    return pl.pallas_call(
        functools.partial(block_kernel, len(stale_pieces), len(got_pieces)),
        out_shape=(
            jax.ShapeDtypeStruct((count, D), BF16),
            jax.ShapeDtypeStruct((count, D), BF16),
            jax.ShapeDtypeStruct((count, 2 * DA), BF16),
            jax.ShapeDtypeStruct((count, 2 * DA), BF16),
        ),
        in_specs=[VMEM] * (len(stale_pieces) + len(got_pieces) + 6),
        out_specs=(VMEM,) * 4,
        scratch_shapes=[pltpu.VMEM((2 * count, 2 * DA), BF16)],
        compiler_params=params(count),
        name="attention_and_next_keys",
    )(*stale_pieces, *got_pieces, x, q, kv, vecs, w_next, wo_block)


def tile_kernel(x_ref, q_ref, sum_ref, state_ref, got_ref, idx_ref, vec_ref, wf_ref, wo_ref, patch_ref):
    attended = attend_end(q_ref[...], got_ref, sum_ref[...], state_ref[...]).astype(BF16)
    branch = dot(attended, wo_ref[...])
    x2 = (x_ref[...].astype(F32) + vec_ref[5:6] * branch).astype(BF16)
    final = normed(x2.astype(F32), vec_ref[7:8], vec_ref[6:7])
    patches = dot_t(final, wf_ref[...]).astype(BF16).astype(F32)
    patch_ref[...] = jnp.zeros_like(patch_ref)
    patch_ref[:, : 4 * LATC] = jnp.where(idx_ref[:, :1] >= 0, patches, 0.0)


def tile_block(x, q, sums, state, got, idx, vecs, w_final, wo_block):
    return pl.pallas_call(
        tile_kernel,
        out_shape=jax.ShapeDtypeStruct((x.shape[0], LANES), F32),
        in_specs=[VMEM] * 9,
        out_specs=VMEM,
        compiler_params=params(got.shape[0]),
        name="tile_attention_and_patches",
    )(x, q, sums, state, got, idx, vecs, w_final, wo_block)


def decode_kernel(
    rows, cols, pitch, patch_ref, got_ref, idx_ref, wp_ref, bin_ref, bup_ref, w_ref, out_ref, f_ref, fb_ref, o_ref
):
    first_core = lax.axis_index("pipe") == 0
    got = got_ref[:pitch]
    above = jnp.where(first_core, 0.0, got)
    below = jnp.where(first_core, got, 0.0)
    rim = [above] + [patch_ref[r * pitch : (r + 1) * pitch] for r in range(rows)] + [below]
    column_in = idx_ref[:pitch, :1] >= 0
    shifted = [[pltpu.roll(p, (-ds) % pitch, 0) if ds else p for ds in (-1, 0, 1)] for p in rim]
    around = []
    for r in range(rows + 2):
        low, high = None, None
        for dr in (-1, 0, 1):
            if not 0 <= r + dr < rows + 2:
                continue
            for ds in range(3):
                tap = (dr + 1) * 3 + ds
                piece = shifted[r + dr][ds]
                if tap == 8:
                    high = piece
                else:
                    piece = pltpu.roll(piece, 4 * LATC * tap, 1) if tap else piece
                    low = piece if low is None else low + piece
        high = jnp.zeros_like(low) if high is None else high
        around.append(jnp.concatenate([low, high], axis=1))
    for p in range(2):
        first = 1 - p
        stacked = jnp.concatenate(around[first : first + rows + 1], axis=0).astype(BF16)
        for q in range(2):
            at = (2 * p + q) * 2 * LANES
            act = dot(stacked, wp_ref[at : at + 2 * LANES]) + bin_ref[...]
            feature = act / (1.0 + jnp.exp(-act))
            for i in range(rows + 1):
                y = 2 * (first + i - 1) + p + 1
                keep = column_in
                if y == 0:
                    keep = keep & jnp.logical_not(first_core)
                if y == 2 * rows + 1:
                    keep = keep & first_core
                kept = jnp.where(keep, feature[i * pitch : (i + 1) * pitch], 0.0)
                for c in range(CH // LANES):
                    part = kept[:, c * LANES : (c + 1) * LANES]
                    f_ref[y, c, pl.ds(RIM - 2 + q, pitch, stride=2), :] = part
    across = 2 * cols
    wide = feature_pitch(cols)
    for y in range(2 * rows + 2):
        for c in range(CH // LANES):
            fb_ref[y * wide : (y + 1) * wide, c * LANES : (c + 1) * LANES] = f_ref[y, c, :wide, :].astype(BF16)

    def product(dy, dx, first, count):
        return dot(fb_ref[first * wide : (first + count) * wide], w_ref[3 * dy + dx])

    sums = []
    for dx in range(3):
        before = product(0, dx, 0, 2 * rows + 1)
        middle = product(1, dx, 1, 2 * rows)
        after = product(2, dx, 1, 2 * rows + 1)

        def rows_of(total, y):
            return total[y * wide : (y + 1) * wide]

        sums.append(
            [
                rows_of(middle, y) + rows_of(before, y + odd) + rows_of(after, y + odd)
                for y in range(2 * rows)
                for odd in range(2)
            ]
        )
    for row in range(4 * rows):
        left, centre, right = (sums[dx][row] for dx in range(3))
        here = slice(RIM, RIM + across)
        even = (centre + right)[here] + left[RIM - 1 : RIM - 1 + across] + bup_ref[...]
        odd = (centre + left)[here] + right[RIM + 1 : RIM + 1 + across] + bup_ref[...]
        for c in range(CH // LANES):
            lanes = slice(c * LANES, (c + 1) * LANES)
            o_ref[row, c, pl.ds(0, across, stride=2), :] = even[:, lanes]
            o_ref[row, c, pl.ds(1, across, stride=2), :] = odd[:, lanes]
            out_ref[row, :, lanes] = o_ref[row, c].astype(BF16)


RIM = 8


def feature_pitch(cols):
    return -(-(2 * cols + 2 * RIM) // 16) * 16


def decode(rows, cols, pitch, patches, got, idx, w_patch, b_in, b_up, w_up):
    return pl.pallas_call(
        functools.partial(decode_kernel, rows, cols, pitch),
        out_shape=jax.ShapeDtypeStruct((4 * rows, 4 * cols, CH), BF16),
        in_specs=[VMEM] * 7,
        out_specs=VMEM,
        scratch_shapes=[
            pltpu.VMEM((2 * rows + 2, CH // LANES, max(2 * pitch + RIM, feature_pitch(cols)), LANES), F32),
            pltpu.VMEM(((2 * rows + 2) * feature_pitch(cols), CH), BF16),
            pltpu.VMEM((4 * rows, CH // LANES, 4 * cols, LANES), F32),
        ],
        compiler_params=params(0),
        name="decoder_convolutions",
    )(patches, got, idx, w_patch, b_in, b_up, w_up)


def patch_selector():
    sel = np.zeros((2, 2, 3, 3, 2, 2, LATC, 9 * LATC), np.float32)
    for p, q, dr, ds, pp, qq in np.ndindex(2, 2, 3, 3, 2, 2):
        dy = 2 * (dr - 1) + pp - p
        dx = 2 * (ds - 1) + qq - q
        if abs(dy) <= 1 and abs(dx) <= 1:
            tap = (dy + 1) * 3 + dx + 1
            for c in range(LATC):
                sel[p, q, dr, ds, pp, qq, c, tap * LATC + c] = 1.0
    sel = sel.reshape(4, 9 * 4 * LATC, 9 * LATC)
    return np.pad(sel, ((0, 0), (0, 2 * LANES - 9 * 4 * LATC), (0, 0))).reshape(-1, 9 * LATC)


def split_of(n):
    inner = 2 ** (int(math.log2(n)) // 2)
    return n // inner, inner


def swapped(block, k_outer, k_inner):
    n = lax.axis_size("patch")
    _, inner = split_of(n)
    return lax.ppermute(block, "patch", [(i ^ (k_outer * inner + k_inner), i) for i in range(n)])


def across_outer(block, outer):
    return [swapped(block, k, 0) for k in range(outer - 1, 0, -1)]


def local(
    tokens,
    stale_kv,
    w_qkv,
    w_out,
    block_table,
    time_table,
    t_index,
    w_final,
    w_in,
    b_in,
    w_up,
    b_up,
):
    section = lax.axis_index("pipe")
    tile = lax.axis_index("patch")
    n_tiles = lax.axis_size("patch")
    swap = [(0, 1), (1, 0)]
    first_core = section == 0
    own_count = tokens.shape[1]
    count = own_count * n_tiles
    rows = count // TC
    cols = TC // n_tiles
    pitch = -(-(cols + 3) // 8) * 8
    outer, inner = split_of(n_tiles)

    own_tokens = lax.dynamic_index_in_dim(tokens, section, 0, keepdims=False)
    w_qkv = jnp.swapaxes(w_qkv, 1, 2)
    w_qkv_other = lax.ppermute(w_qkv, "pipe", swap)
    tables = lax.all_gather(block_table[0], "pipe")
    x_column = across_outer(own_tokens, outer)
    own_stale = stale_kv[0, 1]
    w_out_other = lax.ppermute(w_out, "pipe", swap)

    time_row = lax.dynamic_index_in_dim(time_table, t_index[0], 0, keepdims=False)
    ones = jnp.asarray([[0.0], [1.0], [0.0]], F32)
    vecs = jnp.concatenate(
        [
            time_row[:3] + tables[0] + ones,
            time_row[:3] + tables[1] + ones,
            time_row[3:5] + ones[:2],
        ],
        axis=0,
    )

    padded_rows = -(-rows * pitch // 16) * 16
    place = jnp.arange(padded_rows)
    column = place % pitch - 1 + tile * cols
    inside = (place % pitch < cols + 2) & (place < rows * pitch) & (column >= 0) & (column < TC)
    token = place // pitch * TC + jnp.clip(column, 0, TC - 1)
    source = token // own_count
    k_outer = (source // inner) ^ (tile // inner)
    k_inner = (source % inner) ^ (tile % inner)
    spot = (k_inner * outer + -k_outer % outer) * own_count + token % own_count
    idx = jnp.broadcast_to(jnp.where(inside, spot, -1)[:, None], (padded_rows, LANES)).astype(jnp.int32)

    x_column, w_qkv_other, w_out_other, vecs, idx, own_stale, w_in = lax.optimization_barrier(
        (x_column, w_qkv_other, w_out_other, vecs, idx, own_stale, w_in)
    )
    x_column = jnp.concatenate([own_tokens] + x_column, axis=0)
    x_column, own_stale = lax.optimization_barrier((x_column, own_stale))
    x_pieces = [x_column] + [swapped(x_column, 0, k) for k in range(1, inner)]
    stale_column = across_outer(own_stale, outer)
    stale_line = [swapped(own_stale, 0, k) for k in range(1, inner)]
    w_0, w_1, wo_0, wo_1 = weights_in_vmem(w_qkv, w_qkv_other, w_out, w_out_other)
    x_pieces, stale_column, stale_line, w_0 = lax.optimization_barrier((x_pieces, stale_column, stale_line, w_0))
    stale_column = jnp.concatenate(stale_column, axis=0)
    x_pieces, stale_column = lax.optimization_barrier((x_pieces, stale_column))
    stale_pieces = [own_stale, stale_column] + stale_line + [swapped(stale_column, 0, k) for k in range(1, inner)]
    x, query, fresh, *parts = project(x_pieces, vecs, w_0)
    got_pieces = [lax.ppermute(part, "pipe", swap) for part in parts]
    x, modulated, fresh, send = first_block(stale_pieces, got_pieces, x, query, fresh, vecs, w_1, wo_0)
    got = lax.ppermute(send, "pipe", swap)
    x_tile, q_tile, sums, state = attend_fresh(x, modulated, fresh, idx, w_1)
    patches = tile_block(x_tile, q_tile, sums, state, got, idx, vecs, w_final.T, wo_1)
    patches, w_in = lax.optimization_barrier((patches, w_in))
    w_patch = dot(jnp.asarray(patch_selector(), BF16), w_in).astype(BF16)
    edge = patches
    if rows > 1:
        edge = jnp.where(first_core, patches[(rows - 1) * pitch : rows * pitch], patches[:pitch])
    got = lax.ppermute(edge, "pipe", swap)
    return decode(rows, cols, pitch, patches, got, idx, w_patch, b_in[None], b_up[None], w_up)


def solution(mesh):
    placed = (
        P(None, ("grp", "patch"), None),
        P("pipe", None, ("grp", "patch"), None),
        P("pipe", None, None),
        P("pipe", None, None),
        P("pipe", None, None),
        P(),
        P("grp"),
        P(),
        P(),
        P(),
        P(),
        P(),
    )
    return jax.shard_map(
        local,
        mesh=mesh,
        in_specs=placed,
        out_specs=P(("grp", "pipe"), "patch", None),
        check_vma=False,
    )
```

```python
import functools
import math

import jax
import jax.numpy as jnp
import numpy as np
from jax import lax
from jax.experimental import pallas as pl
from jax.experimental.pallas import tpu as pltpu
from jax.sharding import PartitionSpec as P

D = 1152
DH = 72
HEADS = 8
CH = 512
LATC = 4
TC = 256
DA = 576
DP = 640
SHIFT = 64
EPSILON = 1e-06
QUERY_SCALE = math.log2(math.e) / math.sqrt(DH)
BLOCK = 256
SMALL_BLOCK = 64
LANES = 128

F32 = jnp.float32
BF16 = jnp.bfloat16
VMEM = pl.BlockSpec(memory_space=pltpu.VMEM)
ANY = pl.BlockSpec(memory_space=pl.ANY)


def dot(a, b):
    return jnp.dot(a, b, preferred_element_type=F32)


def dot_t(a, b):
    return lax.dot_general(a, b, (((1,), (1,)), ((), ())), preferred_element_type=F32)


def normed(values, scale, shift):
    average = jnp.mean(values, axis=-1, keepdims=True)
    centred = values - average
    variance = jnp.mean(centred * centred, axis=-1, keepdims=True)
    return (centred * lax.rsqrt(variance + EPSILON) * scale + shift).astype(BF16)


def lane_window(start):
    return start // LANES * LANES, -(-(start + DH) // LANES) * LANES


def head_scores(query, kv_ref, head):
    first, last = lane_window(head * DH)
    lane = lax.broadcasted_iota(jnp.int32, (query.shape[0], last - first), 1) + first
    own = (lane >= head * DH) & (lane < (head + 1) * DH)
    return dot_t(jnp.where(own, query[:, first:last], jnp.zeros((), BF16)), kv_ref[:, first:last])


def value_window(head):
    return lane_window(DA + head * DH)


def weigh(exponent, kv_ref, head):
    first, last = value_window(head)
    return dot(exponent.astype(BF16), kv_ref[:, first:last])


def spread(outs):
    pieces = [None] * (DP // LANES)
    for head, out in enumerate(outs):
        first, last = value_window(head)
        start = DA + head * DH
        lane = lax.broadcasted_iota(jnp.int32, out.shape, 1) + first
        out = jnp.where((lane >= start) & (lane < start + DH), out, 0.0)
        for i in range((last - first) // LANES):
            at = (first - (DA - SHIFT)) // LANES + i
            part = out[:, i * LANES : (i + 1) * LANES]
            pieces[at] = part if pieces[at] is None else pieces[at] + part
    return jnp.concatenate(pieces, axis=1)


def attend(query, kv_ref):
    outs = []
    for head in range(HEADS):
        scores = head_scores(query, kv_ref, head)
        exponent = jnp.exp2(scores - jnp.max(scores, axis=1, keepdims=True))
        total = jnp.sum(exponent, axis=1, keepdims=True)
        outs.append(weigh(exponent, kv_ref, head) * (1.0 / total))
    return spread(outs)


def attend_begin(query, kv_ref):
    outs = []
    lane = lax.broadcasted_iota(jnp.int32, (query.shape[0], LANES), 1)
    state = jnp.zeros((query.shape[0], LANES), F32)
    for head in range(HEADS):
        scores = head_scores(query, kv_ref, head)
        top = jnp.max(scores, axis=1, keepdims=True)
        exponent = jnp.exp2(scores - top)
        total = jnp.sum(exponent, axis=1, keepdims=True)
        outs.append(weigh(exponent, kv_ref, head))
        state = jnp.where(lane == head, top, jnp.where(lane == HEADS + head, total, state))
    return spread(outs), state


def attend_end(query, kv_ref, sums, state):
    outs = []
    for head in range(HEADS):
        scores = head_scores(query, kv_ref, head)
        before, total = state[:, head : head + 1], state[:, HEADS + head : HEADS + head + 1]
        top = jnp.maximum(before, jnp.max(scores, axis=1, keepdims=True))
        exponent = jnp.exp2(scores - top)
        keep = jnp.exp2(before - top)
        total = keep * total + jnp.sum(exponent, axis=1, keepdims=True)
        first, last = value_window(head)
        earlier = sums[:, first - (DA - SHIFT) : last - (DA - SHIFT)]
        outs.append((keep * earlier + weigh(exponent, kv_ref, head)) * (1.0 / total))
    return spread(outs)


def each_block(count, body):
    if count <= BLOCK:
        body(0, count)
    else:

        @pl.loop(0, count // SMALL_BLOCK)
        def _(i):
            body(pl.multiple_of(i * SMALL_BLOCK, SMALL_BLOCK), SMALL_BLOCK)


def params(count):
    return pltpu.CompilerParams(vmem_limit_bytes=(24 if count <= BLOCK else 56) * 1024 * 1024)


def weights_kernel(own_ref, other_ref, wo_own, wo_other, w0_ref, w1_ref, wo0_ref, wo1_ref, sems):
    first = lax.axis_index("pipe") == 0
    pad = jnp.zeros((SHIFT, D), BF16)
    wo0_ref[:SHIFT] = pad
    wo1_ref[:SHIFT] = pad
    outs = (wo0_ref.at[SHIFT:], wo1_ref.at[SHIFT:])
    copies = []
    for i, (in_place, arrived, targets) in enumerate(
        ((own_ref.at[0], other_ref.at[0], (w0_ref, w1_ref)), (wo_own.at[0], wo_other.at[0], outs))
    ):
        for block in range(2):
            own = (first if block == 0 else jnp.logical_not(first))
            sem = sems.at[2 * i + block]
            copies.append(pltpu.make_async_copy(in_place, targets[block], sem))

            @pl.when(own)
            def _():
                pltpu.make_async_copy(in_place, targets[block], sem).start()

            @pl.when(jnp.logical_not(own))
            def _():
                pltpu.make_async_copy(arrived, targets[block], sem).start()

    for copy in copies:
        copy.wait()


def weights_in_vmem(w_own, w_other, wo_own, wo_other):
    return pl.pallas_call(
        weights_kernel,
        out_shape=(jax.ShapeDtypeStruct((3 * DA, D), BF16),) * 2 + (jax.ShapeDtypeStruct((DP, D), BF16),) * 2,
        in_specs=[ANY] * 4,
        out_specs=(VMEM,) * 4,
        scratch_shapes=[pltpu.SemaphoreType.DMA((4,))],
        compiler_params=params(0),
        name="weights_by_block",
    )(in_hbm(w_own), w_other, in_hbm(wo_own), wo_other)


def query_of(modulated, w_ref):
    projected = dot_t(modulated, w_ref[:DP]) * QUERY_SCALE
    lane = lax.broadcasted_iota(jnp.int32, projected.shape, 1)
    return jnp.where(lane < DA, projected, 0.0).astype(BF16)


def join(refs, target):
    at = 0
    for ref in refs:
        rows = ref.shape[0]
        target[at : at + rows] = ref[...]
        at += rows


def project_kernel(n_pieces, *refs):
    piece_refs = refs[:n_pieces]
    vec_ref, w_ref, x_ref, q_ref, kv_ref = refs[n_pieces : n_pieces + 5]
    part_refs = refs[n_pieces + 5 :]
    join(piece_refs, x_ref)

    def body(start, size):
        rows = pl.ds(start, size)
        modulated = normed(x_ref[rows].astype(F32), vec_ref[1:2], vec_ref[0:1])
        kv_ref[rows] = dot_t(modulated, w_ref[DA:]).astype(BF16)
        q_ref[rows] = query_of(modulated, w_ref)

    each_block(x_ref.shape[0], body)
    at = 0
    for ref in part_refs:
        rows = ref.shape[0]
        ref[...] = kv_ref[at : at + rows]
        at += rows


def project(pieces, vecs, weights):
    count = sum(piece.shape[0] for piece in pieces)
    parts = (count // 4,) * 4
    return pl.pallas_call(
        functools.partial(project_kernel, len(pieces)),
        out_shape=(
            jax.ShapeDtypeStruct((count, D), BF16),
            jax.ShapeDtypeStruct((count, DP), BF16),
            jax.ShapeDtypeStruct((count, 2 * DA), BF16),
        )
        + tuple(jax.ShapeDtypeStruct((part, 2 * DA), BF16) for part in parts),
        in_specs=[VMEM] * (len(pieces) + 2),
        out_specs=(VMEM,) * 7,
        compiler_params=params(count),
        name="layer_norm_and_projections",
    )(*pieces, vecs, weights)


def in_hbm(array):
    return pltpu.with_memory_space_constraint(array, pltpu.HBM)


def fresh_kernel(x_ref, mod_ref, kv_ref, idx_ref, w_ref, xt_ref, qt_ref, sum_ref, state_ref, pick_ref):
    tile_rows = idx_ref.shape[0]
    pick_ref[...] = jnp.zeros_like(pick_ref)

    def body(start, size):
        rows = pl.ds(start, size)
        lane = lax.broadcasted_iota(jnp.int32, (tile_rows, size), 1) + start
        chosen = (lane == idx_ref[:, :1]).astype(F32).astype(BF16)
        pick_ref[0] += dot(chosen, mod_ref[rows])
        pick_ref[1] += dot(chosen, x_ref[rows])

    each_block(x_ref.shape[0], body)
    query = query_of(pick_ref[0].astype(BF16), w_ref)
    sum_ref[...], state_ref[...] = attend_begin(query, kv_ref)
    qt_ref[...] = query
    xt_ref[...] = pick_ref[1].astype(BF16)


def attend_fresh(x, modulated, kv, idx, w_block):
    rows = idx.shape[0]
    return pl.pallas_call(
        fresh_kernel,
        out_shape=(
            jax.ShapeDtypeStruct((rows, D), BF16),
            jax.ShapeDtypeStruct((rows, DP), BF16),
            jax.ShapeDtypeStruct((rows, DP), F32),
            jax.ShapeDtypeStruct((rows, LANES), F32),
        ),
        in_specs=[VMEM] * 5,
        out_specs=(VMEM,) * 4,
        scratch_shapes=[pltpu.VMEM((2, rows, D), F32)],
        compiler_params=params(kv.shape[0]),
        name="tile_attention_over_own_keys",
    )(x, modulated, kv, idx, w_block)


def block_kernel(n_pieces, n_got, *refs):
    stale_refs = refs[:n_pieces]
    got_refs = refs[n_pieces : n_pieces + n_got]
    (
        x_ref, q_ref, kv_ref, vec_ref, w1_ref, wo_ref, x1_ref, mod_ref, kv1_ref, send_ref, all_ref,
    ) = refs[n_pieces + n_got :]
    count = x_ref.shape[0]
    first_core = lax.axis_index("pipe") == 0
    join(stale_refs, send_ref)
    all_ref[:count] = kv_ref[...]

    @pl.when(first_core)
    def _():
        join(stale_refs, all_ref.at[count:])

    @pl.when(jnp.logical_not(first_core))
    def _():
        join(got_refs, all_ref.at[count:])


    def body(start, size):
        rows = pl.ds(start, size)
        attended = attend(q_ref[rows], all_ref).astype(BF16)
        branch = dot(attended, wo_ref[...])
        x1 = (x_ref[rows].astype(F32) + vec_ref[2:3] * branch).astype(BF16)
        modulated = normed(x1.astype(F32), vec_ref[4:5], vec_ref[3:4])
        fresh = dot_t(modulated, w1_ref[DA:]).astype(BF16)
        kv1_ref[rows] = fresh

        @pl.when(first_core)
        def _():
            send_ref[rows] = fresh

        x1_ref[rows] = x1
        mod_ref[rows] = modulated

    each_block(count, body)


def first_block(stale_pieces, got_pieces, x, q, kv, vecs, w_next, wo_block):
    count = x.shape[0]
    return pl.pallas_call(
        functools.partial(block_kernel, len(stale_pieces), len(got_pieces)),
        out_shape=(
            jax.ShapeDtypeStruct((count, D), BF16),
            jax.ShapeDtypeStruct((count, D), BF16),
            jax.ShapeDtypeStruct((count, 2 * DA), BF16),
            jax.ShapeDtypeStruct((count, 2 * DA), BF16),
        ),
        in_specs=[VMEM] * (len(stale_pieces) + len(got_pieces) + 6),
        out_specs=(VMEM,) * 4,
        scratch_shapes=[pltpu.VMEM((2 * count, 2 * DA), BF16)],
        compiler_params=params(count),
        name="attention_and_next_keys",
    )(*stale_pieces, *got_pieces, x, q, kv, vecs, w_next, wo_block)


def tile_kernel(x_ref, q_ref, sum_ref, state_ref, got_ref, idx_ref, vec_ref, wf_ref, wo_ref, patch_ref):
    attended = attend_end(q_ref[...], got_ref, sum_ref[...], state_ref[...]).astype(BF16)
    branch = dot(attended, wo_ref[...])
    x2 = (x_ref[...].astype(F32) + vec_ref[5:6] * branch).astype(BF16)
    final = normed(x2.astype(F32), vec_ref[7:8], vec_ref[6:7])
    patches = dot_t(final, wf_ref[...]).astype(BF16).astype(F32)
    patch_ref[...] = jnp.zeros_like(patch_ref)
    patch_ref[:, : 4 * LATC] = jnp.where(idx_ref[:, :1] >= 0, patches, 0.0)


def tile_block(x, q, sums, state, got, idx, vecs, w_final, wo_block):
    return pl.pallas_call(
        tile_kernel,
        out_shape=jax.ShapeDtypeStruct((x.shape[0], LANES), F32),
        in_specs=[VMEM] * 9,
        out_specs=VMEM,
        compiler_params=params(got.shape[0]),
        name="tile_attention_and_patches",
    )(x, q, sums, state, got, idx, vecs, w_final, wo_block)


def decode_kernel(
    rows, cols, pitch, patch_ref, got_ref, idx_ref, wp_ref, bin_ref, bup_ref, w_ref, out_ref, f_ref, fb_ref, o_ref
):
    first_core = lax.axis_index("pipe") == 0
    got = got_ref[:pitch]
    above = jnp.where(first_core, 0.0, got)
    below = jnp.where(first_core, got, 0.0)
    rim = [above] + [patch_ref[r * pitch : (r + 1) * pitch] for r in range(rows)] + [below]
    column_in = idx_ref[:pitch, :1] >= 0
    shifted = [[pltpu.roll(p, (-ds) % pitch, 0) if ds else p for ds in (-1, 0, 1)] for p in rim]
    around = []
    for r in range(rows + 2):
        low, high = None, None
        for dr in (-1, 0, 1):
            if not 0 <= r + dr < rows + 2:
                continue
            for ds in range(3):
                tap = (dr + 1) * 3 + ds
                piece = shifted[r + dr][ds]
                if tap == 8:
                    high = piece
                else:
                    piece = pltpu.roll(piece, 4 * LATC * tap, 1) if tap else piece
                    low = piece if low is None else low + piece
        high = jnp.zeros_like(low) if high is None else high
        around.append(jnp.concatenate([low, high], axis=1))
    for p in range(2):
        first = 1 - p
        stacked = jnp.concatenate(around[first : first + rows + 1], axis=0).astype(BF16)
        for q in range(2):
            at = (2 * p + q) * 2 * LANES
            act = dot(stacked, wp_ref[at : at + 2 * LANES]) + bin_ref[...]
            feature = act / (1.0 + jnp.exp(-act))
            for i in range(rows + 1):
                y = 2 * (first + i - 1) + p + 1
                keep = column_in
                if y == 0:
                    keep = keep & jnp.logical_not(first_core)
                if y == 2 * rows + 1:
                    keep = keep & first_core
                kept = jnp.where(keep, feature[i * pitch : (i + 1) * pitch], 0.0)
                for c in range(CH // LANES):
                    part = kept[:, c * LANES : (c + 1) * LANES]
                    f_ref[y, c, pl.ds(RIM - 2 + q, pitch, stride=2), :] = part
    across = 2 * cols
    wide = feature_pitch(cols)
    for y in range(2 * rows + 2):
        for c in range(CH // LANES):
            fb_ref[y * wide : (y + 1) * wide, c * LANES : (c + 1) * LANES] = f_ref[y, c, :wide, :].astype(BF16)

    def product(dy, dx, first, count):
        return dot(fb_ref[first * wide : (first + count) * wide], w_ref[3 * dy + dx])

    sums = []
    for dx in range(3):
        before = product(0, dx, 0, 2 * rows + 1)
        middle = product(1, dx, 1, 2 * rows)
        after = product(2, dx, 1, 2 * rows + 1)

        def rows_of(total, y):
            return total[y * wide : (y + 1) * wide]

        sums.append(
            [
                rows_of(middle, y) + rows_of(before, y + odd) + rows_of(after, y + odd)
                for y in range(2 * rows)
                for odd in range(2)
            ]
        )
    for row in range(4 * rows):
        left, centre, right = (sums[dx][row] for dx in range(3))
        here = slice(RIM, RIM + across)
        even = (centre + right)[here] + left[RIM - 1 : RIM - 1 + across] + bup_ref[...]
        odd = (centre + left)[here] + right[RIM + 1 : RIM + 1 + across] + bup_ref[...]
        for c in range(CH // LANES):
            lanes = slice(c * LANES, (c + 1) * LANES)
            o_ref[row, c, pl.ds(0, across, stride=2), :] = even[:, lanes]
            o_ref[row, c, pl.ds(1, across, stride=2), :] = odd[:, lanes]
            out_ref[row, :, lanes] = o_ref[row, c, : 2 * across].astype(BF16)


RIM = 8


def feature_pitch(cols):
    return -(-(2 * cols + 2 * RIM) // 16) * 16


def decode(rows, cols, pitch, patches, got, idx, w_patch, b_in, b_up, w_up):
    return pl.pallas_call(
        functools.partial(decode_kernel, rows, cols, pitch),
        out_shape=jax.ShapeDtypeStruct((4 * rows, 4 * cols, CH), BF16),
        in_specs=[VMEM] * 7,
        out_specs=VMEM,
        scratch_shapes=[
            pltpu.VMEM((2 * rows + 2, CH // LANES, max(2 * pitch + RIM, feature_pitch(cols)), LANES), F32),
            pltpu.VMEM(((2 * rows + 2) * feature_pitch(cols), CH), BF16),
            pltpu.VMEM((4 * rows, CH // LANES, 4 * cols + RIM, LANES), F32),
        ],
        compiler_params=params(0),
        name="decoder_convolutions",
    )(patches, got, idx, w_patch, b_in, b_up, w_up)


def patch_selector():
    sel = np.zeros((2, 2, 3, 3, 2, 2, LATC, 9 * LATC), np.float32)
    for p, q, dr, ds, pp, qq in np.ndindex(2, 2, 3, 3, 2, 2):
        dy = 2 * (dr - 1) + pp - p
        dx = 2 * (ds - 1) + qq - q
        if abs(dy) <= 1 and abs(dx) <= 1:
            tap = (dy + 1) * 3 + dx + 1
            for c in range(LATC):
                sel[p, q, dr, ds, pp, qq, c, tap * LATC + c] = 1.0
    sel = sel.reshape(4, 9 * 4 * LATC, 9 * LATC)
    return np.pad(sel, ((0, 0), (0, 2 * LANES - 9 * 4 * LATC), (0, 0))).reshape(-1, 9 * LATC)


def split_of(n):
    inner = 2 ** (int(math.log2(n)) // 2)
    return n // inner, inner


def swapped(block, k_outer, k_inner):
    n = lax.axis_size("patch")
    _, inner = split_of(n)
    return lax.ppermute(block, "patch", [(i ^ (k_outer * inner + k_inner), i) for i in range(n)])


def local(
    tokens,
    stale_kv,
    w_qkv,
    w_out,
    block_table,
    time_table,
    t_index,
    w_final,
    w_in,
    b_in,
    w_up,
    b_up,
):
    section = lax.axis_index("pipe")
    tile = lax.axis_index("patch")
    n_tiles = lax.axis_size("patch")
    swap = [(0, 1), (1, 0)]
    first_core = section == 0
    own_count = tokens.shape[1]
    count = own_count * n_tiles
    rows = count // TC
    cols = TC // n_tiles
    pitch = -(-(cols + 3) // 8) * 8
    outer, inner = split_of(n_tiles)

    own_tokens = lax.dynamic_index_in_dim(tokens, section, 0, keepdims=False)
    w_qkv = jnp.swapaxes(w_qkv, 1, 2)
    w_qkv_other = lax.ppermute(w_qkv, "pipe", swap)
    tables = lax.all_gather(block_table[0], "pipe")
    x_column = [swapped(own_tokens, k, 0) for k in range(1, outer)]
    own_stale = stale_kv[0, 1]
    w_out_other = lax.ppermute(w_out, "pipe", swap)

    time_row = lax.dynamic_index_in_dim(time_table, t_index[0], 0, keepdims=False)
    ones = jnp.asarray([[0.0], [1.0], [0.0]], F32)
    vecs = jnp.concatenate(
        [
            time_row[:3] + tables[0] + ones,
            time_row[:3] + tables[1] + ones,
            time_row[3:5] + ones[:2],
        ],
        axis=0,
    )

    padded_rows = -(-rows * pitch // 16) * 16
    place = jnp.arange(padded_rows)
    column = place % pitch - 1 + tile * cols
    inside = (place % pitch < cols + 2) & (place < rows * pitch) & (column >= 0) & (column < TC)
    token = place // pitch * TC + jnp.clip(column, 0, TC - 1)
    source = token // own_count
    k_outer = (source // inner) ^ (tile // inner)
    k_inner = (source % inner) ^ (tile % inner)
    spot = (k_inner * outer + k_outer) * own_count + token % own_count
    idx = jnp.broadcast_to(jnp.where(inside, spot, -1)[:, None], (padded_rows, LANES)).astype(jnp.int32)

    x_column, w_qkv_other, w_out_other, vecs, idx, own_stale, w_in = lax.optimization_barrier(
        (x_column, w_qkv_other, w_out_other, vecs, idx, own_stale, w_in)
    )
    x_column = jnp.concatenate([own_tokens] + x_column, axis=0)
    x_column, own_stale = lax.optimization_barrier((x_column, own_stale))
    x_pieces = [x_column] + [swapped(x_column, 0, k) for k in range(1, inner)]
    stale_column = [swapped(own_stale, k, 0) for k in range(1, outer)]
    stale_line = [swapped(own_stale, 0, k) for k in range(1, inner)]
    w_0, w_1, wo_0, wo_1 = weights_in_vmem(w_qkv, w_qkv_other, w_out, w_out_other)
    x_pieces, stale_column, stale_line, w_0 = lax.optimization_barrier((x_pieces, stale_column, stale_line, w_0))
    stale_column = jnp.concatenate(stale_column, axis=0)
    x_pieces, stale_column = lax.optimization_barrier((x_pieces, stale_column))
    stale_pieces = [own_stale, stale_column] + stale_line + [swapped(stale_column, 0, k) for k in range(1, inner)]
    x, query, fresh, *parts = project(x_pieces, vecs, w_0)
    got_pieces = [lax.ppermute(part, "pipe", swap) for part in parts]
    x, modulated, fresh, send = first_block(stale_pieces, got_pieces, x, query, fresh, vecs, w_1, wo_0)
    got = lax.ppermute(send, "pipe", swap)
    x_tile, q_tile, sums, state = attend_fresh(x, modulated, fresh, idx, w_1)
    patches = tile_block(x_tile, q_tile, sums, state, got, idx, vecs, w_final.T, wo_1)
    patches, w_in = lax.optimization_barrier((patches, w_in))
    w_patch = dot(jnp.asarray(patch_selector(), BF16), w_in).astype(BF16)
    edge = patches
    if rows > 1:
        edge = jnp.where(first_core, patches[(rows - 1) * pitch : rows * pitch], patches[:pitch])
    got = lax.ppermute(edge, "pipe", swap)
    return decode(rows, cols, pitch, patches, got, idx, w_patch, b_in[None], b_up[None], w_up)


def solution(mesh):
    placed = (
        P(None, ("grp", "patch"), None),
        P("pipe", None, ("grp", "patch"), None),
        P("pipe", None, None),
        P("pipe", None, None),
        P("pipe", None, None),
        P(),
        P("grp"),
        P(),
        P(),
        P(),
        P(),
        P(),
    )
    return jax.shard_map(
        local,
        mesh=mesh,
        in_specs=placed,
        out_specs=P(("grp", "pipe"), "patch", None),
        check_vma=False,
    )
```

```python
import functools
import math

import jax
import jax.numpy as jnp
import numpy as np
from jax import lax
from jax.experimental import pallas as pl
from jax.experimental.pallas import tpu as pltpu
from jax.sharding import PartitionSpec as P

D = 1152
DH = 72
HEADS = 8
CH = 512
LATC = 4
TC = 256
DA = 576
DP = 640
SHIFT = 64
EPSILON = 1e-06
QUERY_SCALE = math.log2(math.e) / math.sqrt(DH)
BLOCK = 256
SMALL_BLOCK = 64
LANES = 128

F32 = jnp.float32
BF16 = jnp.bfloat16
VMEM = pl.BlockSpec(memory_space=pltpu.VMEM)
ANY = pl.BlockSpec(memory_space=pl.ANY)


def dot(a, b):
    return jnp.dot(a, b, preferred_element_type=F32)


def dot_t(a, b):
    return lax.dot_general(a, b, (((1,), (1,)), ((), ())), preferred_element_type=F32)


def normed(values, scale, shift):
    average = jnp.mean(values, axis=-1, keepdims=True)
    centred = values - average
    variance = jnp.mean(centred * centred, axis=-1, keepdims=True)
    return (centred * lax.rsqrt(variance + EPSILON) * scale + shift).astype(BF16)


def lane_window(start):
    return start // LANES * LANES, -(-(start + DH) // LANES) * LANES


def head_scores(query, kv_ref, head):
    first, last = lane_window(head * DH)
    lane = lax.broadcasted_iota(jnp.int32, (query.shape[0], last - first), 1) + first
    own = (lane >= head * DH) & (lane < (head + 1) * DH)
    return dot_t(jnp.where(own, query[:, first:last], jnp.zeros((), BF16)), kv_ref[:, first:last])


def value_window(head):
    return lane_window(DA + head * DH)


def weigh(exponent, kv_ref, head):
    first, last = value_window(head)
    return dot(exponent.astype(BF16), kv_ref[:, first:last])


def spread(outs):
    pieces = [None] * (DP // LANES)
    for head, out in enumerate(outs):
        first, last = value_window(head)
        start = DA + head * DH
        lane = lax.broadcasted_iota(jnp.int32, out.shape, 1) + first
        out = jnp.where((lane >= start) & (lane < start + DH), out, 0.0)
        for i in range((last - first) // LANES):
            at = (first - (DA - SHIFT)) // LANES + i
            part = out[:, i * LANES : (i + 1) * LANES]
            pieces[at] = part if pieces[at] is None else pieces[at] + part
    return jnp.concatenate(pieces, axis=1)


def attend(query, kv_ref):
    outs = []
    for head in range(HEADS):
        scores = head_scores(query, kv_ref, head)
        exponent = jnp.exp2(scores - jnp.max(scores, axis=1, keepdims=True))
        total = jnp.sum(exponent, axis=1, keepdims=True)
        outs.append(weigh(exponent, kv_ref, head) * (1.0 / total))
    return spread(outs)


def attend_begin(query, kv_ref):
    outs = []
    lane = lax.broadcasted_iota(jnp.int32, (query.shape[0], LANES), 1)
    state = jnp.zeros((query.shape[0], LANES), F32)
    for head in range(HEADS):
        scores = head_scores(query, kv_ref, head)
        top = jnp.max(scores, axis=1, keepdims=True)
        exponent = jnp.exp2(scores - top)
        total = jnp.sum(exponent, axis=1, keepdims=True)
        outs.append(weigh(exponent, kv_ref, head))
        state = jnp.where(lane == head, top, jnp.where(lane == HEADS + head, total, state))
    return spread(outs), state


def attend_end(query, kv_ref, sums, state):
    outs = []
    for head in range(HEADS):
        scores = head_scores(query, kv_ref, head)
        before, total = state[:, head : head + 1], state[:, HEADS + head : HEADS + head + 1]
        top = jnp.maximum(before, jnp.max(scores, axis=1, keepdims=True))
        exponent = jnp.exp2(scores - top)
        keep = jnp.exp2(before - top)
        total = keep * total + jnp.sum(exponent, axis=1, keepdims=True)
        first, last = value_window(head)
        earlier = sums[:, first - (DA - SHIFT) : last - (DA - SHIFT)]
        outs.append((keep * earlier + weigh(exponent, kv_ref, head)) * (1.0 / total))
    return spread(outs)


def each_block(count, body):
    if count <= BLOCK:
        body(0, count)
    else:

        @pl.loop(0, count // SMALL_BLOCK)
        def _(i):
            body(pl.multiple_of(i * SMALL_BLOCK, SMALL_BLOCK), SMALL_BLOCK)


def params(count):
    return pltpu.CompilerParams(vmem_limit_bytes=(24 if count <= BLOCK else 56) * 1024 * 1024)


def weights_kernel(own_ref, other_ref, wo_own, wo_other, w0_ref, w1_ref, wo0_ref, wo1_ref, sems):
    first = lax.axis_index("pipe") == 0
    pad = jnp.zeros((SHIFT, D), BF16)
    wo0_ref[:SHIFT] = pad
    wo1_ref[:SHIFT] = pad
    outs = (wo0_ref.at[SHIFT:], wo1_ref.at[SHIFT:])
    copies = []
    for i, (in_place, arrived, targets) in enumerate(
        ((own_ref.at[0], other_ref.at[0], (w0_ref, w1_ref)), (wo_own.at[0], wo_other.at[0], outs))
    ):
        for block in range(2):
            own = (first if block == 0 else jnp.logical_not(first))
            sem = sems.at[2 * i + block]
            copies.append(pltpu.make_async_copy(in_place, targets[block], sem))

            @pl.when(own)
            def _():
                pltpu.make_async_copy(in_place, targets[block], sem).start()

            @pl.when(jnp.logical_not(own))
            def _():
                pltpu.make_async_copy(arrived, targets[block], sem).start()

    for copy in copies:
        copy.wait()


def weights_in_vmem(w_own, w_other, wo_own, wo_other):
    return pl.pallas_call(
        weights_kernel,
        out_shape=(jax.ShapeDtypeStruct((3 * DA, D), BF16),) * 2 + (jax.ShapeDtypeStruct((DP, D), BF16),) * 2,
        in_specs=[ANY] * 4,
        out_specs=(VMEM,) * 4,
        scratch_shapes=[pltpu.SemaphoreType.DMA((4,))],
        compiler_params=params(0),
        name="weights_by_block",
    )(in_hbm(w_own), w_other, in_hbm(wo_own), wo_other)


def query_of(modulated, w_ref):
    projected = dot_t(modulated, w_ref[:DP]) * QUERY_SCALE
    lane = lax.broadcasted_iota(jnp.int32, projected.shape, 1)
    return jnp.where(lane < DA, projected, 0.0).astype(BF16)


def join(refs, target):
    at = 0
    for ref in refs:
        rows = ref.shape[0]
        target[at : at + rows] = ref[...]
        at += rows


def project_kernel(n_pieces, *refs):
    piece_refs = refs[:n_pieces]
    vec_ref, w_ref, x_ref, q_ref, kv_ref = refs[n_pieces : n_pieces + 5]
    part_refs = refs[n_pieces + 5 :]
    join(piece_refs, x_ref)

    def body(start, size):
        rows = pl.ds(start, size)
        modulated = normed(x_ref[rows].astype(F32), vec_ref[1:2], vec_ref[0:1])
        kv_ref[rows] = dot_t(modulated, w_ref[DA:]).astype(BF16)
        q_ref[rows] = query_of(modulated, w_ref)

    each_block(x_ref.shape[0], body)
    at = 0
    for ref in part_refs:
        rows = ref.shape[0]
        ref[...] = kv_ref[at : at + rows]
        at += rows


def project(pieces, vecs, weights):
    count = sum(piece.shape[0] for piece in pieces)
    parts = (count // 4,) * 4
    return pl.pallas_call(
        functools.partial(project_kernel, len(pieces)),
        out_shape=(
            jax.ShapeDtypeStruct((count, D), BF16),
            jax.ShapeDtypeStruct((count, DP), BF16),
            jax.ShapeDtypeStruct((count, 2 * DA), BF16),
        )
        + tuple(jax.ShapeDtypeStruct((part, 2 * DA), BF16) for part in parts),
        in_specs=[VMEM] * (len(pieces) + 2),
        out_specs=(VMEM,) * 7,
        compiler_params=params(count),
        name="layer_norm_and_projections",
    )(*pieces, vecs, weights)


def in_hbm(array):
    return pltpu.with_memory_space_constraint(array, pltpu.HBM)


def fresh_kernel(x_ref, mod_ref, kv_ref, idx_ref, w_ref, xt_ref, qt_ref, sum_ref, state_ref, pick_ref):
    tile_rows = idx_ref.shape[0]
    pick_ref[...] = jnp.zeros_like(pick_ref)

    def body(start, size):
        rows = pl.ds(start, size)
        lane = lax.broadcasted_iota(jnp.int32, (tile_rows, size), 1) + start
        chosen = (lane == idx_ref[:, :1]).astype(F32).astype(BF16)
        pick_ref[0] += dot(chosen, mod_ref[rows])
        pick_ref[1] += dot(chosen, x_ref[rows])

    each_block(x_ref.shape[0], body)
    query = query_of(pick_ref[0].astype(BF16), w_ref)
    sum_ref[...], state_ref[...] = attend_begin(query, kv_ref)
    qt_ref[...] = query
    xt_ref[...] = pick_ref[1].astype(BF16)


def attend_fresh(x, modulated, kv, idx, w_block):
    rows = idx.shape[0]
    return pl.pallas_call(
        fresh_kernel,
        out_shape=(
            jax.ShapeDtypeStruct((rows, D), BF16),
            jax.ShapeDtypeStruct((rows, DP), BF16),
            jax.ShapeDtypeStruct((rows, DP), F32),
            jax.ShapeDtypeStruct((rows, LANES), F32),
        ),
        in_specs=[VMEM] * 5,
        out_specs=(VMEM,) * 4,
        scratch_shapes=[pltpu.VMEM((2, rows, D), F32)],
        compiler_params=params(kv.shape[0]),
        name="tile_attention_over_own_keys",
    )(x, modulated, kv, idx, w_block)


def block_kernel(n_pieces, n_got, *refs):
    stale_refs = refs[:n_pieces]
    got_refs = refs[n_pieces : n_pieces + n_got]
    (
        x_ref, q_ref, kv_ref, vec_ref, w1_ref, wo_ref, x1_ref, mod_ref, kv1_ref, send_ref, all_ref,
    ) = refs[n_pieces + n_got :]
    count = x_ref.shape[0]
    first_core = lax.axis_index("pipe") == 0
    all_ref[:count] = kv_ref[...]

    @pl.when(first_core)
    def _():
        join(stale_refs, all_ref.at[count:])

    @pl.when(jnp.logical_not(first_core))
    def _():
        join(got_refs, all_ref.at[count:])
        join(stale_refs, send_ref)


    def body(start, size):
        rows = pl.ds(start, size)
        attended = attend(q_ref[rows], all_ref).astype(BF16)
        branch = dot(attended, wo_ref[...])
        x1 = (x_ref[rows].astype(F32) + vec_ref[2:3] * branch).astype(BF16)
        modulated = normed(x1.astype(F32), vec_ref[4:5], vec_ref[3:4])
        fresh = dot_t(modulated, w1_ref[DA:]).astype(BF16)
        kv1_ref[rows] = fresh

        @pl.when(first_core)
        def _():
            send_ref[rows] = fresh

        x1_ref[rows] = x1
        mod_ref[rows] = modulated

    each_block(count, body)


def first_block(stale_pieces, got_pieces, x, q, kv, vecs, w_next, wo_block):
    count = x.shape[0]
    return pl.pallas_call(
        functools.partial(block_kernel, len(stale_pieces), len(got_pieces)),
        out_shape=(
            jax.ShapeDtypeStruct((count, D), BF16),
            jax.ShapeDtypeStruct((count, D), BF16),
            jax.ShapeDtypeStruct((count, 2 * DA), BF16),
            jax.ShapeDtypeStruct((count, 2 * DA), BF16),
        ),
        in_specs=[VMEM] * (len(stale_pieces) + len(got_pieces) + 6),
        out_specs=(VMEM,) * 4,
        scratch_shapes=[pltpu.VMEM((2 * count, 2 * DA), BF16)],
        compiler_params=params(count),
        name="attention_and_next_keys",
    )(*stale_pieces, *got_pieces, x, q, kv, vecs, w_next, wo_block)


def tile_kernel(x_ref, q_ref, sum_ref, state_ref, got_ref, idx_ref, vec_ref, wf_ref, wo_ref, patch_ref):
    attended = attend_end(q_ref[...], got_ref, sum_ref[...], state_ref[...]).astype(BF16)
    branch = dot(attended, wo_ref[...])
    x2 = (x_ref[...].astype(F32) + vec_ref[5:6] * branch).astype(BF16)
    final = normed(x2.astype(F32), vec_ref[7:8], vec_ref[6:7])
    patches = dot_t(final, wf_ref[...]).astype(BF16).astype(F32)
    patch_ref[...] = jnp.zeros_like(patch_ref)
    patch_ref[:, : 4 * LATC] = jnp.where(idx_ref[:, :1] >= 0, patches, 0.0)


def tile_block(x, q, sums, state, got, idx, vecs, w_final, wo_block):
    return pl.pallas_call(
        tile_kernel,
        out_shape=jax.ShapeDtypeStruct((x.shape[0], LANES), F32),
        in_specs=[VMEM] * 9,
        out_specs=VMEM,
        compiler_params=params(got.shape[0]),
        name="tile_attention_and_patches",
    )(x, q, sums, state, got, idx, vecs, w_final, wo_block)


def decode_kernel(
    rows, cols, pitch, patch_ref, got_ref, idx_ref, wp_ref, bin_ref, bup_ref, w_ref, out_ref, f_ref, fb_ref, o_ref
):
    first_core = lax.axis_index("pipe") == 0
    got = got_ref[:pitch]
    above = jnp.where(first_core, 0.0, got)
    below = jnp.where(first_core, got, 0.0)
    rim = [above] + [patch_ref[r * pitch : (r + 1) * pitch] for r in range(rows)] + [below]
    column_in = idx_ref[:pitch, :1] >= 0
    shifted = [[pltpu.roll(p, (-ds) % pitch, 0) if ds else p for ds in (-1, 0, 1)] for p in rim]
    around = []
    for r in range(rows + 2):
        low, high = None, None
        for dr in (-1, 0, 1):
            if not 0 <= r + dr < rows + 2:
                continue
            for ds in range(3):
                tap = (dr + 1) * 3 + ds
                piece = shifted[r + dr][ds]
                if tap == 8:
                    high = piece
                else:
                    piece = pltpu.roll(piece, 4 * LATC * tap, 1) if tap else piece
                    low = piece if low is None else low + piece
        high = jnp.zeros_like(low) if high is None else high
        around.append(jnp.concatenate([low, high], axis=1))
    for p in range(2):
        first = 1 - p
        stacked = jnp.concatenate(around[first : first + rows + 1], axis=0).astype(BF16)
        for q in range(2):
            at = (2 * p + q) * 2 * LANES
            act = dot(stacked, wp_ref[at : at + 2 * LANES]) + bin_ref[...]
            feature = act / (1.0 + jnp.exp(-act))
            for i in range(rows + 1):
                y = 2 * (first + i - 1) + p + 1
                keep = column_in
                if y == 0:
                    keep = keep & jnp.logical_not(first_core)
                if y == 2 * rows + 1:
                    keep = keep & first_core
                kept = jnp.where(keep, feature[i * pitch : (i + 1) * pitch], 0.0)
                for c in range(CH // LANES):
                    part = kept[:, c * LANES : (c + 1) * LANES]
                    f_ref[y, c, pl.ds(RIM - 2 + q, pitch, stride=2), :] = part
    across = 2 * cols
    wide = feature_pitch(cols)
    for y in range(2 * rows + 2):
        for c in range(CH // LANES):
            fb_ref[y * wide : (y + 1) * wide, c * LANES : (c + 1) * LANES] = f_ref[y, c, :wide, :].astype(BF16)

    def product(dy, dx, first, count):
        return dot(fb_ref[first * wide : (first + count) * wide], w_ref[3 * dy + dx])

    sums = []
    for dx in range(3):
        before = product(0, dx, 0, 2 * rows + 1)
        middle = product(1, dx, 1, 2 * rows)
        after = product(2, dx, 1, 2 * rows + 1)

        def rows_of(total, y):
            return total[y * wide : (y + 1) * wide]

        sums.append(
            [
                rows_of(middle, y) + rows_of(before, y + odd) + rows_of(after, y + odd)
                for y in range(2 * rows)
                for odd in range(2)
            ]
        )
    for row in range(4 * rows):
        left, centre, right = (sums[dx][row] for dx in range(3))
        here = slice(RIM, RIM + across)
        even = (centre + right)[here] + left[RIM - 1 : RIM - 1 + across] + bup_ref[...]
        odd = (centre + left)[here] + right[RIM + 1 : RIM + 1 + across] + bup_ref[...]
        for c in range(CH // LANES):
            lanes = slice(c * LANES, (c + 1) * LANES)
            o_ref[row, c, pl.ds(0, across, stride=2), :] = even[:, lanes]
            o_ref[row, c, pl.ds(1, across, stride=2), :] = odd[:, lanes]
            out_ref[row, :, lanes] = o_ref[row, c, : 2 * across].astype(BF16)


RIM = 8


def feature_pitch(cols):
    return -(-(2 * cols + 2 * RIM) // 16) * 16


def decode(rows, cols, pitch, patches, got, idx, w_patch, b_in, b_up, w_up):
    return pl.pallas_call(
        functools.partial(decode_kernel, rows, cols, pitch),
        out_shape=jax.ShapeDtypeStruct((4 * rows, 4 * cols, CH), BF16),
        in_specs=[VMEM] * 7,
        out_specs=VMEM,
        scratch_shapes=[
            pltpu.VMEM((2 * rows + 2, CH // LANES, max(2 * pitch + RIM, feature_pitch(cols)), LANES), F32),
            pltpu.VMEM(((2 * rows + 2) * feature_pitch(cols), CH), BF16),
            pltpu.VMEM((4 * rows, CH // LANES, 4 * cols + RIM, LANES), F32),
        ],
        compiler_params=params(0),
        name="decoder_convolutions",
    )(patches, got, idx, w_patch, b_in, b_up, w_up)


def patch_selector():
    sel = np.zeros((2, 2, 3, 3, 2, 2, LATC, 9 * LATC), np.float32)
    for p, q, dr, ds, pp, qq in np.ndindex(2, 2, 3, 3, 2, 2):
        dy = 2 * (dr - 1) + pp - p
        dx = 2 * (ds - 1) + qq - q
        if abs(dy) <= 1 and abs(dx) <= 1:
            tap = (dy + 1) * 3 + dx + 1
            for c in range(LATC):
                sel[p, q, dr, ds, pp, qq, c, tap * LATC + c] = 1.0
    sel = sel.reshape(4, 9 * 4 * LATC, 9 * LATC)
    return np.pad(sel, ((0, 0), (0, 2 * LANES - 9 * 4 * LATC), (0, 0))).reshape(-1, 9 * LATC)


def split_of(n):
    inner = 2 ** (int(math.log2(n)) // 2)
    return n // inner, inner


def swapped(block, k_outer, k_inner):
    n = lax.axis_size("patch")
    _, inner = split_of(n)
    return lax.ppermute(block, "patch", [(i ^ (k_outer * inner + k_inner), i) for i in range(n)])


def local(
    tokens,
    stale_kv,
    w_qkv,
    w_out,
    block_table,
    time_table,
    t_index,
    w_final,
    w_in,
    b_in,
    w_up,
    b_up,
):
    section = lax.axis_index("pipe")
    tile = lax.axis_index("patch")
    n_tiles = lax.axis_size("patch")
    swap = [(0, 1), (1, 0)]
    first_core = section == 0
    own_count = tokens.shape[1]
    count = own_count * n_tiles
    rows = count // TC
    cols = TC // n_tiles
    pitch = -(-(cols + 3) // 8) * 8
    outer, inner = split_of(n_tiles)

    own_tokens = lax.dynamic_index_in_dim(tokens, section, 0, keepdims=False)
    w_qkv = jnp.swapaxes(w_qkv, 1, 2)
    w_qkv_other = lax.ppermute(w_qkv, "pipe", swap)
    tables = lax.all_gather(block_table[0], "pipe")
    x_column = [swapped(own_tokens, k, 0) for k in range(1, outer)]
    own_stale = stale_kv[0, 1]
    w_out_other = lax.ppermute(w_out, "pipe", swap)

    time_row = lax.dynamic_index_in_dim(time_table, t_index[0], 0, keepdims=False)
    ones = jnp.asarray([[0.0], [1.0], [0.0]], F32)
    vecs = jnp.concatenate(
        [
            time_row[:3] + tables[0] + ones,
            time_row[:3] + tables[1] + ones,
            time_row[3:5] + ones[:2],
        ],
        axis=0,
    )

    padded_rows = -(-rows * pitch // 16) * 16
    place = jnp.arange(padded_rows)
    column = place % pitch - 1 + tile * cols
    inside = (place % pitch < cols + 2) & (place < rows * pitch) & (column >= 0) & (column < TC)
    token = place // pitch * TC + jnp.clip(column, 0, TC - 1)
    source = token // own_count
    k_outer = (source // inner) ^ (tile // inner)
    k_inner = (source % inner) ^ (tile % inner)
    spot = (k_inner * outer + k_outer) * own_count + token % own_count
    idx = jnp.broadcast_to(jnp.where(inside, spot, -1)[:, None], (padded_rows, LANES)).astype(jnp.int32)

    x_column, w_qkv_other, w_out_other, vecs, idx, own_stale, w_in = lax.optimization_barrier(
        (x_column, w_qkv_other, w_out_other, vecs, idx, own_stale, w_in)
    )
    x_column = jnp.concatenate([own_tokens] + x_column, axis=0)
    x_column, own_stale = lax.optimization_barrier((x_column, own_stale))
    x_pieces = [x_column] + [swapped(x_column, 0, k) for k in range(1, inner)]
    stale_column = [swapped(own_stale, k, 0) for k in range(1, outer)]
    stale_line = [swapped(own_stale, 0, k) for k in range(1, inner)]
    w_0, w_1, wo_0, wo_1 = weights_in_vmem(w_qkv, w_qkv_other, w_out, w_out_other)
    x_pieces, stale_column, stale_line, w_0 = lax.optimization_barrier((x_pieces, stale_column, stale_line, w_0))
    stale_column = jnp.concatenate(stale_column, axis=0)
    x_pieces, stale_column = lax.optimization_barrier((x_pieces, stale_column))
    stale_pieces = [own_stale, stale_column] + stale_line + [swapped(stale_column, 0, k) for k in range(1, inner)]
    x, query, fresh, *parts = project(x_pieces, vecs, w_0)
    got_pieces = [lax.ppermute(part, "pipe", swap) for part in parts]
    x, modulated, fresh, send = first_block(stale_pieces, got_pieces, x, query, fresh, vecs, w_1, wo_0)
    got = lax.ppermute(send, "pipe", swap)
    x_tile, q_tile, sums, state = attend_fresh(x, modulated, fresh, idx, w_1)
    patches = tile_block(x_tile, q_tile, sums, state, got, idx, vecs, w_final.T, wo_1)
    patches, w_in = lax.optimization_barrier((patches, w_in))
    w_patch = dot(jnp.asarray(patch_selector(), BF16), w_in).astype(BF16)
    edge = patches
    if rows > 1:
        edge = jnp.where(first_core, patches[(rows - 1) * pitch : rows * pitch], patches[:pitch])
    got = lax.ppermute(edge, "pipe", swap)
    return decode(rows, cols, pitch, patches, got, idx, w_patch, b_in[None], b_up[None], w_up)


def solution(mesh):
    placed = (
        P(None, ("grp", "patch"), None),
        P("pipe", None, ("grp", "patch"), None),
        P("pipe", None, None),
        P("pipe", None, None),
        P("pipe", None, None),
        P(),
        P("grp"),
        P(),
        P(),
        P(),
        P(),
        P(),
    )
    return jax.shard_map(
        local,
        mesh=mesh,
        in_specs=placed,
        out_specs=P(("grp", "pipe"), "patch", None),
        check_vma=False,
    )
```
